32 devices in a mesh: dp: 4 (over x, core), head: 8 (over z, y).
Axes of the slice: x: 2, y: 2, z: 4, core: 2. Of those that a mesh axis runs over, the one named last changes fastest.
Arguments:
- hidden: bfloat16 [2048, 1536], P('dp'), may hold values from -6 to 6
- token_prompt: int32 [2048], replicated, may hold values from 0 to 7, never falling along the last dimension, each value on 1 to 512 neighbouring positions
- request_prompt: int32 [16], P('dp'), may hold values from 0 to 7
- in_gain: float32 [1536], replicated, may hold values from 0.1 to 1.9
- w_zx: float32 [1536, 2, 3072], P('dp', None, 'head'), may hold values from -0.15625 to 0.15625
- w_bc: float32 [1536, 256], P('dp'), may hold values from -0.0390625 to 0.0390625
- w_dt: float32 [1536, 48], P('dp', 'head'), may hold values from -0.15625 to 0.15625
- dt_bias: float32 [48], P('head'), may hold values from -3 to -0.5
- a_log: float32 [48], P('head'), may hold values from -9.5 to -1.6
- conv_x: float32 [4, 3072], P(None, 'head'), may hold values from -3 to 3
- conv_bc: float32 [4, 256], replicated, may hold values from -3 to 3
- skip_gain: float32 [48], P('head'), may hold values from 0.5 to 2
- out_gain: float32 [3072], P('head'), may hold values from 0.1 to 1.9
- w_out: bfloat16 [3072, 1536], P('head'), may hold values from -0.109375 to 0.109375
Outputs:
- layer_out: bfloat16 [2048, 1536], P(('dp', 'head'))
- request_states: float32 [16, 48, 64, 128], P('dp', 'head')
The draws below stay inside these ranges and needn't reach their ends.
Inputs may be any that keep to these rules, and one draw needn't show every extreme that they name: `token_prompt`: prompt ids never fall along the tokens; each of the 8 prompts has at least one token.
All inputs are finite; a program needn't handle non-finite values.
Results may differ from the reference program's by a relative error of at most 0.012.
Values may be sent and summed in bfloat16 or wider, within the bound.
No kernel may reach another device: no remote copies, remote signals or barrier semaphores. Data moves between devices by JAX's collectives and lax.ppermute only.
A program may use at most 64 MiB of HBM per device.

```python
import math
import jax
import jax.numpy as jnp
import numpy as np
from jax import lax

D = 1536
HEADS = 48
HDIM = 64
NSTATE = 128
KCONV = 4
BLOCK = 256
PROMPTS = 8
INNER = 3072
TOKENS = 2048
REQUESTS = 16


def set_ends(drawn, own_key, low, high):
    longest = drawn.shape.index(max(drawn.shape))
    spots = []
    for shift in (0, 1):
        where = [jax.random.randint(jax.random.fold_in(own_key, axis), (), 0, length) for axis, length in enumerate(drawn.shape)]
        where[longest] = (where[longest] + shift) % drawn.shape[longest]
        spots.append(tuple(where))
    return drawn.at[spots[0]].set(low).at[spots[1]].set(high)


def block_scale(stream_key, shape, split, smallest, top_value):
    gain, own = 1.0, jax.random.fold_in(stream_key, 6)
    for dim, parts in split:
        draws = jnp.exp(jax.random.uniform(jax.random.fold_in(own, dim), (parts,), jnp.float32, smallest / len(split), top_value / len(split)))
        gain = gain * jnp.repeat(draws, shape[dim] // parts).reshape([-1 if axis == dim else 1 for axis in range(len(shape))])
    return gain


def length_profile(count, total, reach, skew):
    loads = [(1 << 20) // math.isqrt(grade ** skew) + 1 for grade in range(2, count + 1)]
    rest, given = total - reach - (count - 1), [1] * (count - 1)
    while rest > 0:
        movable = [i for i in range(count - 1) if given[i] < reach]
        pool, remaining = sum([loads[i] for i in movable]), rest
        for i in movable:
            extra = min(reach - given[i], max(1, remaining * loads[i] // pool), rest)
            given[i] = given[i] + extra
            rest = rest - extra
    return np.array([reach] + given)


def uneven(key, amount, total, most, skew):
    if amount == 2:
        one = jax.random.randint(key, (), max(1, total - most), min(most, total - 1) + 1)
        return jnp.stack([one, total - one])
    tallies = jnp.asarray(length_profile(amount, total, most, skew), jnp.int32)
    twos = (amount - 1) // 2
    source_of, receiver = tallies[1:1 + 2 * twos:2], tallies[2:2 + 2 * twos:2]
    room = jnp.minimum(source_of - 1, most - receiver)
    moved = jax.random.randint(jax.random.fold_in(key, 1), (twos,), 0, 1 << 20) % (room + 1)
    tallies = tallies.at[1:1 + 2 * twos:2].set(source_of - moved).at[2:2 + 2 * twos:2].set(receiver + moved)
    return tallies[jax.random.permutation(jax.random.fold_in(key, 2), amount)]


def bell_draw(rng, dims, scale, most, shards=(), kind=jnp.bfloat16):
    level = block_scale(rng, dims, shards, -0.22, 0.18) if shards else 1.0
    result = jax.random.normal(rng, dims, jnp.float32) * scale * level
    return jnp.minimum(jnp.maximum(result, -most), most).astype(kind)


def setup_inputs(seed: int = 0) -> dict:
    seeds = jax.random.split(jax.random.key(seed), 15)
    hidden = bell_draw(seeds[0], (TOKENS, D), 1.0, 6.0, ((0, 4),))
    token_prompt = jnp.searchsorted(jnp.cumsum(uneven(seeds[1], PROMPTS, TOKENS, TOKENS // 4, 2)), jnp.arange(TOKENS), side="right").astype(jnp.int32)
    request_prompt = set_ends(jax.random.randint(seeds[2], (REQUESTS,), 0, PROMPTS), jax.random.fold_in(seeds[2], 1), 0, PROMPTS - 1).astype(jnp.int32)
    in_gain = jnp.clip(1.0 + 0.18 * jax.random.normal(seeds[3], (D,), jnp.float32), 0.1, 1.9)
    w_zx = bell_draw(seeds[4], (D, 2, INNER), D ** -0.5, 0.15625, ((0, 4), (2, 8)), jnp.float32)
    w_bc = bell_draw(seeds[5], (D, 2 * NSTATE), (16 * D) ** -0.5, 0.0390625, ((0, 4),), jnp.float32)
    w_dt = bell_draw(seeds[6], (D, HEADS), D ** -0.5, 0.15625, ((0, 4), (1, 8)), jnp.float32)
    dt_bias = jnp.clip(-3.0 + 2.5 * jax.random.uniform(seeds[7], (HEADS,), jnp.float32) ** block_scale(seeds[7], (HEADS,), ((0, 8),), -0.2, 0.2), -3.0, -0.5)
    a_log = jnp.clip(-9.5 + 7.9 * jax.random.uniform(seeds[8], (HEADS,), jnp.float32) ** block_scale(seeds[8], (HEADS,), ((0, 8),), -0.2, 0.2), -9.5, -1.6)
    conv_x = bell_draw(seeds[9], (KCONV, INNER), KCONV ** -0.5, 3.0, ((1, 8),), jnp.float32)
    conv_bc = bell_draw(seeds[10], (KCONV, 2 * NSTATE), KCONV ** -0.5, 3.0, (), jnp.float32)
    skip_gain = jnp.clip(0.5 + 1.5 * jax.random.uniform(seeds[11], (HEADS,), jnp.float32) ** block_scale(seeds[11], (HEADS,), ((0, 8),), -0.2, 0.2), 0.5, 2.0)
    out_gain = jnp.clip(1.0 + 0.18 * jax.random.normal(seeds[12], (INNER,), jnp.float32), 0.1, 1.9)
    w_out = bell_draw(seeds[13], (INNER, D), INNER ** -0.5, 0.109375, ((0, 8),))
    return {"hidden": hidden, "token_prompt": token_prompt, "request_prompt": request_prompt, "in_gain": in_gain, "w_zx": w_zx, "w_bc": w_bc, "w_dt": w_dt, "dt_bias": dt_bias, "a_log": a_log, "conv_x": conv_x, "conv_bc": conv_bc, "skip_gain": skip_gain, "out_gain": out_gain, "w_out": w_out}


EPSILON = 1e-05

def rms_scale(values):
    return lax.rsqrt(lax.optimization_barrier(jnp.mean(values * values, axis=-1, keepdims=True)) + EPSILON)

def conv_core(extended, extended_ids, token_ids, weights):
    length = token_ids.shape[0]
    total = jnp.zeros((length, extended.shape[1]), jnp.float32)
    for offset in range(weights.shape[0]):
        same = (extended_ids[offset:offset + length] == token_ids)[:, None]
        total = total + jnp.where(same, weights[offset] * extended[offset:offset + length].astype(jnp.float32), 0.0)
    return jax.nn.silu(total).astype(jnp.bfloat16)

def causal_conv(signal, weights, token_ids):
    margin = weights.shape[0] - 1
    padded = jnp.concatenate([jnp.zeros((margin, signal.shape[1]), signal.dtype), signal], axis=0)
    padded_ids = jnp.concatenate([jnp.full((margin,), -1, jnp.int32), token_ids])
    return conv_core(padded, padded_ids, token_ids, weights)

def reference(hidden, token_prompt, request_prompt, in_gain, w_zx, w_bc, w_dt, dt_bias, a_log, conv_x, conv_bc, skip_gain, out_gain, w_out):
    hidden_f = hidden.astype(jnp.float32)
    normed = (hidden_f * rms_scale(hidden_f) * in_gain).astype(jnp.bfloat16)
    proj_zx = jnp.dot(normed, w_zx.astype(jnp.bfloat16).reshape(D, 2 * INNER), preferred_element_type=jnp.float32).astype(jnp.bfloat16)
    gate_z = proj_zx[:, :INNER]
    inner_x = proj_zx[:, INNER:]
    proj_bc = jnp.dot(normed, w_bc.astype(jnp.bfloat16), preferred_element_type=jnp.float32).astype(jnp.bfloat16)
    proj_dt = jnp.dot(normed, w_dt.astype(jnp.bfloat16), preferred_element_type=jnp.float32).astype(jnp.bfloat16)
    step_size = jax.nn.softplus(proj_dt.astype(jnp.float32) + dt_bias)
    rate = step_size * -jnp.exp(a_log)
    conv_inner = causal_conv(inner_x, conv_x, token_prompt)
    conv_bc_out = causal_conv(proj_bc, conv_bc, token_prompt)
    blocks = TOKENS // BLOCK
    x_heads = conv_inner.reshape(blocks, BLOCK, HEADS, HDIM)
    b_conv = conv_bc_out[:, :NSTATE].reshape(blocks, BLOCK, NSTATE)
    c_conv = conv_bc_out[:, NSTATE:].reshape(blocks, BLOCK, NSTATE)
    before_ids = jnp.concatenate([jnp.full((1,), -1, jnp.int32), token_prompt[BLOCK - 1:TOKENS - 1:BLOCK]])
    start_pos = jnp.arange(blocks, dtype=jnp.int32) * BLOCK
    prompt_ids = jnp.arange(PROMPTS, dtype=jnp.int32)
    last_index = (lax.optimization_barrier(jnp.sum((token_prompt[None, :] <= prompt_ids[:, None]).astype(jnp.int32), axis=1)) - 1).astype(jnp.int32)
    position = jnp.arange(BLOCK, dtype=jnp.int32)

    def advance(carry, inputs):
        state, table = carry
        x_blk, b_blk, c_blk, step_blk, rate_blk, ids_blk, before_id, start = inputs
        prefix = jnp.cumsum(rate_blk, axis=0)
        prefix_t = prefix.T
        same = (ids_blk[:, None] == ids_blk[None, :]) & (position[None, :] <= position[:, None])
        gaps = prefix_t[:, :, None] - prefix_t[:, None, :]
        decay = jnp.where(same[None], jnp.exp(jnp.where(same[None], gaps, 0.0)), 0.0)
        scores = jnp.dot(c_blk, b_blk.T, preferred_element_type=jnp.float32)
        mixing = (scores[None] * decay * step_blk.T[:, None, :]).astype(jnp.bfloat16)
        y_intra = jnp.einsum('hts,shp->thp', mixing.astype(jnp.float32), x_blk.astype(jnp.float32))
        entering = ids_blk == before_id
        inter_scale = jnp.where(entering[:, None], jnp.exp(prefix), 0.0)
        y_inter = inter_scale[:, :, None] * jnp.einsum('tn,hpn->thp', c_blk.astype(jnp.float32), state, precision=lax.Precision.HIGHEST)
        end_id = ids_blk[-1]
        alive = ids_blk == end_id
        weight_end = jnp.where(alive[None, :], jnp.exp(jnp.where(alive[None, :], prefix_t[:, -1:] - prefix_t, 0.0)), 0.0) * step_blk.T
        b_weighted = (weight_end[:, :, None] * b_blk.astype(jnp.float32)[None]).astype(jnp.bfloat16)
        local_state = jnp.einsum('hsn,shp->hpn', b_weighted.astype(jnp.float32), x_blk.astype(jnp.float32))
        carry_gain = jnp.where(end_id == before_id, jnp.exp(prefix_t[:, -1]), 0.0)
        local_last = last_index - start
        ends_here = (local_last >= 0) & (local_last < BLOCK)
        clipped = jnp.clip(local_last, 0, BLOCK - 1)

        def with_ends():
            prefix_last = prefix[clipped]
            pick = ends_here[:, None] & (ids_blk[None, :] == prompt_ids[:, None]) & (position[None, :] <= clipped[:, None])
            spans = prefix_last[:, :, None] - prefix_t[None]
            weight_last = jnp.where(pick[:, None, :], jnp.exp(jnp.where(pick[:, None, :], spans, 0.0)), 0.0) * step_blk.T[None]
            b_last = (weight_last[..., None] * b_blk.astype(jnp.float32)[None, None]).astype(jnp.bfloat16)
            last_local = jnp.einsum('ghsn,shp->ghpn', b_last.astype(jnp.float32), x_blk.astype(jnp.float32))
            last_gain = jnp.where((ends_here & (prompt_ids == before_id))[:, None], jnp.exp(prefix_last), 0.0)
            return last_local + last_gain[:, :, None, None] * state[None]

        def without_ends():
            return jnp.zeros(table.shape, jnp.float32)
        last_states = lax.cond(jnp.any(ends_here), with_ends, without_ends)
        new_state = carry_gain[:, None, None] * state + local_state
        return ((new_state, table + last_states), y_intra + y_inter)
    init = (jnp.zeros((HEADS, HDIM, NSTATE), jnp.float32), jnp.zeros((PROMPTS, HEADS, HDIM, NSTATE), jnp.float32))
    inputs = (x_heads, b_conv, c_conv, step_size.reshape(blocks, BLOCK, HEADS), rate.reshape(blocks, BLOCK, HEADS), token_prompt.reshape(blocks, BLOCK), before_ids, start_pos)
    (final_state, table), y_blocks = lax.scan(advance, init, inputs)
    ssd_out = y_blocks.reshape(TOKENS, HEADS, HDIM) + skip_gain[None, :, None] * conv_inner.astype(jnp.float32).reshape(TOKENS, HEADS, HDIM)
    gated = ssd_out.reshape(TOKENS, INNER) * jax.nn.silu(gate_z.astype(jnp.float32))
    normed_out = (gated * rms_scale(gated) * out_gain).astype(jnp.bfloat16)
    mixed = jnp.dot(normed_out, w_out, preferred_element_type=jnp.float32)
    layer_out = (hidden_f + mixed).astype(jnp.bfloat16)
    one_hot = (request_prompt[:, None] == prompt_ids[None, :]).astype(jnp.float32)
    request_states = jnp.einsum('rg,ghpn->rhpn', one_hot, table, precision=lax.Precision.HIGHEST)
    return (layer_out, request_states)
```

```python
import functools

import jax
import jax.numpy as jnp
from jax import lax
from jax.experimental import pallas as pl
from jax.experimental.pallas import tpu as pltpu
from jax.sharding import PartitionSpec as P

BLOCK = 256
PROMPTS = 8


EPSILON = 1e-05


def from_behind(shard, axis, by):
    peers = lax.axis_size(axis)
    pairs = [(i, i + by) for i in range(peers) if 0 <= i + by < peers]
    return lax.ppermute(shard, axis, pairs)


def carried_in(shard, axis, combine, identity):
    peers, position = (lax.axis_size(axis), lax.axis_index(axis))
    everything = jax.tree.map(lambda part: lax.all_gather(part, axis), shard)
    start = jax.tree.map(
        lambda part, zero: jnp.broadcast_to(jnp.asarray(zero, part.dtype), part.shape),
        shard,
        identity,
    )

    def step(k, before):
        reached = k < position
        new = combine(before, jax.tree.map(lambda part: part[k], everything))
        return jax.tree.map(lambda a, b: jnp.where(reached, a, b), new, before)

    return lax.fori_loop(0, peers, step, start)


def rms_scale(values):
    return lax.rsqrt(jnp.mean(values * values, axis=-1, keepdims=True) + EPSILON)


def conv_core(extended, extended_ids, token_ids, weights):
    length = token_ids.shape[0]
    total = jnp.zeros((length, extended.shape[1]), jnp.float32)
    for offset in range(weights.shape[0]):
        same = (extended_ids[offset : offset + length] == token_ids)[:, None]
        total = total + jnp.where(
            same, weights[offset] * extended[offset : offset + length].astype(jnp.float32), 0.0
        )
    return jax.nn.silu(total).astype(jnp.bfloat16)


def block_local(x_blk, b_blk, c_blk, step_blk, rate_blk, ids_blk, before_id):
    length = ids_blk.shape[0]
    position = jnp.arange(length, dtype=jnp.int32)
    prefix = jnp.cumsum(rate_blk, axis=0)
    prefix_t = prefix.T
    same = (ids_blk[:, None] == ids_blk[None, :]) & (position[None, :] <= position[:, None])
    gaps = prefix_t[:, :, None] - prefix_t[:, None, :]
    decay = jnp.where(same[None], jnp.exp(jnp.where(same[None], gaps, 0.0)), 0.0)
    scores = jnp.dot(c_blk, b_blk.T, preferred_element_type=jnp.float32)
    mixing = (scores[None] * decay * step_blk.T[:, None, :]).astype(jnp.bfloat16)
    y_intra = jnp.einsum("hts,shp->thp", mixing, x_blk, preferred_element_type=jnp.float32)
    end_id = ids_blk[-1]
    alive = ids_blk == end_id
    weight_end = (
        jnp.where(
            alive[None, :],
            jnp.exp(jnp.where(alive[None, :], prefix_t[:, -1:] - prefix_t, 0.0)),
            0.0,
        )
        * step_blk.T
    )
    b_weighted = (weight_end[:, :, None] * b_blk[None]).astype(jnp.bfloat16)
    local_state = jnp.einsum("hsn,shp->hpn", b_weighted, x_blk, preferred_element_type=jnp.float32)
    carry_gain = jnp.where(end_id == before_id, jnp.exp(prefix_t[:, -1]), 0.0)
    return (y_intra, local_state, carry_gain, prefix)


def block_inter(c_blk, prefix, ids_blk, before_id, state_in):
    entering = ids_blk == before_id
    inter_scale = jnp.where(entering[:, None], jnp.exp(prefix), 0.0)
    return inter_scale[:, :, None] * jnp.einsum(
        "tn,hpn->thp", c_blk.astype(jnp.float32), state_in, precision=lax.Precision.HIGHEST
    )


def block_last(
    last_index, table, x_blk, b_blk, step_blk, prefix, ids_blk, before_id, state_in, start
):
    length = ids_blk.shape[0]
    position = jnp.arange(length, dtype=jnp.int32)
    prompt_ids = jnp.arange(last_index.shape[0], dtype=jnp.int32)
    local_last = last_index - start
    ends_here = (local_last >= 0) & (local_last < length)
    clipped = jnp.clip(local_last, 0, length - 1)

    def with_ends():
        prefix_t = prefix.T
        prefix_last = prefix[clipped]
        pick = (
            ends_here[:, None]
            & (ids_blk[None, :] == prompt_ids[:, None])
            & (position[None, :] <= clipped[:, None])
        )
        spans = prefix_last[:, :, None] - prefix_t[None]
        weight_last = (
            jnp.where(pick[:, None, :], jnp.exp(jnp.where(pick[:, None, :], spans, 0.0)), 0.0)
            * step_blk.T[None]
        )
        b_last = (weight_last[..., None] * b_blk[None, None]).astype(jnp.bfloat16)
        last_local = jnp.einsum("ghsn,shp->ghpn", b_last, x_blk, preferred_element_type=jnp.float32)
        last_gain = jnp.where(
            (ends_here & (prompt_ids == before_id))[:, None], jnp.exp(prefix_last), 0.0
        )
        return table + last_local + last_gain[:, :, None, None] * state_in[None]

    def without_ends():
        return table

    return lax.cond(jnp.any(ends_here), with_ends, without_ends)


def join_states(earlier, later):
    return (earlier[0] * later[0], later[0][:, None, None] * earlier[1] + later[1])


def on_device(
    hidden,
    token_prompt,
    request_prompt,
    in_gain,
    w_zx,
    w_bc,
    w_dt,
    dt_bias,
    a_log,
    conv_x,
    conv_bc,
    skip_gain,
    out_gain,
    w_out,
):
    tok_dev = hidden.shape[0]
    inner_dev = w_zx.shape[2]
    heads_dev = w_dt.shape[1]
    head_dim = inner_dev // heads_dev
    state_width = w_bc.shape[1] // 2
    taps = conv_x.shape[0]
    dp_index = lax.axis_index("dp")
    head_index = lax.axis_index("head")
    head_count = lax.axis_size("head")
    hidden_f = hidden.astype(jnp.float32)
    normed = (hidden_f * rms_scale(hidden_f) * in_gain).astype(jnp.bfloat16)
    pieces = (
        lax.all_gather(w_zx.astype(jnp.bfloat16), "dp", axis=0, tiled=True),
        lax.all_gather(w_dt.astype(jnp.bfloat16), "dp", axis=0, tiled=True),
        lax.all_gather(w_bc.astype(jnp.bfloat16), "dp", axis=0, tiled=True),
    )
    acc_zx, acc_step, acc_bc = tuple(
        (
            jnp.dot(normed, piece.reshape(piece.shape[0], -1), preferred_element_type=jnp.float32)
            for piece in pieces
        )
    )
    proj_bc = acc_bc.astype(jnp.bfloat16)
    proj_zx = acc_zx.astype(jnp.bfloat16)
    gate_z = proj_zx[:, :inner_dev]
    inner_x = proj_zx[:, inner_dev:]
    proj_dt = acc_step.astype(jnp.bfloat16)
    step_size = jax.nn.softplus(proj_dt.astype(jnp.float32) + dt_bias)
    rate = step_size * -jnp.exp(a_log)
    ids_own = lax.dynamic_slice_in_dim(token_prompt, dp_index * tok_dev, tok_dev)
    rim_start = jnp.maximum(dp_index * tok_dev - (taps - 1), 0)
    rim_ids = lax.dynamic_slice_in_dim(token_prompt, rim_start, taps - 1)
    tail_rows = jnp.concatenate(
        [inner_x[tok_dev - taps + 1 :], proj_bc[tok_dev - taps + 1 :]], axis=1
    )
    rim_rows = from_behind(tail_rows, "dp", 1)
    ext_ids = jnp.concatenate([rim_ids, ids_own])
    conv_inner = conv_core(
        jnp.concatenate([rim_rows[:, :inner_dev], inner_x], axis=0), ext_ids, ids_own, conv_x
    )
    conv_bc_out = conv_core(
        jnp.concatenate([rim_rows[:, inner_dev:], proj_bc], axis=0), ext_ids, ids_own, conv_bc
    )
    blocks = tok_dev // BLOCK
    x_heads = conv_inner.reshape(blocks, BLOCK, heads_dev, head_dim)
    b_conv = conv_bc_out[:, :state_width].reshape(blocks, BLOCK, state_width)
    c_conv = conv_bc_out[:, state_width:].reshape(blocks, BLOCK, state_width)
    step_blocks = step_size.reshape(blocks, BLOCK, heads_dev)
    rate_blocks = rate.reshape(blocks, BLOCK, heads_dev)
    id_blocks = ids_own.reshape(blocks, BLOCK)
    prev_last = jnp.where(dp_index > 0, token_prompt[jnp.maximum(dp_index * tok_dev - 1, 0)], -1)
    before_ids = jnp.concatenate([prev_last[None], id_blocks[:-1, -1]])
    y_intra, local_state, carry_gain, prefix = jax.vmap(block_local)(
        x_heads, b_conv, c_conv, step_blocks, rate_blocks, id_blocks, before_ids
    )

    def advance(carry, item):
        gain_acc, state_acc = carry
        gain, block_state = item
        return (
            (gain_acc * gain, gain[:, None, None] * state_acc + block_state),
            (gain_acc, state_acc),
        )

    unit_gain = jnp.ones((heads_dev,), jnp.float32)
    zero_state = jnp.zeros((heads_dev, head_dim, state_width), jnp.float32)
    (dev_gain, dev_state), (prior_gain, prior_state) = lax.scan(
        advance, (unit_gain, zero_state), (carry_gain, local_state)
    )
    scanned = carried_in((dev_gain, dev_state), "dp", join_states, (unit_gain, zero_state))
    incoming = scanned[1]
    block_in = prior_state + prior_gain[:, :, None, None] * incoming[None]
    prompt_ids = jnp.arange(PROMPTS, dtype=jnp.int32)
    last_index = (
        jnp.sum((token_prompt[None, :] <= prompt_ids[:, None]).astype(jnp.int32), axis=1) - 1
    )
    start_pos = (dp_index * blocks + jnp.arange(blocks, dtype=jnp.int32)) * BLOCK
    y_inter = jax.vmap(block_inter)(c_conv, prefix, id_blocks, before_ids, block_in)

    def collect(table, item):
        xb, bb, sb, pb, ib, fb, stb, ob = item
        return (block_last(last_index, table, xb, bb, sb, pb, ib, fb, stb, ob), None)

    empty_table = jnp.zeros((PROMPTS, heads_dev, head_dim, state_width), jnp.float32)
    local_table, unused = lax.scan(
        collect,
        empty_table,
        (x_heads, b_conv, step_blocks, prefix, id_blocks, before_ids, block_in, start_pos),
    )
    ssd_out = (y_intra + y_inter).reshape(tok_dev, heads_dev, head_dim) + skip_gain[
        None, :, None
    ] * conv_inner.astype(jnp.float32).reshape(tok_dev, heads_dev, head_dim)
    gated = ssd_out.reshape(tok_dev, inner_dev) * jax.nn.silu(gate_z.astype(jnp.float32))
    square_sum = lax.psum(jnp.sum(gated * gated, axis=1), "head")
    scale = lax.rsqrt(square_sum / (inner_dev * head_count) + EPSILON)
    normed_out = (gated * scale[:, None] * out_gain).astype(jnp.bfloat16)
    out_rows = tok_dev // head_count
    own_rows = lax.dynamic_slice_in_dim(hidden_f, head_index * out_rows, out_rows, 0)
    mixed = lax.psum_scatter(
        jnp.dot(normed_out, w_out, preferred_element_type=jnp.float32),
        "head",
        scatter_dimension=0,
        tiled=True,
    )
    layer_out = (own_rows + mixed).astype(jnp.bfloat16)
    table = lax.psum(local_table, "dp")
    one_hot = (request_prompt[:, None] == prompt_ids[None, :]).astype(jnp.float32)
    request_states = jnp.einsum("rg,ghpn->rhpn", one_hot, table, precision=lax.Precision.HIGHEST)
    return (layer_out, request_states)


LANES = 128
TILE_ROWS = 16
NEVER = -1e30
MESH_KERNEL_BYTES = 48 * 1024 * 1024


def kernel_params():
    return pltpu.CompilerParams(vmem_limit_bytes=MESH_KERNEL_BYTES)


def in_vmem(count):
    return [pl.BlockSpec(memory_space=pltpu.VMEM)] * count


def exchange(values, axis, bits):
    return lax.ppermute(values, axis, [(i, i ^ bits) for i in range(lax.axis_size(axis))])


def dot32(a, b, a_dim=1, b_dim=0):
    return lax.dot_general(
        a, b, (((a_dim,), (b_dim,)), ((), ())), preferred_element_type=jnp.float32
    )


def silu_tanh(values):
    half = 0.5 * values
    return half + half * jnp.tanh(half)


def widen(columns, pair, head_dim):
    rows = columns.shape[0]
    lane = lax.broadcasted_iota(jnp.int32, (rows, LANES), 1)
    first = jnp.broadcast_to(columns[:, 2 * pair : 2 * pair + 1], (rows, LANES))
    second = jnp.broadcast_to(columns[:, 2 * pair + 1 : 2 * pair + 2], (rows, LANES))
    return jnp.where(lane < head_dim, first, second)


def pack_kernel(req_ref, wzx_ref, wbc_ref, wdt_ref, tail_ref, front_ref, gate_ref, pad_ref):
    rows, bc_width = wbc_ref.shape
    inner = gate_ref.shape[1]
    tiles = inner // LANES
    for j in range(tiles):
        own = slice(j * LANES, (j + 1) * LANES)
        front_ref[0:rows, own] = wzx_ref[pl.ds(2 * j + 1, rows, stride=2 * tiles), :].astype(
            jnp.bfloat16
        )
        gate_ref[:, own] = wzx_ref[pl.ds(2 * j, rows, stride=2 * tiles), :].astype(jnp.bfloat16)
    front_ref[0:rows, inner:] = wbc_ref[...].astype(jnp.bfloat16)
    front_ref[rows:, :] = jnp.zeros((front_ref.shape[0] - rows, inner + bc_width), jnp.bfloat16)
    pad_ref[...] = jnp.zeros_like(pad_ref)
    pad_ref[0 : wdt_ref.shape[0], 0:rows] = wdt_ref[...]
    lane = lax.broadcasted_iota(jnp.int32, (TILE_ROWS, LANES), 1)
    wanted = jnp.zeros((TILE_ROWS, LANES), jnp.float32)
    for r in range(req_ref.shape[0]):
        wanted = jnp.where(lane == r, req_ref[r].astype(jnp.float32), wanted)
    pad_ref[:, rows : rows + LANES] = wanted
    front_ref[rows : rows + TILE_ROWS, 0 : rows + LANES] = pad_ref[...].astype(jnp.bfloat16)
    piece = rows + LANES
    for i in range(tail_ref.shape[1] // piece):
        at = rows + TILE_ROWS * (i + 1)
        front_ref[at : at + TILE_ROWS, 0:piece] = tail_ref[:, i * piece : (i + 1) * piece]


def front_kernel(
    place_ref,
    normed_ref,
    own_ref,
    near_ref,
    far_ref,
    last_ref,
    gain_ref,
    taps_x_ref,
    taps_bc_ref,
    meta_ref,
    order_ref,
    head_ref,
    conv_ref,
    stepx_ref,
    faded_ref,
    prefix_ref,
    leaving_ref,
    middle_ref,
    w_ref,
    extra_ref,
    dtw_ref,
    ext_ref,
    sems,
):
    position = place_ref[0]
    model = normed_ref.shape[1]
    tok = normed_ref.shape[0]
    rows = model // extra_ref.shape[0]
    inner = taps_x_ref.shape[1]
    width = conv_ref.shape[1]
    state_width = (width - inner) // 2
    head_dim = LANES // 2
    pairs = inner // LANES
    copies = []
    for j, buffer in enumerate((own_ref, near_ref, far_ref, last_ref)):
        source = jnp.bitwise_xor(position, j)
        at = pl.multiple_of(source * rows, rows)
        copies.append(
            pltpu.make_async_copy(buffer.at[0:rows], w_ref.at[pl.ds(at, rows)], sems.at[2 * j])
        )
        copies.append(
            pltpu.make_async_copy(
                buffer.at[rows : rows + extra_ref.shape[1]],
                extra_ref.at[source],
                sems.at[2 * j + 1],
            )
        )
    for copy in copies:
        copy.start()
    dtw_ref[...] = jnp.zeros_like(dtw_ref)
    for copy in copies:
        copy.wait()
    for s in range(extra_ref.shape[0]):
        dtw_ref[0:TILE_ROWS, s * rows : (s + 1) * rows] = extra_ref[s, 0:TILE_ROWS, 0:rows]
    behind = jnp.maximum(position - 1, 0)
    piece = rows + LANES
    halo = jnp.concatenate(
        [
            extra_ref[behind, TILE_ROWS * (i + 1) : TILE_ROWS * (i + 2), 0:piece]
            for i in range(model // piece)
        ],
        axis=1,
    ).astype(jnp.float32)
    halo = halo * rms_scale(halo) * gain_ref[...]
    ext_ref[0:TILE_ROWS, :] = dot32(halo.astype(jnp.bfloat16), w_ref[...])
    normed = normed_ref[...]
    for at in range(0, width, 2 * LANES):
        stop = min(at + 2 * LANES, width)
        ext_ref[TILE_ROWS:, at:stop] = dot32(normed, w_ref[:, at:stop])
    raw = dot32(normed, dtw_ref[...], 1, 1) + head_ref[0:1, :]
    step = jnp.maximum(raw, 0.0) + jnp.log1p(jnp.exp(-jnp.abs(raw)))
    lane = lax.broadcasted_iota(jnp.int32, (tok, LANES), 1)
    rate = jnp.where(lane < TILE_ROWS, -step * jnp.exp(head_ref[1:2, :]), 0.0)
    high = rate.astype(jnp.bfloat16).astype(jnp.float32)
    rest = rate - high
    mid = rest.astype(jnp.bfloat16).astype(jnp.float32)
    low = rest - mid
    packed = high + pltpu.roll(mid, TILE_ROWS, 1) + pltpu.roll(low, 2 * TILE_ROWS, 1)
    sums = dot32(order_ref[...], packed.astype(jnp.bfloat16))
    sums = (
        sums
        + pltpu.roll(sums, LANES - TILE_ROWS, 1)
        + pltpu.roll(sums, LANES - 2 * TILE_ROWS, 1)
    )
    prefix = sums[0:tok]
    fade = jnp.exp(sums[tok : 2 * tok])
    prefix_ref[...] = prefix
    fade_middle = jnp.exp(prefix[BLOCK - 1 : BLOCK, :] - prefix[0:BLOCK])
    same = [
        jnp.broadcast_to(meta_ref[:, k : k + 1], (tok, LANES)) for k in range(3)
    ]
    for j in range(width // LANES):
        own = slice(j * LANES, (j + 1) * LANES)
        if j < pairs:
            taps = taps_x_ref[:, own]
        else:
            taps = taps_bc_ref[:, j * LANES - inner : (j + 1) * LANES - inner]
        total = ext_ref[TILE_ROWS : TILE_ROWS + tok, own] * taps[3:4]
        for k in range(1, 4):
            total = total + same[k - 1] * (
                ext_ref[TILE_ROWS - k : TILE_ROWS - k + tok, own] * taps[3 - k : 4 - k]
            )
        conv_ref[:, own] = silu_tanh(total).astype(jnp.bfloat16)
    b_all = conv_ref[:, inner : inner + state_width].astype(jnp.float32)
    b_leaving = (b_all * meta_ref[:, 7:8]).astype(jnp.bfloat16)
    b_middle = (b_all * meta_ref[:, 5:6])[0:BLOCK].astype(jnp.bfloat16)
    for q in range(pairs):
        own = slice(q * LANES, (q + 1) * LANES)
        scaled = conv_ref[:, own].astype(jnp.float32) * widen(step, q, head_dim)
        stepx_ref[:, own] = scaled.astype(jnp.bfloat16)
        faded = (scaled * widen(fade, q, head_dim)).astype(jnp.bfloat16).T
        faded_ref[own, :] = faded
        leaving_ref[own, :] = dot32(faded, b_leaving).astype(jnp.bfloat16)
        to_middle = (scaled[0:BLOCK] * widen(fade_middle, q, head_dim)).astype(jnp.bfloat16).T
        middle_ref[own, :] = dot32(to_middle, b_middle).astype(jnp.bfloat16)


def local_kernel(
    place_ref,
    normed_ref,
    own_ref,
    near_ref,
    far_ref,
    last_ref,
    conv_ref,
    stepx_ref,
    faded_ref,
    prefix_ref,
    middle_ref,
    meta_ref,
    pen_ref,
    skip_ref,
    y_ref,
    gate_ref,
    table_ref,
    w_ref,
    sems,
):
    position = place_ref[0]
    inner = y_ref.shape[1]
    rows = own_ref.shape[0]
    state_width = middle_ref.shape[1]
    head_dim = LANES // 2
    tok = y_ref.shape[0]
    copies = []
    for j, buffer in enumerate((own_ref, near_ref, far_ref, last_ref)):
        at = pl.multiple_of(jnp.bitwise_xor(position, j) * rows, rows)
        copies.append(pltpu.make_async_copy(buffer, w_ref.at[pl.ds(at, rows)], sems.at[j]))
    for copy in copies:
        copy.start()
    lane = lax.broadcasted_iota(jnp.int32, (BLOCK, LANES), 1)
    for b in range(tok // BLOCK):
        own_rows = slice(b * BLOCK, (b + 1) * BLOCK)
        b_blk = conv_ref[own_rows, inner : inner + state_width]
        c_blk = conv_ref[own_rows, inner + state_width :]
        scores = dot32(c_blk, b_blk, 1, 1)
        pen = pen_ref[b]
        prefix = prefix_ref[own_rows, :]
        across = prefix.T
        if b > 0:
            carried = jnp.exp(prefix - prefix_ref[b * BLOCK - 1 : b * BLOCK, :])
            carried = carried * meta_ref[own_rows, 4:5]
            from_middle = dot32(c_blk, middle_ref[...], 1, 1)
        for q in range(inner // LANES):
            own = slice(q * LANES, (q + 1) * LANES)
            x_pair = conv_ref[own_rows, own].astype(jnp.float32)
            out = x_pair * skip_ref[:, own]
            if b > 0:
                out = out + widen(carried, q, head_dim) * from_middle[:, own]
            sx = stepx_ref[own_rows, own].astype(jnp.float32)
            for side in range(2):
                h = 2 * q + side
                gaps = prefix[:, h : h + 1] - across[h : h + 1, :] + pen
                mixing = (scores * jnp.exp(gaps)).astype(jnp.bfloat16)
                kept = (lane < head_dim) if side == 0 else (lane >= head_dim)
                out = out + dot32(mixing, jnp.where(kept, sx, 0.0).astype(jnp.bfloat16))
            y_ref[own_rows, own] = out
    b_all = conv_ref[:, inner : inner + state_width].astype(jnp.float32)
    faded = faded_ref[...]
    for g in range(table_ref.shape[0]):
        ended = jnp.where(meta_ref[:, 6:7] == g, meta_ref[:, 8:9], 0.0)
        table_ref[g] = dot32(faded, (b_all * ended).astype(jnp.bfloat16)).astype(jnp.bfloat16)
    for copy in copies:
        copy.wait()
    normed = normed_ref[...]
    gate_ref[...] = silu_tanh(dot32(normed, w_ref[...]))


def gate_kernel(place_ref, enter_ref, conv_ref, prefix_ref, meta_ref, y_ref, z_ref, *outs):
    scratch = outs[-1]
    outs = outs[:-1]
    inner = y_ref.shape[1]
    state_width = enter_ref.shape[1]
    head_dim = LANES // 2
    c_all = conv_ref[:, inner + state_width :]
    inter = dot32(c_all, enter_ref[...], 1, 1)
    carried = jnp.exp(prefix_ref[...]) * meta_ref[:, 3:4]
    for q in range(inner // LANES):
        own = slice(q * LANES, (q + 1) * LANES)
        value = y_ref[:, own] + widen(carried, q, head_dim) * inter[:, own]
        scratch[:, own] = (value * z_ref[:, own]).astype(jnp.bfloat16)
    members = len(outs)
    part = y_ref.shape[0] // (2 * members)
    half = place_ref[5]
    for j, out in enumerate(outs):
        member = jnp.bitwise_xor(place_ref[4], j)
        for k, side in enumerate((1 - half, half)):
            at = pl.multiple_of((side * members + member) * part, part)
            out[k * part : (k + 1) * part, :] = scratch[pl.ds(at, part), :]


def ends_kernel(place_ref, table_ref, enter_ref, prefix_ref, out_ref):
    out_ref[...] = table_ref[...]
    head_dim = LANES // 2

    @pl.when(place_ref[2] == 1)
    def add():
        prompt = place_ref[1]
        gain = jnp.exp(prefix_ref[pl.ds(place_ref[3], 1), :])
        for h in range(out_ref.shape[1] // head_dim):
            own = slice(h * head_dim, (h + 1) * head_dim)
            term = gain[:, h : h + 1] * enter_ref[own, :].astype(jnp.float32)
            old = table_ref[prompt, own, :].astype(jnp.float32)
            out_ref[prompt, own, :] = (old + term).astype(jnp.bfloat16)


def pick_kernel(wanted_ref, table_ref, other_ref, keep_ref, send_ref):
    count = keep_ref.shape[0]
    for k, out in enumerate((keep_ref, send_ref)):
        for r in range(count):
            g = wanted_ref[k * count + r]
            total = table_ref[g].astype(jnp.float32) + other_ref[g].astype(jnp.float32)
            out[r] = total.astype(jnp.bfloat16)


def out_kernel(place_ref, *refs):
    members = 4
    gated, own_w = refs[:members], refs[members]
    near, swapped = refs[members + 1 : 2 * members], refs[2 * members : 3 * members - 1]
    send_ref, keep_ref = refs[3 * members - 1 :]
    core = place_ref[6]
    half = near[0].shape[1]
    part = send_ref.shape[0]
    values = [g[...] for g in gated]
    for others, side in ((near, core), (swapped, 1 - core)):
        at = pl.multiple_of(side * half, half)
        total = dot32(values[0], own_w[:, pl.ds(at, half)])
        for value, weights in zip(values[1:], others):
            total = total + dot32(value, weights[...])
        send_ref[:, pl.ds(at, half)] = total[0:part].astype(jnp.bfloat16)
        keep_ref[:, pl.ds(at, half)] = total[part:]
    squares = jnp.zeros((2 * part, 1), jnp.float32)
    for value in values:
        wide = value.astype(jnp.float32)
        squares = squares + jnp.sum(wide * wide, axis=1, keepdims=True)
    model = 2 * half
    lane = lax.broadcasted_iota(jnp.int32, (part, LANES), 1)
    high = squares[0:part].astype(jnp.bfloat16).astype(jnp.float32)
    low = squares[0:part] - high
    send_ref[:, model:] = jnp.where(lane == 0, high, low).astype(jnp.bfloat16)
    keep_ref[:, model:] = jnp.broadcast_to(squares[part:], (part, LANES))


def finish_kernel(inner_total, hidden_ref, keep_ref, got_ref, out_ref):
    model = hidden_ref.shape[1]
    squares = keep_ref[:, model : model + 1]
    squares = squares + got_ref[:, model : model + 1].astype(jnp.float32)
    squares = squares + got_ref[:, model + 1 : model + 2].astype(jnp.float32)
    scale = lax.rsqrt(squares / inner_total + EPSILON)
    total = keep_ref[:, 0:model] + got_ref[:, 0:model].astype(jnp.float32)
    out_ref[...] = (hidden_ref[...].astype(jnp.float32) + scale * total).astype(jnp.bfloat16)


def fused_on_device(
    hidden,
    token_prompt,
    request_prompt,
    in_gain,
    w_zx,
    w_bc,
    w_dt,
    dt_bias,
    a_log,
    conv_x,
    conv_bc,
    skip_gain,
    out_gain,
    w_out,
):
    tok, model = hidden.shape
    rows = w_zx.shape[0]
    inner = w_zx.shape[2]
    heads = w_dt.shape[1]
    state_width = w_bc.shape[1] // 2
    width = inner + 2 * state_width
    peers = lax.axis_size("dp")
    head_count = lax.axis_size("head")
    position = lax.axis_index("dp")
    head_index = lax.axis_index("head")
    bf16, f32 = jnp.bfloat16, jnp.float32
    shape = jax.ShapeDtypeStruct
    smem = pl.BlockSpec(memory_space=pltpu.SMEM)
    anywhere = pl.BlockSpec(memory_space=pl.ANY)

    tiles = inner // LANES
    flat = w_zx.reshape(rows, 2, tiles, LANES).transpose(0, 2, 1, 3).reshape(-1, LANES)
    extra = TILE_ROWS * (1 + model // (rows + LANES))
    front_own, gate_own = pl.pallas_call(
        pack_kernel,
        name="pack_weights",
        grid=(1,),
        out_shape=(shape((rows + extra, width), bf16), shape((rows, inner), bf16)),
        in_specs=[
            smem,
            pl.BlockSpec(flat.shape, lambda i: (0, 0)),
            pl.BlockSpec(w_bc.shape, lambda i: (0, 0)),
            pl.BlockSpec((heads, rows), lambda i: (0, 0)),
            pl.BlockSpec((TILE_ROWS, model), lambda i: (tok // TILE_ROWS - 1, 0)),
        ],
        out_specs=(
            pl.BlockSpec((rows + extra, width), lambda i: (0, 0)),
            pl.BlockSpec((rows, inner), lambda i: (0, 0)),
        ),
        scratch_shapes=[pltpu.VMEM((TILE_ROWS, rows + LANES), f32)],
        compiler_params=kernel_params(),
    )(request_prompt, flat, w_bc, w_dt.T, hidden)
    front_far = exchange(front_own, "dp", 2)
    front_near = exchange(front_own, "dp", 1)
    gate_far = exchange(gate_own, "dp", 2)
    gate_near = exchange(gate_own, "dp", 1)
    front_last = exchange(front_far, "dp", 1)
    gate_last = exchange(gate_far, "dp", 1)

    core = position % 2
    scaled_out = (w_out.astype(f32) * out_gain[:, None]).astype(bf16)
    half_width = model // 2
    half_out = lax.dynamic_slice_in_dim(scaled_out, core * half_width, half_width, 1)
    near_out = [exchange(half_out, "head", bits) for bits in (1, 2, 3)]
    swapped_out = [exchange(part, "dp", 1) for part in near_out]

    ids_long = jnp.concatenate([jnp.full((3,), -1, jnp.int32), token_prompt, jnp.full((1,), -1, jnp.int32)])
    window = lax.dynamic_slice_in_dim(ids_long, position * tok, tok + 4)
    ids = window[3 : 3 + tok]
    before, after = window[2], window[3 + tok]
    end_id, middle_id = ids[tok - 1], ids[BLOCK - 1]
    index = jnp.arange(tok, dtype=jnp.int32)
    facts = [ids == window[3 - k : 3 - k + tok] for k in (1, 2, 3)]
    facts += [
        ids == before,
        (ids == middle_id) & (index >= BLOCK),
        (ids == middle_id) & (index < BLOCK),
        ids,
        ids == end_id,
        (ids != end_id) | (after != end_id),
    ]
    meta = jnp.stack([fact.astype(f32) for fact in facts], axis=1)
    meta = jnp.pad(meta, ((0, 0), (0, LANES - meta.shape[1])))
    entered = jnp.sum((ids == before).astype(jnp.int32))
    applies = (entered > 0) & ((before != end_id) | (after != end_id))
    place = jnp.stack(
        [
            position,
            jnp.maximum(before, 0),
            applies.astype(jnp.int32),
            jnp.maximum(entered - 1, 0),
            head_index % 4,
            head_index // 4,
            core,
            0,
        ]
    ).astype(jnp.int32)
    same = ids[:, None] == ids[None, :]
    order = jnp.concatenate(
        [index[None, :] <= index[:, None], (index[None, :] > index[:, None]) & same]
    ).astype(bf16)
    blocks = tok // BLOCK
    pen = jnp.where(same & (index[None, :] <= index[:, None]), 0.0, NEVER).astype(f32)
    pen = jnp.stack(
        [pen[b * BLOCK : (b + 1) * BLOCK, b * BLOCK : (b + 1) * BLOCK] for b in range(blocks)]
    )
    head_rows = jnp.pad(jnp.stack([dt_bias, a_log]), ((0, 0), (0, LANES - heads)))
    skip_row = jnp.repeat(skip_gain, inner // heads)[None, :]

    hidden_f = hidden.astype(f32)
    normed = (hidden_f * rms_scale(hidden_f) * in_gain).astype(bf16)

    conv, stepx, faded, prefix, leaving, middle = pl.pallas_call(
        front_kernel,
        name="project_and_convolve",
        out_shape=(
            shape((tok, width), bf16),
            shape((tok, inner), bf16),
            shape((inner, tok), bf16),
            shape((tok, LANES), f32),
            shape((inner, state_width), bf16),
            shape((inner, state_width), bf16),
        ),
        in_specs=[smem] + in_vmem(1) + [anywhere] * 4 + in_vmem(6),
        out_specs=tuple(in_vmem(6)),
        scratch_shapes=[
            pltpu.VMEM((model, width), bf16),
            pltpu.VMEM((peers, extra, width), bf16),
            pltpu.VMEM((LANES, model), bf16),
            pltpu.VMEM((TILE_ROWS + tok, width), f32),
            pltpu.SemaphoreType.DMA((2 * peers,)),
        ],
        compiler_params=kernel_params(),
        cost_estimate=pl.CostEstimate(
            flops=2 * tok * model * width, bytes_accessed=8_000_000, transcendentals=500_000
        ),
    )(
        place,
        normed,
        front_own,
        front_near,
        front_far,
        front_last,
        in_gain[None, :],
        conv_x,
        conv_bc,
        meta,
        order,
        head_rows,
    )

    entering = lax.ppermute(leaving, "dp", [(i, i + 1) for i in range(peers - 1)])

    y_local, gate, table = pl.pallas_call(
        local_kernel,
        name="mix_within_blocks",
        out_shape=(
            shape((tok, inner), f32),
            shape((tok, inner), f32),
            shape((PROMPTS, inner, state_width), bf16),
        ),
        in_specs=[smem] + in_vmem(1) + [anywhere] * 4 + in_vmem(8),
        out_specs=tuple(in_vmem(3)),
        scratch_shapes=[pltpu.VMEM((model, inner), bf16), pltpu.SemaphoreType.DMA((peers,))],
        compiler_params=kernel_params(),
        cost_estimate=pl.CostEstimate(
            flops=2 * tok * model * inner, bytes_accessed=8_000_000, transcendentals=1_000_000
        ),
    )(
        place,
        normed,
        gate_own,
        gate_near,
        gate_far,
        gate_last,
        conv,
        stepx,
        faded,
        prefix,
        middle,
        meta,
        pen,
        skip_row,
    )

    out_rows = tok // head_count
    gated = pl.pallas_call(
        gate_kernel,
        name="add_entering_and_gate",
        out_shape=tuple(shape((2 * out_rows, inner), bf16) for _ in range(4)),
        in_specs=[smem] + in_vmem(6),
        out_specs=tuple(in_vmem(4)),
        scratch_shapes=[pltpu.VMEM((tok, inner), bf16)],
        compiler_params=kernel_params(),
    )(place, entering, conv, prefix, meta, y_local, gate)
    gated_in = [gated[0]] + [exchange(gated[bits], "head", bits) for bits in (1, 2, 3)]

    table = pl.pallas_call(
        ends_kernel,
        name="add_entering_to_ends",
        out_shape=shape(table.shape, bf16),
        in_specs=[smem] + in_vmem(3),
        out_specs=in_vmem(1)[0],
        compiler_params=kernel_params(),
    )(place, table, entering, prefix)
    table_near = exchange(table, "dp", 1)
    requests = request_prompt.shape[0]
    other_wants = front_far[rows, rows : rows + requests].astype(jnp.int32)
    keep, send = pl.pallas_call(
        pick_kernel,
        name="pick_request_states",
        out_shape=(shape((requests, inner, state_width), bf16),) * 2,
        in_specs=[smem] + in_vmem(2),
        out_specs=tuple(in_vmem(2)),
        compiler_params=kernel_params(),
    )(jnp.concatenate([request_prompt, other_wants]), table, table_near)
    far = exchange(send, "dp", 2)

    sums_send, sums_keep = pl.pallas_call(
        out_kernel,
        name="project_out",
        out_shape=(
            shape((out_rows, model + LANES), bf16),
            shape((out_rows, model + LANES), f32),
        ),
        in_specs=[smem] + in_vmem(11),
        out_specs=tuple(in_vmem(2)),
        compiler_params=kernel_params(),
    )(place, *gated_in, scaled_out, *near_out, *swapped_out)
    sums_in = exchange(sums_send, "head", 4)
    own_hidden = lax.dynamic_slice_in_dim(hidden, head_index * out_rows, out_rows, 0)
    layer_out = pl.pallas_call(
        functools.partial(finish_kernel, inner * head_count),
        name="scale_and_add_hidden",
        out_shape=shape((out_rows, model), bf16),
        in_specs=in_vmem(3),
        out_specs=in_vmem(1)[0],
        compiler_params=kernel_params(),
    )(own_hidden, sums_keep, sums_in)
    request_states = keep.astype(f32) + far.astype(f32)
    return (
        layer_out,
        request_states.reshape(requests, heads, inner // heads, state_width),
    )


def fits_fused(mesh):
    return dict(mesh.shape) == {"dp": 4, "head": 8}


def solution(mesh):
    in_specs = (
        P("dp", None),
        P(),
        P("dp"),
        P(),
        P("dp", None, "head"),
        P("dp", None),
        P("dp", "head"),
        P("head"),
        P("head"),
        P(None, "head"),
        P(),
        P("head"),
        P("head"),
        P("head", None),
    )
    out_specs = (P(("dp", "head"), None), P("dp", "head", None, None))
    program = fused_on_device if fits_fused(mesh) else on_device
    return jax.shard_map(
        program, mesh=mesh, in_specs=in_specs, out_specs=out_specs, check_vma=False
    )
```

```python
import functools

import jax
import jax.numpy as jnp
from jax import lax
from jax.experimental import pallas as pl
from jax.experimental.pallas import tpu as pltpu
from jax.sharding import PartitionSpec as P

BLOCK = 256
PROMPTS = 8


EPSILON = 1e-05


def from_behind(shard, axis, by):
    peers = lax.axis_size(axis)
    pairs = [(i, i + by) for i in range(peers) if 0 <= i + by < peers]
    return lax.ppermute(shard, axis, pairs)


def carried_in(shard, axis, combine, identity):
    peers, position = (lax.axis_size(axis), lax.axis_index(axis))
    everything = jax.tree.map(lambda part: lax.all_gather(part, axis), shard)
    start = jax.tree.map(
        lambda part, zero: jnp.broadcast_to(jnp.asarray(zero, part.dtype), part.shape),
        shard,
        identity,
    )

    def step(k, before):
        reached = k < position
        new = combine(before, jax.tree.map(lambda part: part[k], everything))
        return jax.tree.map(lambda a, b: jnp.where(reached, a, b), new, before)

    return lax.fori_loop(0, peers, step, start)


def rms_scale(values):
    return lax.rsqrt(jnp.mean(values * values, axis=-1, keepdims=True) + EPSILON)


def conv_core(extended, extended_ids, token_ids, weights):
    length = token_ids.shape[0]
    total = jnp.zeros((length, extended.shape[1]), jnp.float32)
    for offset in range(weights.shape[0]):
        same = (extended_ids[offset : offset + length] == token_ids)[:, None]
        total = total + jnp.where(
            same, weights[offset] * extended[offset : offset + length].astype(jnp.float32), 0.0
        )
    return jax.nn.silu(total).astype(jnp.bfloat16)


def block_local(x_blk, b_blk, c_blk, step_blk, rate_blk, ids_blk, before_id):
    length = ids_blk.shape[0]
    position = jnp.arange(length, dtype=jnp.int32)
    prefix = jnp.cumsum(rate_blk, axis=0)
    prefix_t = prefix.T
    same = (ids_blk[:, None] == ids_blk[None, :]) & (position[None, :] <= position[:, None])
    gaps = prefix_t[:, :, None] - prefix_t[:, None, :]
    decay = jnp.where(same[None], jnp.exp(jnp.where(same[None], gaps, 0.0)), 0.0)
    scores = jnp.dot(c_blk, b_blk.T, preferred_element_type=jnp.float32)
    mixing = (scores[None] * decay * step_blk.T[:, None, :]).astype(jnp.bfloat16)
    y_intra = jnp.einsum("hts,shp->thp", mixing, x_blk, preferred_element_type=jnp.float32)
    end_id = ids_blk[-1]
    alive = ids_blk == end_id
    weight_end = (
        jnp.where(
            alive[None, :],
            jnp.exp(jnp.where(alive[None, :], prefix_t[:, -1:] - prefix_t, 0.0)),
            0.0,
        )
        * step_blk.T
    )
    b_weighted = (weight_end[:, :, None] * b_blk[None]).astype(jnp.bfloat16)
    local_state = jnp.einsum("hsn,shp->hpn", b_weighted, x_blk, preferred_element_type=jnp.float32)
    carry_gain = jnp.where(end_id == before_id, jnp.exp(prefix_t[:, -1]), 0.0)
    return (y_intra, local_state, carry_gain, prefix)


def block_inter(c_blk, prefix, ids_blk, before_id, state_in):
    entering = ids_blk == before_id
    inter_scale = jnp.where(entering[:, None], jnp.exp(prefix), 0.0)
    return inter_scale[:, :, None] * jnp.einsum(
        "tn,hpn->thp", c_blk.astype(jnp.float32), state_in, precision=lax.Precision.HIGHEST
    )


def block_last(
    last_index, table, x_blk, b_blk, step_blk, prefix, ids_blk, before_id, state_in, start
):
    length = ids_blk.shape[0]
    position = jnp.arange(length, dtype=jnp.int32)
    prompt_ids = jnp.arange(last_index.shape[0], dtype=jnp.int32)
    local_last = last_index - start
    ends_here = (local_last >= 0) & (local_last < length)
    clipped = jnp.clip(local_last, 0, length - 1)

    def with_ends():
        prefix_t = prefix.T
        prefix_last = prefix[clipped]
        pick = (
            ends_here[:, None]
            & (ids_blk[None, :] == prompt_ids[:, None])
            & (position[None, :] <= clipped[:, None])
        )
        spans = prefix_last[:, :, None] - prefix_t[None]
        weight_last = (
            jnp.where(pick[:, None, :], jnp.exp(jnp.where(pick[:, None, :], spans, 0.0)), 0.0)
            * step_blk.T[None]
        )
        b_last = (weight_last[..., None] * b_blk[None, None]).astype(jnp.bfloat16)
        last_local = jnp.einsum("ghsn,shp->ghpn", b_last, x_blk, preferred_element_type=jnp.float32)
        last_gain = jnp.where(
            (ends_here & (prompt_ids == before_id))[:, None], jnp.exp(prefix_last), 0.0
        )
        return table + last_local + last_gain[:, :, None, None] * state_in[None]

    def without_ends():
        return table

    return lax.cond(jnp.any(ends_here), with_ends, without_ends)


def join_states(earlier, later):
    return (earlier[0] * later[0], later[0][:, None, None] * earlier[1] + later[1])


def on_device(
    hidden,
    token_prompt,
    request_prompt,
    in_gain,
    w_zx,
    w_bc,
    w_dt,
    dt_bias,
    a_log,
    conv_x,
    conv_bc,
    skip_gain,
    out_gain,
    w_out,
):
    tok_dev = hidden.shape[0]
    inner_dev = w_zx.shape[2]
    heads_dev = w_dt.shape[1]
    head_dim = inner_dev // heads_dev
    state_width = w_bc.shape[1] // 2
    taps = conv_x.shape[0]
    dp_index = lax.axis_index("dp")
    head_index = lax.axis_index("head")
    head_count = lax.axis_size("head")
    hidden_f = hidden.astype(jnp.float32)
    normed = (hidden_f * rms_scale(hidden_f) * in_gain).astype(jnp.bfloat16)
    pieces = (
        lax.all_gather(w_zx.astype(jnp.bfloat16), "dp", axis=0, tiled=True),
        lax.all_gather(w_dt.astype(jnp.bfloat16), "dp", axis=0, tiled=True),
        lax.all_gather(w_bc.astype(jnp.bfloat16), "dp", axis=0, tiled=True),
    )
    acc_zx, acc_step, acc_bc = tuple(
        (
            jnp.dot(normed, piece.reshape(piece.shape[0], -1), preferred_element_type=jnp.float32)
            for piece in pieces
        )
    )
    proj_bc = acc_bc.astype(jnp.bfloat16)
    proj_zx = acc_zx.astype(jnp.bfloat16)
    gate_z = proj_zx[:, :inner_dev]
    inner_x = proj_zx[:, inner_dev:]
    proj_dt = acc_step.astype(jnp.bfloat16)
    step_size = jax.nn.softplus(proj_dt.astype(jnp.float32) + dt_bias)
    rate = step_size * -jnp.exp(a_log)
    ids_own = lax.dynamic_slice_in_dim(token_prompt, dp_index * tok_dev, tok_dev)
    rim_start = jnp.maximum(dp_index * tok_dev - (taps - 1), 0)
    rim_ids = lax.dynamic_slice_in_dim(token_prompt, rim_start, taps - 1)
    tail_rows = jnp.concatenate(
        [inner_x[tok_dev - taps + 1 :], proj_bc[tok_dev - taps + 1 :]], axis=1
    )
    rim_rows = from_behind(tail_rows, "dp", 1)
    ext_ids = jnp.concatenate([rim_ids, ids_own])
    conv_inner = conv_core(
        jnp.concatenate([rim_rows[:, :inner_dev], inner_x], axis=0), ext_ids, ids_own, conv_x
    )
    conv_bc_out = conv_core(
        jnp.concatenate([rim_rows[:, inner_dev:], proj_bc], axis=0), ext_ids, ids_own, conv_bc
    )
    blocks = tok_dev // BLOCK
    x_heads = conv_inner.reshape(blocks, BLOCK, heads_dev, head_dim)
    b_conv = conv_bc_out[:, :state_width].reshape(blocks, BLOCK, state_width)
    c_conv = conv_bc_out[:, state_width:].reshape(blocks, BLOCK, state_width)
    step_blocks = step_size.reshape(blocks, BLOCK, heads_dev)
    rate_blocks = rate.reshape(blocks, BLOCK, heads_dev)
    id_blocks = ids_own.reshape(blocks, BLOCK)
    prev_last = jnp.where(dp_index > 0, token_prompt[jnp.maximum(dp_index * tok_dev - 1, 0)], -1)
    before_ids = jnp.concatenate([prev_last[None], id_blocks[:-1, -1]])
    y_intra, local_state, carry_gain, prefix = jax.vmap(block_local)(
        x_heads, b_conv, c_conv, step_blocks, rate_blocks, id_blocks, before_ids
    )

    def advance(carry, item):
        gain_acc, state_acc = carry
        gain, block_state = item
        return (
            (gain_acc * gain, gain[:, None, None] * state_acc + block_state),
            (gain_acc, state_acc),
        )

    unit_gain = jnp.ones((heads_dev,), jnp.float32)
    zero_state = jnp.zeros((heads_dev, head_dim, state_width), jnp.float32)
    (dev_gain, dev_state), (prior_gain, prior_state) = lax.scan(
        advance, (unit_gain, zero_state), (carry_gain, local_state)
    )
    scanned = carried_in((dev_gain, dev_state), "dp", join_states, (unit_gain, zero_state))
    incoming = scanned[1]
    block_in = prior_state + prior_gain[:, :, None, None] * incoming[None]
    prompt_ids = jnp.arange(PROMPTS, dtype=jnp.int32)
    last_index = (
        jnp.sum((token_prompt[None, :] <= prompt_ids[:, None]).astype(jnp.int32), axis=1) - 1
    )
    start_pos = (dp_index * blocks + jnp.arange(blocks, dtype=jnp.int32)) * BLOCK
    y_inter = jax.vmap(block_inter)(c_conv, prefix, id_blocks, before_ids, block_in)

    def collect(table, item):
        xb, bb, sb, pb, ib, fb, stb, ob = item
        return (block_last(last_index, table, xb, bb, sb, pb, ib, fb, stb, ob), None)

    empty_table = jnp.zeros((PROMPTS, heads_dev, head_dim, state_width), jnp.float32)
    local_table, unused = lax.scan(
        collect,
        empty_table,
        (x_heads, b_conv, step_blocks, prefix, id_blocks, before_ids, block_in, start_pos),
    )
    ssd_out = (y_intra + y_inter).reshape(tok_dev, heads_dev, head_dim) + skip_gain[
        None, :, None
    ] * conv_inner.astype(jnp.float32).reshape(tok_dev, heads_dev, head_dim)
    gated = ssd_out.reshape(tok_dev, inner_dev) * jax.nn.silu(gate_z.astype(jnp.float32))
    square_sum = lax.psum(jnp.sum(gated * gated, axis=1), "head")
    scale = lax.rsqrt(square_sum / (inner_dev * head_count) + EPSILON)
    normed_out = (gated * scale[:, None] * out_gain).astype(jnp.bfloat16)
    out_rows = tok_dev // head_count
    own_rows = lax.dynamic_slice_in_dim(hidden_f, head_index * out_rows, out_rows, 0)
    mixed = lax.psum_scatter(
        jnp.dot(normed_out, w_out, preferred_element_type=jnp.float32),
        "head",
        scatter_dimension=0,
        tiled=True,
    )
    layer_out = (own_rows + mixed).astype(jnp.bfloat16)
    table = lax.psum(local_table, "dp")
    one_hot = (request_prompt[:, None] == prompt_ids[None, :]).astype(jnp.float32)
    request_states = jnp.einsum("rg,ghpn->rhpn", one_hot, table, precision=lax.Precision.HIGHEST)
    return (layer_out, request_states)


LANES = 128
TILE_ROWS = 16
NEVER = -1e30


def kernel_params(mebibytes):
    return pltpu.CompilerParams(vmem_limit_bytes=mebibytes << 20)


def in_vmem(count):
    return [pl.BlockSpec(memory_space=pltpu.VMEM)] * count


def exchange(values, axis, bits):
    return lax.ppermute(values, axis, [(i, i ^ bits) for i in range(lax.axis_size(axis))])


def dot32(a, b, a_dim=1, b_dim=0):
    return lax.dot_general(
        a, b, (((a_dim,), (b_dim,)), ((), ())), preferred_element_type=jnp.float32
    )


def silu_tanh(values):
    half = 0.5 * values
    return half + half * jnp.tanh(half)


def widen(columns, pair, head_dim):
    rows = columns.shape[0]
    lane = lax.broadcasted_iota(jnp.int32, (rows, LANES), 1)
    first = jnp.broadcast_to(columns[:, 2 * pair : 2 * pair + 1], (rows, LANES))
    second = jnp.broadcast_to(columns[:, 2 * pair + 1 : 2 * pair + 2], (rows, LANES))
    return jnp.where(lane < head_dim, first, second)


def pack_kernel(
    req_ref,
    wzx_ref,
    wbc_ref,
    wdt_ref,
    hidden_ref,
    front_ref,
    gate_ref,
    tiles_ref,
    bc_ref,
    dt_ref,
    tail_ref,
    front_v,
    gate_v,
    pad_ref,
    sems,
):
    rows, bc_width = bc_ref.shape
    tok = hidden_ref.shape[0]
    inner = gate_v.shape[1]
    tiles = inner // LANES
    pieces = [(wdt_ref, dt_ref), (hidden_ref.at[tok - TILE_ROWS : tok], tail_ref), (wbc_ref, bc_ref)]
    for j in range(tiles):
        pieces.append((wzx_ref.at[:, :, j * LANES : (j + 1) * LANES], tiles_ref.at[j]))
    arrivals = [
        pltpu.make_async_copy(source, target, sems.at[k])
        for k, (source, target) in enumerate(pieces)
    ]
    for copy in arrivals:
        copy.start()
    front_v[rows:, :] = jnp.zeros((front_v.shape[0] - rows, inner + bc_width), jnp.bfloat16)
    pad_ref[...] = jnp.zeros_like(pad_ref)
    lane = lax.broadcasted_iota(jnp.int32, (TILE_ROWS, LANES), 1)
    wanted = jnp.zeros((TILE_ROWS, LANES), jnp.float32)
    for r in range(req_ref.shape[0]):
        wanted = jnp.where(lane == r, req_ref[r].astype(jnp.float32), wanted)
    pad_ref[:, rows : rows + LANES] = wanted
    arrivals[0].wait()
    pad_ref[0 : dt_ref.shape[0], 0:rows] = dt_ref[...]
    front_v[rows : rows + TILE_ROWS, 0 : rows + LANES] = pad_ref[...].astype(jnp.bfloat16)
    arrivals[1].wait()
    piece = rows + LANES
    for i in range(tail_ref.shape[1] // piece):
        at = rows + TILE_ROWS * (i + 1)
        front_v[at : at + TILE_ROWS, 0:piece] = tail_ref[:, i * piece : (i + 1) * piece]
    arrivals[2].wait()
    front_v[0:rows, inner:] = bc_ref[...].astype(jnp.bfloat16)
    for j in range(tiles):
        arrivals[3 + j].wait()
        pair = tiles_ref.at[j].reshape(2 * rows, LANES)
        front_v[0:rows, j * LANES : (j + 1) * LANES] = pair[pl.ds(1, rows, stride=2), :].astype(
            jnp.bfloat16
        )
    front_out = pltpu.make_async_copy(front_v, front_ref, sems.at[3 + tiles])
    front_out.start()
    for j in range(tiles):
        pair = tiles_ref.at[j].reshape(2 * rows, LANES)
        gate_v[:, j * LANES : (j + 1) * LANES] = pair[pl.ds(0, rows, stride=2), :].astype(
            jnp.bfloat16
        )
    gate_out = pltpu.make_async_copy(gate_v, gate_ref, sems.at[4 + tiles])
    gate_out.start()
    front_out.wait()
    gate_out.wait()


def facts_kernel(
    ids_ref,
    hidden_hbm,
    gain_ref,
    normed_ref,
    meta_ref,
    order_ref,
    pen_ref,
    hidden_ref,
    sem,
):
    tok = hidden_ref.shape[0]
    arrival = pltpu.make_async_copy(hidden_hbm, hidden_ref, sem)
    arrival.start()
    position = lax.axis_index("dp")
    start = pl.multiple_of(position * tok, tok)
    ids_i = ids_ref[:, pl.ds(start, tok)]
    behind = pl.multiple_of(jnp.maximum(start - LANES, 0), LANES)
    edge = ids_ref[:, pl.ds(behind, LANES)]
    edge = jnp.where(position > 0, edge, -1)
    ahead = pl.multiple_of(jnp.minimum(start + tok, ids_ref.shape[1] - LANES), LANES)
    after = jnp.where(start + tok < ids_ref.shape[1], ids_ref[:, pl.ds(ahead, LANES)], -1)
    after = after[:, 0:1].astype(jnp.float32)
    long = jnp.concatenate([edge, ids_i], axis=1).astype(jnp.float32)
    ids = ids_i.astype(jnp.float32)
    index = lax.broadcasted_iota(jnp.int32, (1, tok), 1)
    before, last = long[:, LANES - 1 : LANES], ids[:, tok - 1 : tok]
    middle = ids[:, BLOCK - 1 : BLOCK]
    one, zero = jnp.ones((1, tok), jnp.float32), jnp.zeros((1, tok), jnp.float32)
    flag = lambda what: jnp.where(what, one, zero)
    rows = [flag(ids == pltpu.roll(long, k, 1)[:, LANES:]) for k in (1, 2, 3)]
    rows.append(flag(ids == before))
    rows.append(flag((ids == middle) & (index >= BLOCK)))
    rows.append(flag((ids == middle) & (index < BLOCK)))
    rows.append(ids)
    rows.append(flag(ids == last))
    rows.append(flag((ids != last) | (after != last)))
    rows = jnp.concatenate(rows + [jnp.zeros((LANES - len(rows), tok), jnp.float32)], axis=0)
    facts = rows.T
    meta_ref[...] = facts
    column = facts[:, 6:7]
    here = lax.broadcasted_iota(jnp.int32, (tok, tok), 0)
    there = lax.broadcasted_iota(jnp.int32, (tok, tok), 1)
    same = column == ids
    order_ref[0:tok, :] = jnp.where(there <= here, 1.0, 0.0).astype(jnp.bfloat16)
    order_ref[tok:, :] = jnp.where((there > here) & same, 1.0, 0.0).astype(jnp.bfloat16)
    pen = jnp.where((there <= here) & same, 0.0, NEVER)
    for b in range(tok // BLOCK):
        own = slice(b * BLOCK, (b + 1) * BLOCK)
        pen_ref[b] = pen[own, own]
    arrival.wait()
    hidden = hidden_ref[...].astype(jnp.float32)
    normed_ref[...] = (hidden * rms_scale(hidden) * gain_ref[...]).astype(jnp.bfloat16)


def scale_kernel(w_ref, gain_ref, whole_ref, half_ref):
    rows, model = w_ref.shape
    half = half_ref.shape[1]
    gain = jnp.broadcast_to(gain_ref[...], (LANES, rows)).T
    for j in range(model // LANES):
        own = slice(j * LANES, (j + 1) * LANES)
        whole_ref[:, own] = (w_ref[:, own].astype(jnp.float32) * gain).astype(jnp.bfloat16)
    at = pl.multiple_of((lax.axis_index("dp") % 2) * half, half)
    half_ref[...] = whole_ref[:, pl.ds(at, half)]


def front_kernel(
    normed_ref,
    own_ref,
    near_ref,
    far_ref,
    last_ref,
    gain_ref,
    taps_x_ref,
    taps_bc_ref,
    meta_ref,
    order_ref,
    bias_ref,
    decay_ref,
    conv_ref,
    stepx_ref,
    faded_ref,
    prefix_ref,
    leaving_ref,
    middle_ref,
    w_ref,
    extra_ref,
    dtw_ref,
    ext_ref,
    sems,
):
    position = lax.axis_index("dp")
    model = normed_ref.shape[1]
    tok = normed_ref.shape[0]
    rows = model // extra_ref.shape[0]
    inner = taps_x_ref.shape[1]
    width = conv_ref.shape[1]
    state_width = (width - inner) // 2
    head_dim = LANES // 2
    pairs = inner // LANES
    copies = []
    for j, buffer in enumerate((own_ref, near_ref, far_ref, last_ref)):
        source = jnp.bitwise_xor(position, j)
        at = pl.multiple_of(source * rows, rows)
        copies.append(
            pltpu.make_async_copy(buffer.at[0:rows], w_ref.at[pl.ds(at, rows)], sems.at[2 * j])
        )
        copies.append(
            pltpu.make_async_copy(
                buffer.at[rows : rows + extra_ref.shape[1]],
                extra_ref.at[source],
                sems.at[2 * j + 1],
            )
        )
    for copy in copies:
        copy.start()
    dtw_ref[...] = jnp.zeros_like(dtw_ref)
    for copy in copies:
        copy.wait()
    for s in range(extra_ref.shape[0]):
        dtw_ref[0:TILE_ROWS, s * rows : (s + 1) * rows] = extra_ref[s, 0:TILE_ROWS, 0:rows]
    behind = jnp.maximum(position - 1, 0)
    piece = rows + LANES
    halo = jnp.concatenate(
        [
            extra_ref[behind, TILE_ROWS * (i + 1) : TILE_ROWS * (i + 2), 0:piece]
            for i in range(model // piece)
        ],
        axis=1,
    ).astype(jnp.float32)
    halo = halo * rms_scale(halo) * gain_ref[...]
    ext_ref[0:TILE_ROWS, :] = dot32(halo.astype(jnp.bfloat16), w_ref[...])
    normed = normed_ref[...]
    for at in range(0, width, 2 * LANES):
        stop = min(at + 2 * LANES, width)
        ext_ref[TILE_ROWS:, at:stop] = dot32(normed, w_ref[:, at:stop])
    head_lane = lax.broadcasted_iota(jnp.int32, (1, LANES), 1)
    bias = jnp.zeros((1, LANES), jnp.float32)
    decay = jnp.zeros((1, LANES), jnp.float32)
    for h in range(bias_ref.shape[0]):
        bias = jnp.where(head_lane == h, bias_ref[h], bias)
        decay = jnp.where(head_lane == h, decay_ref[h], decay)
    raw = dot32(normed, dtw_ref[...], 1, 1) + bias
    step = jnp.maximum(raw, 0.0) + jnp.log1p(jnp.exp(-jnp.abs(raw)))
    lane = lax.broadcasted_iota(jnp.int32, (tok, LANES), 1)
    rate = jnp.where(lane < TILE_ROWS, -step * jnp.exp(decay), 0.0)
    high = rate.astype(jnp.bfloat16).astype(jnp.float32)
    rest = rate - high
    mid = rest.astype(jnp.bfloat16).astype(jnp.float32)
    low = rest - mid
    packed = high + pltpu.roll(mid, TILE_ROWS, 1) + pltpu.roll(low, 2 * TILE_ROWS, 1)
    sums = dot32(order_ref[...], packed.astype(jnp.bfloat16))
    sums = (
        sums
        + pltpu.roll(sums, LANES - TILE_ROWS, 1)
        + pltpu.roll(sums, LANES - 2 * TILE_ROWS, 1)
    )
    prefix = sums[0:tok]
    fade = jnp.exp(sums[tok : 2 * tok])
    prefix_ref[...] = prefix
    fade_middle = jnp.exp(prefix[BLOCK - 1 : BLOCK, :] - prefix[0:BLOCK])
    same = [
        jnp.broadcast_to(meta_ref[:, k : k + 1], (tok, LANES)) for k in range(3)
    ]
    for j in range(width // LANES):
        own = slice(j * LANES, (j + 1) * LANES)
        if j < pairs:
            taps = taps_x_ref[:, own]
        else:
            taps = taps_bc_ref[:, j * LANES - inner : (j + 1) * LANES - inner]
        total = ext_ref[TILE_ROWS : TILE_ROWS + tok, own] * taps[3:4]
        for k in range(1, 4):
            total = total + same[k - 1] * (
                ext_ref[TILE_ROWS - k : TILE_ROWS - k + tok, own] * taps[3 - k : 4 - k]
            )
        conv_ref[:, own] = silu_tanh(total).astype(jnp.bfloat16)
    b_all = conv_ref[:, inner : inner + state_width].astype(jnp.float32)
    b_leaving = (b_all * meta_ref[:, 7:8]).astype(jnp.bfloat16)
    b_middle = (b_all * meta_ref[:, 5:6])[0:BLOCK].astype(jnp.bfloat16)
    for q in range(pairs):
        own = slice(q * LANES, (q + 1) * LANES)
        scaled = conv_ref[:, own].astype(jnp.float32) * widen(step, q, head_dim)
        stepx_ref[:, own] = scaled.astype(jnp.bfloat16)
        faded = (scaled * widen(fade, q, head_dim)).astype(jnp.bfloat16).T
        faded_ref[own, :] = faded
        leaving_ref[own, :] = dot32(faded, b_leaving).astype(jnp.bfloat16)
        to_middle = (scaled[0:BLOCK] * widen(fade_middle, q, head_dim)).astype(jnp.bfloat16).T
        middle_ref[own, :] = dot32(to_middle, b_middle).astype(jnp.bfloat16)


def table_kernel(conv_ref, faded_ref, meta_ref, table_ref):
    inner = faded_ref.shape[0]
    state_width = table_ref.shape[2]
    b_all = conv_ref[:, inner : inner + state_width].astype(jnp.float32)
    faded = faded_ref[...]
    for g in range(table_ref.shape[0]):
        ended = jnp.where(meta_ref[:, 6:7] == g, meta_ref[:, 8:9], 0.0)
        table_ref[g] = dot32(faded, (b_all * ended).astype(jnp.bfloat16)).astype(jnp.bfloat16)


def local_kernel(
    normed_ref,
    own_ref,
    near_ref,
    far_ref,
    last_ref,
    conv_ref,
    stepx_ref,
    prefix_ref,
    middle_ref,
    meta_ref,
    pen_ref,
    skip_ref,
    y_ref,
    gate_ref,
    w_ref,
    sems,
):
    position = lax.axis_index("dp")
    inner = y_ref.shape[1]
    rows = own_ref.shape[0]
    state_width = middle_ref.shape[1]
    head_dim = LANES // 2
    tok = y_ref.shape[0]
    copies = []
    for j, buffer in enumerate((own_ref, near_ref, far_ref, last_ref)):
        at = pl.multiple_of(jnp.bitwise_xor(position, j) * rows, rows)
        copies.append(pltpu.make_async_copy(buffer, w_ref.at[pl.ds(at, rows)], sems.at[j]))
    for copy in copies:
        copy.start()
    lane = lax.broadcasted_iota(jnp.int32, (BLOCK, LANES), 1)
    for b in range(tok // BLOCK):
        own_rows = slice(b * BLOCK, (b + 1) * BLOCK)
        b_blk = conv_ref[own_rows, inner : inner + state_width]
        c_blk = conv_ref[own_rows, inner + state_width :]
        scores = dot32(c_blk, b_blk, 1, 1)
        pen = pen_ref[b]
        prefix = prefix_ref[own_rows, :]
        across = prefix.T
        if b > 0:
            carried = jnp.exp(prefix - prefix_ref[b * BLOCK - 1 : b * BLOCK, :])
            carried = carried * meta_ref[own_rows, 4:5]
            from_middle = dot32(c_blk, middle_ref[...], 1, 1)
        for q in range(inner // LANES):
            own = slice(q * LANES, (q + 1) * LANES)
            x_pair = conv_ref[own_rows, own].astype(jnp.float32)
            out = x_pair * jnp.where(lane < head_dim, skip_ref[2 * q], skip_ref[2 * q + 1])
            if b > 0:
                out = out + widen(carried, q, head_dim) * from_middle[:, own]
            sx = stepx_ref[own_rows, own].astype(jnp.float32)
            for side in range(2):
                h = 2 * q + side
                gaps = prefix[:, h : h + 1] - across[h : h + 1, :] + pen
                mixing = (scores * jnp.exp(gaps)).astype(jnp.bfloat16)
                kept = (lane < head_dim) if side == 0 else (lane >= head_dim)
                out = out + dot32(mixing, jnp.where(kept, sx, 0.0).astype(jnp.bfloat16))
            y_ref[own_rows, own] = out
    for copy in copies:
        copy.wait()
    normed = normed_ref[...]
    gate_ref[...] = silu_tanh(dot32(normed, w_ref[...]))


def before_device(ids_ref, position, tok):
    return jnp.where(position > 0, ids_ref[jnp.maximum(position * tok - 1, 0)], -1)


def gate_kernel(ids_ref, enter_ref, conv_ref, prefix_ref, meta_ref, y_ref, z_ref, *outs):
    scratch, add_ref = outs[-1], outs[-2]
    outs = outs[:-2]
    inner = y_ref.shape[1]
    state_width = enter_ref.shape[1]
    head_dim = LANES // 2
    tok = y_ref.shape[0]
    c_all = conv_ref[:, inner + state_width :]
    inter = dot32(c_all, enter_ref[...], 1, 1)
    prefix = prefix_ref[...]
    carried = jnp.exp(prefix) * meta_ref[:, 3:4]
    for q in range(inner // LANES):
        own = slice(q * LANES, (q + 1) * LANES)
        value = y_ref[:, own] + widen(carried, q, head_dim) * inter[:, own]
        scratch[:, own] = (value * z_ref[:, own]).astype(jnp.bfloat16)
    position = lax.axis_index("dp")
    before = before_device(ids_ref, position, tok)
    stop = (position + 1) * tok
    after = ids_ref[jnp.minimum(stop, ids_ref.shape[0] - 1)]
    goes_on = (after == before) & (stop < ids_ref.shape[0])
    ended = (ids_ref[position * tok] == before) & ((ids_ref[stop - 1] != before) | ~goes_on)
    inside = jnp.where(meta_ref[:, 3:4] > 0.0, prefix, 0.0)
    gain = jnp.exp(jnp.min(inside, axis=0, keepdims=True)) * jnp.where(ended, 1.0, 0.0)
    for h in range(inner // head_dim):
        own = slice(h * head_dim, (h + 1) * head_dim)
        term = gain[:, h : h + 1] * enter_ref[own, :].astype(jnp.float32)
        add_ref[own, :] = term.astype(jnp.bfloat16)
    members = len(outs)
    part = y_ref.shape[0] // (2 * members)
    half = lax.axis_index("head") // 4
    for j, out in enumerate(outs):
        member = jnp.bitwise_xor(lax.axis_index("head") % 4, j)
        for k, side in enumerate((1 - half, half)):
            at = pl.multiple_of((side * members + member) * part, part)
            out[k * part : (k + 1) * part, :] = scratch[pl.ds(at, part), :]


def pick_kernel(
    ids_ref,
    own_ref,
    far_ref,
    table_ref,
    other_ref,
    add_ref,
    other_add_ref,
    keep_ref,
    send_ref,
    far_v,
    sem,
):
    count = keep_ref.shape[0]
    rows = far_ref.shape[0] - 4 * TILE_ROWS
    arrival = pltpu.make_async_copy(
        far_ref.at[rows : rows + TILE_ROWS, rows : rows + LANES], far_v, sem
    )
    arrival.start()
    position = lax.axis_index("dp")
    tok = ids_ref.shape[0] // lax.axis_size("dp")
    before = before_device(ids_ref, position, tok)
    other_before = before_device(ids_ref, jnp.bitwise_xor(position, 1), tok)
    add = add_ref[...].astype(jnp.float32)
    other_add = other_add_ref[...].astype(jnp.float32)

    def pick(g):
        total = table_ref[g].astype(jnp.float32) + other_ref[g].astype(jnp.float32)
        total = total + jnp.where(g == before, 1.0, 0.0) * add
        return total + jnp.where(g == other_before, 1.0, 0.0) * other_add

    arrival.wait()
    wanted = far_v[...].astype(jnp.float32)[0:1, :]
    lane = lax.broadcasted_iota(jnp.int32, (1, LANES), 1)
    for r in range(count):
        other = jnp.sum(jnp.where(lane == r, wanted, 0.0)).astype(jnp.int32)
        send_ref[r] = pick(other).astype(jnp.bfloat16)
    for r in range(count):
        keep_ref[r] = pick(own_ref[r]).astype(jnp.bfloat16)


def out_kernel(*refs):
    members = 4
    gated, buffers = refs[:members], refs[members : 3 * members - 1]
    send_ref, keep_ref, own_ref, part_ref, sems = refs[3 * members - 1 :]
    core = lax.axis_index("dp") % 2
    half = part_ref.shape[2]
    part = send_ref.shape[0]
    copies = [pltpu.make_async_copy(buffers[0], own_ref, sems.at[0])]
    for k, buffer in enumerate(buffers[1:]):
        copies.append(pltpu.make_async_copy(buffer, part_ref.at[k], sems.at[k + 1]))
    for copy in copies:
        copy.start()
    values = [g[...] for g in gated]
    squares = jnp.zeros((2 * part, 1), jnp.float32)
    for value in values:
        wide = value.astype(jnp.float32)
        squares = squares + jnp.sum(wide * wide, axis=1, keepdims=True)
    model = 2 * half
    lane = lax.broadcasted_iota(jnp.int32, (part, LANES), 1)
    high = squares[0:part].astype(jnp.bfloat16).astype(jnp.float32)
    low = squares[0:part] - high
    send_ref[:, model:] = jnp.where(lane == 0, high, low).astype(jnp.bfloat16)
    keep_ref[:, model:] = jnp.broadcast_to(squares[part:], (part, LANES))
    copies[0].wait()
    for k, side in enumerate((core, 1 - core)):
        at = pl.multiple_of(side * half, half)
        total = dot32(values[0], own_ref[:, pl.ds(at, half)])
        for j in range(1, members):
            slot = k * (members - 1) + j - 1
            copies[slot + 1].wait()
            total = total + dot32(values[j], part_ref[slot])
        send_ref[:, pl.ds(at, half)] = total[0:part].astype(jnp.bfloat16)
        keep_ref[:, pl.ds(at, half)] = total[part:]


def finish_kernel(inner_total, hidden_all, keep_ref, got_ref, out_ref, hidden_ref, sem):
    part, model = hidden_ref.shape
    at = pl.multiple_of(lax.axis_index("head") * part, part)
    arrival = pltpu.make_async_copy(hidden_all.at[pl.ds(at, part)], hidden_ref, sem)
    arrival.start()
    squares = keep_ref[:, model : model + 1]
    squares = squares + got_ref[:, model : model + 1].astype(jnp.float32)
    squares = squares + got_ref[:, model + 1 : model + 2].astype(jnp.float32)
    scale = lax.rsqrt(squares / inner_total + EPSILON)
    total = keep_ref[:, 0:model] + got_ref[:, 0:model].astype(jnp.float32)
    arrival.wait()
    out_ref[...] = (hidden_ref[...].astype(jnp.float32) + scale * total).astype(jnp.bfloat16)


def join_kernel(keep_ref, far_ref, out_ref):
    out_ref[...] = keep_ref[...].astype(jnp.float32) + far_ref[...].astype(jnp.float32)


def fused_on_device(
    hidden,
    token_prompt,
    request_prompt,
    in_gain,
    w_zx,
    w_bc,
    w_dt,
    dt_bias,
    a_log,
    conv_x,
    conv_bc,
    skip_gain,
    out_gain,
    w_out,
):
    tok, model = hidden.shape
    rows = w_zx.shape[0]
    inner = w_zx.shape[2]
    heads = w_dt.shape[1]
    state_width = w_bc.shape[1] // 2
    width = inner + 2 * state_width
    peers = lax.axis_size("dp")
    head_count = lax.axis_size("head")
    bf16, f32 = jnp.bfloat16, jnp.float32
    shape = jax.ShapeDtypeStruct
    smem = pl.BlockSpec(memory_space=pltpu.SMEM)
    in_hbm = pl.BlockSpec(memory_space=pltpu.HBM)

    extra = TILE_ROWS * (1 + model // (rows + LANES))
    front_own, gate_own = pl.pallas_call(
        pack_kernel,
        name="pack_weights",
        out_shape=(shape((rows + extra, width), bf16), shape((rows, inner), bf16)),
        in_specs=[smem] + [in_hbm] * 4,
        out_specs=(in_hbm, in_hbm),
        scratch_shapes=[
            pltpu.VMEM((inner // LANES, rows, 2, LANES), f32),
            pltpu.VMEM(w_bc.shape, f32),
            pltpu.VMEM((heads, rows), f32),
            pltpu.VMEM((TILE_ROWS, model), bf16),
            pltpu.VMEM((rows + extra, width), bf16),
            pltpu.VMEM((rows, inner), bf16),
            pltpu.VMEM((TILE_ROWS, rows + LANES), f32),
            pltpu.SemaphoreType.DMA((5 + inner // LANES,)),
        ],
        compiler_params=kernel_params(60),
    )(request_prompt, w_zx, w_bc, w_dt.T, hidden)
    blocks = tok // BLOCK
    normed, meta, order, pen = pl.pallas_call(
        facts_kernel,
        name="norm_and_token_facts",
        out_shape=(
            shape((tok, model), bf16),
            shape((tok, LANES), f32),
            shape((2 * tok, tok), bf16),
            shape((blocks, BLOCK, BLOCK), f32),
        ),
        in_specs=in_vmem(1) + [in_hbm] + in_vmem(1),
        out_specs=tuple(in_vmem(4)),
        scratch_shapes=[pltpu.VMEM((tok, model), bf16), pltpu.SemaphoreType.DMA],
        compiler_params=kernel_params(16),
        cost_estimate=pl.CostEstimate(
            flops=10 * tok * model, bytes_accessed=8_000_000, transcendentals=tok
        ),
    )(token_prompt[None, :], hidden, in_gain[None, :])
    half_width = model // 2
    scaled_out, half_out = pl.pallas_call(
        scale_kernel,
        name="scale_out_rows",
        out_shape=(shape(w_out.shape, bf16), shape((inner, half_width), bf16)),
        in_specs=in_vmem(2),
        out_specs=tuple(in_vmem(2)),
        compiler_params=kernel_params(8),
    )(w_out, out_gain[None, :])
    near_out = [exchange(half_out, "head", bits) for bits in (1, 2)]

    front_far = exchange(front_own, "dp", 2)
    front_near = exchange(front_own, "dp", 1)
    front_far, gate_own, normed, meta, order, pen = lax.optimization_barrier(
        (front_far, gate_own, normed, meta, order, pen)
    )
    front_last = exchange(front_far, "dp", 1)
    gate_far = exchange(gate_own, "dp", 2)
    gate_near = exchange(gate_own, "dp", 1)
    gate_last = exchange(gate_far, "dp", 1)
    half_out, *near_out, front_last = lax.optimization_barrier((half_out, *near_out, front_last))
    near_out.append(exchange(half_out, "head", 3))
    swapped_out = [exchange(part, "dp", 1) for part in near_out]

    half_width = model // 2
    scaled_out, half_out = pl.pallas_call(
        scale_kernel,
        name="scale_out_rows",
        out_shape=(shape(w_out.shape, bf16), shape((inner, half_width), bf16)),
        in_specs=in_vmem(2),
        out_specs=tuple(in_vmem(2)),
        compiler_params=kernel_params(8),
    )(w_out, out_gain[None, :])
    near_out = [exchange(half_out, "head", bits) for bits in (1, 2)]

    front_far = exchange(front_own, "dp", 2)
    front_near = exchange(front_own, "dp", 1)
    front_far, gate_own, normed, meta, order, pen = lax.optimization_barrier(
        (front_far, gate_own, normed, meta, order, pen)
    )
    front_last = exchange(front_far, "dp", 1)
    gate_far = exchange(gate_own, "dp", 2)
    gate_near = exchange(gate_own, "dp", 1)
    gate_last = exchange(gate_far, "dp", 1)
    half_out, *near_out, front_last = lax.optimization_barrier((half_out, *near_out, front_last))
    near_out.append(exchange(half_out, "head", 3))
    swapped_out = [exchange(part, "dp", 1) for part in near_out]

    head_rows = jnp.pad(jnp.stack([dt_bias, a_log]), ((0, 0), (0, LANES - heads)))

    conv, stepx, faded, prefix, leaving, middle = pl.pallas_call(
        front_kernel,
        name="project_and_convolve",
        out_shape=(
            shape((tok, width), bf16),
            shape((tok, inner), bf16),
            shape((inner, tok), bf16),
            shape((tok, LANES), f32),
            shape((inner, state_width), bf16),
            shape((inner, state_width), bf16),
        ),
        in_specs=in_vmem(1) + [in_hbm] * 4 + in_vmem(5) + [smem] * 2,
        out_specs=tuple(in_vmem(6)),
        scratch_shapes=[
            pltpu.VMEM((model, width), bf16),
            pltpu.VMEM((peers, extra, width), bf16),
            pltpu.VMEM((LANES, model), bf16),
            pltpu.VMEM((TILE_ROWS + tok, width), f32),
            pltpu.SemaphoreType.DMA((2 * peers,)),
        ],
        compiler_params=kernel_params(24),
        cost_estimate=pl.CostEstimate(
            flops=2 * tok * model * width, bytes_accessed=8_000_000, transcendentals=500_000
        ),
    )(
        normed,
        front_own,
        front_near,
        front_far,
        front_last,
        in_gain[None, :],
        conv_x,
        conv_bc,
        meta,
        order,
        dt_bias,
        a_log,
    )

    entering = lax.ppermute(leaving, "dp", [(i, i + 1) for i in range(peers - 1)])

    table = pl.pallas_call(
        table_kernel,
        name="sum_ended_states",
        out_shape=shape((PROMPTS, inner, state_width), bf16),
        in_specs=in_vmem(3),
        out_specs=in_vmem(1)[0],
        compiler_params=kernel_params(8),
        cost_estimate=pl.CostEstimate(
            flops=2 * tok * inner * state_width * PROMPTS, bytes_accessed=2_000_000, transcendentals=0
        ),
    )(conv, faded, meta)
    table_near = exchange(table, "dp", 1)

    y_local, gate = pl.pallas_call(
        local_kernel,
        name="mix_within_blocks",
        out_shape=(
            shape((tok, inner), f32),
            shape((tok, inner), f32),
        ),
        in_specs=in_vmem(1) + [in_hbm] * 4 + in_vmem(6) + [smem],
        out_specs=tuple(in_vmem(2)),
        scratch_shapes=[pltpu.VMEM((model, inner), bf16), pltpu.SemaphoreType.DMA((peers,))],
        compiler_params=kernel_params(24),
        cost_estimate=pl.CostEstimate(
            flops=2 * tok * model * inner, bytes_accessed=8_000_000, transcendentals=1_000_000
        ),
    )(
        normed,
        gate_own,
        gate_near,
        gate_far,
        gate_last,
        conv,
        stepx,
        prefix,
        middle,
        meta,
        pen,
        skip_gain,
    )

    out_rows = tok // head_count
    *gated, add = pl.pallas_call(
        gate_kernel,
        name="add_entering_and_gate",
        out_shape=tuple(shape((2 * out_rows, inner), bf16) for _ in range(4))
        + (shape((inner, state_width), bf16),),
        in_specs=[smem] + in_vmem(6),
        out_specs=tuple(in_vmem(5)),
        scratch_shapes=[pltpu.VMEM((tok, inner), bf16)],
        compiler_params=kernel_params(8),
    )(token_prompt, entering, conv, prefix, meta, y_local, gate)
    gated_in = [gated[0]] + [exchange(gated[bits], "head", bits) for bits in (1, 2, 3)]

    near_add = exchange(add, "dp", 1)
    requests = request_prompt.shape[0]
    keep, send = pl.pallas_call(
        pick_kernel,
        name="pick_request_states",
        out_shape=(shape((requests, inner, state_width), bf16),) * 2,
        in_specs=[smem, smem, in_hbm] + in_vmem(4),
        out_specs=tuple(in_vmem(2)),
        scratch_shapes=[pltpu.VMEM((TILE_ROWS, LANES), bf16), pltpu.SemaphoreType.DMA],
        compiler_params=kernel_params(8),
    )(token_prompt, request_prompt, front_far, table, table_near, add, near_add)
    far = exchange(send, "dp", 2)

    sums_send, sums_keep = pl.pallas_call(
        out_kernel,
        name="project_out",
        out_shape=(
            shape((out_rows, model + LANES), bf16),
            shape((out_rows, model + LANES), f32),
        ),
        in_specs=in_vmem(4) + [in_hbm] * 7,
        out_specs=tuple(in_vmem(2)),
        scratch_shapes=[
            pltpu.VMEM((inner, model), bf16),
            pltpu.VMEM((6, inner, half_width), bf16),
            pltpu.SemaphoreType.DMA((7,)),
        ],
        compiler_params=kernel_params(20),
        cost_estimate=pl.CostEstimate(
            flops=16 * out_rows * inner * model, bytes_accessed=6_000_000, transcendentals=0
        ),
    )(*gated_in, scaled_out, *near_out, *swapped_out)
    sums_in = exchange(sums_send, "head", 4)
    layer_out = pl.pallas_call(
        functools.partial(finish_kernel, inner * head_count),
        name="scale_and_add_hidden",
        out_shape=shape((out_rows, model), bf16),
        in_specs=[in_hbm] + in_vmem(2),
        out_specs=in_vmem(1)[0],
        scratch_shapes=[pltpu.VMEM((out_rows, model), bf16), pltpu.SemaphoreType.DMA],
        compiler_params=kernel_params(4),
    )(hidden, sums_keep, sums_in)
    request_states = pl.pallas_call(
        join_kernel,
        name="join_request_states",
        out_shape=shape(keep.shape, f32),
        in_specs=in_vmem(2),
        out_specs=in_vmem(1)[0],
        compiler_params=kernel_params(4),
    )(keep, far)
    return (
        layer_out,
        request_states.reshape(requests, heads, inner // heads, state_width),
    )


def fits_fused(mesh):
    return dict(mesh.shape) == {"dp": 4, "head": 8}


def solution(mesh):
    in_specs = (
        P("dp", None),
        P(),
        P("dp"),
        P(),
        P("dp", None, "head"),
        P("dp", None),
        P("dp", "head"),
        P("head"),
        P("head"),
        P(None, "head"),
        P(),
        P("head"),
        P("head"),
        P("head", None),
    )
    out_specs = (P(("dp", "head"), None), P("dp", "head", None, None))
    program = fused_on_device if fits_fused(mesh) else on_device
    return jax.shard_map(
        program, mesh=mesh, in_specs=in_specs, out_specs=out_specs, check_vma=False
    )
```

```python
import functools

import jax
import jax.numpy as jnp
from jax import lax
from jax.experimental import pallas as pl
from jax.experimental.pallas import tpu as pltpu
from jax.sharding import PartitionSpec as P

BLOCK = 256
PROMPTS = 8


EPSILON = 1e-05


def from_behind(shard, axis, by):
    peers = lax.axis_size(axis)
    pairs = [(i, i + by) for i in range(peers) if 0 <= i + by < peers]
    return lax.ppermute(shard, axis, pairs)


def carried_in(shard, axis, combine, identity):
    peers, position = (lax.axis_size(axis), lax.axis_index(axis))
    everything = jax.tree.map(lambda part: lax.all_gather(part, axis), shard)
    start = jax.tree.map(
        lambda part, zero: jnp.broadcast_to(jnp.asarray(zero, part.dtype), part.shape),
        shard,
        identity,
    )

    def step(k, before):
        reached = k < position
        new = combine(before, jax.tree.map(lambda part: part[k], everything))
        return jax.tree.map(lambda a, b: jnp.where(reached, a, b), new, before)

    return lax.fori_loop(0, peers, step, start)


def rms_scale(values):
    return lax.rsqrt(jnp.mean(values * values, axis=-1, keepdims=True) + EPSILON)


def conv_core(extended, extended_ids, token_ids, weights):
    length = token_ids.shape[0]
    total = jnp.zeros((length, extended.shape[1]), jnp.float32)
    for offset in range(weights.shape[0]):
        same = (extended_ids[offset : offset + length] == token_ids)[:, None]
        total = total + jnp.where(
            same, weights[offset] * extended[offset : offset + length].astype(jnp.float32), 0.0
        )
    return jax.nn.silu(total).astype(jnp.bfloat16)


def block_local(x_blk, b_blk, c_blk, step_blk, rate_blk, ids_blk, before_id):
    length = ids_blk.shape[0]
    position = jnp.arange(length, dtype=jnp.int32)
    prefix = jnp.cumsum(rate_blk, axis=0)
    prefix_t = prefix.T
    same = (ids_blk[:, None] == ids_blk[None, :]) & (position[None, :] <= position[:, None])
    gaps = prefix_t[:, :, None] - prefix_t[:, None, :]
    decay = jnp.where(same[None], jnp.exp(jnp.where(same[None], gaps, 0.0)), 0.0)
    scores = jnp.dot(c_blk, b_blk.T, preferred_element_type=jnp.float32)
    mixing = (scores[None] * decay * step_blk.T[:, None, :]).astype(jnp.bfloat16)
    y_intra = jnp.einsum("hts,shp->thp", mixing, x_blk, preferred_element_type=jnp.float32)
    end_id = ids_blk[-1]
    alive = ids_blk == end_id
    weight_end = (
        jnp.where(
            alive[None, :],
            jnp.exp(jnp.where(alive[None, :], prefix_t[:, -1:] - prefix_t, 0.0)),
            0.0,
        )
        * step_blk.T
    )
    b_weighted = (weight_end[:, :, None] * b_blk[None]).astype(jnp.bfloat16)
    local_state = jnp.einsum("hsn,shp->hpn", b_weighted, x_blk, preferred_element_type=jnp.float32)
    carry_gain = jnp.where(end_id == before_id, jnp.exp(prefix_t[:, -1]), 0.0)
    return (y_intra, local_state, carry_gain, prefix)


def block_inter(c_blk, prefix, ids_blk, before_id, state_in):
    entering = ids_blk == before_id
    inter_scale = jnp.where(entering[:, None], jnp.exp(prefix), 0.0)
    return inter_scale[:, :, None] * jnp.einsum(
        "tn,hpn->thp", c_blk.astype(jnp.float32), state_in, precision=lax.Precision.HIGHEST
    )


def block_last(
    last_index, table, x_blk, b_blk, step_blk, prefix, ids_blk, before_id, state_in, start
):
    length = ids_blk.shape[0]
    position = jnp.arange(length, dtype=jnp.int32)
    prompt_ids = jnp.arange(last_index.shape[0], dtype=jnp.int32)
    local_last = last_index - start
    ends_here = (local_last >= 0) & (local_last < length)
    clipped = jnp.clip(local_last, 0, length - 1)

    def with_ends():
        prefix_t = prefix.T
        prefix_last = prefix[clipped]
        pick = (
            ends_here[:, None]
            & (ids_blk[None, :] == prompt_ids[:, None])
            & (position[None, :] <= clipped[:, None])
        )
        spans = prefix_last[:, :, None] - prefix_t[None]
        weight_last = (
            jnp.where(pick[:, None, :], jnp.exp(jnp.where(pick[:, None, :], spans, 0.0)), 0.0)
            * step_blk.T[None]
        )
        b_last = (weight_last[..., None] * b_blk[None, None]).astype(jnp.bfloat16)
        last_local = jnp.einsum("ghsn,shp->ghpn", b_last, x_blk, preferred_element_type=jnp.float32)
        last_gain = jnp.where(
            (ends_here & (prompt_ids == before_id))[:, None], jnp.exp(prefix_last), 0.0
        )
        return table + last_local + last_gain[:, :, None, None] * state_in[None]

    def without_ends():
        return table

    return lax.cond(jnp.any(ends_here), with_ends, without_ends)


def join_states(earlier, later):
    return (earlier[0] * later[0], later[0][:, None, None] * earlier[1] + later[1])


def on_device(
    hidden,
    token_prompt,
    request_prompt,
    in_gain,
    w_zx,
    w_bc,
    w_dt,
    dt_bias,
    a_log,
    conv_x,
    conv_bc,
    skip_gain,
    out_gain,
    w_out,
):
    tok_dev = hidden.shape[0]
    inner_dev = w_zx.shape[2]
    heads_dev = w_dt.shape[1]
    head_dim = inner_dev // heads_dev
    state_width = w_bc.shape[1] // 2
    taps = conv_x.shape[0]
    dp_index = lax.axis_index("dp")
    head_index = lax.axis_index("head")
    head_count = lax.axis_size("head")
    hidden_f = hidden.astype(jnp.float32)
    normed = (hidden_f * rms_scale(hidden_f) * in_gain).astype(jnp.bfloat16)
    pieces = (
        lax.all_gather(w_zx.astype(jnp.bfloat16), "dp", axis=0, tiled=True),
        lax.all_gather(w_dt.astype(jnp.bfloat16), "dp", axis=0, tiled=True),
        lax.all_gather(w_bc.astype(jnp.bfloat16), "dp", axis=0, tiled=True),
    )
    acc_zx, acc_step, acc_bc = tuple(
        (
            jnp.dot(normed, piece.reshape(piece.shape[0], -1), preferred_element_type=jnp.float32)
            for piece in pieces
        )
    )
    proj_bc = acc_bc.astype(jnp.bfloat16)
    proj_zx = acc_zx.astype(jnp.bfloat16)
    gate_z = proj_zx[:, :inner_dev]
    inner_x = proj_zx[:, inner_dev:]
    proj_dt = acc_step.astype(jnp.bfloat16)
    step_size = jax.nn.softplus(proj_dt.astype(jnp.float32) + dt_bias)
    rate = step_size * -jnp.exp(a_log)
    ids_own = lax.dynamic_slice_in_dim(token_prompt, dp_index * tok_dev, tok_dev)
    rim_start = jnp.maximum(dp_index * tok_dev - (taps - 1), 0)
    rim_ids = lax.dynamic_slice_in_dim(token_prompt, rim_start, taps - 1)
    tail_rows = jnp.concatenate(
        [inner_x[tok_dev - taps + 1 :], proj_bc[tok_dev - taps + 1 :]], axis=1
    )
    rim_rows = from_behind(tail_rows, "dp", 1)
    ext_ids = jnp.concatenate([rim_ids, ids_own])
    conv_inner = conv_core(
        jnp.concatenate([rim_rows[:, :inner_dev], inner_x], axis=0), ext_ids, ids_own, conv_x
    )
    conv_bc_out = conv_core(
        jnp.concatenate([rim_rows[:, inner_dev:], proj_bc], axis=0), ext_ids, ids_own, conv_bc
    )
    blocks = tok_dev // BLOCK
    x_heads = conv_inner.reshape(blocks, BLOCK, heads_dev, head_dim)
    b_conv = conv_bc_out[:, :state_width].reshape(blocks, BLOCK, state_width)
    c_conv = conv_bc_out[:, state_width:].reshape(blocks, BLOCK, state_width)
    step_blocks = step_size.reshape(blocks, BLOCK, heads_dev)
    rate_blocks = rate.reshape(blocks, BLOCK, heads_dev)
    id_blocks = ids_own.reshape(blocks, BLOCK)
    prev_last = jnp.where(dp_index > 0, token_prompt[jnp.maximum(dp_index * tok_dev - 1, 0)], -1)
    before_ids = jnp.concatenate([prev_last[None], id_blocks[:-1, -1]])
    y_intra, local_state, carry_gain, prefix = jax.vmap(block_local)(
        x_heads, b_conv, c_conv, step_blocks, rate_blocks, id_blocks, before_ids
    )

    def advance(carry, item):
        gain_acc, state_acc = carry
        gain, block_state = item
        return (
            (gain_acc * gain, gain[:, None, None] * state_acc + block_state),
            (gain_acc, state_acc),
        )

    unit_gain = jnp.ones((heads_dev,), jnp.float32)
    zero_state = jnp.zeros((heads_dev, head_dim, state_width), jnp.float32)
    (dev_gain, dev_state), (prior_gain, prior_state) = lax.scan(
        advance, (unit_gain, zero_state), (carry_gain, local_state)
    )
    scanned = carried_in((dev_gain, dev_state), "dp", join_states, (unit_gain, zero_state))
    incoming = scanned[1]
    block_in = prior_state + prior_gain[:, :, None, None] * incoming[None]
    prompt_ids = jnp.arange(PROMPTS, dtype=jnp.int32)
    last_index = (
        jnp.sum((token_prompt[None, :] <= prompt_ids[:, None]).astype(jnp.int32), axis=1) - 1
    )
    start_pos = (dp_index * blocks + jnp.arange(blocks, dtype=jnp.int32)) * BLOCK
    y_inter = jax.vmap(block_inter)(c_conv, prefix, id_blocks, before_ids, block_in)

    def collect(table, item):
        xb, bb, sb, pb, ib, fb, stb, ob = item
        return (block_last(last_index, table, xb, bb, sb, pb, ib, fb, stb, ob), None)

    empty_table = jnp.zeros((PROMPTS, heads_dev, head_dim, state_width), jnp.float32)
    local_table, unused = lax.scan(
        collect,
        empty_table,
        (x_heads, b_conv, step_blocks, prefix, id_blocks, before_ids, block_in, start_pos),
    )
    ssd_out = (y_intra + y_inter).reshape(tok_dev, heads_dev, head_dim) + skip_gain[
        None, :, None
    ] * conv_inner.astype(jnp.float32).reshape(tok_dev, heads_dev, head_dim)
    gated = ssd_out.reshape(tok_dev, inner_dev) * jax.nn.silu(gate_z.astype(jnp.float32))
    square_sum = lax.psum(jnp.sum(gated * gated, axis=1), "head")
    scale = lax.rsqrt(square_sum / (inner_dev * head_count) + EPSILON)
    normed_out = (gated * scale[:, None] * out_gain).astype(jnp.bfloat16)
    out_rows = tok_dev // head_count
    own_rows = lax.dynamic_slice_in_dim(hidden_f, head_index * out_rows, out_rows, 0)
    mixed = lax.psum_scatter(
        jnp.dot(normed_out, w_out, preferred_element_type=jnp.float32),
        "head",
        scatter_dimension=0,
        tiled=True,
    )
    layer_out = (own_rows + mixed).astype(jnp.bfloat16)
    table = lax.psum(local_table, "dp")
    one_hot = (request_prompt[:, None] == prompt_ids[None, :]).astype(jnp.float32)
    request_states = jnp.einsum("rg,ghpn->rhpn", one_hot, table, precision=lax.Precision.HIGHEST)
    return (layer_out, request_states)


LANES = 128
TILE_ROWS = 16
NEVER = -1e30
Y_NEAR, Z_NEAR, Z_FAR = 1, 2, 4
RELATED = (0, Y_NEAR, Z_FAR, Y_NEAR | Z_FAR)
LITTLE = pl.CostEstimate(flops=1000, bytes_accessed=1000, transcendentals=0)


def kernel_params(mebibytes):
    return pltpu.CompilerParams(vmem_limit_bytes=mebibytes << 20)


def in_vmem(count):
    return [pl.BlockSpec(memory_space=pltpu.VMEM)] * count


def exchange(values, axis, bits):
    return lax.ppermute(values, axis, [(i, i ^ bits) for i in range(lax.axis_size(axis))])


def dot32(a, b, a_dim=1, b_dim=0):
    return lax.dot_general(
        a, b, (((a_dim,), (b_dim,)), ((), ())), preferred_element_type=jnp.float32
    )


def silu_tanh(values):
    half = 0.5 * values
    return half + half * jnp.tanh(half)


def widen(columns, pair, head_dim):
    rows = columns.shape[0]
    lane = lax.broadcasted_iota(jnp.int32, (rows, LANES), 1)
    first = jnp.broadcast_to(columns[:, 2 * pair : 2 * pair + 1], (rows, LANES))
    second = jnp.broadcast_to(columns[:, 2 * pair + 1 : 2 * pair + 2], (rows, LANES))
    return jnp.where(lane < head_dim, first, second)


def pack_first_kernel(
    req_ref, wbc_ref, wdt_ref, hidden_ref, first_ref, bc_v, dt_v, tail_v, dt_wide, sems
):
    rows, width = bc_v.shape
    tok, model = hidden_ref.shape
    arrivals = [
        pltpu.make_async_copy(source, target, sems.at[k])
        for k, (source, target) in enumerate(
            (
                (wdt_ref, dt_v),
                (hidden_ref.at[tok - TILE_ROWS : tok], tail_v),
                (wbc_ref, bc_v),
            )
        )
    ]
    for copy in arrivals:
        copy.start()
    dt_wide[...] = jnp.zeros_like(dt_wide)
    lane = lax.broadcasted_iota(jnp.int32, (1, LANES), 1)
    wanted = jnp.zeros((1, LANES), jnp.float32)
    for r in range(req_ref.shape[0]):
        wanted = jnp.where(lane == r, req_ref[r].astype(jnp.float32), wanted)
    dt_wide[0:1, rows : rows + LANES] = wanted
    arrivals[0].wait()
    dt_wide[0 : dt_v.shape[0], 0:rows] = dt_v[...]
    arrivals[1].wait()
    upper = lax.broadcasted_iota(jnp.int32, (TILE_ROWS, model), 0) < TILE_ROWS // 2
    below = jnp.where(upper, dt_wide[...], tail_v[...].astype(jnp.float32)).astype(jnp.bfloat16)
    for i in range(model // width):
        at = rows + TILE_ROWS * i
        first_ref[at : at + TILE_ROWS, :] = below[:, i * width : (i + 1) * width]
    arrivals[2].wait()
    first_ref[0:rows, :] = bc_v[...].astype(jnp.bfloat16)


def pack_rest_kernel(wzx_ref, x_ref, gate_ref, tiles_ref, sems):
    rows, inner = x_ref.shape
    arrivals = [
        pltpu.make_async_copy(
            wzx_ref.at[:, :, j * LANES : (j + 1) * LANES], tiles_ref.at[j], sems.at[j]
        )
        for j in range(inner // LANES)
    ]
    for copy in arrivals:
        copy.start()
    for j, copy in enumerate(arrivals):
        copy.wait()
        own = slice(j * LANES, (j + 1) * LANES)
        pair = tiles_ref.at[j].reshape(2 * rows, LANES)
        x_ref[:, own] = pair[pl.ds(1, rows, stride=2), :].astype(jnp.bfloat16)
        gate_ref[:, own] = pair[pl.ds(0, rows, stride=2), :].astype(jnp.bfloat16)


def facts_kernel(
    ids_ref,
    hidden_hbm,
    gain_ref,
    normed_ref,
    meta_ref,
    order_ref,
    pen_ref,
    hidden_ref,
    sem,
):
    tok = hidden_ref.shape[0]
    arrival = pltpu.make_async_copy(hidden_hbm, hidden_ref, sem)
    arrival.start()
    position = lax.axis_index("dp")
    start = pl.multiple_of(position * tok, tok)
    ids_i = ids_ref[:, pl.ds(start, tok)]
    behind = pl.multiple_of(jnp.maximum(start - LANES, 0), LANES)
    edge = ids_ref[:, pl.ds(behind, LANES)]
    edge = jnp.where(position > 0, edge, -1)
    ahead = pl.multiple_of(jnp.minimum(start + tok, ids_ref.shape[1] - LANES), LANES)
    after = jnp.where(start + tok < ids_ref.shape[1], ids_ref[:, pl.ds(ahead, LANES)], -1)
    after = after[:, 0:1].astype(jnp.float32)
    long = jnp.concatenate([edge, ids_i], axis=1).astype(jnp.float32)
    ids = ids_i.astype(jnp.float32)
    index = lax.broadcasted_iota(jnp.int32, (1, tok), 1)
    before, last = long[:, LANES - 1 : LANES], ids[:, tok - 1 : tok]
    middle = ids[:, BLOCK - 1 : BLOCK]
    one, zero = jnp.ones((1, tok), jnp.float32), jnp.zeros((1, tok), jnp.float32)
    flag = lambda what: jnp.where(what, one, zero)
    rows = [flag(ids == pltpu.roll(long, k, 1)[:, LANES:]) for k in (1, 2, 3)]
    rows.append(flag(ids == before))
    rows.append(flag((ids == middle) & (index >= BLOCK)))
    rows.append(flag((ids == middle) & (index < BLOCK)))
    rows.append(ids)
    rows.append(flag(ids == last))
    rows.append(flag((ids != last) | (after != last)))
    rows = jnp.concatenate(rows + [jnp.zeros((LANES - len(rows), tok), jnp.float32)], axis=0)
    facts = rows.T
    meta_ref[...] = facts
    column = facts[:, 6:7]
    here = lax.broadcasted_iota(jnp.int32, (tok, tok), 0)
    there = lax.broadcasted_iota(jnp.int32, (tok, tok), 1)
    same = column == ids
    order_ref[0:tok, :] = jnp.where(there <= here, 1.0, 0.0).astype(jnp.bfloat16)
    order_ref[tok:, :] = jnp.where((there > here) & same, 1.0, 0.0).astype(jnp.bfloat16)
    pen = jnp.where((there <= here) & same, 0.0, NEVER)
    for b in range(tok // BLOCK):
        own = slice(b * BLOCK, (b + 1) * BLOCK)
        pen_ref[b] = pen[own, own]
    arrival.wait()
    hidden = hidden_ref[...].astype(jnp.float32)
    normed_ref[...] = (hidden * rms_scale(hidden) * gain_ref[...]).astype(jnp.bfloat16)


def scale_kernel(w_ref, gain_ref, whole_ref, part_ref):
    rows, model = w_ref.shape
    width = part_ref.shape[1]
    gain = jnp.broadcast_to(gain_ref[...], (LANES, rows)).T
    for j in range(model // LANES):
        own = slice(j * LANES, (j + 1) * LANES)
        whole_ref[:, own] = (w_ref[:, own].astype(jnp.float32) * gain).astype(jnp.bfloat16)
    at = pl.multiple_of((lax.axis_index("dp") % 2) * width, LANES)
    part_ref[...] = whole_ref[:, pl.ds(at, width)]


def gather_rows(position, buffers, rows, w_ref, sems):
    copies = []
    for j, buffer in enumerate(buffers):
        at = pl.multiple_of(jnp.bitwise_xor(position, j) * rows, rows)
        copies.append(
            pltpu.make_async_copy(buffer.at[0:rows], w_ref.at[pl.ds(at, rows)], sems.at[j])
        )
    return copies


def project_rows(normed, halo, w, ext_ref, at, stop):
    ext_ref[0:TILE_ROWS, at:stop] = dot32(halo, w)
    ext_ref[TILE_ROWS:, at:stop] = dot32(normed, w)


def convolve(ext_ref, own, taps, same):
    tok = same[0].shape[0]
    total = ext_ref[TILE_ROWS : TILE_ROWS + tok, own] * taps[3:4]
    for k in range(1, 4):
        total = total + same[k - 1] * (
            ext_ref[TILE_ROWS - k : TILE_ROWS - k + tok, own] * taps[3 - k : 4 - k]
        )
    return silu_tanh(total)


def first_kernel(
    normed_ref,
    own_ref,
    near_ref,
    far_ref,
    last_ref,
    gain_ref,
    taps_ref,
    meta_ref,
    order_ref,
    bias_ref,
    decay_ref,
    bc_ref,
    step_ref,
    prefix_ref,
    fade_ref,
    halo_ref,
    w_ref,
    extra_ref,
    dtw_ref,
    ext_ref,
    sems,
):
    position = lax.axis_index("dp")
    tok, model = normed_ref.shape
    peers, extra, width = extra_ref.shape
    rows = model // peers
    buffers = (own_ref, near_ref, far_ref, last_ref)
    copies = gather_rows(position, buffers, rows, w_ref, sems)
    for j, buffer in enumerate(buffers):
        copies.append(
            pltpu.make_async_copy(
                buffer.at[rows : rows + extra],
                extra_ref.at[jnp.bitwise_xor(position, j)],
                sems.at[peers + j],
            )
        )
    for copy in copies:
        copy.start()
    dtw_ref[...] = jnp.zeros_like(dtw_ref)
    for copy in copies:
        copy.wait()
    pieces = model // width
    for s in range(peers):
        below = jnp.concatenate(
            [extra_ref[s, i * TILE_ROWS : (i + 1) * TILE_ROWS, :] for i in range(pieces)], axis=1
        )
        row = lax.broadcasted_iota(jnp.int32, (TILE_ROWS, rows), 0)
        steps = jnp.where(row < bias_ref.shape[0], below[:, 0:rows].astype(jnp.float32), 0.0)
        dtw_ref[0:TILE_ROWS, s * rows : (s + 1) * rows] = steps.astype(jnp.bfloat16)
    behind = jnp.maximum(position - 1, 0)
    halo = jnp.concatenate(
        [extra_ref[behind, i * TILE_ROWS : (i + 1) * TILE_ROWS, :] for i in range(pieces)], axis=1
    ).astype(jnp.float32)
    halo = (halo * rms_scale(halo) * gain_ref[...]).astype(jnp.bfloat16)
    halo_ref[...] = halo
    normed = normed_ref[...]
    head_lane = lax.broadcasted_iota(jnp.int32, (1, LANES), 1)
    bias = jnp.zeros((1, LANES), jnp.float32)
    decay = jnp.zeros((1, LANES), jnp.float32)
    for h in range(bias_ref.shape[0]):
        bias = jnp.where(head_lane == h, bias_ref[h], bias)
        decay = jnp.where(head_lane == h, decay_ref[h], decay)
    raw = dot32(normed, dtw_ref[...], 1, 1) + bias
    step = jnp.maximum(raw, 0.0) + jnp.log1p(jnp.exp(-jnp.abs(raw)))
    step_ref[...] = step
    lane = lax.broadcasted_iota(jnp.int32, (tok, LANES), 1)
    rate = jnp.where(lane < TILE_ROWS, -step * jnp.exp(decay), 0.0)
    high = rate.astype(jnp.bfloat16).astype(jnp.float32)
    rest = rate - high
    mid = rest.astype(jnp.bfloat16).astype(jnp.float32)
    low = rest - mid
    packed = high + pltpu.roll(mid, TILE_ROWS, 1) + pltpu.roll(low, 2 * TILE_ROWS, 1)
    sums = dot32(order_ref[...], packed.astype(jnp.bfloat16))
    sums = (
        sums
        + pltpu.roll(sums, LANES - TILE_ROWS, 1)
        + pltpu.roll(sums, LANES - 2 * TILE_ROWS, 1)
    )
    prefix_ref[...] = sums[0:tok]
    fade_ref[...] = jnp.exp(sums[tok : 2 * tok])
    project_rows(normed, halo, w_ref[...], ext_ref, 0, width)
    same = [jnp.broadcast_to(meta_ref[:, k : k + 1], (tok, LANES)) for k in range(3)]
    for j in range(width // LANES):
        own = slice(j * LANES, (j + 1) * LANES)
        bc_ref[:, own] = convolve(ext_ref, own, taps_ref[:, own], same).astype(jnp.bfloat16)


def inner_kernel(
    normed_ref,
    own_ref,
    near_ref,
    far_ref,
    last_ref,
    halo_ref,
    taps_ref,
    meta_ref,
    bc_ref,
    step_ref,
    prefix_ref,
    fade_ref,
    x_ref,
    stepx_ref,
    faded_ref,
    leaving_ref,
    middle_ref,
    w_ref,
    ext_ref,
    sems,
):
    position = lax.axis_index("dp")
    tok = normed_ref.shape[0]
    inner = x_ref.shape[1]
    rows = own_ref.shape[0]
    head_dim = LANES // 2
    copies = gather_rows(position, (own_ref, near_ref, far_ref, last_ref), rows, w_ref, sems)
    for copy in copies:
        copy.start()
    state_width = leaving_ref.shape[1]
    step = step_ref[...]
    fade = fade_ref[...]
    fade_middle = jnp.exp(prefix_ref[BLOCK - 1 : BLOCK, :] - prefix_ref[0:BLOCK, :])
    b_all = bc_ref[:, 0:state_width].astype(jnp.float32)
    b_leaving = (b_all * meta_ref[:, 7:8]).astype(jnp.bfloat16)
    b_middle = (b_all * meta_ref[:, 5:6])[0:BLOCK].astype(jnp.bfloat16)
    same = [jnp.broadcast_to(meta_ref[:, k : k + 1], (tok, LANES)) for k in range(3)]
    for copy in copies:
        copy.wait()
    project_rows(normed_ref[...], halo_ref[...], w_ref[...], ext_ref, 0, inner)
    for q in range(inner // LANES):
        own = slice(q * LANES, (q + 1) * LANES)
        rounded = convolve(ext_ref, own, taps_ref[:, own], same).astype(jnp.bfloat16)
        x_ref[:, own] = rounded
        scaled = rounded.astype(jnp.float32) * widen(step, q, head_dim)
        stepx_ref[:, own] = scaled.astype(jnp.bfloat16)
        faded = (scaled * widen(fade, q, head_dim)).astype(jnp.bfloat16).T
        faded_ref[own, :] = faded
        leaving_ref[own, :] = dot32(faded, b_leaving).astype(jnp.bfloat16)
        to_middle = (scaled[0:BLOCK] * widen(fade_middle, q, head_dim)).astype(jnp.bfloat16).T
        middle_ref[own, :] = dot32(to_middle, b_middle).astype(jnp.bfloat16)


def table_kernel(bc_ref, faded_ref, meta_ref, *table_refs):
    rows, state_width = table_refs[0].shape[1:]
    b_all = bc_ref[:, 0:state_width].astype(jnp.float32)
    for g in range(table_refs[0].shape[0]):
        ended = jnp.where(meta_ref[:, 6:7] == g, meta_ref[:, 8:9], 0.0)
        b_ended = (b_all * ended).astype(jnp.bfloat16)
        for k, table_ref in enumerate(table_refs):
            faded = faded_ref[k * rows : (k + 1) * rows, :]
            table_ref[g] = dot32(faded, b_ended).astype(jnp.bfloat16)


def local_kernel(
    x_ref,
    bc_ref,
    stepx_ref,
    prefix_ref,
    middle_ref,
    meta_ref,
    pen_ref,
    skip_ref,
    y_ref,
):
    inner = y_ref.shape[1]
    state_width = middle_ref.shape[1]
    head_dim = LANES // 2
    tok = y_ref.shape[0]
    lane = lax.broadcasted_iota(jnp.int32, (BLOCK, LANES), 1)
    for b in range(tok // BLOCK):
        own_rows = slice(b * BLOCK, (b + 1) * BLOCK)
        b_blk = bc_ref[own_rows, 0:state_width]
        c_blk = bc_ref[own_rows, state_width:]
        scores = dot32(c_blk, b_blk, 1, 1)
        pen = pen_ref[b]
        prefix = prefix_ref[own_rows, :]
        across = prefix.T
        if b > 0:
            carried = jnp.exp(prefix - prefix_ref[b * BLOCK - 1 : b * BLOCK, :])
            carried = carried * meta_ref[own_rows, 4:5]
            from_middle = dot32(c_blk, middle_ref[...], 1, 1)
        for q in range(inner // LANES):
            own = slice(q * LANES, (q + 1) * LANES)
            x_pair = x_ref[own_rows, own].astype(jnp.float32)
            out = x_pair * jnp.where(lane < head_dim, skip_ref[2 * q], skip_ref[2 * q + 1])
            if b > 0:
                out = out + widen(carried, q, head_dim) * from_middle[:, own]
            sx = stepx_ref[own_rows, own].astype(jnp.float32)
            for side in range(2):
                h = 2 * q + side
                gaps = prefix[:, h : h + 1] - across[h : h + 1, :] + pen
                mixing = (scores * jnp.exp(gaps)).astype(jnp.bfloat16)
                kept = (lane < head_dim) if side == 0 else (lane >= head_dim)
                out = out + dot32(mixing, jnp.where(kept, sx, 0.0).astype(jnp.bfloat16))
            y_ref[own_rows, own] = out


def z_kernel(normed_ref, own_ref, near_ref, far_ref, last_ref, gate_ref, w_ref, sems):
    rows = own_ref.shape[0]
    position = lax.axis_index("dp")
    copies = gather_rows(position, (own_ref, near_ref, far_ref, last_ref), rows, w_ref, sems)
    for copy in copies:
        copy.start()
    for copy in copies:
        copy.wait()
    gate_ref[...] = silu_tanh(dot32(normed_ref[...], w_ref[...]))


def before_device(ids_ref, position, tok):
    return jnp.where(position > 0, ids_ref[jnp.maximum(position * tok - 1, 0)], -1)


def gate_kernel(
    ids_ref, enter_ref, bc_ref, prefix_ref, meta_ref, y_ref, z_ref, arrived_ref, *outs
):
    scratch, add_ref = outs[-1], outs[-2]
    outs = outs[:-2]
    inner = y_ref.shape[1]
    state_width = enter_ref.shape[1]
    head_dim = LANES // 2
    tok = y_ref.shape[0]
    c_all = bc_ref[:, state_width:]
    inter = dot32(c_all, enter_ref[...], 1, 1)
    prefix = prefix_ref[...]
    carried = jnp.exp(prefix) * meta_ref[:, 3:4]
    for q in range(inner // LANES):
        own = slice(q * LANES, (q + 1) * LANES)
        value = y_ref[:, own] + widen(carried, q, head_dim) * inter[:, own]
        scratch[:, own] = (value * z_ref[:, own]).astype(jnp.bfloat16)
    position = lax.axis_index("dp")
    before = before_device(ids_ref, position, tok)
    stop = (position + 1) * tok
    after = ids_ref[jnp.minimum(stop, ids_ref.shape[0] - 1)]
    goes_on = (after == before) & (stop < ids_ref.shape[0])
    ended = (ids_ref[position * tok] == before) & ((ids_ref[stop - 1] != before) | ~goes_on)
    inside = jnp.where(meta_ref[:, 3:4] > 0.0, prefix, 0.0)
    gain = jnp.exp(jnp.min(inside, axis=0, keepdims=True)) * jnp.where(ended, 1.0, 0.0)
    for h in range(inner // head_dim):
        own = slice(h * head_dim, (h + 1) * head_dim)
        term = gain[:, h : h + 1] * enter_ref[own, :].astype(jnp.float32)
        add_ref[own, :] = term.astype(jnp.bfloat16)
    head = lax.axis_index("head")
    part = outs[0].shape[0] // len(RELATED)
    for out, owner in zip(outs, (head, jnp.bitwise_xor(head, Z_NEAR))):
        for k, bits in enumerate(RELATED):
            at = pl.multiple_of(jnp.bitwise_xor(owner, bits) * part, part)
            out[k * part : (k + 1) * part, :] = scratch[pl.ds(at, part), :]


def pick_kernel(own_ref, far_ref, *refs):
    tables, others, (keep_ref, send_ref, far_v, sem) = refs[:2], refs[2:4], refs[4:]
    count = keep_ref.shape[0]
    rows = far_ref.shape[0] - 6 * TILE_ROWS
    width = far_ref.shape[1]
    model_rows = rows // width
    at = rows + TILE_ROWS * model_rows
    lanes = rows - model_rows * width
    arrival = pltpu.make_async_copy(
        far_ref.at[at : at + TILE_ROWS, lanes : lanes + LANES], far_v, sem
    )
    arrival.start()

    def pick(out_ref, r, g):
        half = tables[0].shape[1]
        for k, (table_ref, other_ref) in enumerate(zip(tables, others)):
            total = table_ref[g].astype(jnp.float32) + other_ref[g].astype(jnp.float32)
            out_ref[r, k * half : (k + 1) * half] = total.astype(jnp.bfloat16)

    for r in range(count):
        pick(keep_ref, r, own_ref[r])
    arrival.wait()
    wanted = far_v[...].astype(jnp.float32)[0:1, :]
    lane = lax.broadcasted_iota(jnp.int32, (1, LANES), 1)
    for r in range(count):
        pick(send_ref, r, jnp.sum(jnp.where(lane == r, wanted, 0.0)).astype(jnp.int32))


def split_squares(squares):
    lane = lax.broadcasted_iota(jnp.int32, (squares.shape[0], LANES), 1)
    high = squares.astype(jnp.bfloat16).astype(jnp.float32)
    return jnp.where(lane == 0, high, squares - high).astype(jnp.bfloat16)


def joined_squares(ref, model):
    high = ref[:, model : model + 1].astype(jnp.float32)
    return high + ref[:, model + 1 : model + 2].astype(jnp.float32)


def out_kernel(
    kept_ref,
    got_ref,
    own_hbm,
    part_ref,
    near_ref,
    keep_ref,
    near_out,
    pass_ref,
    cross_out,
    own_ref,
    other_ref,
    sums_ref,
    sems,
):
    core = lax.axis_index("dp") % 2
    width = part_ref.shape[1]
    rows, model = sums_ref.shape
    part = keep_ref.shape[0]
    copies = [pltpu.make_async_copy(own_hbm, own_ref, sems.at[2])]
    for j, buffer in enumerate((part_ref, near_ref)):
        at = pl.multiple_of(jnp.bitwise_xor(core, j) * width, LANES)
        copies.append(
            pltpu.make_async_copy(buffer, other_ref.at[:, pl.ds(at, width)], sems.at[j])
        )
    for copy in copies:
        copy.start()
    kept, got = kept_ref[...], got_ref[...]
    squares = jnp.zeros((rows, 1), jnp.float32)
    for value in (kept, got):
        wide = value.astype(jnp.float32)
        squares = squares + jnp.sum(wide * wide, axis=1, keepdims=True)
    copies[0].wait()
    sums_ref[...] = dot32(kept, own_ref[...])
    for copy in copies[1:]:
        copy.wait()
    sums_ref[...] += dot32(got, other_ref[...])
    for k, out in enumerate((keep_ref, near_out, pass_ref, cross_out)):
        own = slice(k * part, (k + 1) * part)
        out[:, 0:model] = sums_ref[own, :].astype(out.dtype)
        if out.dtype == jnp.bfloat16:
            out[:, model:] = split_squares(squares[own])
        else:
            out[:, model:] = jnp.broadcast_to(squares[own], (part, LANES))


def pass_kernel(pass_ref, cross_ref, out_ref):
    model = out_ref.shape[1] - LANES
    total = pass_ref[:, 0:model] + cross_ref[:, 0:model].astype(jnp.float32)
    out_ref[:, 0:model] = total.astype(jnp.bfloat16)
    squares = pass_ref[:, model : model + 1] + joined_squares(cross_ref, model)
    out_ref[:, model:] = split_squares(squares)


def finish_kernel(inner_total, hidden_all, joined_ref, keep_ref, *refs):
    got, (out_ref, hidden_ref, sem) = refs[:-3], refs[-3:]
    part, model = hidden_ref.shape
    at = pl.multiple_of(lax.axis_index("head") * part, part)
    arrival = pltpu.make_async_copy(hidden_all.at[pl.ds(at, part)], hidden_ref, sem)
    arrival.start()
    squares = keep_ref[:, model : model + 1]
    total = keep_ref[:, 0:model]
    for ref in got:
        squares = squares + joined_squares(ref, model)
        total = total + ref[:, 0:model].astype(jnp.float32)
    scale = lax.rsqrt(squares / inner_total + EPSILON)
    arrival.wait()
    out_ref[...] = (hidden_ref[...].astype(jnp.float32) + scale * total).astype(jnp.bfloat16)


def join_kernel(ids_ref, own_ref, keep_ref, far_ref, *refs):
    adds, (out_ref, done_ref) = refs[:4], refs[-2:]
    done_ref[...] = jnp.zeros_like(done_ref)
    position = lax.axis_index("dp")
    tok = ids_ref.shape[0] // lax.axis_size("dp")
    befores = [
        before_device(ids_ref, jnp.bitwise_xor(position, j), tok) for j in range(len(adds))
    ]
    for r in range(keep_ref.shape[0]):
        total = keep_ref[r].astype(jnp.float32) + far_ref[r].astype(jnp.float32)
        out_ref[r] = total
        for add_ref, before in zip(adds, befores):

            @pl.when(own_ref[r] == before)
            def _():
                out_ref[r] = out_ref[r] + add_ref[...].astype(jnp.float32)


def fused_on_device(
    hidden,
    token_prompt,
    request_prompt,
    in_gain,
    w_zx,
    w_bc,
    w_dt,
    dt_bias,
    a_log,
    conv_x,
    conv_bc,
    skip_gain,
    out_gain,
    w_out,
):
    tok, model = hidden.shape
    rows = w_zx.shape[0]
    inner = w_zx.shape[2]
    heads = w_dt.shape[1]
    state_width = w_bc.shape[1] // 2
    width = inner + 2 * state_width
    peers = lax.axis_size("dp")
    head_count = lax.axis_size("head")
    bf16, f32 = jnp.bfloat16, jnp.float32
    shape = jax.ShapeDtypeStruct
    smem = pl.BlockSpec(memory_space=pltpu.SMEM)
    anywhere = pl.BlockSpec(memory_space=pl.ANY)
    in_hbm = pl.BlockSpec(memory_space=pltpu.HBM)

    extra = TILE_ROWS * (model // (2 * state_width))
    first_own = pl.pallas_call(
        pack_first_kernel,
        name="pack_first_weights",
        out_shape=shape((rows + extra, 2 * state_width), bf16),
        in_specs=[smem] + [in_hbm] * 3,
        out_specs=in_vmem(1)[0],
        scratch_shapes=[
            pltpu.VMEM(w_bc.shape, f32),
            pltpu.VMEM((heads, rows), f32),
            pltpu.VMEM((TILE_ROWS, model), bf16),
            pltpu.VMEM((TILE_ROWS, model), f32),
            pltpu.SemaphoreType.DMA((3,)),
        ],
        compiler_params=kernel_params(60),
        cost_estimate=LITTLE,
    )(request_prompt, w_bc, w_dt.T, hidden)
    first_far = exchange(first_own, "dp", 2)
    first_near = exchange(first_own, "dp", 1)
    x_own, gate_own = pl.pallas_call(
        pack_rest_kernel,
        name="pack_x_and_gate_weights",
        out_shape=(shape((rows, inner), bf16), shape((rows, inner), bf16)),
        in_specs=[in_hbm],
        out_specs=tuple(in_vmem(2)),
        scratch_shapes=[
            pltpu.VMEM((inner // LANES, rows, 2, LANES), f32),
            pltpu.SemaphoreType.DMA((inner // LANES,)),
        ],
        compiler_params=kernel_params(8),
        cost_estimate=LITTLE,
    )(w_zx)

    blocks = tok // BLOCK
    normed, meta, order, pen = pl.pallas_call(
        facts_kernel,
        name="norm_and_token_facts",
        out_shape=(
            shape((tok, model), bf16),
            shape((tok, LANES), f32),
            shape((2 * tok, tok), bf16),
            shape((blocks, BLOCK, BLOCK), f32),
        ),
        in_specs=in_vmem(1) + [in_hbm] + in_vmem(1),
        out_specs=tuple(in_vmem(4)),
        scratch_shapes=[pltpu.VMEM((tok, model), bf16), pltpu.SemaphoreType.DMA],
        compiler_params=kernel_params(16),
        cost_estimate=LITTLE,
    )(token_prompt[None, :], hidden, in_gain[None, :])
    scaled_out, half_out = pl.pallas_call(
        scale_kernel,
        name="scale_out_rows",
        out_shape=(shape(w_out.shape, bf16), shape((inner, model // 2), bf16)),
        in_specs=in_vmem(2),
        out_specs=tuple(in_vmem(2)),
        compiler_params=kernel_params(8),
        cost_estimate=LITTLE,
    )(w_out, out_gain[None, :])
    out_part = exchange(half_out, "head", Z_NEAR)
    out_near = exchange(out_part, "dp", 1)

    first_far, x_own, normed, meta, order, pen = lax.optimization_barrier(
        (first_far, x_own, normed, meta, order, pen)
    )
    x_far = exchange(x_own, "dp", 2)
    first_last = exchange(first_far, "dp", 1)
    x_near = exchange(x_own, "dp", 1)
    bc, step, prefix, fade, halo = pl.pallas_call(
        first_kernel,
        name="project_b_c_and_steps",
        out_shape=(
            shape((tok, 2 * state_width), bf16),
            shape((tok, LANES), f32),
            shape((tok, LANES), f32),
            shape((tok, LANES), f32),
            shape((TILE_ROWS, model), bf16),
        ),
        in_specs=in_vmem(1) + [anywhere] * 4 + in_vmem(4) + [smem] * 2,
        out_specs=tuple(in_vmem(5)),
        scratch_shapes=[
            pltpu.VMEM((model, 2 * state_width), bf16),
            pltpu.VMEM((peers, extra, 2 * state_width), bf16),
            pltpu.VMEM((LANES, model), bf16),
            pltpu.VMEM((TILE_ROWS + tok, 2 * state_width), f32),
            pltpu.SemaphoreType.DMA((2 * peers,)),
        ],
        compiler_params=kernel_params(14),
        cost_estimate=LITTLE,
    )(
        normed,
        first_own,
        first_near,
        first_far,
        first_last,
        in_gain[None, :],
        conv_bc,
        meta,
        order,
        dt_bias,
        a_log,
    )
    x_far, gate_own, bc, step, prefix, fade, halo = lax.optimization_barrier(
        (x_far, gate_own, bc, step, prefix, fade, halo)
    )
    x_last = exchange(x_far, "dp", 1)
    gate_far = exchange(gate_own, "dp", 2)
    gate_near = exchange(gate_own, "dp", 1)
    x, stepx, faded, leaving, middle = pl.pallas_call(
        inner_kernel,
        name="project_and_convolve_x",
        out_shape=(
            shape((tok, inner), bf16),
            shape((tok, inner), bf16),
            shape((inner, tok), bf16),
            shape((inner, state_width), bf16),
            shape((inner, state_width), bf16),
        ),
        in_specs=in_vmem(1) + [anywhere] * 4 + in_vmem(7),
        out_specs=tuple(in_vmem(5)),
        scratch_shapes=[
            pltpu.VMEM((model, inner), bf16),
            pltpu.VMEM((TILE_ROWS + tok, inner), f32),
            pltpu.SemaphoreType.DMA((peers,)),
        ],
        compiler_params=kernel_params(14),
        cost_estimate=LITTLE,
    )(
        normed,
        x_own,
        x_near,
        x_far,
        x_last,
        halo,
        conv_x,
        meta,
        bc,
        step,
        prefix,
        fade,
    )

    entering = lax.ppermute(leaving, "dp", [(i, i + 1) for i in range(peers - 1)])
    gate_far, entering = lax.optimization_barrier((gate_far, entering))
    gate_last = exchange(gate_far, "dp", 1)

    y_local = pl.pallas_call(
        local_kernel,
        name="mix_within_blocks",
        out_shape=shape((tok, inner), f32),
        in_specs=in_vmem(7) + [smem],
        out_specs=in_vmem(1)[0],
        compiler_params=kernel_params(14),
        cost_estimate=LITTLE,
    )(x, bc, stepx, prefix, middle, meta, pen, skip_gain)
    tables = pl.pallas_call(
        table_kernel,
        name="sum_ended_states",
        out_shape=(shape((PROMPTS, inner // 2, state_width), bf16),) * 2,
        in_specs=in_vmem(3),
        out_specs=tuple(in_vmem(2)),
        compiler_params=kernel_params(8),
        cost_estimate=LITTLE,
    )(bc, faded, meta)
    tables_near = [exchange(table, "dp", 1) for table in tables]

    gate = pl.pallas_call(
        z_kernel,
        name="project_gate",
        out_shape=shape((tok, inner), f32),
        in_specs=in_vmem(1) + [anywhere] * 4,
        out_specs=in_vmem(1)[0],
        scratch_shapes=[pltpu.VMEM((model, inner), bf16), pltpu.SemaphoreType.DMA((peers,))],
        compiler_params=kernel_params(8),
        cost_estimate=LITTLE,
    )(normed, gate_own, gate_near, gate_far, gate_last)

    out_rows = tok // head_count
    gated_kept, gated_sent, add = pl.pallas_call(
        gate_kernel,
        name="add_entering_and_gate",
        out_shape=(shape((tok // 2, inner), bf16),) * 2 + (shape((inner, state_width), bf16),),
        in_specs=[smem] + in_vmem(6) + [anywhere],
        out_specs=tuple(in_vmem(3)),
        scratch_shapes=[pltpu.VMEM((tok, inner), bf16)],
        compiler_params=kernel_params(8),
        cost_estimate=LITTLE,
    )(token_prompt, entering, bc, prefix, meta, y_local, gate, out_near)
    gated_got = exchange(gated_sent, "head", Z_NEAR)

    requests = request_prompt.shape[0]
    keep, send = pl.pallas_call(
        pick_kernel,
        name="pick_request_states",
        out_shape=(shape((requests, inner, state_width), bf16),) * 2,
        in_specs=[smem, anywhere] + in_vmem(4),
        out_specs=tuple(in_vmem(2)),
        scratch_shapes=[pltpu.VMEM((TILE_ROWS, LANES), bf16), pltpu.SemaphoreType.DMA],
        compiler_params=kernel_params(8),
        cost_estimate=LITTLE,
    )(request_prompt, first_far, *tables, *tables_near)
    far = exchange(send, "dp", 2)
    adds = [add, exchange(add, "dp", 1), exchange(add, "dp", 2)]
    adds.append(exchange(adds[2], "dp", 1))

    sums_shape = (out_rows, model + LANES)
    sums_keep, sums_near, sums_pass, sums_cross = pl.pallas_call(
        out_kernel,
        name="project_out",
        out_shape=tuple(shape(sums_shape, kind) for kind in (f32, bf16, f32, bf16)),
        in_specs=in_vmem(2) + [anywhere] * 3,
        out_specs=tuple(in_vmem(4)),
        scratch_shapes=[
            pltpu.VMEM((inner, model), bf16),
            pltpu.VMEM((inner, model), bf16),
            pltpu.VMEM((tok // 2, model), f32),
            pltpu.SemaphoreType.DMA((3,)),
        ],
        compiler_params=kernel_params(14),
        cost_estimate=LITTLE,
    )(gated_kept, gated_got, scaled_out, out_part, out_near)
    cross = exchange(sums_cross, "head", Y_NEAR)
    cross, sums_near = lax.optimization_barrier((cross, sums_near))
    sums_near = exchange(sums_near, "head", Y_NEAR)
    passed = pl.pallas_call(
        pass_kernel,
        name="add_sums_to_pass_on",
        out_shape=shape(sums_shape, bf16),
        in_specs=in_vmem(2),
        out_specs=in_vmem(1)[0],
        compiler_params=kernel_params(4),
        cost_estimate=LITTLE,
    )(sums_pass, cross)
    passed = exchange(passed, "head", Z_FAR)
    request_states, joined = pl.pallas_call(
        join_kernel,
        name="join_request_states",
        out_shape=(shape(keep.shape, f32), shape((8, LANES), f32)),
        in_specs=[smem] * 2 + in_vmem(6) + [anywhere],
        out_specs=tuple(in_vmem(2)),
        compiler_params=kernel_params(6),
        cost_estimate=LITTLE,
    )(token_prompt, request_prompt, keep, far, *adds, sums_keep)
    layer_out = pl.pallas_call(
        functools.partial(finish_kernel, inner * head_count),
        name="scale_and_add_hidden",
        out_shape=shape((out_rows, model), bf16),
        in_specs=[in_hbm, anywhere] + in_vmem(3),
        out_specs=in_vmem(1)[0],
        scratch_shapes=[pltpu.VMEM((out_rows, model), bf16), pltpu.SemaphoreType.DMA],
        compiler_params=kernel_params(4),
        cost_estimate=LITTLE,
    )(hidden, joined, sums_keep, sums_near, passed)
    return (
        layer_out,
        request_states.reshape(requests, heads, inner // heads, state_width),
    )


def fits_fused(mesh):
    return dict(mesh.shape) == {"dp": 4, "head": 8}


def solution(mesh):
    in_specs = (
        P("dp", None),
        P(),
        P("dp"),
        P(),
        P("dp", None, "head"),
        P("dp", None),
        P("dp", "head"),
        P("head"),
        P("head"),
        P(None, "head"),
        P(),
        P("head"),
        P("head"),
        P("head", None),
    )
    out_specs = (P(("dp", "head"), None), P("dp", "head", None, None))
    program = fused_on_device if fits_fused(mesh) else on_device
    return jax.shard_map(
        program, mesh=mesh, in_specs=in_specs, out_specs=out_specs, check_vma=False
    )
```

```python
import functools

import jax
import jax.numpy as jnp
from jax import lax
from jax.experimental import pallas as pl
from jax.experimental.pallas import tpu as pltpu
from jax.sharding import PartitionSpec as P

BLOCK = 256
PROMPTS = 8


EPSILON = 1e-05


def from_behind(shard, axis, by):
    peers = lax.axis_size(axis)
    pairs = [(i, i + by) for i in range(peers) if 0 <= i + by < peers]
    return lax.ppermute(shard, axis, pairs)


def carried_in(shard, axis, combine, identity):
    peers, position = (lax.axis_size(axis), lax.axis_index(axis))
    everything = jax.tree.map(lambda part: lax.all_gather(part, axis), shard)
    start = jax.tree.map(
        lambda part, zero: jnp.broadcast_to(jnp.asarray(zero, part.dtype), part.shape),
        shard,
        identity,
    )

    def step(k, before):
        reached = k < position
        new = combine(before, jax.tree.map(lambda part: part[k], everything))
        return jax.tree.map(lambda a, b: jnp.where(reached, a, b), new, before)

    return lax.fori_loop(0, peers, step, start)


def rms_scale(values):
    return lax.rsqrt(jnp.mean(values * values, axis=-1, keepdims=True) + EPSILON)


def conv_core(extended, extended_ids, token_ids, weights):
    length = token_ids.shape[0]
    total = jnp.zeros((length, extended.shape[1]), jnp.float32)
    for offset in range(weights.shape[0]):
        same = (extended_ids[offset : offset + length] == token_ids)[:, None]
        total = total + jnp.where(
            same, weights[offset] * extended[offset : offset + length].astype(jnp.float32), 0.0
        )
    return jax.nn.silu(total).astype(jnp.bfloat16)


def block_local(x_blk, b_blk, c_blk, step_blk, rate_blk, ids_blk, before_id):
    length = ids_blk.shape[0]
    position = jnp.arange(length, dtype=jnp.int32)
    prefix = jnp.cumsum(rate_blk, axis=0)
    prefix_t = prefix.T
    same = (ids_blk[:, None] == ids_blk[None, :]) & (position[None, :] <= position[:, None])
    gaps = prefix_t[:, :, None] - prefix_t[:, None, :]
    decay = jnp.where(same[None], jnp.exp(jnp.where(same[None], gaps, 0.0)), 0.0)
    scores = jnp.dot(c_blk, b_blk.T, preferred_element_type=jnp.float32)
    mixing = (scores[None] * decay * step_blk.T[:, None, :]).astype(jnp.bfloat16)
    y_intra = jnp.einsum("hts,shp->thp", mixing, x_blk, preferred_element_type=jnp.float32)
    end_id = ids_blk[-1]
    alive = ids_blk == end_id
    weight_end = (
        jnp.where(
            alive[None, :],
            jnp.exp(jnp.where(alive[None, :], prefix_t[:, -1:] - prefix_t, 0.0)),
            0.0,
        )
        * step_blk.T
    )
    b_weighted = (weight_end[:, :, None] * b_blk[None]).astype(jnp.bfloat16)
    local_state = jnp.einsum("hsn,shp->hpn", b_weighted, x_blk, preferred_element_type=jnp.float32)
    carry_gain = jnp.where(end_id == before_id, jnp.exp(prefix_t[:, -1]), 0.0)
    return (y_intra, local_state, carry_gain, prefix)


def block_inter(c_blk, prefix, ids_blk, before_id, state_in):
    entering = ids_blk == before_id
    inter_scale = jnp.where(entering[:, None], jnp.exp(prefix), 0.0)
    return inter_scale[:, :, None] * jnp.einsum(
        "tn,hpn->thp", c_blk.astype(jnp.float32), state_in, precision=lax.Precision.HIGHEST
    )


def block_last(
    last_index, table, x_blk, b_blk, step_blk, prefix, ids_blk, before_id, state_in, start
):
    length = ids_blk.shape[0]
    position = jnp.arange(length, dtype=jnp.int32)
    prompt_ids = jnp.arange(last_index.shape[0], dtype=jnp.int32)
    local_last = last_index - start
    ends_here = (local_last >= 0) & (local_last < length)
    clipped = jnp.clip(local_last, 0, length - 1)

    def with_ends():
        prefix_t = prefix.T
        prefix_last = prefix[clipped]
        pick = (
            ends_here[:, None]
            & (ids_blk[None, :] == prompt_ids[:, None])
            & (position[None, :] <= clipped[:, None])
        )
        spans = prefix_last[:, :, None] - prefix_t[None]
        weight_last = (
            jnp.where(pick[:, None, :], jnp.exp(jnp.where(pick[:, None, :], spans, 0.0)), 0.0)
            * step_blk.T[None]
        )
        b_last = (weight_last[..., None] * b_blk[None, None]).astype(jnp.bfloat16)
        last_local = jnp.einsum("ghsn,shp->ghpn", b_last, x_blk, preferred_element_type=jnp.float32)
        last_gain = jnp.where(
            (ends_here & (prompt_ids == before_id))[:, None], jnp.exp(prefix_last), 0.0
        )
        return table + last_local + last_gain[:, :, None, None] * state_in[None]

    def without_ends():
        return table

    return lax.cond(jnp.any(ends_here), with_ends, without_ends)


def join_states(earlier, later):
    return (earlier[0] * later[0], later[0][:, None, None] * earlier[1] + later[1])


def on_device(
    hidden,
    token_prompt,
    request_prompt,
    in_gain,
    w_zx,
    w_bc,
    w_dt,
    dt_bias,
    a_log,
    conv_x,
    conv_bc,
    skip_gain,
    out_gain,
    w_out,
):
    tok_dev = hidden.shape[0]
    inner_dev = w_zx.shape[2]
    heads_dev = w_dt.shape[1]
    head_dim = inner_dev // heads_dev
    state_width = w_bc.shape[1] // 2
    taps = conv_x.shape[0]
    dp_index = lax.axis_index("dp")
    head_index = lax.axis_index("head")
    head_count = lax.axis_size("head")
    hidden_f = hidden.astype(jnp.float32)
    normed = (hidden_f * rms_scale(hidden_f) * in_gain).astype(jnp.bfloat16)
    pieces = (
        lax.all_gather(w_zx.astype(jnp.bfloat16), "dp", axis=0, tiled=True),
        lax.all_gather(w_dt.astype(jnp.bfloat16), "dp", axis=0, tiled=True),
        lax.all_gather(w_bc.astype(jnp.bfloat16), "dp", axis=0, tiled=True),
    )
    acc_zx, acc_step, acc_bc = tuple(
        (
            jnp.dot(normed, piece.reshape(piece.shape[0], -1), preferred_element_type=jnp.float32)
            for piece in pieces
        )
    )
    proj_bc = acc_bc.astype(jnp.bfloat16)
    proj_zx = acc_zx.astype(jnp.bfloat16)
    gate_z = proj_zx[:, :inner_dev]
    inner_x = proj_zx[:, inner_dev:]
    proj_dt = acc_step.astype(jnp.bfloat16)
    step_size = jax.nn.softplus(proj_dt.astype(jnp.float32) + dt_bias)
    rate = step_size * -jnp.exp(a_log)
    ids_own = lax.dynamic_slice_in_dim(token_prompt, dp_index * tok_dev, tok_dev)
    rim_start = jnp.maximum(dp_index * tok_dev - (taps - 1), 0)
    rim_ids = lax.dynamic_slice_in_dim(token_prompt, rim_start, taps - 1)
    tail_rows = jnp.concatenate(
        [inner_x[tok_dev - taps + 1 :], proj_bc[tok_dev - taps + 1 :]], axis=1
    )
    rim_rows = from_behind(tail_rows, "dp", 1)
    ext_ids = jnp.concatenate([rim_ids, ids_own])
    conv_inner = conv_core(
        jnp.concatenate([rim_rows[:, :inner_dev], inner_x], axis=0), ext_ids, ids_own, conv_x
    )
    conv_bc_out = conv_core(
        jnp.concatenate([rim_rows[:, inner_dev:], proj_bc], axis=0), ext_ids, ids_own, conv_bc
    )
    blocks = tok_dev // BLOCK
    x_heads = conv_inner.reshape(blocks, BLOCK, heads_dev, head_dim)
    b_conv = conv_bc_out[:, :state_width].reshape(blocks, BLOCK, state_width)
    c_conv = conv_bc_out[:, state_width:].reshape(blocks, BLOCK, state_width)
    step_blocks = step_size.reshape(blocks, BLOCK, heads_dev)
    rate_blocks = rate.reshape(blocks, BLOCK, heads_dev)
    id_blocks = ids_own.reshape(blocks, BLOCK)
    prev_last = jnp.where(dp_index > 0, token_prompt[jnp.maximum(dp_index * tok_dev - 1, 0)], -1)
    before_ids = jnp.concatenate([prev_last[None], id_blocks[:-1, -1]])
    y_intra, local_state, carry_gain, prefix = jax.vmap(block_local)(
        x_heads, b_conv, c_conv, step_blocks, rate_blocks, id_blocks, before_ids
    )

    def advance(carry, item):
        gain_acc, state_acc = carry
        gain, block_state = item
        return (
            (gain_acc * gain, gain[:, None, None] * state_acc + block_state),
            (gain_acc, state_acc),
        )

    unit_gain = jnp.ones((heads_dev,), jnp.float32)
    zero_state = jnp.zeros((heads_dev, head_dim, state_width), jnp.float32)
    (dev_gain, dev_state), (prior_gain, prior_state) = lax.scan(
        advance, (unit_gain, zero_state), (carry_gain, local_state)
    )
    scanned = carried_in((dev_gain, dev_state), "dp", join_states, (unit_gain, zero_state))
    incoming = scanned[1]
    block_in = prior_state + prior_gain[:, :, None, None] * incoming[None]
    prompt_ids = jnp.arange(PROMPTS, dtype=jnp.int32)
    last_index = (
        jnp.sum((token_prompt[None, :] <= prompt_ids[:, None]).astype(jnp.int32), axis=1) - 1
    )
    start_pos = (dp_index * blocks + jnp.arange(blocks, dtype=jnp.int32)) * BLOCK
    y_inter = jax.vmap(block_inter)(c_conv, prefix, id_blocks, before_ids, block_in)

    def collect(table, item):
        xb, bb, sb, pb, ib, fb, stb, ob = item
        return (block_last(last_index, table, xb, bb, sb, pb, ib, fb, stb, ob), None)

    empty_table = jnp.zeros((PROMPTS, heads_dev, head_dim, state_width), jnp.float32)
    local_table, unused = lax.scan(
        collect,
        empty_table,
        (x_heads, b_conv, step_blocks, prefix, id_blocks, before_ids, block_in, start_pos),
    )
    ssd_out = (y_intra + y_inter).reshape(tok_dev, heads_dev, head_dim) + skip_gain[
        None, :, None
    ] * conv_inner.astype(jnp.float32).reshape(tok_dev, heads_dev, head_dim)
    gated = ssd_out.reshape(tok_dev, inner_dev) * jax.nn.silu(gate_z.astype(jnp.float32))
    square_sum = lax.psum(jnp.sum(gated * gated, axis=1), "head")
    scale = lax.rsqrt(square_sum / (inner_dev * head_count) + EPSILON)
    normed_out = (gated * scale[:, None] * out_gain).astype(jnp.bfloat16)
    out_rows = tok_dev // head_count
    own_rows = lax.dynamic_slice_in_dim(hidden_f, head_index * out_rows, out_rows, 0)
    mixed = lax.psum_scatter(
        jnp.dot(normed_out, w_out, preferred_element_type=jnp.float32),
        "head",
        scatter_dimension=0,
        tiled=True,
    )
    layer_out = (own_rows + mixed).astype(jnp.bfloat16)
    table = lax.psum(local_table, "dp")
    one_hot = (request_prompt[:, None] == prompt_ids[None, :]).astype(jnp.float32)
    request_states = jnp.einsum("rg,ghpn->rhpn", one_hot, table, precision=lax.Precision.HIGHEST)
    return (layer_out, request_states)


LANES = 128
TILE_ROWS = 16
NEVER = -1e30
Y_NEAR, Z_NEAR, Z_FAR = 1, 2, 4
PASSED = (Z_FAR, Y_NEAR | Z_FAR)
STAYING = (0, Y_NEAR)
LITTLE = pl.CostEstimate(flops=1000, bytes_accessed=1000, transcendentals=0)


def kernel_params(mebibytes):
    return pltpu.CompilerParams(vmem_limit_bytes=mebibytes << 20)


def in_vmem(count):
    return [pl.BlockSpec(memory_space=pltpu.VMEM)] * count


def exchange(values, axis, bits):
    return lax.ppermute(values, axis, [(i, i ^ bits) for i in range(lax.axis_size(axis))])


def dot32(a, b, a_dim=1, b_dim=0):
    return lax.dot_general(
        a, b, (((a_dim,), (b_dim,)), ((), ())), preferred_element_type=jnp.float32
    )


def silu_tanh(values):
    half = 0.5 * values
    return half + half * jnp.tanh(half)


def widen(columns, pair, head_dim):
    rows = columns.shape[0]
    lane = lax.broadcasted_iota(jnp.int32, (rows, LANES), 1)
    first = jnp.broadcast_to(columns[:, 2 * pair : 2 * pair + 1], (rows, LANES))
    second = jnp.broadcast_to(columns[:, 2 * pair + 1 : 2 * pair + 2], (rows, LANES))
    return jnp.where(lane < head_dim, first, second)


def pack_first_kernel(
    req_ref, wbc_ref, wdt_ref, hidden_ref, first_ref, req_v, bc_v, dt_v, tail_v, dt_wide, sems
):
    rows, width = bc_v.shape
    tok, model = hidden_ref.shape
    arrivals = [
        pltpu.make_async_copy(source, target, sems.at[k])
        for k, (source, target) in enumerate(
            (
                (req_ref, req_v),
                (wdt_ref, dt_v),
                (hidden_ref.at[tok - TILE_ROWS : tok], tail_v),
                (wbc_ref, bc_v),
            )
        )
    ]
    for copy in arrivals:
        copy.start()
    dt_wide[...] = jnp.zeros_like(dt_wide)
    arrivals[0].wait()
    dt_wide[0:1, rows : rows + req_v.shape[1]] = req_v[...].astype(jnp.float32)
    arrivals[1].wait()
    dt_wide[0 : dt_v.shape[0], 0:rows] = dt_v[...]
    arrivals[2].wait()
    upper = lax.broadcasted_iota(jnp.int32, (TILE_ROWS, model), 0) < TILE_ROWS // 2
    below = jnp.where(upper, dt_wide[...], tail_v[...].astype(jnp.float32)).astype(jnp.bfloat16)
    for i in range(model // width):
        at = rows + TILE_ROWS * i
        first_ref[at : at + TILE_ROWS, :] = below[:, i * width : (i + 1) * width]
    arrivals[3].wait()
    first_ref[0:rows, :] = bc_v[...].astype(jnp.bfloat16)


def pack_rest_kernel(wzx_ref, x_ref, gate_ref, tiles_ref, sems):
    rows, inner = x_ref.shape
    arrivals = [
        pltpu.make_async_copy(
            wzx_ref.at[:, :, j * LANES : (j + 1) * LANES], tiles_ref.at[j], sems.at[j]
        )
        for j in range(inner // LANES)
    ]
    for copy in arrivals:
        copy.start()
    for j, copy in enumerate(arrivals):
        copy.wait()
        own = slice(j * LANES, (j + 1) * LANES)
        pair = tiles_ref.at[j].reshape(2 * rows, LANES)
        x_ref[:, own] = pair[pl.ds(1, rows, stride=2), :].astype(jnp.bfloat16)
        gate_ref[:, own] = pair[pl.ds(0, rows, stride=2), :].astype(jnp.bfloat16)


def facts_kernel(
    ids_ref,
    hidden_hbm,
    gain_ref,
    normed_ref,
    meta_ref,
    order_ref,
    pen_ref,
    hidden_ref,
    sem,
):
    tok = hidden_ref.shape[0]
    arrival = pltpu.make_async_copy(hidden_hbm, hidden_ref, sem)
    arrival.start()
    position = lax.axis_index("dp")
    start = pl.multiple_of(position * tok, tok)
    ids_i = ids_ref[:, pl.ds(start, tok)]
    behind = pl.multiple_of(jnp.maximum(start - LANES, 0), LANES)
    edge = ids_ref[:, pl.ds(behind, LANES)]
    edge = jnp.where(position > 0, edge, -1)
    ahead = pl.multiple_of(jnp.minimum(start + tok, ids_ref.shape[1] - LANES), LANES)
    after = jnp.where(start + tok < ids_ref.shape[1], ids_ref[:, pl.ds(ahead, LANES)], -1)
    after = after[:, 0:1].astype(jnp.float32)
    long = jnp.concatenate([edge, ids_i], axis=1).astype(jnp.float32)
    ids = ids_i.astype(jnp.float32)
    index = lax.broadcasted_iota(jnp.int32, (1, tok), 1)
    before, last = long[:, LANES - 1 : LANES], ids[:, tok - 1 : tok]
    middle = ids[:, BLOCK - 1 : BLOCK]
    one, zero = jnp.ones((1, tok), jnp.float32), jnp.zeros((1, tok), jnp.float32)
    flag = lambda what: jnp.where(what, one, zero)
    rows = [flag(ids == pltpu.roll(long, k, 1)[:, LANES:]) for k in (1, 2, 3)]
    rows.append(flag(ids == before))
    rows.append(flag((ids == middle) & (index >= BLOCK)))
    rows.append(flag((ids == middle) & (index < BLOCK)))
    rows.append(ids)
    rows.append(flag(ids == last))
    rows.append(flag((ids != last) | (after != last)))
    rows = jnp.concatenate(rows + [jnp.zeros((LANES - len(rows), tok), jnp.float32)], axis=0)
    facts = rows.T
    meta_ref[...] = facts
    column = facts[:, 6:7]
    here = lax.broadcasted_iota(jnp.int32, (tok, tok), 0)
    there = lax.broadcasted_iota(jnp.int32, (tok, tok), 1)
    same = column == ids
    order_ref[0:tok, :] = jnp.where(there <= here, 1.0, 0.0).astype(jnp.bfloat16)
    order_ref[tok:, :] = jnp.where((there > here) & same, 1.0, 0.0).astype(jnp.bfloat16)
    pen = jnp.where((there <= here) & same, 0.0, NEVER)
    for b in range(tok // BLOCK):
        own = slice(b * BLOCK, (b + 1) * BLOCK)
        pen_ref[b] = pen[own, own]
    arrival.wait()
    hidden = hidden_ref[...].astype(jnp.float32)
    normed_ref[...] = (hidden * rms_scale(hidden) * gain_ref[...]).astype(jnp.bfloat16)


def scale_kernel(w_ref, gain_ref, whole_ref, part_ref):
    rows, model = w_ref.shape
    width = part_ref.shape[1]
    gain = jnp.broadcast_to(gain_ref[...], (LANES, rows)).T
    for j in range(model // LANES):
        own = slice(j * LANES, (j + 1) * LANES)
        whole_ref[:, own] = (w_ref[:, own].astype(jnp.float32) * gain).astype(jnp.bfloat16)
    at = pl.multiple_of((lax.axis_index("dp") % 2) * width, LANES)
    part_ref[...] = whole_ref[:, pl.ds(at, width)]


def gather_rows(position, buffers, rows, w_ref, sems):
    copies = []
    for j, buffer in enumerate(buffers):
        at = pl.multiple_of(jnp.bitwise_xor(position, j) * rows, rows)
        copies.append(
            pltpu.make_async_copy(buffer.at[0:rows], w_ref.at[pl.ds(at, rows)], sems.at[j])
        )
    return copies


def project_rows(normed, halo, w, ext_ref, at, stop):
    ext_ref[0:TILE_ROWS, at:stop] = dot32(halo, w)
    ext_ref[TILE_ROWS:, at:stop] = dot32(normed, w)


def convolve(ext_ref, own, taps, same):
    tok = same[0].shape[0]
    total = ext_ref[TILE_ROWS : TILE_ROWS + tok, own] * taps[3:4]
    for k in range(1, 4):
        total = total + same[k - 1] * (
            ext_ref[TILE_ROWS - k : TILE_ROWS - k + tok, own] * taps[3 - k : 4 - k]
        )
    return silu_tanh(total)


def first_kernel(
    normed_ref,
    own_ref,
    near_ref,
    far_ref,
    last_ref,
    gain_ref,
    taps_ref,
    meta_ref,
    order_ref,
    bias_ref,
    decay_ref,
    bc_ref,
    step_ref,
    prefix_ref,
    fade_ref,
    halo_ref,
    w_ref,
    extra_ref,
    dtw_ref,
    ext_ref,
    sems,
):
    position = lax.axis_index("dp")
    tok, model = normed_ref.shape
    peers, extra, width = extra_ref.shape
    rows = model // peers
    buffers = (own_ref, near_ref, far_ref, last_ref)
    copies = gather_rows(position, buffers, rows, w_ref, sems)
    for j, buffer in enumerate(buffers):
        copies.append(
            pltpu.make_async_copy(
                buffer.at[rows : rows + extra],
                extra_ref.at[jnp.bitwise_xor(position, j)],
                sems.at[peers + j],
            )
        )
    for copy in copies:
        copy.start()
    dtw_ref[...] = jnp.zeros_like(dtw_ref)
    for copy in copies:
        copy.wait()
    pieces = model // width
    for s in range(peers):
        below = jnp.concatenate(
            [extra_ref[s, i * TILE_ROWS : (i + 1) * TILE_ROWS, :] for i in range(pieces)], axis=1
        )
        row = lax.broadcasted_iota(jnp.int32, (TILE_ROWS, rows), 0)
        steps = jnp.where(row < bias_ref.shape[0], below[:, 0:rows].astype(jnp.float32), 0.0)
        dtw_ref[0:TILE_ROWS, s * rows : (s + 1) * rows] = steps.astype(jnp.bfloat16)
    behind = jnp.maximum(position - 1, 0)
    halo = jnp.concatenate(
        [extra_ref[behind, i * TILE_ROWS : (i + 1) * TILE_ROWS, :] for i in range(pieces)], axis=1
    ).astype(jnp.float32)
    halo = (halo * rms_scale(halo) * gain_ref[...]).astype(jnp.bfloat16)
    halo_ref[...] = halo
    normed = normed_ref[...]
    head_lane = lax.broadcasted_iota(jnp.int32, (1, LANES), 1)
    bias = jnp.zeros((1, LANES), jnp.float32)
    decay = jnp.zeros((1, LANES), jnp.float32)
    for h in range(bias_ref.shape[0]):
        bias = jnp.where(head_lane == h, bias_ref[h], bias)
        decay = jnp.where(head_lane == h, decay_ref[h], decay)
    raw = dot32(normed, dtw_ref[...], 1, 1) + bias
    step = jnp.maximum(raw, 0.0) + jnp.log1p(jnp.exp(-jnp.abs(raw)))
    step_ref[...] = step
    lane = lax.broadcasted_iota(jnp.int32, (tok, LANES), 1)
    rate = jnp.where(lane < TILE_ROWS, -step * jnp.exp(decay), 0.0)
    high = rate.astype(jnp.bfloat16).astype(jnp.float32)
    rest = rate - high
    mid = rest.astype(jnp.bfloat16).astype(jnp.float32)
    low = rest - mid
    packed = high + pltpu.roll(mid, TILE_ROWS, 1) + pltpu.roll(low, 2 * TILE_ROWS, 1)
    sums = dot32(order_ref[...], packed.astype(jnp.bfloat16))
    sums = (
        sums
        + pltpu.roll(sums, LANES - TILE_ROWS, 1)
        + pltpu.roll(sums, LANES - 2 * TILE_ROWS, 1)
    )
    prefix_ref[...] = sums[0:tok]
    fade_ref[...] = jnp.exp(sums[tok : 2 * tok])
    project_rows(normed, halo, w_ref[...], ext_ref, 0, width)
    same = [jnp.broadcast_to(meta_ref[:, k : k + 1], (tok, LANES)) for k in range(3)]
    for j in range(width // LANES):
        own = slice(j * LANES, (j + 1) * LANES)
        bc_ref[:, own] = convolve(ext_ref, own, taps_ref[:, own], same).astype(jnp.bfloat16)


def inner_kernel(
    normed_ref,
    own_ref,
    near_ref,
    far_ref,
    last_ref,
    halo_ref,
    taps_ref,
    meta_ref,
    bc_ref,
    step_ref,
    fade_ref,
    x_ref,
    stepx_ref,
    faded_ref,
    leaving_ref,
    w_ref,
    ext_ref,
    sems,
):
    position = lax.axis_index("dp")
    tok = normed_ref.shape[0]
    inner = x_ref.shape[1]
    rows = own_ref.shape[0]
    head_dim = LANES // 2
    copies = gather_rows(position, (own_ref, near_ref, far_ref, last_ref), rows, w_ref, sems)
    for copy in copies:
        copy.start()
    state_width = leaving_ref.shape[1]
    step = step_ref[...]
    fade = fade_ref[...]
    b_all = bc_ref[:, 0:state_width].astype(jnp.float32)
    b_leaving = (b_all * meta_ref[:, 7:8]).astype(jnp.bfloat16)
    same = [jnp.broadcast_to(meta_ref[:, k : k + 1], (tok, LANES)) for k in range(3)]
    for copy in copies:
        copy.wait()
    project_rows(normed_ref[...], halo_ref[...], w_ref[...], ext_ref, 0, inner)
    for q in range(inner // LANES):
        own = slice(q * LANES, (q + 1) * LANES)
        rounded = convolve(ext_ref, own, taps_ref[:, own], same).astype(jnp.bfloat16)
        x_ref[:, own] = rounded
        scaled = rounded.astype(jnp.float32) * widen(step, q, head_dim)
        stepx_ref[:, own] = scaled.astype(jnp.bfloat16)
        faded = (scaled * widen(fade, q, head_dim)).astype(jnp.bfloat16).T
        faded_ref[own, :] = faded
        leaving_ref[own, :] = dot32(faded, b_leaving).astype(jnp.bfloat16)


def before_device(ids_ref, position, tok):
    return jnp.where(position > 0, ids_ref[jnp.maximum(position * tok - 1, 0)], -1)


def table_kernel(ids_ref, bc_ref, faded_ref, meta_ref, prefix_ref, enter_ref, *table_refs):
    rows, state_width = table_refs[0].shape[1:]
    head_dim = LANES // 2
    tok = bc_ref.shape[0]
    b_all = bc_ref[:, 0:state_width].astype(jnp.float32)
    for g in range(table_refs[0].shape[0]):
        ended = jnp.where(meta_ref[:, 6:7] == g, meta_ref[:, 8:9], 0.0)
        b_ended = (b_all * ended).astype(jnp.bfloat16)
        for k, table_ref in enumerate(table_refs):
            faded = faded_ref[k * rows : (k + 1) * rows, :]
            table_ref[g] = dot32(faded, b_ended).astype(jnp.bfloat16)
    position = lax.axis_index("dp")
    before = before_device(ids_ref, position, tok)
    stop = (position + 1) * tok
    after = ids_ref[jnp.minimum(stop, ids_ref.shape[0] - 1)]
    goes_on = (after == before) & (stop < ids_ref.shape[0])
    ended = (ids_ref[position * tok] == before) & ((ids_ref[stop - 1] != before) | ~goes_on)

    @pl.when(ended)
    def add():
        inside = jnp.where(meta_ref[:, 3:4] > 0.0, prefix_ref[...], 0.0)
        gain = jnp.exp(jnp.min(inside, axis=0, keepdims=True))
        chunk = head_dim // 2
        for n in range(faded_ref.shape[0] // chunk):
            table_ref = table_refs[n * chunk // rows]
            own = slice(n * chunk % rows, n * chunk % rows + chunk)
            h = n * chunk // head_dim
            entering = enter_ref[n * chunk : (n + 1) * chunk, :].astype(jnp.float32)
            old = table_ref[before, own, :].astype(jnp.float32)
            table_ref[before, own, :] = (old + gain[:, h : h + 1] * entering).astype(jnp.bfloat16)


def local_kernel(
    x_ref,
    bc_ref,
    stepx_ref,
    prefix_ref,
    meta_ref,
    pen_ref,
    skip_ref,
    y_ref,
):
    inner = y_ref.shape[1]
    state_width = bc_ref.shape[1] // 2
    head_dim = LANES // 2
    tok = y_ref.shape[0]
    lane = lax.broadcasted_iota(jnp.int32, (BLOCK, LANES), 1)
    for b in range(tok // BLOCK):
        own_rows = slice(b * BLOCK, (b + 1) * BLOCK)
        b_blk = bc_ref[own_rows, 0:state_width]
        c_blk = bc_ref[own_rows, state_width:]
        scores = dot32(c_blk, b_blk, 1, 1)
        pen = pen_ref[b]
        prefix = prefix_ref[own_rows, :]
        across = prefix.T
        if b > 0:
            carried = jnp.exp(prefix - prefix_ref[b * BLOCK - 1 : b * BLOCK, :])
            carried = carried * meta_ref[own_rows, 4:5]
            before_rows = slice((b - 1) * BLOCK, b * BLOCK)
            before = prefix_ref[before_rows, :]
            fade = jnp.exp(before[BLOCK - 1 : BLOCK, :] - before)
            b_before = bc_ref[before_rows, 0:state_width].astype(jnp.float32)
            b_before = (b_before * meta_ref[before_rows, 5:6]).astype(jnp.bfloat16)
        for q in range(inner // LANES):
            own = slice(q * LANES, (q + 1) * LANES)
            x_pair = x_ref[own_rows, own].astype(jnp.float32)
            out = x_pair * jnp.where(lane < head_dim, skip_ref[2 * q], skip_ref[2 * q + 1])
            if b > 0:
                faded = stepx_ref[before_rows, own].astype(jnp.float32) * widen(fade, q, head_dim)
                middle = dot32(faded.astype(jnp.bfloat16).T, b_before).astype(jnp.bfloat16)
                out = out + widen(carried, q, head_dim) * dot32(c_blk, middle, 1, 1)
            sx = stepx_ref[own_rows, own].astype(jnp.float32)
            for side in range(2):
                h = 2 * q + side
                gaps = prefix[:, h : h + 1] - across[h : h + 1, :] + pen
                mixing = (scores * jnp.exp(gaps)).astype(jnp.bfloat16)
                kept = (lane < head_dim) if side == 0 else (lane >= head_dim)
                out = out + dot32(mixing, jnp.where(kept, sx, 0.0).astype(jnp.bfloat16))
            y_ref[own_rows, own] = out


def z_most_kernel(normed_ref, own_ref, near_ref, far_ref, most_ref):
    position = lax.axis_index("dp")
    rows = own_ref.shape[0]
    total = 0.0
    for j, w_ref in enumerate((own_ref, near_ref, far_ref)):
        at = pl.multiple_of(jnp.bitwise_xor(position, j) * rows, LANES)
        total = total + dot32(normed_ref[:, pl.ds(at, rows)], w_ref[...])
    most_ref[...] = total


def z_last_kernel(normed_ref, last_ref, most_ref, gate_ref):
    rows = last_ref.shape[0]
    at = pl.multiple_of(jnp.bitwise_xor(lax.axis_index("dp"), 3) * rows, LANES)
    gate_ref[...] = silu_tanh(most_ref[...] + dot32(normed_ref[:, pl.ds(at, rows)], last_ref[...]))


def gate_kernel(enter_ref, bc_ref, prefix_ref, meta_ref, y_ref, z_ref, arrived_ref, *outs):
    scratch = outs[-1]
    inner = y_ref.shape[1]
    state_width = enter_ref.shape[1]
    head_dim = LANES // 2
    c_all = bc_ref[:, state_width:]
    inter = dot32(c_all, enter_ref[...], 1, 1)
    carried = jnp.exp(prefix_ref[...]) * meta_ref[:, 3:4]
    for q in range(inner // LANES):
        own = slice(q * LANES, (q + 1) * LANES)
        value = y_ref[:, own] + widen(carried, q, head_dim) * inter[:, own]
        scratch[:, own] = (value * z_ref[:, own]).astype(jnp.bfloat16)
    head = lax.axis_index("head")
    part = outs[0].shape[0] // 2
    for n, related in enumerate((PASSED, STAYING)):
        for out, owner in zip(outs[2 * n : 2 * n + 2], (head, jnp.bitwise_xor(head, Z_NEAR))):
            for k, bits in enumerate(related):
                at = pl.multiple_of(jnp.bitwise_xor(owner, bits) * part, part)
                out[k * part : (k + 1) * part, :] = scratch[pl.ds(at, part), :]


def pick_kernel(own_ref, far_ref, *refs):
    tables, others, (keep_ref, send_ref, send_last_ref, far_v, sem) = refs[:4], refs[4:8], refs[8:]
    count = keep_ref.shape[0]
    part = tables[0].shape[1]
    rows = far_ref.shape[0] - 6 * TILE_ROWS
    width = far_ref.shape[1]
    model_rows = rows // width
    at = rows + TILE_ROWS * model_rows
    lanes = rows - model_rows * width
    arrival = pltpu.make_async_copy(
        far_ref.at[at : at + TILE_ROWS, lanes : lanes + LANES], far_v, sem
    )
    arrival.start()

    def pick(k, g):
        total = tables[k][g].astype(jnp.float32) + others[k][g].astype(jnp.float32)
        return total.astype(jnp.bfloat16)

    for r in range(count):
        for k in range(len(tables)):
            keep_ref[r, k * part : (k + 1) * part] = pick(k, own_ref[r])
    arrival.wait()
    wanted = far_v[...].astype(jnp.float32)[0:1, :]
    lane = lax.broadcasted_iota(jnp.int32, (1, LANES), 1)
    for r in range(count):
        g = jnp.sum(jnp.where(lane == r, wanted, 0.0)).astype(jnp.int32)
        for k in range(len(tables) - 1):
            send_ref[r, k * part : (k + 1) * part] = pick(k, g)
        send_last_ref[r] = pick(len(tables) - 1, g)


def split_squares(squares):
    lane = lax.broadcasted_iota(jnp.int32, (squares.shape[0], LANES), 1)
    high = squares.astype(jnp.bfloat16).astype(jnp.float32)
    return jnp.where(lane == 0, high, squares - high).astype(jnp.bfloat16)


def joined_squares(ref, model):
    high = ref[:, model : model + 1].astype(jnp.float32)
    return high + ref[:, model + 1 : model + 2].astype(jnp.float32)


def out_kernel(kept_ref, got_ref, own_ref, part_ref, near_ref, wide_out, bf16_out, sums_ref):
    core = lax.axis_index("dp") % 2
    width = part_ref.shape[1]
    rows, model = sums_ref.shape
    part = wide_out.shape[0]
    kept, got = kept_ref[...], got_ref[...]
    squares = jnp.zeros((rows, 1), jnp.float32)
    for value in (kept, got):
        wide = value.astype(jnp.float32)
        squares = squares + jnp.sum(wide * wide, axis=1, keepdims=True)
    for j, other_ref in enumerate((part_ref, near_ref)):
        at = pl.multiple_of(jnp.bitwise_xor(core, j) * width, LANES)
        own = dot32(kept, own_ref[:, pl.ds(at, width)])
        sums_ref[:, pl.ds(at, width)] = own + dot32(got, other_ref[...])
    wide_out[:, 0:model] = sums_ref[0:part, :]
    wide_out[:, model:] = jnp.broadcast_to(squares[0:part], (part, LANES))
    bf16_out[:, 0:model] = sums_ref[part:, :].astype(jnp.bfloat16)
    bf16_out[:, model:] = split_squares(squares[part:])


def pass_kernel(pass_ref, cross_ref, out_ref):
    model = out_ref.shape[1] - LANES
    total = pass_ref[:, 0:model] + cross_ref[:, 0:model].astype(jnp.float32)
    out_ref[:, 0:model] = total.astype(jnp.bfloat16)
    squares = pass_ref[:, model : model + 1] + joined_squares(cross_ref, model)
    out_ref[:, model:] = split_squares(squares)


def finish_kernel(inner_total, hidden_all, joined_ref, keep_ref, *refs):
    got, (out_ref, hidden_ref, sem) = refs[:-3], refs[-3:]
    part, model = hidden_ref.shape
    at = pl.multiple_of(lax.axis_index("head") * part, part)
    arrival = pltpu.make_async_copy(hidden_all.at[pl.ds(at, part)], hidden_ref, sem)
    arrival.start()
    squares = keep_ref[:, model : model + 1]
    total = keep_ref[:, 0:model]
    for ref in got:
        squares = squares + joined_squares(ref, model)
        total = total + ref[:, 0:model].astype(jnp.float32)
    scale = lax.rsqrt(squares / inner_total + EPSILON)
    arrival.wait()
    out_ref[...] = (hidden_ref[...].astype(jnp.float32) + scale * total).astype(jnp.bfloat16)


def join_kernel(keep_ref, *refs):
    fars, (out_ref, done_ref) = refs[:-2], refs[-2:]
    done_ref[...] = jnp.zeros_like(done_ref)
    at = 0
    for far_ref in fars:
        own = slice(at, at + far_ref.shape[1])
        out_ref[:, own] = keep_ref[:, own].astype(jnp.float32) + far_ref[...].astype(jnp.float32)
        at += far_ref.shape[1]


def fused_on_device(
    hidden,
    token_prompt,
    request_prompt,
    in_gain,
    w_zx,
    w_bc,
    w_dt,
    dt_bias,
    a_log,
    conv_x,
    conv_bc,
    skip_gain,
    out_gain,
    w_out,
):
    tok, model = hidden.shape
    rows = w_zx.shape[0]
    inner = w_zx.shape[2]
    heads = w_dt.shape[1]
    state_width = w_bc.shape[1] // 2
    tiles = inner // LANES
    peers = lax.axis_size("dp")
    head_count = lax.axis_size("head")
    bf16, f32 = jnp.bfloat16, jnp.float32
    shape = jax.ShapeDtypeStruct
    smem = pl.BlockSpec(memory_space=pltpu.SMEM)
    anywhere = pl.BlockSpec(memory_space=pl.ANY)
    in_hbm = pl.BlockSpec(memory_space=pltpu.HBM)

    extra = TILE_ROWS * (model // (2 * state_width))
    first_own = pl.pallas_call(
        pack_first_kernel,
        name="pack_first_weights",
        out_shape=shape((rows + extra, 2 * state_width), bf16),
        in_specs=[in_hbm] * 4,
        out_specs=in_vmem(1)[0],
        scratch_shapes=[
            pltpu.VMEM((1, request_prompt.shape[0]), jnp.int32),
            pltpu.VMEM(w_bc.shape, f32),
            pltpu.VMEM((heads, rows), f32),
            pltpu.VMEM((TILE_ROWS, model), bf16),
            pltpu.VMEM((TILE_ROWS, model), f32),
            pltpu.SemaphoreType.DMA((4,)),
        ],
        compiler_params=kernel_params(60),
        cost_estimate=LITTLE,
    )(request_prompt[None, :], w_bc, w_dt.T, hidden)
    first_far = exchange(first_own, "dp", 2)
    first_near = exchange(first_own, "dp", 1)
    x_own, gate_own = pl.pallas_call(
        pack_rest_kernel,
        name="pack_x_and_gate_weights",
        out_shape=(shape((rows, inner), bf16), shape((rows, inner), bf16)),
        in_specs=[in_hbm],
        out_specs=tuple(in_vmem(2)),
        scratch_shapes=[
            pltpu.VMEM((inner // LANES, rows, 2, LANES), f32),
            pltpu.SemaphoreType.DMA((inner // LANES,)),
        ],
        compiler_params=kernel_params(8),
        cost_estimate=LITTLE,
    )(w_zx)

    blocks = tok // BLOCK
    normed, meta, order, pen = pl.pallas_call(
        facts_kernel,
        name="norm_and_token_facts",
        out_shape=(
            shape((tok, model), bf16),
            shape((tok, LANES), f32),
            shape((2 * tok, tok), bf16),
            shape((blocks, BLOCK, BLOCK), f32),
        ),
        in_specs=in_vmem(1) + [in_hbm] + in_vmem(1),
        out_specs=tuple(in_vmem(4)),
        scratch_shapes=[pltpu.VMEM((tok, model), bf16), pltpu.SemaphoreType.DMA],
        compiler_params=kernel_params(16),
        cost_estimate=LITTLE,
    )(token_prompt[None, :], hidden, in_gain[None, :])
    scaled_out, half_out = pl.pallas_call(
        scale_kernel,
        name="scale_out_rows",
        out_shape=(shape(w_out.shape, bf16), shape((inner, model // 2), bf16)),
        in_specs=in_vmem(2),
        out_specs=tuple(in_vmem(2)),
        compiler_params=kernel_params(8),
        cost_estimate=LITTLE,
    )(w_out, out_gain[None, :])
    out_part = exchange(half_out, "head", Z_NEAR)
    out_near = exchange(out_part, "dp", 1)

    x_far = exchange(x_own, "dp", 2)
    first_far, first_near, normed, meta, order, pen, x_own, gate_own = lax.optimization_barrier(
        (first_far, first_near, normed, meta, order, pen, x_own, gate_own)
    )
    x_near = exchange(x_own, "dp", 1)
    gate_near = exchange(gate_own, "dp", 1)
    first_last = exchange(first_far, "dp", 1)
    bc, step, prefix, fade, halo = pl.pallas_call(
        first_kernel,
        name="project_b_c_and_steps",
        out_shape=(
            shape((tok, 2 * state_width), bf16),
            shape((tok, LANES), f32),
            shape((tok, LANES), f32),
            shape((tok, LANES), f32),
            shape((TILE_ROWS, model), bf16),
        ),
        in_specs=in_vmem(1) + [anywhere] * 4 + in_vmem(4) + [smem] * 2,
        out_specs=tuple(in_vmem(5)),
        scratch_shapes=[
            pltpu.VMEM((model, 2 * state_width), bf16),
            pltpu.VMEM((peers, extra, 2 * state_width), bf16),
            pltpu.VMEM((LANES, model), bf16),
            pltpu.VMEM((TILE_ROWS + tok, 2 * state_width), f32),
            pltpu.SemaphoreType.DMA((2 * peers,)),
        ],
        compiler_params=kernel_params(14),
        cost_estimate=LITTLE,
    )(
        normed,
        first_own,
        first_near,
        first_far,
        first_last,
        in_gain[None, :],
        conv_bc,
        meta,
        order,
        dt_bias,
        a_log,
    )
    x_far, gate_own, bc, step, prefix, fade, halo = lax.optimization_barrier(
        (x_far, gate_own, bc, step, prefix, fade, halo)
    )
    x_last = exchange(x_far, "dp", 1)
    gate_far = exchange(gate_own, "dp", 2)
    x, stepx, faded, leaving = pl.pallas_call(
        inner_kernel,
        name="project_and_convolve_x",
        out_shape=(
            shape((tok, inner), bf16),
            shape((tok, inner), bf16),
            shape((inner, tok), bf16),
            shape((inner, state_width), bf16),
        ),
        in_specs=in_vmem(1) + [anywhere] * 4 + in_vmem(6),
        out_specs=tuple(in_vmem(4)),
        scratch_shapes=[
            pltpu.VMEM((model, inner), bf16),
            pltpu.VMEM((TILE_ROWS + tok, inner), f32),
            pltpu.SemaphoreType.DMA((peers,)),
        ],
        compiler_params=kernel_params(14),
        cost_estimate=LITTLE,
    )(
        normed,
        x_own,
        x_near,
        x_far,
        x_last,
        halo,
        conv_x,
        meta,
        bc,
        step,
        fade,
    )

    entering = lax.ppermute(leaving, "dp", [(i, i + 1) for i in range(peers - 1)])

    y_local = pl.pallas_call(
        local_kernel,
        name="mix_within_blocks",
        out_shape=shape((tok, inner), f32),
        in_specs=in_vmem(6) + [smem],
        out_specs=in_vmem(1)[0],
        compiler_params=kernel_params(14),
        cost_estimate=LITTLE,
    )(x, bc, stepx, prefix, meta, pen, skip_gain)
    gate_far, gate_near, entering, y_local = lax.optimization_barrier(
        (gate_far, gate_near, entering, y_local)
    )
    gate_last = exchange(gate_far, "dp", 1)
    tables = pl.pallas_call(
        table_kernel,
        name="sum_ended_states",
        out_shape=(shape((PROMPTS, inner // 4, state_width), bf16),) * 4,
        in_specs=[smem] + in_vmem(5),
        out_specs=tuple(in_vmem(4)),
        compiler_params=kernel_params(8),
        cost_estimate=LITTLE,
    )(token_prompt, bc, faded, meta, prefix, entering)
    tables_near = [exchange(table, "dp", 1) for table in tables]

    gate_most = pl.pallas_call(
        z_most_kernel,
        name="project_gate_most",
        out_shape=shape((tok, inner), f32),
        in_specs=in_vmem(4),
        out_specs=in_vmem(1)[0],
        compiler_params=kernel_params(8),
        cost_estimate=LITTLE,
    )(normed, gate_own, gate_near, gate_far)
    gate = pl.pallas_call(
        z_last_kernel,
        name="project_gate_last",
        out_shape=shape((tok, inner), f32),
        in_specs=in_vmem(3),
        out_specs=in_vmem(1)[0],
        compiler_params=kernel_params(8),
        cost_estimate=LITTLE,
    )(normed, gate_last, gate_most)

    out_rows = tok // head_count
    kept_first, sent_first, kept_rest, sent_rest = pl.pallas_call(
        gate_kernel,
        name="add_entering_and_gate",
        out_shape=(shape((2 * out_rows, inner), bf16),) * 4,
        in_specs=in_vmem(6) + [anywhere],
        out_specs=tuple(in_vmem(4)),
        scratch_shapes=[pltpu.VMEM((tok, inner), bf16)],
        compiler_params=kernel_params(8),
        cost_estimate=LITTLE,
    )(entering, bc, prefix, meta, y_local, gate, out_near)
    got_first = exchange(sent_first, "head", Z_NEAR)
    got_rest = exchange(sent_rest, "head", Z_NEAR)

    requests = request_prompt.shape[0]
    part = inner // 4
    keep, *sends = pl.pallas_call(
        pick_kernel,
        name="pick_request_states",
        out_shape=tuple(
            shape((requests, size, state_width), bf16) for size in (inner, inner - part, part)
        ),
        in_specs=[smem, anywhere] + in_vmem(8),
        out_specs=tuple(in_vmem(3)),
        scratch_shapes=[pltpu.VMEM((TILE_ROWS, LANES), bf16), pltpu.SemaphoreType.DMA],
        compiler_params=kernel_params(8),
        cost_estimate=LITTLE,
    )(request_prompt, first_far, *tables, *tables_near)
    fars = [exchange(send, "dp", 2) for send in sends]

    sums_shape = (out_rows, model + LANES)
    project = pl.pallas_call(
        out_kernel,
        name="project_out",
        out_shape=(shape(sums_shape, f32), shape(sums_shape, bf16)),
        in_specs=in_vmem(5),
        out_specs=tuple(in_vmem(2)),
        scratch_shapes=[pltpu.VMEM((2 * out_rows, model), f32)],
        compiler_params=kernel_params(8),
        cost_estimate=LITTLE,
    )
    sums_pass, sums_cross = project(kept_first, got_first, scaled_out, out_part, out_near)
    sums_keep, sums_near = project(kept_rest, got_rest, scaled_out, out_part, out_near)
    cross = exchange(sums_cross, "head", Y_NEAR)
    cross, sums_near = lax.optimization_barrier((cross, sums_near))
    sums_near = exchange(sums_near, "head", Y_NEAR)
    passed = pl.pallas_call(
        pass_kernel,
        name="add_sums_to_pass_on",
        out_shape=shape(sums_shape, bf16),
        in_specs=in_vmem(2),
        out_specs=in_vmem(1)[0],
        compiler_params=kernel_params(4),
        cost_estimate=LITTLE,
    )(sums_pass, cross)
    passed = exchange(passed, "head", Z_FAR)
    request_states, joined = pl.pallas_call(
        join_kernel,
        name="join_request_states",
        out_shape=(shape((requests, inner, state_width), f32), shape((8, LANES), f32)),
        in_specs=in_vmem(3),
        out_specs=tuple(in_vmem(2)),
        compiler_params=kernel_params(6),
        cost_estimate=LITTLE,
    )(keep, *fars)
    layer_out = pl.pallas_call(
        functools.partial(finish_kernel, inner * head_count),
        name="scale_and_add_hidden",
        out_shape=shape((out_rows, model), bf16),
        in_specs=[in_hbm, anywhere] + in_vmem(3),
        out_specs=in_vmem(1)[0],
        scratch_shapes=[pltpu.VMEM((out_rows, model), bf16), pltpu.SemaphoreType.DMA],
        compiler_params=kernel_params(4),
        cost_estimate=LITTLE,
    )(hidden, joined, sums_keep, sums_near, passed)
    return (
        layer_out,
        request_states.reshape(requests, heads, inner // heads, state_width),
    )


def fits_fused(mesh):
    return dict(mesh.shape) == {"dp": 4, "head": 8}


def solution(mesh):
    in_specs = (
        P("dp", None),
        P(),
        P("dp"),
        P(),
        P("dp", None, "head"),
        P("dp", None),
        P("dp", "head"),
        P("head"),
        P("head"),
        P(None, "head"),
        P(),
        P("head"),
        P("head"),
        P("head", None),
    )
    out_specs = (P(("dp", "head"), None), P("dp", "head", None, None))
    program = fused_on_device if fits_fused(mesh) else on_device
    return jax.shard_map(
        program, mesh=mesh, in_specs=in_specs, out_specs=out_specs, check_vma=False
    )
```

```python
import functools

import jax
import jax.numpy as jnp
from jax import lax
from jax.experimental import pallas as pl
from jax.experimental.pallas import tpu as pltpu
from jax.sharding import PartitionSpec as P

BLOCK = 256
PROMPTS = 8


EPSILON = 1e-05


def from_behind(shard, axis, by):
    peers = lax.axis_size(axis)
    pairs = [(i, i + by) for i in range(peers) if 0 <= i + by < peers]
    return lax.ppermute(shard, axis, pairs)


def carried_in(shard, axis, combine, identity):
    peers, position = (lax.axis_size(axis), lax.axis_index(axis))
    everything = jax.tree.map(lambda part: lax.all_gather(part, axis), shard)
    start = jax.tree.map(
        lambda part, zero: jnp.broadcast_to(jnp.asarray(zero, part.dtype), part.shape),
        shard,
        identity,
    )

    def step(k, before):
        reached = k < position
        new = combine(before, jax.tree.map(lambda part: part[k], everything))
        return jax.tree.map(lambda a, b: jnp.where(reached, a, b), new, before)

    return lax.fori_loop(0, peers, step, start)


def rms_scale(values):
    return lax.rsqrt(jnp.mean(values * values, axis=-1, keepdims=True) + EPSILON)


def conv_core(extended, extended_ids, token_ids, weights):
    length = token_ids.shape[0]
    total = jnp.zeros((length, extended.shape[1]), jnp.float32)
    for offset in range(weights.shape[0]):
        same = (extended_ids[offset : offset + length] == token_ids)[:, None]
        total = total + jnp.where(
            same, weights[offset] * extended[offset : offset + length].astype(jnp.float32), 0.0
        )
    return jax.nn.silu(total).astype(jnp.bfloat16)


def block_local(x_blk, b_blk, c_blk, step_blk, rate_blk, ids_blk, before_id):
    length = ids_blk.shape[0]
    position = jnp.arange(length, dtype=jnp.int32)
    prefix = jnp.cumsum(rate_blk, axis=0)
    prefix_t = prefix.T
    same = (ids_blk[:, None] == ids_blk[None, :]) & (position[None, :] <= position[:, None])
    gaps = prefix_t[:, :, None] - prefix_t[:, None, :]
    decay = jnp.where(same[None], jnp.exp(jnp.where(same[None], gaps, 0.0)), 0.0)
    scores = jnp.dot(c_blk, b_blk.T, preferred_element_type=jnp.float32)
    mixing = (scores[None] * decay * step_blk.T[:, None, :]).astype(jnp.bfloat16)
    y_intra = jnp.einsum("hts,shp->thp", mixing, x_blk, preferred_element_type=jnp.float32)
    end_id = ids_blk[-1]
    alive = ids_blk == end_id
    weight_end = (
        jnp.where(
            alive[None, :],
            jnp.exp(jnp.where(alive[None, :], prefix_t[:, -1:] - prefix_t, 0.0)),
            0.0,
        )
        * step_blk.T
    )
    b_weighted = (weight_end[:, :, None] * b_blk[None]).astype(jnp.bfloat16)
    local_state = jnp.einsum("hsn,shp->hpn", b_weighted, x_blk, preferred_element_type=jnp.float32)
    carry_gain = jnp.where(end_id == before_id, jnp.exp(prefix_t[:, -1]), 0.0)
    return (y_intra, local_state, carry_gain, prefix)


def block_inter(c_blk, prefix, ids_blk, before_id, state_in):
    entering = ids_blk == before_id
    inter_scale = jnp.where(entering[:, None], jnp.exp(prefix), 0.0)
    return inter_scale[:, :, None] * jnp.einsum(
        "tn,hpn->thp", c_blk.astype(jnp.float32), state_in, precision=lax.Precision.HIGHEST
    )


def block_last(
    last_index, table, x_blk, b_blk, step_blk, prefix, ids_blk, before_id, state_in, start
):
    length = ids_blk.shape[0]
    position = jnp.arange(length, dtype=jnp.int32)
    prompt_ids = jnp.arange(last_index.shape[0], dtype=jnp.int32)
    local_last = last_index - start
    ends_here = (local_last >= 0) & (local_last < length)
    clipped = jnp.clip(local_last, 0, length - 1)

    def with_ends():
        prefix_t = prefix.T
        prefix_last = prefix[clipped]
        pick = (
            ends_here[:, None]
            & (ids_blk[None, :] == prompt_ids[:, None])
            & (position[None, :] <= clipped[:, None])
        )
        spans = prefix_last[:, :, None] - prefix_t[None]
        weight_last = (
            jnp.where(pick[:, None, :], jnp.exp(jnp.where(pick[:, None, :], spans, 0.0)), 0.0)
            * step_blk.T[None]
        )
        b_last = (weight_last[..., None] * b_blk[None, None]).astype(jnp.bfloat16)
        last_local = jnp.einsum("ghsn,shp->ghpn", b_last, x_blk, preferred_element_type=jnp.float32)
        last_gain = jnp.where(
            (ends_here & (prompt_ids == before_id))[:, None], jnp.exp(prefix_last), 0.0
        )
        return table + last_local + last_gain[:, :, None, None] * state_in[None]

    def without_ends():
        return table

    return lax.cond(jnp.any(ends_here), with_ends, without_ends)


def join_states(earlier, later):
    return (earlier[0] * later[0], later[0][:, None, None] * earlier[1] + later[1])


def on_device(
    hidden,
    token_prompt,
    request_prompt,
    in_gain,
    w_zx,
    w_bc,
    w_dt,
    dt_bias,
    a_log,
    conv_x,
    conv_bc,
    skip_gain,
    out_gain,
    w_out,
):
    tok_dev = hidden.shape[0]
    inner_dev = w_zx.shape[2]
    heads_dev = w_dt.shape[1]
    head_dim = inner_dev // heads_dev
    state_width = w_bc.shape[1] // 2
    taps = conv_x.shape[0]
    dp_index = lax.axis_index("dp")
    head_index = lax.axis_index("head")
    head_count = lax.axis_size("head")
    hidden_f = hidden.astype(jnp.float32)
    normed = (hidden_f * rms_scale(hidden_f) * in_gain).astype(jnp.bfloat16)
    pieces = (
        lax.all_gather(w_zx.astype(jnp.bfloat16), "dp", axis=0, tiled=True),
        lax.all_gather(w_dt.astype(jnp.bfloat16), "dp", axis=0, tiled=True),
        lax.all_gather(w_bc.astype(jnp.bfloat16), "dp", axis=0, tiled=True),
    )
    acc_zx, acc_step, acc_bc = tuple(
        (
            jnp.dot(normed, piece.reshape(piece.shape[0], -1), preferred_element_type=jnp.float32)
            for piece in pieces
        )
    )
    proj_bc = acc_bc.astype(jnp.bfloat16)
    proj_zx = acc_zx.astype(jnp.bfloat16)
    gate_z = proj_zx[:, :inner_dev]
    inner_x = proj_zx[:, inner_dev:]
    proj_dt = acc_step.astype(jnp.bfloat16)
    step_size = jax.nn.softplus(proj_dt.astype(jnp.float32) + dt_bias)
    rate = step_size * -jnp.exp(a_log)
    ids_own = lax.dynamic_slice_in_dim(token_prompt, dp_index * tok_dev, tok_dev)
    rim_start = jnp.maximum(dp_index * tok_dev - (taps - 1), 0)
    rim_ids = lax.dynamic_slice_in_dim(token_prompt, rim_start, taps - 1)
    tail_rows = jnp.concatenate(
        [inner_x[tok_dev - taps + 1 :], proj_bc[tok_dev - taps + 1 :]], axis=1
    )
    rim_rows = from_behind(tail_rows, "dp", 1)
    ext_ids = jnp.concatenate([rim_ids, ids_own])
    conv_inner = conv_core(
        jnp.concatenate([rim_rows[:, :inner_dev], inner_x], axis=0), ext_ids, ids_own, conv_x
    )
    conv_bc_out = conv_core(
        jnp.concatenate([rim_rows[:, inner_dev:], proj_bc], axis=0), ext_ids, ids_own, conv_bc
    )
    blocks = tok_dev // BLOCK
    x_heads = conv_inner.reshape(blocks, BLOCK, heads_dev, head_dim)
    b_conv = conv_bc_out[:, :state_width].reshape(blocks, BLOCK, state_width)
    c_conv = conv_bc_out[:, state_width:].reshape(blocks, BLOCK, state_width)
    step_blocks = step_size.reshape(blocks, BLOCK, heads_dev)
    rate_blocks = rate.reshape(blocks, BLOCK, heads_dev)
    id_blocks = ids_own.reshape(blocks, BLOCK)
    prev_last = jnp.where(dp_index > 0, token_prompt[jnp.maximum(dp_index * tok_dev - 1, 0)], -1)
    before_ids = jnp.concatenate([prev_last[None], id_blocks[:-1, -1]])
    y_intra, local_state, carry_gain, prefix = jax.vmap(block_local)(
        x_heads, b_conv, c_conv, step_blocks, rate_blocks, id_blocks, before_ids
    )

    def advance(carry, item):
        gain_acc, state_acc = carry
        gain, block_state = item
        return (
            (gain_acc * gain, gain[:, None, None] * state_acc + block_state),
            (gain_acc, state_acc),
        )

    unit_gain = jnp.ones((heads_dev,), jnp.float32)
    zero_state = jnp.zeros((heads_dev, head_dim, state_width), jnp.float32)
    (dev_gain, dev_state), (prior_gain, prior_state) = lax.scan(
        advance, (unit_gain, zero_state), (carry_gain, local_state)
    )
    scanned = carried_in((dev_gain, dev_state), "dp", join_states, (unit_gain, zero_state))
    incoming = scanned[1]
    block_in = prior_state + prior_gain[:, :, None, None] * incoming[None]
    prompt_ids = jnp.arange(PROMPTS, dtype=jnp.int32)
    last_index = (
        jnp.sum((token_prompt[None, :] <= prompt_ids[:, None]).astype(jnp.int32), axis=1) - 1
    )
    start_pos = (dp_index * blocks + jnp.arange(blocks, dtype=jnp.int32)) * BLOCK
    y_inter = jax.vmap(block_inter)(c_conv, prefix, id_blocks, before_ids, block_in)

    def collect(table, item):
        xb, bb, sb, pb, ib, fb, stb, ob = item
        return (block_last(last_index, table, xb, bb, sb, pb, ib, fb, stb, ob), None)

    empty_table = jnp.zeros((PROMPTS, heads_dev, head_dim, state_width), jnp.float32)
    local_table, unused = lax.scan(
        collect,
        empty_table,
        (x_heads, b_conv, step_blocks, prefix, id_blocks, before_ids, block_in, start_pos),
    )
    ssd_out = (y_intra + y_inter).reshape(tok_dev, heads_dev, head_dim) + skip_gain[
        None, :, None
    ] * conv_inner.astype(jnp.float32).reshape(tok_dev, heads_dev, head_dim)
    gated = ssd_out.reshape(tok_dev, inner_dev) * jax.nn.silu(gate_z.astype(jnp.float32))
    square_sum = lax.psum(jnp.sum(gated * gated, axis=1), "head")
    scale = lax.rsqrt(square_sum / (inner_dev * head_count) + EPSILON)
    normed_out = (gated * scale[:, None] * out_gain).astype(jnp.bfloat16)
    out_rows = tok_dev // head_count
    own_rows = lax.dynamic_slice_in_dim(hidden_f, head_index * out_rows, out_rows, 0)
    mixed = lax.psum_scatter(
        jnp.dot(normed_out, w_out, preferred_element_type=jnp.float32),
        "head",
        scatter_dimension=0,
        tiled=True,
    )
    layer_out = (own_rows + mixed).astype(jnp.bfloat16)
    table = lax.psum(local_table, "dp")
    one_hot = (request_prompt[:, None] == prompt_ids[None, :]).astype(jnp.float32)
    request_states = jnp.einsum("rg,ghpn->rhpn", one_hot, table, precision=lax.Precision.HIGHEST)
    return (layer_out, request_states)


LANES = 128
TILE_ROWS = 16
NEVER = -1e30
Y_NEAR, Z_NEAR, Z_FAR = 1, 2, 4
PASSED = (Z_FAR, Y_NEAR | Z_FAR)
STAYING = (0, Y_NEAR)
LITTLE = pl.CostEstimate(flops=1000, bytes_accessed=1000, transcendentals=0)


def kernel_params(mebibytes):
    return pltpu.CompilerParams(vmem_limit_bytes=mebibytes << 20)


def in_vmem(count):
    return [pl.BlockSpec(memory_space=pltpu.VMEM)] * count


def exchange(values, axis, bits):
    return lax.ppermute(values, axis, [(i, i ^ bits) for i in range(lax.axis_size(axis))])


def dot32(a, b, a_dim=1, b_dim=0):
    return lax.dot_general(
        a, b, (((a_dim,), (b_dim,)), ((), ())), preferred_element_type=jnp.float32
    )


def silu_tanh(values):
    half = 0.5 * values
    return half + half * jnp.tanh(half)


def widen(columns, pair, head_dim):
    rows = columns.shape[0]
    lane = lax.broadcasted_iota(jnp.int32, (rows, LANES), 1)
    first = jnp.broadcast_to(columns[:, 2 * pair : 2 * pair + 1], (rows, LANES))
    second = jnp.broadcast_to(columns[:, 2 * pair + 1 : 2 * pair + 2], (rows, LANES))
    return jnp.where(lane < head_dim, first, second)


def pack_first_kernel(
    req_ref, wbc_ref, wdt_ref, hidden_ref, first_ref, req_v, bc_v, dt_v, tail_v, dt_wide, sems
):
    rows, width = bc_v.shape
    tok, model = hidden_ref.shape
    arrivals = [
        pltpu.make_async_copy(source, target, sems.at[k])
        for k, (source, target) in enumerate(
            (
                (req_ref, req_v),
                (wdt_ref, dt_v),
                (hidden_ref.at[tok - TILE_ROWS : tok], tail_v),
                (wbc_ref, bc_v),
            )
        )
    ]
    for copy in arrivals:
        copy.start()
    dt_wide[...] = jnp.zeros_like(dt_wide)
    arrivals[0].wait()
    dt_wide[0:1, rows : rows + req_v.shape[1]] = req_v[...].astype(jnp.float32)
    arrivals[1].wait()
    dt_wide[0 : dt_v.shape[0], 0:rows] = dt_v[...]
    arrivals[2].wait()
    upper = lax.broadcasted_iota(jnp.int32, (TILE_ROWS, model), 0) < TILE_ROWS // 2
    below = jnp.where(upper, dt_wide[...], tail_v[...].astype(jnp.float32)).astype(jnp.bfloat16)
    for i in range(model // width):
        at = rows + TILE_ROWS * i
        first_ref[at : at + TILE_ROWS, :] = below[:, i * width : (i + 1) * width]
    arrivals[3].wait()
    first_ref[0:rows, :] = bc_v[...].astype(jnp.bfloat16)


def pack_rest_kernel(wzx_ref, x_ref, gate_ref, tiles_ref, sems):
    rows, inner = x_ref.shape
    arrivals = [
        pltpu.make_async_copy(
            wzx_ref.at[:, :, j * LANES : (j + 1) * LANES], tiles_ref.at[j], sems.at[j]
        )
        for j in range(inner // LANES)
    ]
    for copy in arrivals:
        copy.start()
    for j, copy in enumerate(arrivals):
        copy.wait()
        own = slice(j * LANES, (j + 1) * LANES)
        pair = tiles_ref.at[j].reshape(2 * rows, LANES)
        x_ref[:, own] = pair[pl.ds(1, rows, stride=2), :].astype(jnp.bfloat16)
        gate_ref[:, own] = pair[pl.ds(0, rows, stride=2), :].astype(jnp.bfloat16)


def facts_kernel(
    ids_ref,
    hidden_hbm,
    gain_ref,
    normed_ref,
    meta_ref,
    order_ref,
    pen_ref,
    rows_ref,
    hidden_ref,
    sem,
):
    tok = hidden_ref.shape[0]
    arrival = pltpu.make_async_copy(hidden_hbm, hidden_ref, sem)
    arrival.start()
    position = lax.axis_index("dp")
    start = pl.multiple_of(position * tok, tok)
    ids_i = ids_ref[:, pl.ds(start, tok)]
    behind = pl.multiple_of(jnp.maximum(start - LANES, 0), LANES)
    edge = ids_ref[:, pl.ds(behind, LANES)]
    edge = jnp.where(position > 0, edge, -1)
    ahead = pl.multiple_of(jnp.minimum(start + tok, ids_ref.shape[1] - LANES), LANES)
    after = jnp.where(start + tok < ids_ref.shape[1], ids_ref[:, pl.ds(ahead, LANES)], -1)
    after = after[:, 0:1].astype(jnp.float32)
    long = jnp.concatenate([edge, ids_i], axis=1).astype(jnp.float32)
    ids = ids_i.astype(jnp.float32)
    index = lax.broadcasted_iota(jnp.int32, (1, tok), 1)
    before, last = long[:, LANES - 1 : LANES], ids[:, tok - 1 : tok]
    middle = ids[:, BLOCK - 1 : BLOCK]
    one, zero = jnp.ones((1, tok), jnp.float32), jnp.zeros((1, tok), jnp.float32)
    flag = lambda what: jnp.where(what, one, zero)
    rows = [flag(ids == pltpu.roll(long, k, 1)[:, LANES:]) for k in (1, 2, 3)]
    rows.append(flag(ids == before))
    rows.append(flag((ids == middle) & (index >= BLOCK)))
    rows.append(flag((ids == middle) & (index < BLOCK)))
    rows.append(ids)
    rows.append(flag(ids == last))
    rows.append(flag((ids != last) | (after != last)))
    rows = jnp.concatenate(rows + [jnp.zeros((LANES - len(rows), tok), jnp.float32)], axis=0)
    facts = rows.T
    meta_ref[...] = facts
    column = facts[:, 6:7]
    here = lax.broadcasted_iota(jnp.int32, (tok, tok), 0)
    there = lax.broadcasted_iota(jnp.int32, (tok, tok), 1)
    same = column == ids
    order_ref[0:tok, :] = jnp.where(there <= here, 1.0, 0.0).astype(jnp.bfloat16)
    order_ref[tok:, :] = jnp.where((there > here) & same, 1.0, 0.0).astype(jnp.bfloat16)
    pen = jnp.where((there <= here) & same, 0.0, NEVER)
    for b in range(tok // BLOCK):
        own = slice(b * BLOCK, (b + 1) * BLOCK)
        pen_ref[b] = pen[own, own]
    arrival.wait()
    part = rows_ref.shape[0]
    at = pl.multiple_of(lax.axis_index("head") * part, part)
    rows_ref[...] = hidden_ref[pl.ds(at, part), :]
    hidden = hidden_ref[...].astype(jnp.float32)
    normed_ref[...] = (hidden * rms_scale(hidden) * gain_ref[...]).astype(jnp.bfloat16)


def scale_kernel(w_ref, gain_ref, whole_ref, part_ref):
    rows, model = w_ref.shape
    width = part_ref.shape[1]
    gain = jnp.broadcast_to(gain_ref[...], (LANES, rows)).T
    for j in range(model // LANES):
        own = slice(j * LANES, (j + 1) * LANES)
        whole_ref[:, own] = (w_ref[:, own].astype(jnp.float32) * gain).astype(jnp.bfloat16)
    at = pl.multiple_of((lax.axis_index("dp") % 2) * width, LANES)
    part_ref[...] = whole_ref[:, pl.ds(at, width)]


def gather_rows(position, buffers, rows, w_ref, sems):
    copies = []
    for j, buffer in enumerate(buffers):
        at = pl.multiple_of(jnp.bitwise_xor(position, j) * rows, rows)
        copies.append(
            pltpu.make_async_copy(buffer.at[0:rows], w_ref.at[pl.ds(at, rows)], sems.at[j])
        )
    return copies


def project_rows(normed, halo, w, ext_ref, at, stop):
    ext_ref[0:TILE_ROWS, at:stop] = dot32(halo, w)
    ext_ref[TILE_ROWS:, at:stop] = dot32(normed, w)


def convolve(ext_ref, own, taps, same):
    tok = same[0].shape[0]
    total = ext_ref[TILE_ROWS : TILE_ROWS + tok, own] * taps[3:4]
    for k in range(1, 4):
        total = total + same[k - 1] * (
            ext_ref[TILE_ROWS - k : TILE_ROWS - k + tok, own] * taps[3 - k : 4 - k]
        )
    return silu_tanh(total)


def below_rows(buffer, rows):
    count = (buffer.shape[0] - rows) // TILE_ROWS
    return jnp.concatenate(
        [buffer[rows + i * TILE_ROWS : rows + (i + 1) * TILE_ROWS, :] for i in range(count)], axis=1
    )


def project_shard(normed_ref, buffer, j, steps, dtw_ref):
    rows = dtw_ref.shape[1]
    at = pl.multiple_of(jnp.bitwise_xor(lax.axis_index("dp"), j) * rows, LANES)
    normed = normed_ref[:, pl.ds(at, rows)]
    row = lax.broadcasted_iota(jnp.int32, (TILE_ROWS, rows), 0)
    below = below_rows(buffer, rows)[:, 0:rows].astype(jnp.float32)
    dtw_ref[0:TILE_ROWS, :] = jnp.where(row < steps, below, 0.0).astype(jnp.bfloat16)
    return dot32(normed, buffer[0:rows, :]), dot32(normed, dtw_ref[...], 1, 1)


def first_most_kernel(steps, normed_ref, own_ref, near_ref, most_ref, raw_ref, dtw_ref):
    dtw_ref[...] = jnp.zeros_like(dtw_ref)
    most, raw = project_shard(normed_ref, own_ref, 0, steps, dtw_ref)
    more, more_raw = project_shard(normed_ref, near_ref, 1, steps, dtw_ref)
    most_ref[...] = most + more
    raw_ref[...] = raw + more_raw


def first_kernel(
    normed_ref,
    most_ref,
    most_raw_ref,
    own_ref,
    near_ref,
    far_ref,
    last_ref,
    gain_ref,
    taps_ref,
    meta_ref,
    order_ref,
    bias_ref,
    decay_ref,
    bc_ref,
    step_ref,
    prefix_ref,
    fade_ref,
    halo_ref,
    halo_rows_ref,
    dtw_ref,
    ext_ref,
):
    position = lax.axis_index("dp")
    tok, model = normed_ref.shape
    width = bc_ref.shape[1]
    rows = dtw_ref.shape[1]
    buffers = (own_ref, near_ref, far_ref, last_ref)
    for j, buffer in enumerate(buffers):
        halo_rows_ref[jnp.bitwise_xor(position, j)] = below_rows(buffer, rows)
    halo = halo_rows_ref[jnp.maximum(position - 1, 0)].astype(jnp.float32)
    halo_ref[...] = (halo * rms_scale(halo) * gain_ref[...]).astype(jnp.bfloat16)
    halo_sum = 0.0
    for j, buffer in enumerate(buffers):
        at = pl.multiple_of(jnp.bitwise_xor(position, j) * rows, LANES)
        halo_sum = halo_sum + dot32(halo_ref[:, pl.ds(at, rows)], buffer[0:rows, :])
    ext_ref[0:TILE_ROWS, :] = halo_sum
    dtw_ref[...] = jnp.zeros_like(dtw_ref)
    steps = bias_ref.shape[0]
    most, raw = project_shard(normed_ref, far_ref, 2, steps, dtw_ref)
    more, more_raw = project_shard(normed_ref, last_ref, 3, steps, dtw_ref)
    ext_ref[TILE_ROWS:, :] = most_ref[...] + most + more
    head_lane = lax.broadcasted_iota(jnp.int32, (1, LANES), 1)
    bias = jnp.zeros((1, LANES), jnp.float32)
    decay = jnp.zeros((1, LANES), jnp.float32)
    for h in range(steps):
        bias = jnp.where(head_lane == h, bias_ref[h], bias)
        decay = jnp.where(head_lane == h, decay_ref[h], decay)
    raw = most_raw_ref[...] + raw + more_raw + bias
    step = jnp.maximum(raw, 0.0) + jnp.log1p(jnp.exp(-jnp.abs(raw)))
    step_ref[...] = step
    lane = lax.broadcasted_iota(jnp.int32, (tok, LANES), 1)
    rate = jnp.where(lane < TILE_ROWS, -step * jnp.exp(decay), 0.0)
    high = rate.astype(jnp.bfloat16).astype(jnp.float32)
    rest = rate - high
    mid = rest.astype(jnp.bfloat16).astype(jnp.float32)
    low = rest - mid
    packed = high + pltpu.roll(mid, TILE_ROWS, 1) + pltpu.roll(low, 2 * TILE_ROWS, 1)
    sums = dot32(order_ref[...], packed.astype(jnp.bfloat16))
    sums = (
        sums
        + pltpu.roll(sums, LANES - TILE_ROWS, 1)
        + pltpu.roll(sums, LANES - 2 * TILE_ROWS, 1)
    )
    prefix_ref[...] = sums[0:tok]
    fade_ref[...] = jnp.exp(sums[tok : 2 * tok])
    same = [jnp.broadcast_to(meta_ref[:, k : k + 1], (tok, LANES)) for k in range(3)]
    for j in range(width // LANES):
        own = slice(j * LANES, (j + 1) * LANES)
        bc_ref[:, own] = convolve(ext_ref, own, taps_ref[:, own], same).astype(jnp.bfloat16)


def inner_kernel(
    normed_ref,
    own_ref,
    near_ref,
    far_ref,
    last_ref,
    halo_ref,
    taps_ref,
    meta_ref,
    bc_ref,
    step_ref,
    fade_ref,
    x_ref,
    stepx_ref,
    faded_ref,
    leaving_ref,
    w_ref,
    ext_ref,
    sems,
):
    position = lax.axis_index("dp")
    tok = normed_ref.shape[0]
    inner = x_ref.shape[1]
    rows = own_ref.shape[0]
    head_dim = LANES // 2
    copies = gather_rows(position, (own_ref, near_ref, far_ref, last_ref), rows, w_ref, sems)
    for copy in copies:
        copy.start()
    state_width = leaving_ref.shape[1]
    step = step_ref[...]
    fade = fade_ref[...]
    b_all = bc_ref[:, 0:state_width].astype(jnp.float32)
    b_leaving = (b_all * meta_ref[:, 7:8]).astype(jnp.bfloat16)
    same = [jnp.broadcast_to(meta_ref[:, k : k + 1], (tok, LANES)) for k in range(3)]
    for copy in copies:
        copy.wait()
    project_rows(normed_ref[...], halo_ref[...], w_ref[...], ext_ref, 0, inner)
    for q in range(inner // LANES):
        own = slice(q * LANES, (q + 1) * LANES)
        rounded = convolve(ext_ref, own, taps_ref[:, own], same).astype(jnp.bfloat16)
        x_ref[:, own] = rounded
        scaled = rounded.astype(jnp.float32) * widen(step, q, head_dim)
        stepx_ref[:, own] = scaled.astype(jnp.bfloat16)
        faded = (scaled * widen(fade, q, head_dim)).astype(jnp.bfloat16).T
        faded_ref[own, :] = faded
        leaving_ref[own, :] = dot32(faded, b_leaving).astype(jnp.bfloat16)


def before_device(ids_ref, position, tok):
    return jnp.where(position > 0, ids_ref[jnp.maximum(position * tok - 1, 0)], -1)


def table_kernel(ids_ref, bc_ref, faded_ref, meta_ref, prefix_ref, enter_ref, *table_refs):
    rows, state_width = table_refs[0].shape[1:]
    head_dim = LANES // 2
    tok = bc_ref.shape[0]
    b_all = bc_ref[:, 0:state_width].astype(jnp.float32)
    owner = jnp.where(meta_ref[:, 8:9] > 0.0, meta_ref[:, 6:7], -1.0)
    owner = jnp.broadcast_to(owner, (tok, state_width))
    for g in range(0, table_refs[0].shape[0], 2):
        pair = [jnp.where(owner == g + k, b_all, 0.0).astype(jnp.bfloat16) for k in range(2)]
        sums = dot32(faded_ref[...], jnp.concatenate(pair, axis=1)).astype(jnp.bfloat16)
        for n, table_ref in enumerate(table_refs):
            for k in range(2):
                table_ref[g + k] = sums[
                    n * rows : (n + 1) * rows, k * state_width : (k + 1) * state_width
                ]
    position = lax.axis_index("dp")
    before = before_device(ids_ref, position, tok)
    stop = (position + 1) * tok
    after = ids_ref[jnp.minimum(stop, ids_ref.shape[0] - 1)]
    goes_on = (after == before) & (stop < ids_ref.shape[0])
    ended = (ids_ref[position * tok] == before) & ((ids_ref[stop - 1] != before) | ~goes_on)

    @pl.when(ended)
    def add():
        inside = jnp.where(meta_ref[:, 3:4] > 0.0, prefix_ref[...], 0.0)
        gain = jnp.exp(jnp.min(inside, axis=0, keepdims=True))
        chunk = head_dim // 2
        for n in range(faded_ref.shape[0] // chunk):
            table_ref = table_refs[n * chunk // rows]
            own = slice(n * chunk % rows, n * chunk % rows + chunk)
            h = n * chunk // head_dim
            entering = enter_ref[n * chunk : (n + 1) * chunk, :].astype(jnp.float32)
            old = table_ref[before, own, :].astype(jnp.float32)
            table_ref[before, own, :] = (old + gain[:, h : h + 1] * entering).astype(jnp.bfloat16)


def local_kernel(
    x_ref,
    bc_ref,
    stepx_ref,
    prefix_ref,
    meta_ref,
    pen_ref,
    skip_ref,
    y_ref,
):
    inner = y_ref.shape[1]
    state_width = bc_ref.shape[1] // 2
    head_dim = LANES // 2
    tok = y_ref.shape[0]
    lane = lax.broadcasted_iota(jnp.int32, (BLOCK, LANES), 1)
    half = BLOCK // 2
    for b in range(tok // BLOCK):
        own_rows = slice(b * BLOCK, (b + 1) * BLOCK)
        b_blk = bc_ref[own_rows, 0:state_width]
        c_blk = bc_ref[own_rows, state_width:]
        scores = dot32(c_blk, b_blk, 1, 1)
        pen = pen_ref[b]
        prefix = prefix_ref[own_rows, :]
        across = prefix.T
        if b > 0:
            carried = jnp.exp(prefix - prefix_ref[b * BLOCK - 1 : b * BLOCK, :])
            carried = carried * meta_ref[own_rows, 4:5]
            before_rows = slice((b - 1) * BLOCK, b * BLOCK)
            before = prefix_ref[before_rows, :]
            fade = jnp.exp(before[BLOCK - 1 : BLOCK, :] - before)
            b_before = bc_ref[before_rows, 0:state_width].astype(jnp.float32)
            b_before = (b_before * meta_ref[before_rows, 5:6]).astype(jnp.bfloat16)
        for q in range(inner // LANES):
            own = slice(q * LANES, (q + 1) * LANES)
            x_pair = x_ref[own_rows, own].astype(jnp.float32)
            out = x_pair * jnp.where(lane < head_dim, skip_ref[2 * q], skip_ref[2 * q + 1])
            if b > 0:
                faded = stepx_ref[before_rows, own].astype(jnp.float32) * widen(fade, q, head_dim)
                middle = dot32(faded.astype(jnp.bfloat16).T, b_before).astype(jnp.bfloat16)
                out = out + widen(carried, q, head_dim) * dot32(c_blk, middle, 1, 1)
            sx = stepx_ref[own_rows, own].astype(jnp.float32)
            sides = [jnp.where(lane < head_dim, sx, 0.0), jnp.where(lane >= head_dim, sx, 0.0)]
            sides = [side.astype(jnp.bfloat16) for side in sides]
            for rows, seen in ((slice(0, half), half), (slice(half, BLOCK), BLOCK)):
                part = out[rows]
                for side in range(2):
                    h = 2 * q + side
                    gaps = prefix[rows, h : h + 1] - across[h : h + 1, 0:seen] + pen[rows, 0:seen]
                    mixing = (scores[rows, 0:seen] * jnp.exp(gaps)).astype(jnp.bfloat16)
                    part = part + dot32(mixing, sides[side][0:seen])
                y_ref[b * BLOCK + rows.start : b * BLOCK + rows.stop, own] = part


def z_most_kernel(normed_ref, own_ref, near_ref, far_ref, most_ref):
    position = lax.axis_index("dp")
    rows = own_ref.shape[0]
    total = 0.0
    for j, w_ref in enumerate((own_ref, near_ref, far_ref)):
        at = pl.multiple_of(jnp.bitwise_xor(position, j) * rows, LANES)
        total = total + dot32(normed_ref[:, pl.ds(at, rows)], w_ref[...])
    most_ref[...] = total


def z_last_kernel(normed_ref, last_ref, most_ref, gate_ref):
    rows = last_ref.shape[0]
    at = pl.multiple_of(jnp.bitwise_xor(lax.axis_index("dp"), 3) * rows, LANES)
    gate_ref[...] = silu_tanh(most_ref[...] + dot32(normed_ref[:, pl.ds(at, rows)], last_ref[...]))


def gate_kernel(enter_ref, bc_ref, prefix_ref, meta_ref, y_ref, z_ref, arrived_ref, *outs):
    scratch = outs[-1]
    inner = y_ref.shape[1]
    state_width = enter_ref.shape[1]
    head_dim = LANES // 2
    c_all = bc_ref[:, state_width:]
    inter = dot32(c_all, enter_ref[...], 1, 1)
    carried = jnp.exp(prefix_ref[...]) * meta_ref[:, 3:4]
    for q in range(inner // LANES):
        own = slice(q * LANES, (q + 1) * LANES)
        value = y_ref[:, own] + widen(carried, q, head_dim) * inter[:, own]
        scratch[:, own] = (value * z_ref[:, own]).astype(jnp.bfloat16)
    head = lax.axis_index("head")
    part = outs[0].shape[0] // 2
    for n, related in enumerate((PASSED, STAYING)):
        for out, owner in zip(outs[2 * n : 2 * n + 2], (head, jnp.bitwise_xor(head, Z_NEAR))):
            for k, bits in enumerate(related):
                at = pl.multiple_of(jnp.bitwise_xor(owner, bits) * part, part)
                out[k * part : (k + 1) * part, :] = scratch[pl.ds(at, part), :]


def pick_kernel(own_ref, far_ref, *refs):
    tables, others, (keep_ref, send_ref, send_last_ref, far_v, sem) = refs[:4], refs[4:8], refs[8:]
    count = keep_ref.shape[0]
    part = tables[0].shape[1]
    rows = far_ref.shape[0] - 6 * TILE_ROWS
    width = far_ref.shape[1]
    model_rows = rows // width
    at = rows + TILE_ROWS * model_rows
    lanes = rows - model_rows * width
    arrival = pltpu.make_async_copy(
        far_ref.at[at : at + TILE_ROWS, lanes : lanes + LANES], far_v, sem
    )
    arrival.start()

    def pick(k, g):
        total = tables[k][g].astype(jnp.float32) + others[k][g].astype(jnp.float32)
        return total.astype(jnp.bfloat16)

    for r in range(count):
        for k in range(len(tables)):
            keep_ref[r, k * part : (k + 1) * part] = pick(k, own_ref[r])
    arrival.wait()
    wanted = far_v[...].astype(jnp.float32)[0:1, :]
    lane = lax.broadcasted_iota(jnp.int32, (1, LANES), 1)
    for r in range(count):
        g = jnp.sum(jnp.where(lane == r, wanted, 0.0)).astype(jnp.int32)
        for k in range(len(tables) - 1):
            send_ref[r, k * part : (k + 1) * part] = pick(k, g)
        send_last_ref[r] = pick(len(tables) - 1, g)


def split_squares(squares):
    lane = lax.broadcasted_iota(jnp.int32, (squares.shape[0], LANES), 1)
    high = squares.astype(jnp.bfloat16).astype(jnp.float32)
    return jnp.where(lane == 0, high, squares - high).astype(jnp.bfloat16)


def joined_squares(ref, model):
    high = ref[:, model : model + 1].astype(jnp.float32)
    return high + ref[:, model + 1 : model + 2].astype(jnp.float32)


def out_kernel(kept_ref, got_ref, own_ref, part_ref, near_ref, wide_out, bf16_out, sums_ref):
    core = lax.axis_index("dp") % 2
    width = part_ref.shape[1]
    rows, model = sums_ref.shape
    part = wide_out.shape[0]
    kept, got = kept_ref[...], got_ref[...]
    squares = jnp.zeros((rows, 1), jnp.float32)
    for value in (kept, got):
        wide = value.astype(jnp.float32)
        squares = squares + jnp.sum(wide * wide, axis=1, keepdims=True)
    for j, other_ref in enumerate((part_ref, near_ref)):
        at = pl.multiple_of(jnp.bitwise_xor(core, j) * width, LANES)
        own = dot32(kept, own_ref[:, pl.ds(at, width)])
        sums_ref[:, pl.ds(at, width)] = own + dot32(got, other_ref[...])
    wide_out[:, 0:model] = sums_ref[0:part, :]
    wide_out[:, model:] = jnp.broadcast_to(squares[0:part], (part, LANES))
    bf16_out[:, 0:model] = sums_ref[part:, :].astype(jnp.bfloat16)
    bf16_out[:, model:] = split_squares(squares[part:])


def pass_kernel(pass_ref, cross_ref, out_ref):
    model = out_ref.shape[1] - LANES
    total = pass_ref[:, 0:model] + cross_ref[:, 0:model].astype(jnp.float32)
    out_ref[:, 0:model] = total.astype(jnp.bfloat16)
    squares = pass_ref[:, model : model + 1] + joined_squares(cross_ref, model)
    out_ref[:, model:] = split_squares(squares)


def finish_kernel(inner_total, hidden_ref, joined_ref, keep_ref, *refs):
    got, out_ref = refs[:-1], refs[-1]
    model = hidden_ref.shape[1]
    squares = keep_ref[:, model : model + 1]
    total = keep_ref[:, 0:model]
    for ref in got:
        squares = squares + joined_squares(ref, model)
        total = total + ref[:, 0:model].astype(jnp.float32)
    scale = lax.rsqrt(squares / inner_total + EPSILON)
    out_ref[...] = (hidden_ref[...].astype(jnp.float32) + scale * total).astype(jnp.bfloat16)


def join_kernel(keep_ref, *refs):
    fars, (out_ref, done_ref) = refs[:-2], refs[-2:]
    done_ref[...] = jnp.zeros_like(done_ref)
    at = 0
    for far_ref in fars:
        own = slice(at, at + far_ref.shape[1])
        out_ref[:, own] = keep_ref[:, own].astype(jnp.float32) + far_ref[...].astype(jnp.float32)
        at += far_ref.shape[1]


def fused_on_device(
    hidden,
    token_prompt,
    request_prompt,
    in_gain,
    w_zx,
    w_bc,
    w_dt,
    dt_bias,
    a_log,
    conv_x,
    conv_bc,
    skip_gain,
    out_gain,
    w_out,
):
    tok, model = hidden.shape
    rows = w_zx.shape[0]
    inner = w_zx.shape[2]
    heads = w_dt.shape[1]
    state_width = w_bc.shape[1] // 2
    tiles = inner // LANES
    peers = lax.axis_size("dp")
    head_count = lax.axis_size("head")
    bf16, f32 = jnp.bfloat16, jnp.float32
    shape = jax.ShapeDtypeStruct
    smem = pl.BlockSpec(memory_space=pltpu.SMEM)
    anywhere = pl.BlockSpec(memory_space=pl.ANY)
    in_hbm = pl.BlockSpec(memory_space=pltpu.HBM)

    extra = TILE_ROWS * (model // (2 * state_width))
    first_own = pl.pallas_call(
        pack_first_kernel,
        name="pack_first_weights",
        out_shape=shape((rows + extra, 2 * state_width), bf16),
        in_specs=[in_hbm] * 4,
        out_specs=in_vmem(1)[0],
        scratch_shapes=[
            pltpu.VMEM((1, request_prompt.shape[0]), jnp.int32),
            pltpu.VMEM(w_bc.shape, f32),
            pltpu.VMEM((heads, rows), f32),
            pltpu.VMEM((TILE_ROWS, model), bf16),
            pltpu.VMEM((TILE_ROWS, model), f32),
            pltpu.SemaphoreType.DMA((4,)),
        ],
        compiler_params=kernel_params(60),
        cost_estimate=LITTLE,
    )(request_prompt[None, :], w_bc, w_dt.T, hidden)
    first_far = exchange(first_own, "dp", 2)
    first_near = exchange(first_own, "dp", 1)
    x_own, gate_own = pl.pallas_call(
        pack_rest_kernel,
        name="pack_x_and_gate_weights",
        out_shape=(shape((rows, inner), bf16), shape((rows, inner), bf16)),
        in_specs=[in_hbm],
        out_specs=tuple(in_vmem(2)),
        scratch_shapes=[
            pltpu.VMEM((inner // LANES, rows, 2, LANES), f32),
            pltpu.SemaphoreType.DMA((inner // LANES,)),
        ],
        compiler_params=kernel_params(8),
        cost_estimate=LITTLE,
    )(w_zx)

    blocks = tok // BLOCK
    normed, meta, order, pen, own_hidden = pl.pallas_call(
        facts_kernel,
        name="norm_and_token_facts",
        out_shape=(
            shape((tok, model), bf16),
            shape((tok, LANES), f32),
            shape((2 * tok, tok), bf16),
            shape((blocks, BLOCK, BLOCK), f32),
            shape((tok // head_count, model), bf16),
        ),
        in_specs=in_vmem(1) + [in_hbm] + in_vmem(1),
        out_specs=tuple(in_vmem(5)),
        scratch_shapes=[pltpu.VMEM((tok, model), bf16), pltpu.SemaphoreType.DMA],
        compiler_params=kernel_params(16),
        cost_estimate=LITTLE,
    )(token_prompt[None, :], hidden, in_gain[None, :])
    scaled_out, half_out = pl.pallas_call(
        scale_kernel,
        name="scale_out_rows",
        out_shape=(shape(w_out.shape, bf16), shape((inner, model // 2), bf16)),
        in_specs=in_vmem(2),
        out_specs=tuple(in_vmem(2)),
        compiler_params=kernel_params(8),
        cost_estimate=LITTLE,
    )(w_out, out_gain[None, :])
    out_part = exchange(half_out, "head", Z_NEAR)
    out_near = exchange(out_part, "dp", 1)

    x_far = exchange(x_own, "dp", 2)
    first_most, first_raw = pl.pallas_call(
        functools.partial(first_most_kernel, heads),
        name="project_b_c_and_steps_of_chip",
        out_shape=(shape((tok, 2 * state_width), f32), shape((tok, LANES), f32)),
        in_specs=in_vmem(3),
        out_specs=tuple(in_vmem(2)),
        scratch_shapes=[pltpu.VMEM((LANES, rows), bf16)],
        compiler_params=kernel_params(8),
        cost_estimate=LITTLE,
    )(normed, first_own, first_near)
    first_far, first_most, first_raw, meta, order, pen, x_own, gate_own = lax.optimization_barrier(
        (first_far, first_most, first_raw, meta, order, pen, x_own, gate_own)
    )
    x_near = exchange(x_own, "dp", 1)
    gate_near = exchange(gate_own, "dp", 1)
    first_last = exchange(first_far, "dp", 1)
    bc, step, prefix, fade, halo = pl.pallas_call(
        first_kernel,
        name="project_b_c_and_steps",
        out_shape=(
            shape((tok, 2 * state_width), bf16),
            shape((tok, LANES), f32),
            shape((tok, LANES), f32),
            shape((tok, LANES), f32),
            shape((TILE_ROWS, model), bf16),
        ),
        in_specs=in_vmem(11) + [smem] * 2,
        out_specs=tuple(in_vmem(5)),
        scratch_shapes=[
            pltpu.VMEM((peers, TILE_ROWS, model), bf16),
            pltpu.VMEM((LANES, rows), bf16),
            pltpu.VMEM((TILE_ROWS + tok, 2 * state_width), f32),
        ],
        compiler_params=kernel_params(14),
        cost_estimate=LITTLE,
    )(
        normed,
        first_most,
        first_raw,
        first_own,
        first_near,
        first_far,
        first_last,
        in_gain[None, :],
        conv_bc,
        meta,
        order,
        dt_bias,
        a_log,
    )
    x_far, gate_own, bc, step, prefix, fade, halo = lax.optimization_barrier(
        (x_far, gate_own, bc, step, prefix, fade, halo)
    )
    x_last = exchange(x_far, "dp", 1)
    gate_far = exchange(gate_own, "dp", 2)
    x, stepx, faded, leaving = pl.pallas_call(
        inner_kernel,
        name="project_and_convolve_x",
        out_shape=(
            shape((tok, inner), bf16),
            shape((tok, inner), bf16),
            shape((inner, tok), bf16),
            shape((inner, state_width), bf16),
        ),
        in_specs=in_vmem(1) + [anywhere] * 4 + in_vmem(6),
        out_specs=tuple(in_vmem(4)),
        scratch_shapes=[
            pltpu.VMEM((model, inner), bf16),
            pltpu.VMEM((TILE_ROWS + tok, inner), f32),
            pltpu.SemaphoreType.DMA((peers,)),
        ],
        compiler_params=kernel_params(14),
        cost_estimate=LITTLE,
    )(
        normed,
        x_own,
        x_near,
        x_far,
        x_last,
        halo,
        conv_x,
        meta,
        bc,
        step,
        fade,
    )

    entering = lax.ppermute(leaving, "dp", [(i, i + 1) for i in range(peers - 1)])

    y_local = pl.pallas_call(
        local_kernel,
        name="mix_within_blocks",
        out_shape=shape((tok, inner), f32),
        in_specs=in_vmem(6) + [smem],
        out_specs=in_vmem(1)[0],
        compiler_params=kernel_params(14),
        cost_estimate=LITTLE,
    )(x, bc, stepx, prefix, meta, pen, skip_gain)
    gate_far, gate_near, entering, y_local = lax.optimization_barrier(
        (gate_far, gate_near, entering, y_local)
    )
    gate_last = exchange(gate_far, "dp", 1)
    tables = pl.pallas_call(
        table_kernel,
        name="sum_ended_states",
        out_shape=(shape((PROMPTS, inner // 4, state_width), bf16),) * 4,
        in_specs=[smem] + in_vmem(5),
        out_specs=tuple(in_vmem(4)),
        compiler_params=kernel_params(8),
        cost_estimate=LITTLE,
    )(token_prompt, bc, faded, meta, prefix, entering)
    tables_near = [exchange(table, "dp", 1) for table in tables]

    gate_most = pl.pallas_call(
        z_most_kernel,
        name="project_gate_most",
        out_shape=shape((tok, inner), f32),
        in_specs=in_vmem(4),
        out_specs=in_vmem(1)[0],
        compiler_params=kernel_params(8),
        cost_estimate=LITTLE,
    )(normed, gate_own, gate_near, gate_far)
    gate = pl.pallas_call(
        z_last_kernel,
        name="project_gate_last",
        out_shape=shape((tok, inner), f32),
        in_specs=in_vmem(3),
        out_specs=in_vmem(1)[0],
        compiler_params=kernel_params(8),
        cost_estimate=LITTLE,
    )(normed, gate_last, gate_most)

    out_rows = tok // head_count
    kept_first, sent_first, kept_rest, sent_rest = pl.pallas_call(
        gate_kernel,
        name="add_entering_and_gate",
        out_shape=(shape((2 * out_rows, inner), bf16),) * 4,
        in_specs=in_vmem(6) + [anywhere],
        out_specs=tuple(in_vmem(4)),
        scratch_shapes=[pltpu.VMEM((tok, inner), bf16)],
        compiler_params=kernel_params(8),
        cost_estimate=LITTLE,
    )(entering, bc, prefix, meta, y_local, gate, out_near)
    got_first = exchange(sent_first, "head", Z_NEAR)
    got_rest = exchange(sent_rest, "head", Z_NEAR)

    requests = request_prompt.shape[0]
    part = inner // 4
    keep, *sends = pl.pallas_call(
        pick_kernel,
        name="pick_request_states",
        out_shape=tuple(
            shape((requests, size, state_width), bf16) for size in (inner, inner - part, part)
        ),
        in_specs=[smem, anywhere] + in_vmem(8),
        out_specs=tuple(in_vmem(3)),
        scratch_shapes=[pltpu.VMEM((TILE_ROWS, LANES), bf16), pltpu.SemaphoreType.DMA],
        compiler_params=kernel_params(8),
        cost_estimate=LITTLE,
    )(request_prompt, first_far, *tables, *tables_near)
    fars = [exchange(send, "dp", 2) for send in sends]

    sums_shape = (out_rows, model + LANES)
    project = pl.pallas_call(
        out_kernel,
        name="project_out",
        out_shape=(shape(sums_shape, f32), shape(sums_shape, bf16)),
        in_specs=in_vmem(5),
        out_specs=tuple(in_vmem(2)),
        scratch_shapes=[pltpu.VMEM((2 * out_rows, model), f32)],
        compiler_params=kernel_params(8),
        cost_estimate=LITTLE,
    )
    sums_pass, sums_cross = project(kept_first, got_first, scaled_out, out_part, out_near)
    sums_keep, sums_near = project(kept_rest, got_rest, scaled_out, out_part, out_near)
    cross = exchange(sums_cross, "head", Y_NEAR)
    cross, sums_near = lax.optimization_barrier((cross, sums_near))
    sums_near = exchange(sums_near, "head", Y_NEAR)
    passed = pl.pallas_call(
        pass_kernel,
        name="add_sums_to_pass_on",
        out_shape=shape(sums_shape, bf16),
        in_specs=in_vmem(2),
        out_specs=in_vmem(1)[0],
        compiler_params=kernel_params(4),
        cost_estimate=LITTLE,
    )(sums_pass, cross)
    passed = exchange(passed, "head", Z_FAR)
    request_states, joined = pl.pallas_call(
        join_kernel,
        name="join_request_states",
        out_shape=(shape((requests, inner, state_width), f32), shape((8, LANES), f32)),
        in_specs=in_vmem(3),
        out_specs=tuple(in_vmem(2)),
        compiler_params=kernel_params(6),
        cost_estimate=LITTLE,
    )(keep, *fars)
    layer_out = pl.pallas_call(
        functools.partial(finish_kernel, inner * head_count),
        name="scale_and_add_hidden",
        out_shape=shape((out_rows, model), bf16),
        in_specs=in_vmem(1) + [anywhere] + in_vmem(3),
        out_specs=in_vmem(1)[0],
        compiler_params=kernel_params(4),
        cost_estimate=LITTLE,
    )(own_hidden, joined, sums_keep, sums_near, passed)
    return (
        layer_out,
        request_states.reshape(requests, heads, inner // heads, state_width),
    )


def fits_fused(mesh):
    return dict(mesh.shape) == {"dp": 4, "head": 8}


def solution(mesh):
    in_specs = (
        P("dp", None),
        P(),
        P("dp"),
        P(),
        P("dp", None, "head"),
        P("dp", None),
        P("dp", "head"),
        P("head"),
        P("head"),
        P(None, "head"),
        P(),
        P("head"),
        P("head"),
        P("head", None),
    )
    out_specs = (P(("dp", "head"), None), P("dp", "head", None, None))
    program = fused_on_device if fits_fused(mesh) else on_device
    return jax.shard_map(
        program, mesh=mesh, in_specs=in_specs, out_specs=out_specs, check_vma=False
    )
```

```python
import functools

import jax
import jax.numpy as jnp
from jax import lax
from jax.experimental import pallas as pl
from jax.experimental.pallas import tpu as pltpu
from jax.sharding import PartitionSpec as P

BLOCK = 256
PROMPTS = 8


EPSILON = 1e-05


def from_behind(shard, axis, by):
    peers = lax.axis_size(axis)
    pairs = [(i, i + by) for i in range(peers) if 0 <= i + by < peers]
    return lax.ppermute(shard, axis, pairs)


def carried_in(shard, axis, combine, identity):
    peers, position = (lax.axis_size(axis), lax.axis_index(axis))
    everything = jax.tree.map(lambda part: lax.all_gather(part, axis), shard)
    start = jax.tree.map(
        lambda part, zero: jnp.broadcast_to(jnp.asarray(zero, part.dtype), part.shape),
        shard,
        identity,
    )

    def step(k, before):
        reached = k < position
        new = combine(before, jax.tree.map(lambda part: part[k], everything))
        return jax.tree.map(lambda a, b: jnp.where(reached, a, b), new, before)

    return lax.fori_loop(0, peers, step, start)


def rms_scale(values):
    return lax.rsqrt(jnp.mean(values * values, axis=-1, keepdims=True) + EPSILON)


def conv_core(extended, extended_ids, token_ids, weights):
    length = token_ids.shape[0]
    total = jnp.zeros((length, extended.shape[1]), jnp.float32)
    for offset in range(weights.shape[0]):
        same = (extended_ids[offset : offset + length] == token_ids)[:, None]
        total = total + jnp.where(
            same, weights[offset] * extended[offset : offset + length].astype(jnp.float32), 0.0
        )
    return jax.nn.silu(total).astype(jnp.bfloat16)


def block_local(x_blk, b_blk, c_blk, step_blk, rate_blk, ids_blk, before_id):
    length = ids_blk.shape[0]
    position = jnp.arange(length, dtype=jnp.int32)
    prefix = jnp.cumsum(rate_blk, axis=0)
    prefix_t = prefix.T
    same = (ids_blk[:, None] == ids_blk[None, :]) & (position[None, :] <= position[:, None])
    gaps = prefix_t[:, :, None] - prefix_t[:, None, :]
    decay = jnp.where(same[None], jnp.exp(jnp.where(same[None], gaps, 0.0)), 0.0)
    scores = jnp.dot(c_blk, b_blk.T, preferred_element_type=jnp.float32)
    mixing = (scores[None] * decay * step_blk.T[:, None, :]).astype(jnp.bfloat16)
    y_intra = jnp.einsum("hts,shp->thp", mixing, x_blk, preferred_element_type=jnp.float32)
    end_id = ids_blk[-1]
    alive = ids_blk == end_id
    weight_end = (
        jnp.where(
            alive[None, :],
            jnp.exp(jnp.where(alive[None, :], prefix_t[:, -1:] - prefix_t, 0.0)),
            0.0,
        )
        * step_blk.T
    )
    b_weighted = (weight_end[:, :, None] * b_blk[None]).astype(jnp.bfloat16)
    local_state = jnp.einsum("hsn,shp->hpn", b_weighted, x_blk, preferred_element_type=jnp.float32)
    carry_gain = jnp.where(end_id == before_id, jnp.exp(prefix_t[:, -1]), 0.0)
    return (y_intra, local_state, carry_gain, prefix)


def block_inter(c_blk, prefix, ids_blk, before_id, state_in):
    entering = ids_blk == before_id
    inter_scale = jnp.where(entering[:, None], jnp.exp(prefix), 0.0)
    return inter_scale[:, :, None] * jnp.einsum(
        "tn,hpn->thp", c_blk.astype(jnp.float32), state_in, precision=lax.Precision.HIGHEST
    )


def block_last(
    last_index, table, x_blk, b_blk, step_blk, prefix, ids_blk, before_id, state_in, start
):
    length = ids_blk.shape[0]
    position = jnp.arange(length, dtype=jnp.int32)
    prompt_ids = jnp.arange(last_index.shape[0], dtype=jnp.int32)
    local_last = last_index - start
    ends_here = (local_last >= 0) & (local_last < length)
    clipped = jnp.clip(local_last, 0, length - 1)

    def with_ends():
        prefix_t = prefix.T
        prefix_last = prefix[clipped]
        pick = (
            ends_here[:, None]
            & (ids_blk[None, :] == prompt_ids[:, None])
            & (position[None, :] <= clipped[:, None])
        )
        spans = prefix_last[:, :, None] - prefix_t[None]
        weight_last = (
            jnp.where(pick[:, None, :], jnp.exp(jnp.where(pick[:, None, :], spans, 0.0)), 0.0)
            * step_blk.T[None]
        )
        b_last = (weight_last[..., None] * b_blk[None, None]).astype(jnp.bfloat16)
        last_local = jnp.einsum("ghsn,shp->ghpn", b_last, x_blk, preferred_element_type=jnp.float32)
        last_gain = jnp.where(
            (ends_here & (prompt_ids == before_id))[:, None], jnp.exp(prefix_last), 0.0
        )
        return table + last_local + last_gain[:, :, None, None] * state_in[None]

    def without_ends():
        return table

    return lax.cond(jnp.any(ends_here), with_ends, without_ends)


def join_states(earlier, later):
    return (earlier[0] * later[0], later[0][:, None, None] * earlier[1] + later[1])


def on_device(
    hidden,
    token_prompt,
    request_prompt,
    in_gain,
    w_zx,
    w_bc,
    w_dt,
    dt_bias,
    a_log,
    conv_x,
    conv_bc,
    skip_gain,
    out_gain,
    w_out,
):
    tok_dev = hidden.shape[0]
    inner_dev = w_zx.shape[2]
    heads_dev = w_dt.shape[1]
    head_dim = inner_dev // heads_dev
    state_width = w_bc.shape[1] // 2
    taps = conv_x.shape[0]
    dp_index = lax.axis_index("dp")
    head_index = lax.axis_index("head")
    head_count = lax.axis_size("head")
    hidden_f = hidden.astype(jnp.float32)
    normed = (hidden_f * rms_scale(hidden_f) * in_gain).astype(jnp.bfloat16)
    pieces = (
        lax.all_gather(w_zx.astype(jnp.bfloat16), "dp", axis=0, tiled=True),
        lax.all_gather(w_dt.astype(jnp.bfloat16), "dp", axis=0, tiled=True),
        lax.all_gather(w_bc.astype(jnp.bfloat16), "dp", axis=0, tiled=True),
    )
    acc_zx, acc_step, acc_bc = tuple(
        (
            jnp.dot(normed, piece.reshape(piece.shape[0], -1), preferred_element_type=jnp.float32)
            for piece in pieces
        )
    )
    proj_bc = acc_bc.astype(jnp.bfloat16)
    proj_zx = acc_zx.astype(jnp.bfloat16)
    gate_z = proj_zx[:, :inner_dev]
    inner_x = proj_zx[:, inner_dev:]
    proj_dt = acc_step.astype(jnp.bfloat16)
    step_size = jax.nn.softplus(proj_dt.astype(jnp.float32) + dt_bias)
    rate = step_size * -jnp.exp(a_log)
    ids_own = lax.dynamic_slice_in_dim(token_prompt, dp_index * tok_dev, tok_dev)
    rim_start = jnp.maximum(dp_index * tok_dev - (taps - 1), 0)
    rim_ids = lax.dynamic_slice_in_dim(token_prompt, rim_start, taps - 1)
    tail_rows = jnp.concatenate(
        [inner_x[tok_dev - taps + 1 :], proj_bc[tok_dev - taps + 1 :]], axis=1
    )
    rim_rows = from_behind(tail_rows, "dp", 1)
    ext_ids = jnp.concatenate([rim_ids, ids_own])
    conv_inner = conv_core(
        jnp.concatenate([rim_rows[:, :inner_dev], inner_x], axis=0), ext_ids, ids_own, conv_x
    )
    conv_bc_out = conv_core(
        jnp.concatenate([rim_rows[:, inner_dev:], proj_bc], axis=0), ext_ids, ids_own, conv_bc
    )
    blocks = tok_dev // BLOCK
    x_heads = conv_inner.reshape(blocks, BLOCK, heads_dev, head_dim)
    b_conv = conv_bc_out[:, :state_width].reshape(blocks, BLOCK, state_width)
    c_conv = conv_bc_out[:, state_width:].reshape(blocks, BLOCK, state_width)
    step_blocks = step_size.reshape(blocks, BLOCK, heads_dev)
    rate_blocks = rate.reshape(blocks, BLOCK, heads_dev)
    id_blocks = ids_own.reshape(blocks, BLOCK)
    prev_last = jnp.where(dp_index > 0, token_prompt[jnp.maximum(dp_index * tok_dev - 1, 0)], -1)
    before_ids = jnp.concatenate([prev_last[None], id_blocks[:-1, -1]])
    y_intra, local_state, carry_gain, prefix = jax.vmap(block_local)(
        x_heads, b_conv, c_conv, step_blocks, rate_blocks, id_blocks, before_ids
    )

    def advance(carry, item):
        gain_acc, state_acc = carry
        gain, block_state = item
        return (
            (gain_acc * gain, gain[:, None, None] * state_acc + block_state),
            (gain_acc, state_acc),
        )

    unit_gain = jnp.ones((heads_dev,), jnp.float32)
    zero_state = jnp.zeros((heads_dev, head_dim, state_width), jnp.float32)
    (dev_gain, dev_state), (prior_gain, prior_state) = lax.scan(
        advance, (unit_gain, zero_state), (carry_gain, local_state)
    )
    scanned = carried_in((dev_gain, dev_state), "dp", join_states, (unit_gain, zero_state))
    incoming = scanned[1]
    block_in = prior_state + prior_gain[:, :, None, None] * incoming[None]
    prompt_ids = jnp.arange(PROMPTS, dtype=jnp.int32)
    last_index = (
        jnp.sum((token_prompt[None, :] <= prompt_ids[:, None]).astype(jnp.int32), axis=1) - 1
    )
    start_pos = (dp_index * blocks + jnp.arange(blocks, dtype=jnp.int32)) * BLOCK
    y_inter = jax.vmap(block_inter)(c_conv, prefix, id_blocks, before_ids, block_in)

    def collect(table, item):
        xb, bb, sb, pb, ib, fb, stb, ob = item
        return (block_last(last_index, table, xb, bb, sb, pb, ib, fb, stb, ob), None)

    empty_table = jnp.zeros((PROMPTS, heads_dev, head_dim, state_width), jnp.float32)
    local_table, unused = lax.scan(
        collect,
        empty_table,
        (x_heads, b_conv, step_blocks, prefix, id_blocks, before_ids, block_in, start_pos),
    )
    ssd_out = (y_intra + y_inter).reshape(tok_dev, heads_dev, head_dim) + skip_gain[
        None, :, None
    ] * conv_inner.astype(jnp.float32).reshape(tok_dev, heads_dev, head_dim)
    gated = ssd_out.reshape(tok_dev, inner_dev) * jax.nn.silu(gate_z.astype(jnp.float32))
    square_sum = lax.psum(jnp.sum(gated * gated, axis=1), "head")
    scale = lax.rsqrt(square_sum / (inner_dev * head_count) + EPSILON)
    normed_out = (gated * scale[:, None] * out_gain).astype(jnp.bfloat16)
    out_rows = tok_dev // head_count
    own_rows = lax.dynamic_slice_in_dim(hidden_f, head_index * out_rows, out_rows, 0)
    mixed = lax.psum_scatter(
        jnp.dot(normed_out, w_out, preferred_element_type=jnp.float32),
        "head",
        scatter_dimension=0,
        tiled=True,
    )
    layer_out = (own_rows + mixed).astype(jnp.bfloat16)
    table = lax.psum(local_table, "dp")
    one_hot = (request_prompt[:, None] == prompt_ids[None, :]).astype(jnp.float32)
    request_states = jnp.einsum("rg,ghpn->rhpn", one_hot, table, precision=lax.Precision.HIGHEST)
    return (layer_out, request_states)


LANES = 128
TILE_ROWS = 16
NEVER = -1e30
Y_NEAR, Z_NEAR, Z_FAR = 1, 2, 4
PASSED = (Z_FAR, Y_NEAR | Z_FAR)
STAYING = (0, Y_NEAR)
LITTLE = pl.CostEstimate(flops=1000, bytes_accessed=1000, transcendentals=0)


def kernel_params(mebibytes):
    return pltpu.CompilerParams(vmem_limit_bytes=mebibytes << 20)


def in_vmem(count):
    return [pl.BlockSpec(memory_space=pltpu.VMEM)] * count


def exchange(values, axis, bits):
    return lax.ppermute(values, axis, [(i, i ^ bits) for i in range(lax.axis_size(axis))])


def dot32(a, b, a_dim=1, b_dim=0):
    return lax.dot_general(
        a, b, (((a_dim,), (b_dim,)), ((), ())), preferred_element_type=jnp.float32
    )


def silu_tanh(values):
    half = 0.5 * values
    return half + half * jnp.tanh(half)


def widen(columns, pair, head_dim):
    rows = columns.shape[0]
    lane = lax.broadcasted_iota(jnp.int32, (rows, LANES), 1)
    first = jnp.broadcast_to(columns[:, 2 * pair : 2 * pair + 1], (rows, LANES))
    second = jnp.broadcast_to(columns[:, 2 * pair + 1 : 2 * pair + 2], (rows, LANES))
    return jnp.where(lane < head_dim, first, second)


def pack_first_kernel(
    req_ref, wbc_ref, wdt_ref, hidden_ref, first_ref, req_v, bc_v, dt_v, tail_v, dt_wide, sems
):
    rows, width = bc_v.shape
    tok, model = hidden_ref.shape
    arrivals = [
        pltpu.make_async_copy(source, target, sems.at[k])
        for k, (source, target) in enumerate(
            (
                (req_ref, req_v),
                (wdt_ref, dt_v),
                (hidden_ref.at[tok - TILE_ROWS : tok], tail_v),
                (wbc_ref, bc_v),
            )
        )
    ]
    for copy in arrivals:
        copy.start()
    dt_wide[...] = jnp.zeros_like(dt_wide)
    arrivals[0].wait()
    dt_wide[0:1, rows : rows + req_v.shape[1]] = req_v[...].astype(jnp.float32)
    arrivals[1].wait()
    dt_wide[0 : dt_v.shape[0], 0:rows] = dt_v[...]
    arrivals[2].wait()
    upper = lax.broadcasted_iota(jnp.int32, (TILE_ROWS, model), 0) < TILE_ROWS // 2
    below = jnp.where(upper, dt_wide[...], tail_v[...].astype(jnp.float32)).astype(jnp.bfloat16)
    for i in range(model // width):
        at = rows + TILE_ROWS * i
        first_ref[at : at + TILE_ROWS, :] = below[:, i * width : (i + 1) * width]
    arrivals[3].wait()
    first_ref[0:rows, :] = bc_v[...].astype(jnp.bfloat16)


def pack_rest_kernel(wzx_ref, x_ref, gate_ref, tiles_ref, sems):
    rows, inner = x_ref.shape
    arrivals = [
        pltpu.make_async_copy(
            wzx_ref.at[:, :, j * LANES : (j + 1) * LANES], tiles_ref.at[j], sems.at[j]
        )
        for j in range(inner // LANES)
    ]
    for copy in arrivals:
        copy.start()
    for j, copy in enumerate(arrivals):
        copy.wait()
        own = slice(j * LANES, (j + 1) * LANES)
        pair = tiles_ref.at[j].reshape(2 * rows, LANES)
        x_ref[:, own] = pair[pl.ds(1, rows, stride=2), :].astype(jnp.bfloat16)
        gate_ref[:, own] = pair[pl.ds(0, rows, stride=2), :].astype(jnp.bfloat16)


def facts_kernel(
    ids_ref,
    hidden_hbm,
    gain_ref,
    normed_ref,
    meta_ref,
    order_ref,
    pen_ref,
    rows_ref,
    hidden_ref,
    sem,
):
    tok = hidden_ref.shape[0]
    arrival = pltpu.make_async_copy(hidden_hbm, hidden_ref, sem)
    arrival.start()
    position = lax.axis_index("dp")
    start = pl.multiple_of(position * tok, tok)
    ids_i = ids_ref[:, pl.ds(start, tok)]
    behind = pl.multiple_of(jnp.maximum(start - LANES, 0), LANES)
    edge = ids_ref[:, pl.ds(behind, LANES)]
    edge = jnp.where(position > 0, edge, -1)
    ahead = pl.multiple_of(jnp.minimum(start + tok, ids_ref.shape[1] - LANES), LANES)
    after = jnp.where(start + tok < ids_ref.shape[1], ids_ref[:, pl.ds(ahead, LANES)], -1)
    after = after[:, 0:1].astype(jnp.float32)
    long = jnp.concatenate([edge, ids_i], axis=1).astype(jnp.float32)
    ids = ids_i.astype(jnp.float32)
    index = lax.broadcasted_iota(jnp.int32, (1, tok), 1)
    before, last = long[:, LANES - 1 : LANES], ids[:, tok - 1 : tok]
    middle = ids[:, BLOCK - 1 : BLOCK]
    one, zero = jnp.ones((1, tok), jnp.float32), jnp.zeros((1, tok), jnp.float32)
    flag = lambda what: jnp.where(what, one, zero)
    rows = [flag(ids == pltpu.roll(long, k, 1)[:, LANES:]) for k in (1, 2, 3)]
    rows.append(flag(ids == before))
    rows.append(flag((ids == middle) & (index >= BLOCK)))
    rows.append(flag((ids == middle) & (index < BLOCK)))
    rows.append(ids)
    rows.append(flag(ids == last))
    rows.append(flag((ids != last) | (after != last)))
    rows = jnp.concatenate(rows + [jnp.zeros((LANES - len(rows), tok), jnp.float32)], axis=0)
    facts = rows.T
    meta_ref[...] = facts
    column = facts[:, 6:7]
    here = lax.broadcasted_iota(jnp.int32, (tok, tok), 0)
    there = lax.broadcasted_iota(jnp.int32, (tok, tok), 1)
    same = column == ids
    order_ref[0:tok, :] = jnp.where(there <= here, 1.0, 0.0).astype(jnp.bfloat16)
    order_ref[tok:, :] = jnp.where((there > here) & same, 1.0, 0.0).astype(jnp.bfloat16)
    pen = jnp.where((there <= here) & same, 0.0, NEVER)
    for b in range(tok // BLOCK):
        own = slice(b * BLOCK, (b + 1) * BLOCK)
        pen_ref[b] = pen[own, own]
    arrival.wait()
    part = rows_ref.shape[0]
    at = pl.multiple_of(lax.axis_index("head") * part, part)
    rows_ref[...] = hidden_ref[pl.ds(at, part), :]
    hidden = hidden_ref[...].astype(jnp.float32)
    normed_ref[...] = (hidden * rms_scale(hidden) * gain_ref[...]).astype(jnp.bfloat16)


def scale_kernel(w_ref, gain_ref, whole_ref, part_ref):
    rows, model = w_ref.shape
    width = part_ref.shape[1]
    gain = jnp.broadcast_to(gain_ref[...], (LANES, rows)).T
    for j in range(model // LANES):
        own = slice(j * LANES, (j + 1) * LANES)
        whole_ref[:, own] = (w_ref[:, own].astype(jnp.float32) * gain).astype(jnp.bfloat16)
    at = pl.multiple_of((lax.axis_index("dp") % 2) * width, LANES)
    part_ref[...] = whole_ref[:, pl.ds(at, width)]


def convolve(ext_ref, own, taps, same):
    tok = same[0].shape[0]
    total = ext_ref[TILE_ROWS : TILE_ROWS + tok, own] * taps[3:4]
    for k in range(1, 4):
        total = total + same[k - 1] * (
            ext_ref[TILE_ROWS - k : TILE_ROWS - k + tok, own] * taps[3 - k : 4 - k]
        )
    return silu_tanh(total)


def below_rows(buffer, rows):
    count = (buffer.shape[0] - rows) // TILE_ROWS
    return jnp.concatenate(
        [buffer[rows + i * TILE_ROWS : rows + (i + 1) * TILE_ROWS, :] for i in range(count)], axis=1
    )


def project_shard(normed_ref, buffer, j, steps, dtw_ref):
    rows = dtw_ref.shape[1]
    at = pl.multiple_of(jnp.bitwise_xor(lax.axis_index("dp"), j) * rows, LANES)
    normed = normed_ref[:, pl.ds(at, rows)]
    row = lax.broadcasted_iota(jnp.int32, (TILE_ROWS, rows), 0)
    below = below_rows(buffer, rows)[:, 0:rows].astype(jnp.float32)
    dtw_ref[0:TILE_ROWS, :] = jnp.where(row < steps, below, 0.0).astype(jnp.bfloat16)
    return dot32(normed, buffer[0:rows, :]), dot32(normed, dtw_ref[...], 1, 1)


def first_most_kernel(steps, normed_ref, own_ref, near_ref, most_ref, raw_ref, dtw_ref):
    dtw_ref[...] = jnp.zeros_like(dtw_ref)
    most, raw = project_shard(normed_ref, own_ref, 0, steps, dtw_ref)
    more, more_raw = project_shard(normed_ref, near_ref, 1, steps, dtw_ref)
    most_ref[...] = most + more
    raw_ref[...] = raw + more_raw


def first_kernel(
    normed_ref,
    most_ref,
    most_raw_ref,
    own_ref,
    near_ref,
    far_ref,
    last_ref,
    gain_ref,
    taps_ref,
    meta_ref,
    order_ref,
    bias_ref,
    decay_ref,
    bc_ref,
    step_ref,
    prefix_ref,
    fade_ref,
    halo_ref,
    halo_rows_ref,
    dtw_ref,
    ext_ref,
):
    position = lax.axis_index("dp")
    tok, model = normed_ref.shape
    width = bc_ref.shape[1]
    rows = dtw_ref.shape[1]
    buffers = (own_ref, near_ref, far_ref, last_ref)
    for j, buffer in enumerate(buffers):
        halo_rows_ref[jnp.bitwise_xor(position, j)] = below_rows(buffer, rows)
    halo = halo_rows_ref[jnp.maximum(position - 1, 0)].astype(jnp.float32)
    halo_ref[...] = (halo * rms_scale(halo) * gain_ref[...]).astype(jnp.bfloat16)
    halo_sum = 0.0
    for j, buffer in enumerate(buffers):
        at = pl.multiple_of(jnp.bitwise_xor(position, j) * rows, LANES)
        halo_sum = halo_sum + dot32(halo_ref[:, pl.ds(at, rows)], buffer[0:rows, :])
    ext_ref[0:TILE_ROWS, :] = halo_sum
    dtw_ref[...] = jnp.zeros_like(dtw_ref)
    steps = bias_ref.shape[0]
    most, raw = project_shard(normed_ref, far_ref, 2, steps, dtw_ref)
    more, more_raw = project_shard(normed_ref, last_ref, 3, steps, dtw_ref)
    ext_ref[TILE_ROWS:, :] = most_ref[...] + most + more
    head_lane = lax.broadcasted_iota(jnp.int32, (1, LANES), 1)
    bias = jnp.zeros((1, LANES), jnp.float32)
    decay = jnp.zeros((1, LANES), jnp.float32)
    for h in range(steps):
        bias = jnp.where(head_lane == h, bias_ref[h], bias)
        decay = jnp.where(head_lane == h, decay_ref[h], decay)
    raw = most_raw_ref[...] + raw + more_raw + bias
    step = jnp.maximum(raw, 0.0) + jnp.log1p(jnp.exp(-jnp.abs(raw)))
    step_ref[...] = step
    lane = lax.broadcasted_iota(jnp.int32, (tok, LANES), 1)
    rate = jnp.where(lane < TILE_ROWS, -step * jnp.exp(decay), 0.0)
    high = rate.astype(jnp.bfloat16).astype(jnp.float32)
    rest = rate - high
    mid = rest.astype(jnp.bfloat16).astype(jnp.float32)
    low = rest - mid
    packed = high + pltpu.roll(mid, TILE_ROWS, 1) + pltpu.roll(low, 2 * TILE_ROWS, 1)
    sums = dot32(order_ref[...], packed.astype(jnp.bfloat16))
    sums = (
        sums
        + pltpu.roll(sums, LANES - TILE_ROWS, 1)
        + pltpu.roll(sums, LANES - 2 * TILE_ROWS, 1)
    )
    prefix_ref[...] = sums[0:tok]
    fade_ref[...] = jnp.exp(sums[tok : 2 * tok])
    same = [jnp.broadcast_to(meta_ref[:, k : k + 1], (tok, LANES)) for k in range(3)]
    for j in range(width // LANES):
        own = slice(j * LANES, (j + 1) * LANES)
        bc_ref[:, own] = convolve(ext_ref, own, taps_ref[:, own], same).astype(jnp.bfloat16)


def shard_product(normed_ref, j, w_ref):
    rows = w_ref.shape[0]
    at = pl.multiple_of(jnp.bitwise_xor(lax.axis_index("dp"), j) * rows, LANES)
    return dot32(normed_ref[:, pl.ds(at, rows)], w_ref[...])


def inner_most_kernel(normed_ref, own_ref, near_ref, most_ref):
    most_ref[...] = shard_product(normed_ref, 0, own_ref) + shard_product(normed_ref, 1, near_ref)


def inner_far_kernel(normed_ref, most_ref, far_ref, sum_ref, first_ref, second_ref):
    half = first_ref.shape[0]
    first_ref[...] = far_ref[0:half, :]
    second_ref[...] = far_ref[half:, :]
    sum_ref[...] = most_ref[...] + shard_product(normed_ref, 2, far_ref)


def inner_kernel(
    normed_ref,
    most_ref,
    own_ref,
    near_ref,
    far_ref,
    last_first_ref,
    last_second_ref,
    halo_ref,
    taps_ref,
    meta_ref,
    bc_ref,
    step_ref,
    fade_ref,
    x_ref,
    stepx_ref,
    faded_ref,
    leaving_ref,
    ext_ref,
):
    tok = normed_ref.shape[0]
    inner = x_ref.shape[1]
    head_dim = LANES // 2
    rows = far_ref.shape[0]
    at = pl.multiple_of(jnp.bitwise_xor(lax.axis_index("dp"), 3) * rows, LANES)
    last = jnp.concatenate([last_first_ref[...], last_second_ref[...]], axis=0)
    ext_ref[0:TILE_ROWS, :] = sum(
        shard_product(halo_ref, j, w_ref) for j, w_ref in enumerate((own_ref, near_ref, far_ref))
    ) + dot32(halo_ref[:, pl.ds(at, rows)], last)
    ext_ref[TILE_ROWS:, :] = most_ref[...] + dot32(normed_ref[:, pl.ds(at, rows)], last)
    state_width = leaving_ref.shape[1]
    step = step_ref[...]
    fade = fade_ref[...]
    b_all = bc_ref[:, 0:state_width].astype(jnp.float32)
    b_leaving = (b_all * meta_ref[:, 7:8]).astype(jnp.bfloat16)
    same = [jnp.broadcast_to(meta_ref[:, k : k + 1], (tok, LANES)) for k in range(3)]
    for q in range(inner // LANES):
        own = slice(q * LANES, (q + 1) * LANES)
        rounded = convolve(ext_ref, own, taps_ref[:, own], same).astype(jnp.bfloat16)
        x_ref[:, own] = rounded
        scaled = rounded.astype(jnp.float32) * widen(step, q, head_dim)
        stepx_ref[:, own] = scaled.astype(jnp.bfloat16)
        faded = (scaled * widen(fade, q, head_dim)).astype(jnp.bfloat16).T
        faded_ref[own, :] = faded
        leaving_ref[own, :] = dot32(faded, b_leaving).astype(jnp.bfloat16)


def before_device(ids_ref, position, tok):
    return jnp.where(position > 0, ids_ref[jnp.maximum(position * tok - 1, 0)], -1)


def table_kernel(ids_ref, bc_ref, faded_ref, meta_ref, prefix_ref, enter_ref, *refs):
    table_refs = refs[2:]
    rows, state_width = table_refs[0].shape[1:]
    head_dim = LANES // 2
    tok = bc_ref.shape[0]
    b_all = bc_ref[:, 0:state_width].astype(jnp.float32)
    owner = jnp.where(meta_ref[:, 8:9] > 0.0, meta_ref[:, 6:7], -1.0)
    owner = jnp.broadcast_to(owner, (tok, state_width))
    for g in range(0, table_refs[0].shape[0], 2):
        pair = [jnp.where(owner == g + k, b_all, 0.0).astype(jnp.bfloat16) for k in range(2)]
        sums = dot32(faded_ref[...], jnp.concatenate(pair, axis=1)).astype(jnp.bfloat16)
        for n, table_ref in enumerate(table_refs):
            for k in range(2):
                table_ref[g + k] = sums[
                    n * rows : (n + 1) * rows, k * state_width : (k + 1) * state_width
                ]
    position = lax.axis_index("dp")
    before = before_device(ids_ref, position, tok)
    stop = (position + 1) * tok
    after = ids_ref[jnp.minimum(stop, ids_ref.shape[0] - 1)]
    goes_on = (after == before) & (stop < ids_ref.shape[0])
    ended = (ids_ref[position * tok] == before) & ((ids_ref[stop - 1] != before) | ~goes_on)

    @pl.when(ended)
    def add():
        inside = jnp.where(meta_ref[:, 3:4] > 0.0, prefix_ref[...], 0.0)
        gain = jnp.exp(jnp.min(inside, axis=0, keepdims=True))
        chunk = head_dim // 2
        for n in range(faded_ref.shape[0] // chunk):
            table_ref = table_refs[n * chunk // rows]
            own = slice(n * chunk % rows, n * chunk % rows + chunk)
            h = n * chunk // head_dim
            entering = enter_ref[n * chunk : (n + 1) * chunk, :].astype(jnp.float32)
            old = table_ref[before, own, :].astype(jnp.float32)
            table_ref[before, own, :] = (old + gain[:, h : h + 1] * entering).astype(jnp.bfloat16)


def mixing_kernel(bc_ref, prefix_ref, pen_ref, mixing_ref):
    blocks, heads = mixing_ref.shape[0:2]
    state_width = bc_ref.shape[1] // 2
    half = BLOCK // 2
    for b in range(blocks):
        own_rows = slice(b * BLOCK, (b + 1) * BLOCK)
        scores = dot32(bc_ref[own_rows, state_width:], bc_ref[own_rows, 0:state_width], 1, 1)
        prefix = prefix_ref[own_rows, :]
        across = prefix.T
        for h in range(heads):
            for rows, seen in ((slice(0, half), half), (slice(half, BLOCK), BLOCK)):
                gaps = prefix[rows, h : h + 1] - across[h : h + 1, 0:seen] + pen_ref[b, rows, 0:seen]
                mixing_ref[b, h, rows, 0:seen] = (scores[rows, 0:seen] * jnp.exp(gaps)).astype(
                    jnp.bfloat16
                )


def local_kernel(x_ref, bc_ref, stepx_ref, prefix_ref, meta_ref, mixing_ref, skip_ref, y_ref):
    inner = y_ref.shape[1]
    state_width = bc_ref.shape[1] // 2
    head_dim = LANES // 2
    tok = y_ref.shape[0]
    half = BLOCK // 2
    lane = lax.broadcasted_iota(jnp.int32, (BLOCK, LANES), 1)
    for b in range(tok // BLOCK):
        own_rows = slice(b * BLOCK, (b + 1) * BLOCK)
        c_blk = bc_ref[own_rows, state_width:]
        if b > 0:
            before_rows = slice((b - 1) * BLOCK, b * BLOCK)
            before = prefix_ref[before_rows, :]
            carried = jnp.exp(prefix_ref[own_rows, :] - before[BLOCK - 1 : BLOCK, :])
            carried = carried * meta_ref[own_rows, 4:5]
            fade = jnp.exp(before[BLOCK - 1 : BLOCK, :] - before)
            b_before = bc_ref[before_rows, 0:state_width].astype(jnp.float32)
            b_before = (b_before * meta_ref[before_rows, 5:6]).astype(jnp.bfloat16)
        for q in range(inner // LANES):
            own = slice(q * LANES, (q + 1) * LANES)
            x_pair = x_ref[own_rows, own].astype(jnp.float32)
            out = x_pair * jnp.where(lane < head_dim, skip_ref[2 * q], skip_ref[2 * q + 1])
            if b > 0:
                faded = stepx_ref[before_rows, own].astype(jnp.float32) * widen(fade, q, head_dim)
                middle = dot32(faded.astype(jnp.bfloat16).T, b_before).astype(jnp.bfloat16)
                out = out + widen(carried, q, head_dim) * dot32(c_blk, middle, 1, 1)
            sx = stepx_ref[own_rows, own].astype(jnp.float32)
            sides = [jnp.where(lane < head_dim, sx, 0.0), jnp.where(lane >= head_dim, sx, 0.0)]
            sides = [side.astype(jnp.bfloat16) for side in sides]
            for rows, seen in ((slice(0, half), half), (slice(half, BLOCK), BLOCK)):
                part = out[rows]
                for side in range(2):
                    mixing = mixing_ref[b, 2 * q + side, rows, 0:seen]
                    part = part + dot32(mixing, sides[side][0:seen])
                y_ref[b * BLOCK + rows.start : b * BLOCK + rows.stop, own] = part


def z_most_kernel(
    normed_ref, own_ref, near_ref, far_ref, part_ref, most_ref, first_ref, second_ref
):
    half = first_ref.shape[0]
    first_ref[...] = part_ref[0:half, :]
    second_ref[...] = part_ref[half:, :]
    most_ref[...] = sum(
        shard_product(normed_ref, j, w_ref) for j, w_ref in enumerate((own_ref, near_ref, far_ref))
    )


def z_last_kernel(normed_ref, last_ref, most_ref, gate_ref):
    gate_ref[...] = silu_tanh(most_ref[...] + shard_product(normed_ref, 3, last_ref))


def gate_kernel(enter_ref, bc_ref, prefix_ref, meta_ref, y_ref, z_ref, *outs):
    scratch, outs = outs[-1], outs[:-1]
    inner = y_ref.shape[1]
    state_width = enter_ref.shape[1]
    head_dim = LANES // 2
    c_all = bc_ref[:, state_width:]
    inter = dot32(c_all, enter_ref[...], 1, 1)
    carried = jnp.exp(prefix_ref[...]) * meta_ref[:, 3:4]
    for q in range(inner // LANES):
        own = slice(q * LANES, (q + 1) * LANES)
        value = y_ref[:, own] + widen(carried, q, head_dim) * inter[:, own]
        scratch[:, own] = (value * z_ref[:, own]).astype(jnp.bfloat16)
    head = lax.axis_index("head")
    part = outs[0].shape[0] // 2
    for n, related in enumerate((PASSED, STAYING)):
        for out, owner in zip(outs[2 * n : 2 * n + 2], (head, jnp.bitwise_xor(head, Z_NEAR))):
            for k, bits in enumerate(related):
                at = pl.multiple_of(jnp.bitwise_xor(owner, bits) * part, part)
                out[k * part : (k + 1) * part, :] = scratch[pl.ds(at, part), :]


def pick_kernel(own_ref, far_ref, *refs):
    tables, others, (keep_ref, send_ref, send_last_ref, far_v, sem) = refs[:4], refs[4:8], refs[8:]
    count = keep_ref.shape[0]
    part = tables[0].shape[1]
    rows = far_ref.shape[0] - 6 * TILE_ROWS
    width = far_ref.shape[1]
    model_rows = rows // width
    at = rows + TILE_ROWS * model_rows
    lanes = rows - model_rows * width
    arrival = pltpu.make_async_copy(
        far_ref.at[at : at + TILE_ROWS, lanes : lanes + LANES], far_v, sem
    )
    arrival.start()

    def pick(k, g):
        total = tables[k][g].astype(jnp.float32) + others[k][g].astype(jnp.float32)
        return total.astype(jnp.bfloat16)

    for r in range(count):
        for k in range(len(tables)):
            keep_ref[r, k * part : (k + 1) * part] = pick(k, own_ref[r])
    arrival.wait()
    wanted = far_v[...].astype(jnp.float32)[0:1, :]
    lane = lax.broadcasted_iota(jnp.int32, (1, LANES), 1)
    for r in range(count):
        g = jnp.sum(jnp.where(lane == r, wanted, 0.0)).astype(jnp.int32)
        for k in range(len(tables) - 1):
            send_ref[r, k * part : (k + 1) * part] = pick(k, g)
        send_last_ref[r] = pick(len(tables) - 1, g)


def split_squares(squares):
    lane = lax.broadcasted_iota(jnp.int32, (squares.shape[0], LANES), 1)
    high = squares.astype(jnp.bfloat16).astype(jnp.float32)
    return jnp.where(lane == 0, high, squares - high).astype(jnp.bfloat16)


def joined_squares(ref, model):
    high = ref[:, model : model + 1].astype(jnp.float32)
    return high + ref[:, model + 1 : model + 2].astype(jnp.float32)


def out_kernel(kept_ref, got_ref, own_ref, part_ref, first_ref, second_ref, wide_out, *refs):
    outs, sums_ref = refs[:-1], refs[-1]
    near = jnp.concatenate([first_ref[...], second_ref[...]], axis=0)
    core = lax.axis_index("dp") % 2
    width = part_ref.shape[1]
    rows, model = sums_ref.shape
    part = wide_out.shape[0]
    kept, got = kept_ref[...], got_ref[...]
    squares = jnp.zeros((rows, 1), jnp.float32)
    for value in (kept, got):
        wide = value.astype(jnp.float32)
        squares = squares + jnp.sum(wide * wide, axis=1, keepdims=True)
    for j, other in enumerate((part_ref[...], near)):
        at = pl.multiple_of(jnp.bitwise_xor(core, j) * width, LANES)
        own = dot32(kept, own_ref[:, pl.ds(at, width)])
        sums_ref[:, pl.ds(at, width)] = own + dot32(got, other)
    wide_out[:, 0:model] = sums_ref[0:part, :]
    wide_out[:, model:] = jnp.broadcast_to(squares[0:part], (part, LANES))
    size = part // len(outs)
    for k, out in enumerate(outs):
        own = slice(part + k * size, part + (k + 1) * size)
        out[:, 0:model] = sums_ref[own, :].astype(jnp.bfloat16)
        out[:, model:] = split_squares(squares[own])


def pass_kernel(pass_ref, cross_ref, arrived_ref, out_ref):
    model = out_ref.shape[1] - LANES
    total = pass_ref[:, 0:model] + cross_ref[:, 0:model].astype(jnp.float32)
    out_ref[:, 0:model] = total.astype(jnp.bfloat16)
    squares = pass_ref[:, model : model + 1] + joined_squares(cross_ref, model)
    out_ref[:, model:] = split_squares(squares)


def finish_kernel(inner_total, hidden_ref, joined_ref, keep_ref, passed_ref, *refs):
    nears, out_ref = refs[:-1], refs[-1]
    model = hidden_ref.shape[1]
    size = nears[0].shape[0]
    for k, near_ref in enumerate(nears):
        own = slice(k * size, (k + 1) * size)
        squares = keep_ref[own, model : model + 1] + joined_squares(near_ref, model)
        squares = squares + joined_squares(passed_ref.at[own], model)
        scale = lax.rsqrt(squares / inner_total + EPSILON)
        total = keep_ref[own, 0:model] + near_ref[:, 0:model].astype(jnp.float32)
        total = total + passed_ref[own, 0:model].astype(jnp.float32)
        hidden = hidden_ref[own, :].astype(jnp.float32)
        out_ref[own, :] = (hidden + scale * total).astype(jnp.bfloat16)


def join_kernel(keep_ref, *refs):
    fars, (out_ref, done_ref) = refs[:-2], refs[-2:]
    done_ref[...] = jnp.zeros_like(done_ref)
    at = 0
    for far_ref in fars:
        own = slice(at, at + far_ref.shape[1])
        out_ref[:, own] = keep_ref[:, own].astype(jnp.float32) + far_ref[...].astype(jnp.float32)
        at += far_ref.shape[1]


def fused_on_device(
    hidden,
    token_prompt,
    request_prompt,
    in_gain,
    w_zx,
    w_bc,
    w_dt,
    dt_bias,
    a_log,
    conv_x,
    conv_bc,
    skip_gain,
    out_gain,
    w_out,
):
    tok, model = hidden.shape
    rows = w_zx.shape[0]
    inner = w_zx.shape[2]
    heads = w_dt.shape[1]
    state_width = w_bc.shape[1] // 2
    tiles = inner // LANES
    peers = lax.axis_size("dp")
    head_count = lax.axis_size("head")
    bf16, f32 = jnp.bfloat16, jnp.float32
    shape = jax.ShapeDtypeStruct
    smem = pl.BlockSpec(memory_space=pltpu.SMEM)
    anywhere = pl.BlockSpec(memory_space=pl.ANY)
    in_hbm = pl.BlockSpec(memory_space=pltpu.HBM)

    extra = TILE_ROWS * (model // (2 * state_width))
    first_own = pl.pallas_call(
        pack_first_kernel,
        name="pack_first_weights",
        out_shape=shape((rows + extra, 2 * state_width), bf16),
        in_specs=[in_hbm] * 4,
        out_specs=in_vmem(1)[0],
        scratch_shapes=[
            pltpu.VMEM((1, request_prompt.shape[0]), jnp.int32),
            pltpu.VMEM(w_bc.shape, f32),
            pltpu.VMEM((heads, rows), f32),
            pltpu.VMEM((TILE_ROWS, model), bf16),
            pltpu.VMEM((TILE_ROWS, model), f32),
            pltpu.SemaphoreType.DMA((4,)),
        ],
        compiler_params=kernel_params(60),
        cost_estimate=LITTLE,
    )(request_prompt[None, :], w_bc, w_dt.T, hidden)
    first_far = exchange(first_own, "dp", 2)
    first_near = exchange(first_own, "dp", 1)
    x_own, gate_own = pl.pallas_call(
        pack_rest_kernel,
        name="pack_x_and_gate_weights",
        out_shape=(shape((rows, inner), bf16), shape((rows, inner), bf16)),
        in_specs=[in_hbm],
        out_specs=tuple(in_vmem(2)),
        scratch_shapes=[
            pltpu.VMEM((inner // LANES, rows, 2, LANES), f32),
            pltpu.SemaphoreType.DMA((inner // LANES,)),
        ],
        compiler_params=kernel_params(8),
        cost_estimate=LITTLE,
    )(w_zx)

    blocks = tok // BLOCK
    normed, meta, order, pen, own_hidden = pl.pallas_call(
        facts_kernel,
        name="norm_and_token_facts",
        out_shape=(
            shape((tok, model), bf16),
            shape((tok, LANES), f32),
            shape((2 * tok, tok), bf16),
            shape((blocks, BLOCK, BLOCK), f32),
            shape((tok // head_count, model), bf16),
        ),
        in_specs=in_vmem(1) + [in_hbm] + in_vmem(1),
        out_specs=tuple(in_vmem(5)),
        scratch_shapes=[pltpu.VMEM((tok, model), bf16), pltpu.SemaphoreType.DMA],
        compiler_params=kernel_params(16),
        cost_estimate=LITTLE,
    )(token_prompt[None, :], hidden, in_gain[None, :])
    scaled_out, half_out = pl.pallas_call(
        scale_kernel,
        name="scale_out_rows",
        out_shape=(shape(w_out.shape, bf16), shape((inner, model // 2), bf16)),
        in_specs=in_vmem(2),
        out_specs=tuple(in_vmem(2)),
        compiler_params=kernel_params(8),
        cost_estimate=LITTLE,
    )(w_out, out_gain[None, :])
    out_part = exchange(half_out, "head", Z_NEAR)

    x_far = exchange(x_own, "dp", 2)
    first_most, first_raw = pl.pallas_call(
        functools.partial(first_most_kernel, heads),
        name="project_b_c_and_steps_of_chip",
        out_shape=(shape((tok, 2 * state_width), f32), shape((tok, LANES), f32)),
        in_specs=in_vmem(3),
        out_specs=tuple(in_vmem(2)),
        scratch_shapes=[pltpu.VMEM((LANES, rows), bf16)],
        compiler_params=kernel_params(8),
        cost_estimate=LITTLE,
    )(normed, first_own, first_near)
    x_near = exchange(x_own, "dp", 1)
    first_far, first_most, first_raw, meta, order, pen, gate_own = lax.optimization_barrier(
        (first_far, first_most, first_raw, meta, order, pen, gate_own)
    )
    gate_near = exchange(gate_own, "dp", 1)
    first_last = exchange(first_far, "dp", 1)
    bc, step, prefix, fade, halo = pl.pallas_call(
        first_kernel,
        name="project_b_c_and_steps",
        out_shape=(
            shape((tok, 2 * state_width), bf16),
            shape((tok, LANES), f32),
            shape((tok, LANES), f32),
            shape((tok, LANES), f32),
            shape((TILE_ROWS, model), bf16),
        ),
        in_specs=in_vmem(11) + [smem] * 2,
        out_specs=tuple(in_vmem(5)),
        scratch_shapes=[
            pltpu.VMEM((peers, TILE_ROWS, model), bf16),
            pltpu.VMEM((LANES, rows), bf16),
            pltpu.VMEM((TILE_ROWS + tok, 2 * state_width), f32),
        ],
        compiler_params=kernel_params(14),
        cost_estimate=LITTLE,
    )(
        normed,
        first_most,
        first_raw,
        first_own,
        first_near,
        first_far,
        first_last,
        in_gain[None, :],
        conv_bc,
        meta,
        order,
        dt_bias,
        a_log,
    )
    x_most = pl.pallas_call(
        inner_most_kernel,
        name="project_x_of_chip",
        out_shape=shape((tok, inner), f32),
        in_specs=in_vmem(3),
        out_specs=in_vmem(1)[0],
        compiler_params=kernel_params(8),
        cost_estimate=LITTLE,
    )(normed, x_own, x_near)
    mixing = pl.pallas_call(
        mixing_kernel,
        name="mixing_weights",
        out_shape=shape((blocks, heads, BLOCK, BLOCK), bf16),
        in_specs=in_vmem(3),
        out_specs=in_vmem(1)[0],
        compiler_params=kernel_params(8),
        cost_estimate=LITTLE,
    )(bc, prefix, pen)
    x_far, x_most, bc, step, prefix, fade, halo, mixing = lax.optimization_barrier(
        (x_far, x_most, bc, step, prefix, fade, halo, mixing)
    )
    x_most, *x_halves = pl.pallas_call(
        inner_far_kernel,
        name="project_x_of_far_device",
        out_shape=(shape((tok, inner), f32),) + (shape((rows // 2, inner), bf16),) * 2,
        in_specs=in_vmem(3),
        out_specs=tuple(in_vmem(3)),
        compiler_params=kernel_params(8),
        cost_estimate=LITTLE,
    )(normed, x_most, x_far)
    x_last = [exchange(part, "dp", 1) for part in x_halves]
    gate_far = exchange(gate_own, "dp", 2)
    x, stepx, faded, leaving = pl.pallas_call(
        inner_kernel,
        name="project_and_convolve_x",
        out_shape=(
            shape((tok, inner), bf16),
            shape((tok, inner), bf16),
            shape((inner, tok), bf16),
            shape((inner, state_width), bf16),
        ),
        in_specs=in_vmem(13),
        out_specs=tuple(in_vmem(4)),
        scratch_shapes=[pltpu.VMEM((TILE_ROWS + tok, inner), f32)],
        compiler_params=kernel_params(14),
        cost_estimate=LITTLE,
    )(
        normed,
        x_most,
        x_own,
        x_near,
        x_far,
        *x_last,
        halo,
        conv_x,
        meta,
        bc,
        step,
        fade,
    )

    entering = lax.ppermute(leaving, "dp", [(i, i + 1) for i in range(peers - 1)])

    y_local = pl.pallas_call(
        local_kernel,
        name="mix_within_blocks",
        out_shape=shape((tok, inner), f32),
        in_specs=in_vmem(6) + [smem],
        out_specs=in_vmem(1)[0],
        compiler_params=kernel_params(14),
        cost_estimate=LITTLE,
    )(x, bc, stepx, prefix, meta, mixing, skip_gain)
    gate_far, gate_near, entering, y_local = lax.optimization_barrier(
        (gate_far, gate_near, entering, y_local)
    )
    gate_last = exchange(gate_far, "dp", 1)
    gate_most, *out_halves = pl.pallas_call(
        z_most_kernel,
        name="project_gate_most",
        out_shape=(shape((tok, inner), f32),) + (shape((inner // 2, model // 2), bf16),) * 2,
        in_specs=in_vmem(5),
        out_specs=tuple(in_vmem(3)),
        compiler_params=kernel_params(8),
        cost_estimate=LITTLE,
    )(normed, gate_own, gate_near, gate_far, out_part)
    out_near = [exchange(part, "dp", 1) for part in out_halves]
    tables = pl.pallas_call(
        table_kernel,
        name="sum_ended_states",
        out_shape=(shape((PROMPTS, inner // 4, state_width), bf16),) * 4,
        in_specs=[smem] + in_vmem(5) + [anywhere] * 2,
        out_specs=tuple(in_vmem(4)),
        compiler_params=kernel_params(8),
        cost_estimate=LITTLE,
    )(token_prompt, bc, faded, meta, prefix, entering, *out_near)
    tables_near = [exchange(table, "dp", 1) for table in tables]

    gate = pl.pallas_call(
        z_last_kernel,
        name="project_gate_last",
        out_shape=shape((tok, inner), f32),
        in_specs=in_vmem(3),
        out_specs=in_vmem(1)[0],
        compiler_params=kernel_params(8),
        cost_estimate=LITTLE,
    )(normed, gate_last, gate_most)

    out_rows = tok // head_count
    kept_first, sent_first, kept_rest, sent_rest = pl.pallas_call(
        gate_kernel,
        name="add_entering_and_gate",
        out_shape=(shape((2 * out_rows, inner), bf16),) * 4,
        in_specs=in_vmem(6),
        out_specs=tuple(in_vmem(4)),
        scratch_shapes=[pltpu.VMEM((tok, inner), bf16)],
        compiler_params=kernel_params(8),
        cost_estimate=LITTLE,
    )(entering, bc, prefix, meta, y_local, gate)
    got_first = exchange(sent_first, "head", Z_NEAR)
    got_rest = exchange(sent_rest, "head", Z_NEAR)

    requests = request_prompt.shape[0]
    part = inner // 4
    keep, *sends = pl.pallas_call(
        pick_kernel,
        name="pick_request_states",
        out_shape=tuple(
            shape((requests, size, state_width), bf16) for size in (inner, inner - part, part)
        ),
        in_specs=[smem, anywhere] + in_vmem(8),
        out_specs=tuple(in_vmem(3)),
        scratch_shapes=[pltpu.VMEM((TILE_ROWS, LANES), bf16), pltpu.SemaphoreType.DMA],
        compiler_params=kernel_params(8),
        cost_estimate=LITTLE,
    )(request_prompt, first_far, *tables, *tables_near)
    fars = [exchange(send, "dp", 2) for send in sends]

    sums_shape = (out_rows, model + LANES)

    def project(kept, got, pieces):
        piece = (out_rows // pieces, model + LANES)
        return pl.pallas_call(
            out_kernel,
            name="project_out",
            out_shape=(shape(sums_shape, f32),) + (shape(piece, bf16),) * pieces,
            in_specs=in_vmem(6),
            out_specs=tuple(in_vmem(1 + pieces)),
            scratch_shapes=[pltpu.VMEM((2 * out_rows, model), f32)],
            compiler_params=kernel_params(8),
            cost_estimate=LITTLE,
        )(kept, got, scaled_out, out_part, *out_near)

    sums_pass, sums_cross = project(kept_first, got_first, 1)
    cross = exchange(sums_cross, "head", Y_NEAR)
    passed = pl.pallas_call(
        pass_kernel,
        name="add_sums_to_pass_on",
        out_shape=shape(sums_shape, bf16),
        in_specs=in_vmem(2) + [anywhere],
        out_specs=in_vmem(1)[0],
        compiler_params=kernel_params(4),
        cost_estimate=LITTLE,
    )(sums_pass, cross, got_rest)
    got_rest, passed = lax.optimization_barrier((got_rest, passed))
    passed = exchange(passed, "head", Z_FAR)
    sums_keep, *sums_near = project(kept_rest, got_rest, 2)
    sums_near = [exchange(part, "head", Y_NEAR) for part in sums_near]
    request_states, joined = pl.pallas_call(
        join_kernel,
        name="join_request_states",
        out_shape=(shape((requests, inner, state_width), f32), shape((8, LANES), f32)),
        in_specs=in_vmem(3),
        out_specs=tuple(in_vmem(2)),
        compiler_params=kernel_params(6),
        cost_estimate=LITTLE,
    )(keep, *fars)
    layer_out = pl.pallas_call(
        functools.partial(finish_kernel, inner * head_count),
        name="scale_and_add_hidden",
        out_shape=shape((out_rows, model), bf16),
        in_specs=in_vmem(1) + [anywhere] + in_vmem(4),
        out_specs=in_vmem(1)[0],
        compiler_params=kernel_params(4),
        cost_estimate=LITTLE,
    )(own_hidden, joined, sums_keep, passed, *sums_near)
    return (
        layer_out,
        request_states.reshape(requests, heads, inner // heads, state_width),
    )


def fits_fused(mesh):
    return dict(mesh.shape) == {"dp": 4, "head": 8}


def solution(mesh):
    in_specs = (
        P("dp", None),
        P(),
        P("dp"),
        P(),
        P("dp", None, "head"),
        P("dp", None),
        P("dp", "head"),
        P("head"),
        P("head"),
        P(None, "head"),
        P(),
        P("head"),
        P("head"),
        P("head", None),
    )
    out_specs = (P(("dp", "head"), None), P("dp", "head", None, None))
    program = fused_on_device if fits_fused(mesh) else on_device
    return jax.shard_map(
        program, mesh=mesh, in_specs=in_specs, out_specs=out_specs, check_vma=False
    )
```

```python
import functools

import jax
import jax.numpy as jnp
from jax import lax
from jax.experimental import pallas as pl
from jax.experimental.pallas import tpu as pltpu
from jax.sharding import PartitionSpec as P

BLOCK = 256
PROMPTS = 8


EPSILON = 1e-05


def from_behind(shard, axis, by):
    peers = lax.axis_size(axis)
    pairs = [(i, i + by) for i in range(peers) if 0 <= i + by < peers]
    return lax.ppermute(shard, axis, pairs)


def carried_in(shard, axis, combine, identity):
    peers, position = (lax.axis_size(axis), lax.axis_index(axis))
    everything = jax.tree.map(lambda part: lax.all_gather(part, axis), shard)
    start = jax.tree.map(
        lambda part, zero: jnp.broadcast_to(jnp.asarray(zero, part.dtype), part.shape),
        shard,
        identity,
    )

    def step(k, before):
        reached = k < position
        new = combine(before, jax.tree.map(lambda part: part[k], everything))
        return jax.tree.map(lambda a, b: jnp.where(reached, a, b), new, before)

    return lax.fori_loop(0, peers, step, start)


def rms_scale(values):
    return lax.rsqrt(jnp.mean(values * values, axis=-1, keepdims=True) + EPSILON)


def conv_core(extended, extended_ids, token_ids, weights):
    length = token_ids.shape[0]
    total = jnp.zeros((length, extended.shape[1]), jnp.float32)
    for offset in range(weights.shape[0]):
        same = (extended_ids[offset : offset + length] == token_ids)[:, None]
        total = total + jnp.where(
            same, weights[offset] * extended[offset : offset + length].astype(jnp.float32), 0.0
        )
    return jax.nn.silu(total).astype(jnp.bfloat16)


def block_local(x_blk, b_blk, c_blk, step_blk, rate_blk, ids_blk, before_id):
    length = ids_blk.shape[0]
    position = jnp.arange(length, dtype=jnp.int32)
    prefix = jnp.cumsum(rate_blk, axis=0)
    prefix_t = prefix.T
    same = (ids_blk[:, None] == ids_blk[None, :]) & (position[None, :] <= position[:, None])
    gaps = prefix_t[:, :, None] - prefix_t[:, None, :]
    decay = jnp.where(same[None], jnp.exp(jnp.where(same[None], gaps, 0.0)), 0.0)
    scores = jnp.dot(c_blk, b_blk.T, preferred_element_type=jnp.float32)
    mixing = (scores[None] * decay * step_blk.T[:, None, :]).astype(jnp.bfloat16)
    y_intra = jnp.einsum("hts,shp->thp", mixing, x_blk, preferred_element_type=jnp.float32)
    end_id = ids_blk[-1]
    alive = ids_blk == end_id
    weight_end = (
        jnp.where(
            alive[None, :],
            jnp.exp(jnp.where(alive[None, :], prefix_t[:, -1:] - prefix_t, 0.0)),
            0.0,
        )
        * step_blk.T
    )
    b_weighted = (weight_end[:, :, None] * b_blk[None]).astype(jnp.bfloat16)
    local_state = jnp.einsum("hsn,shp->hpn", b_weighted, x_blk, preferred_element_type=jnp.float32)
    carry_gain = jnp.where(end_id == before_id, jnp.exp(prefix_t[:, -1]), 0.0)
    return (y_intra, local_state, carry_gain, prefix)


def block_inter(c_blk, prefix, ids_blk, before_id, state_in):
    entering = ids_blk == before_id
    inter_scale = jnp.where(entering[:, None], jnp.exp(prefix), 0.0)
    return inter_scale[:, :, None] * jnp.einsum(
        "tn,hpn->thp", c_blk.astype(jnp.float32), state_in, precision=lax.Precision.HIGHEST
    )


def block_last(
    last_index, table, x_blk, b_blk, step_blk, prefix, ids_blk, before_id, state_in, start
):
    length = ids_blk.shape[0]
    position = jnp.arange(length, dtype=jnp.int32)
    prompt_ids = jnp.arange(last_index.shape[0], dtype=jnp.int32)
    local_last = last_index - start
    ends_here = (local_last >= 0) & (local_last < length)
    clipped = jnp.clip(local_last, 0, length - 1)

    def with_ends():
        prefix_t = prefix.T
        prefix_last = prefix[clipped]
        pick = (
            ends_here[:, None]
            & (ids_blk[None, :] == prompt_ids[:, None])
            & (position[None, :] <= clipped[:, None])
        )
        spans = prefix_last[:, :, None] - prefix_t[None]
        weight_last = (
            jnp.where(pick[:, None, :], jnp.exp(jnp.where(pick[:, None, :], spans, 0.0)), 0.0)
            * step_blk.T[None]
        )
        b_last = (weight_last[..., None] * b_blk[None, None]).astype(jnp.bfloat16)
        last_local = jnp.einsum("ghsn,shp->ghpn", b_last, x_blk, preferred_element_type=jnp.float32)
        last_gain = jnp.where(
            (ends_here & (prompt_ids == before_id))[:, None], jnp.exp(prefix_last), 0.0
        )
        return table + last_local + last_gain[:, :, None, None] * state_in[None]

    def without_ends():
        return table

    return lax.cond(jnp.any(ends_here), with_ends, without_ends)


def join_states(earlier, later):
    return (earlier[0] * later[0], later[0][:, None, None] * earlier[1] + later[1])


def on_device(
    hidden,
    token_prompt,
    request_prompt,
    in_gain,
    w_zx,
    w_bc,
    w_dt,
    dt_bias,
    a_log,
    conv_x,
    conv_bc,
    skip_gain,
    out_gain,
    w_out,
):
    tok_dev = hidden.shape[0]
    inner_dev = w_zx.shape[2]
    heads_dev = w_dt.shape[1]
    head_dim = inner_dev // heads_dev
    state_width = w_bc.shape[1] // 2
    taps = conv_x.shape[0]
    dp_index = lax.axis_index("dp")
    head_index = lax.axis_index("head")
    head_count = lax.axis_size("head")
    hidden_f = hidden.astype(jnp.float32)
    normed = (hidden_f * rms_scale(hidden_f) * in_gain).astype(jnp.bfloat16)
    pieces = (
        lax.all_gather(w_zx.astype(jnp.bfloat16), "dp", axis=0, tiled=True),
        lax.all_gather(w_dt.astype(jnp.bfloat16), "dp", axis=0, tiled=True),
        lax.all_gather(w_bc.astype(jnp.bfloat16), "dp", axis=0, tiled=True),
    )
    acc_zx, acc_step, acc_bc = tuple(
        (
            jnp.dot(normed, piece.reshape(piece.shape[0], -1), preferred_element_type=jnp.float32)
            for piece in pieces
        )
    )
    proj_bc = acc_bc.astype(jnp.bfloat16)
    proj_zx = acc_zx.astype(jnp.bfloat16)
    gate_z = proj_zx[:, :inner_dev]
    inner_x = proj_zx[:, inner_dev:]
    proj_dt = acc_step.astype(jnp.bfloat16)
    step_size = jax.nn.softplus(proj_dt.astype(jnp.float32) + dt_bias)
    rate = step_size * -jnp.exp(a_log)
    ids_own = lax.dynamic_slice_in_dim(token_prompt, dp_index * tok_dev, tok_dev)
    rim_start = jnp.maximum(dp_index * tok_dev - (taps - 1), 0)
    rim_ids = lax.dynamic_slice_in_dim(token_prompt, rim_start, taps - 1)
    tail_rows = jnp.concatenate(
        [inner_x[tok_dev - taps + 1 :], proj_bc[tok_dev - taps + 1 :]], axis=1
    )
    rim_rows = from_behind(tail_rows, "dp", 1)
    ext_ids = jnp.concatenate([rim_ids, ids_own])
    conv_inner = conv_core(
        jnp.concatenate([rim_rows[:, :inner_dev], inner_x], axis=0), ext_ids, ids_own, conv_x
    )
    conv_bc_out = conv_core(
        jnp.concatenate([rim_rows[:, inner_dev:], proj_bc], axis=0), ext_ids, ids_own, conv_bc
    )
    blocks = tok_dev // BLOCK
    x_heads = conv_inner.reshape(blocks, BLOCK, heads_dev, head_dim)
    b_conv = conv_bc_out[:, :state_width].reshape(blocks, BLOCK, state_width)
    c_conv = conv_bc_out[:, state_width:].reshape(blocks, BLOCK, state_width)
    step_blocks = step_size.reshape(blocks, BLOCK, heads_dev)
    rate_blocks = rate.reshape(blocks, BLOCK, heads_dev)
    id_blocks = ids_own.reshape(blocks, BLOCK)
    prev_last = jnp.where(dp_index > 0, token_prompt[jnp.maximum(dp_index * tok_dev - 1, 0)], -1)
    before_ids = jnp.concatenate([prev_last[None], id_blocks[:-1, -1]])
    y_intra, local_state, carry_gain, prefix = jax.vmap(block_local)(
        x_heads, b_conv, c_conv, step_blocks, rate_blocks, id_blocks, before_ids
    )

    def advance(carry, item):
        gain_acc, state_acc = carry
        gain, block_state = item
        return (
            (gain_acc * gain, gain[:, None, None] * state_acc + block_state),
            (gain_acc, state_acc),
        )

    unit_gain = jnp.ones((heads_dev,), jnp.float32)
    zero_state = jnp.zeros((heads_dev, head_dim, state_width), jnp.float32)
    (dev_gain, dev_state), (prior_gain, prior_state) = lax.scan(
        advance, (unit_gain, zero_state), (carry_gain, local_state)
    )
    scanned = carried_in((dev_gain, dev_state), "dp", join_states, (unit_gain, zero_state))
    incoming = scanned[1]
    block_in = prior_state + prior_gain[:, :, None, None] * incoming[None]
    prompt_ids = jnp.arange(PROMPTS, dtype=jnp.int32)
    last_index = (
        jnp.sum((token_prompt[None, :] <= prompt_ids[:, None]).astype(jnp.int32), axis=1) - 1
    )
    start_pos = (dp_index * blocks + jnp.arange(blocks, dtype=jnp.int32)) * BLOCK
    y_inter = jax.vmap(block_inter)(c_conv, prefix, id_blocks, before_ids, block_in)

    def collect(table, item):
        xb, bb, sb, pb, ib, fb, stb, ob = item
        return (block_last(last_index, table, xb, bb, sb, pb, ib, fb, stb, ob), None)

    empty_table = jnp.zeros((PROMPTS, heads_dev, head_dim, state_width), jnp.float32)
    local_table, unused = lax.scan(
        collect,
        empty_table,
        (x_heads, b_conv, step_blocks, prefix, id_blocks, before_ids, block_in, start_pos),
    )
    ssd_out = (y_intra + y_inter).reshape(tok_dev, heads_dev, head_dim) + skip_gain[
        None, :, None
    ] * conv_inner.astype(jnp.float32).reshape(tok_dev, heads_dev, head_dim)
    gated = ssd_out.reshape(tok_dev, inner_dev) * jax.nn.silu(gate_z.astype(jnp.float32))
    square_sum = lax.psum(jnp.sum(gated * gated, axis=1), "head")
    scale = lax.rsqrt(square_sum / (inner_dev * head_count) + EPSILON)
    normed_out = (gated * scale[:, None] * out_gain).astype(jnp.bfloat16)
    out_rows = tok_dev // head_count
    own_rows = lax.dynamic_slice_in_dim(hidden_f, head_index * out_rows, out_rows, 0)
    mixed = lax.psum_scatter(
        jnp.dot(normed_out, w_out, preferred_element_type=jnp.float32),
        "head",
        scatter_dimension=0,
        tiled=True,
    )
    layer_out = (own_rows + mixed).astype(jnp.bfloat16)
    table = lax.psum(local_table, "dp")
    one_hot = (request_prompt[:, None] == prompt_ids[None, :]).astype(jnp.float32)
    request_states = jnp.einsum("rg,ghpn->rhpn", one_hot, table, precision=lax.Precision.HIGHEST)
    return (layer_out, request_states)


LANES = 128
TILE_ROWS = 16
NEVER = -1e30
Y_NEAR, Z_NEAR, Z_FAR = 1, 2, 4
PASSED = (Z_FAR, Y_NEAR | Z_FAR)
STAYING = (0, Y_NEAR)
LITTLE = pl.CostEstimate(flops=1000, bytes_accessed=1000, transcendentals=0)


def kernel_params(mebibytes):
    return pltpu.CompilerParams(vmem_limit_bytes=mebibytes << 20)


def in_vmem(count):
    return [pl.BlockSpec(memory_space=pltpu.VMEM)] * count


def exchange(values, axis, bits):
    return lax.ppermute(values, axis, [(i, i ^ bits) for i in range(lax.axis_size(axis))])


def dot32(a, b, a_dim=1, b_dim=0):
    return lax.dot_general(
        a, b, (((a_dim,), (b_dim,)), ((), ())), preferred_element_type=jnp.float32
    )


def silu_tanh(values):
    half = 0.5 * values
    return half + half * jnp.tanh(half)


def widen(columns, pair, head_dim):
    rows = columns.shape[0]
    lane = lax.broadcasted_iota(jnp.int32, (rows, LANES), 1)
    first = jnp.broadcast_to(columns[:, 2 * pair : 2 * pair + 1], (rows, LANES))
    second = jnp.broadcast_to(columns[:, 2 * pair + 1 : 2 * pair + 2], (rows, LANES))
    return jnp.where(lane < head_dim, first, second)


def pack_first_kernel(
    req_ref, wbc_ref, wdt_ref, hidden_ref, first_ref, req_v, bc_v, dt_v, tail_v, dt_wide, sems
):
    rows, width = bc_v.shape
    tok, model = hidden_ref.shape
    arrivals = [
        pltpu.make_async_copy(source, target, sems.at[k])
        for k, (source, target) in enumerate(
            (
                (req_ref, req_v),
                (wdt_ref, dt_v),
                (hidden_ref.at[tok - TILE_ROWS : tok], tail_v),
                (wbc_ref, bc_v),
            )
        )
    ]
    for copy in arrivals:
        copy.start()
    dt_wide[...] = jnp.zeros_like(dt_wide)
    arrivals[0].wait()
    dt_wide[0:1, rows : rows + req_v.shape[1]] = req_v[...].astype(jnp.float32)
    arrivals[1].wait()
    dt_wide[0 : dt_v.shape[0], 0:rows] = dt_v[...]
    arrivals[2].wait()
    upper = lax.broadcasted_iota(jnp.int32, (TILE_ROWS, model), 0) < TILE_ROWS // 2
    below = jnp.where(upper, dt_wide[...], tail_v[...].astype(jnp.float32)).astype(jnp.bfloat16)
    for i in range(model // width):
        at = rows + TILE_ROWS * i
        first_ref[at : at + TILE_ROWS, :] = below[:, i * width : (i + 1) * width]
    arrivals[3].wait()
    first_ref[0:rows, :] = bc_v[...].astype(jnp.bfloat16)


def pack_rest_kernel(wzx_ref, x_ref, gate_ref, tiles_ref, sems):
    rows, inner = x_ref.shape
    arrivals = [
        pltpu.make_async_copy(
            wzx_ref.at[:, :, j * LANES : (j + 1) * LANES], tiles_ref.at[j], sems.at[j]
        )
        for j in range(inner // LANES)
    ]
    for copy in arrivals:
        copy.start()
    for j, copy in enumerate(arrivals):
        copy.wait()
        own = slice(j * LANES, (j + 1) * LANES)
        pair = tiles_ref.at[j].reshape(2 * rows, LANES)
        x_ref[:, own] = pair[pl.ds(1, rows, stride=2), :].astype(jnp.bfloat16)
        gate_ref[:, own] = pair[pl.ds(0, rows, stride=2), :].astype(jnp.bfloat16)


def facts_kernel(
    ids_ref,
    hidden_hbm,
    gain_ref,
    normed_ref,
    meta_ref,
    order_ref,
    pen_ref,
    rows_ref,
    hidden_ref,
    sem,
):
    tok = hidden_ref.shape[0]
    arrival = pltpu.make_async_copy(hidden_hbm, hidden_ref, sem)
    arrival.start()
    position = lax.axis_index("dp")
    start = pl.multiple_of(position * tok, tok)
    ids_i = ids_ref[:, pl.ds(start, tok)]
    behind = pl.multiple_of(jnp.maximum(start - LANES, 0), LANES)
    edge = ids_ref[:, pl.ds(behind, LANES)]
    edge = jnp.where(position > 0, edge, -1)
    ahead = pl.multiple_of(jnp.minimum(start + tok, ids_ref.shape[1] - LANES), LANES)
    after = jnp.where(start + tok < ids_ref.shape[1], ids_ref[:, pl.ds(ahead, LANES)], -1)
    after = after[:, 0:1].astype(jnp.float32)
    long = jnp.concatenate([edge, ids_i], axis=1).astype(jnp.float32)
    ids = ids_i.astype(jnp.float32)
    index = lax.broadcasted_iota(jnp.int32, (1, tok), 1)
    before, last = long[:, LANES - 1 : LANES], ids[:, tok - 1 : tok]
    middle = ids[:, BLOCK - 1 : BLOCK]
    one, zero = jnp.ones((1, tok), jnp.float32), jnp.zeros((1, tok), jnp.float32)
    flag = lambda what: jnp.where(what, one, zero)
    rows = [flag(ids == pltpu.roll(long, k, 1)[:, LANES:]) for k in (1, 2, 3)]
    rows.append(flag(ids == before))
    rows.append(flag((ids == middle) & (index >= BLOCK)))
    rows.append(flag((ids == middle) & (index < BLOCK)))
    rows.append(ids)
    rows.append(flag(ids == last))
    rows.append(flag((ids != last) | (after != last)))
    rows = jnp.concatenate(rows + [jnp.zeros((LANES - len(rows), tok), jnp.float32)], axis=0)
    facts = rows.T
    meta_ref[...] = facts
    column = facts[:, 6:7]
    here = lax.broadcasted_iota(jnp.int32, (tok, tok), 0)
    there = lax.broadcasted_iota(jnp.int32, (tok, tok), 1)
    same = column == ids
    order_ref[0:tok, :] = jnp.where(there <= here, 1.0, 0.0).astype(jnp.bfloat16)
    order_ref[tok:, :] = jnp.where((there > here) & same, 1.0, 0.0).astype(jnp.bfloat16)
    pen = jnp.where((there <= here) & same, 0.0, NEVER)
    for b in range(tok // BLOCK):
        own = slice(b * BLOCK, (b + 1) * BLOCK)
        pen_ref[b] = pen[own, own]
    arrival.wait()
    part = rows_ref.shape[0]
    at = pl.multiple_of(lax.axis_index("head") * part, part)
    rows_ref[...] = hidden_ref[pl.ds(at, part), :]
    hidden = hidden_ref[...].astype(jnp.float32)
    normed_ref[...] = (hidden * rms_scale(hidden) * gain_ref[...]).astype(jnp.bfloat16)


def scale_kernel(w_ref, gain_ref, whole_ref, part_ref):
    rows, model = w_ref.shape
    width = part_ref.shape[1]
    gain = jnp.broadcast_to(gain_ref[...], (LANES, rows)).T
    for j in range(model // LANES):
        own = slice(j * LANES, (j + 1) * LANES)
        whole_ref[:, own] = (w_ref[:, own].astype(jnp.float32) * gain).astype(jnp.bfloat16)
    at = pl.multiple_of((lax.axis_index("dp") % 2) * width, LANES)
    part_ref[...] = whole_ref[:, pl.ds(at, width)]


def convolve(ext_ref, own, taps, same):
    tok = same[0].shape[0]
    total = ext_ref[TILE_ROWS : TILE_ROWS + tok, own] * taps[3:4]
    for k in range(1, 4):
        total = total + same[k - 1] * (
            ext_ref[TILE_ROWS - k : TILE_ROWS - k + tok, own] * taps[3 - k : 4 - k]
        )
    return silu_tanh(total)


def below_rows(buffer, rows):
    count = (buffer.shape[0] - rows) // TILE_ROWS
    return jnp.concatenate(
        [buffer[rows + i * TILE_ROWS : rows + (i + 1) * TILE_ROWS, :] for i in range(count)], axis=1
    )


def project_shard(normed_ref, buffer, j, steps, dtw_ref):
    rows = dtw_ref.shape[1]
    at = pl.multiple_of(jnp.bitwise_xor(lax.axis_index("dp"), j) * rows, LANES)
    normed = normed_ref[:, pl.ds(at, rows)]
    row = lax.broadcasted_iota(jnp.int32, (TILE_ROWS, rows), 0)
    below = below_rows(buffer, rows)[:, 0:rows].astype(jnp.float32)
    dtw_ref[0:TILE_ROWS, :] = jnp.where(row < steps, below, 0.0).astype(jnp.bfloat16)
    return dot32(normed, buffer[0:rows, :]), dot32(normed, dtw_ref[...], 1, 1)


def first_most_kernel(steps, normed_ref, own_ref, near_ref, most_ref, raw_ref, dtw_ref):
    dtw_ref[...] = jnp.zeros_like(dtw_ref)
    most, raw = project_shard(normed_ref, own_ref, 0, steps, dtw_ref)
    more, more_raw = project_shard(normed_ref, near_ref, 1, steps, dtw_ref)
    most_ref[...] = most + more
    raw_ref[...] = raw + more_raw


def first_kernel(
    normed_ref,
    most_ref,
    most_raw_ref,
    own_ref,
    near_ref,
    far_ref,
    last_ref,
    gain_ref,
    taps_ref,
    meta_ref,
    order_ref,
    bias_ref,
    decay_ref,
    bc_ref,
    step_ref,
    prefix_ref,
    fade_ref,
    halo_ref,
    halo_rows_ref,
    dtw_ref,
    ext_ref,
):
    position = lax.axis_index("dp")
    tok, model = normed_ref.shape
    width = bc_ref.shape[1]
    rows = dtw_ref.shape[1]
    buffers = (own_ref, near_ref, far_ref, last_ref)
    for j, buffer in enumerate(buffers):
        halo_rows_ref[jnp.bitwise_xor(position, j)] = below_rows(buffer, rows)
    halo = halo_rows_ref[jnp.maximum(position - 1, 0)].astype(jnp.float32)
    halo_ref[...] = (halo * rms_scale(halo) * gain_ref[...]).astype(jnp.bfloat16)
    halo_sum = 0.0
    for j, buffer in enumerate(buffers):
        at = pl.multiple_of(jnp.bitwise_xor(position, j) * rows, LANES)
        halo_sum = halo_sum + dot32(halo_ref[:, pl.ds(at, rows)], buffer[0:rows, :])
    ext_ref[0:TILE_ROWS, :] = halo_sum
    dtw_ref[...] = jnp.zeros_like(dtw_ref)
    steps = bias_ref.shape[0]
    most, raw = project_shard(normed_ref, far_ref, 2, steps, dtw_ref)
    more, more_raw = project_shard(normed_ref, last_ref, 3, steps, dtw_ref)
    ext_ref[TILE_ROWS:, :] = most_ref[...] + most + more
    head_lane = lax.broadcasted_iota(jnp.int32, (1, LANES), 1)
    bias = jnp.zeros((1, LANES), jnp.float32)
    decay = jnp.zeros((1, LANES), jnp.float32)
    for h in range(steps):
        bias = jnp.where(head_lane == h, bias_ref[h], bias)
        decay = jnp.where(head_lane == h, decay_ref[h], decay)
    raw = most_raw_ref[...] + raw + more_raw + bias
    step = jnp.maximum(raw, 0.0) + jnp.log1p(jnp.exp(-jnp.abs(raw)))
    step_ref[...] = step
    lane = lax.broadcasted_iota(jnp.int32, (tok, LANES), 1)
    rate = jnp.where(lane < TILE_ROWS, -step * jnp.exp(decay), 0.0)
    high = rate.astype(jnp.bfloat16).astype(jnp.float32)
    rest = rate - high
    mid = rest.astype(jnp.bfloat16).astype(jnp.float32)
    low = rest - mid
    packed = high + pltpu.roll(mid, TILE_ROWS, 1) + pltpu.roll(low, 2 * TILE_ROWS, 1)
    sums = dot32(order_ref[...], packed.astype(jnp.bfloat16))
    sums = (
        sums
        + pltpu.roll(sums, LANES - TILE_ROWS, 1)
        + pltpu.roll(sums, LANES - 2 * TILE_ROWS, 1)
    )
    prefix_ref[...] = sums[0:tok]
    fade_ref[...] = jnp.exp(sums[tok : 2 * tok])
    same = [jnp.broadcast_to(meta_ref[:, k : k + 1], (tok, LANES)) for k in range(3)]
    for j in range(width // LANES):
        own = slice(j * LANES, (j + 1) * LANES)
        bc_ref[:, own] = convolve(ext_ref, own, taps_ref[:, own], same).astype(jnp.bfloat16)


def shard_product(normed_ref, j, w_ref):
    rows = w_ref.shape[0]
    at = pl.multiple_of(jnp.bitwise_xor(lax.axis_index("dp"), j) * rows, LANES)
    return dot32(normed_ref[:, pl.ds(at, rows)], w_ref[...])


def inner_most_kernel(normed_ref, own_ref, near_ref, most_ref):
    most_ref[...] = shard_product(normed_ref, 0, own_ref) + shard_product(normed_ref, 1, near_ref)


def inner_kernel(
    normed_ref,
    most_ref,
    own_ref,
    near_ref,
    far_ref,
    last_ref,
    halo_ref,
    taps_ref,
    meta_ref,
    bc_ref,
    step_ref,
    fade_ref,
    x_ref,
    stepx_ref,
    faded_ref,
    leaving_ref,
    ext_ref,
):
    tok = normed_ref.shape[0]
    inner = x_ref.shape[1]
    head_dim = LANES // 2
    ext_ref[0:TILE_ROWS, :] = sum(
        shard_product(halo_ref, j, w_ref)
        for j, w_ref in enumerate((own_ref, near_ref, far_ref, last_ref))
    )
    ext_ref[TILE_ROWS:, :] = (
        most_ref[...] + shard_product(normed_ref, 2, far_ref) + shard_product(normed_ref, 3, last_ref)
    )
    state_width = leaving_ref.shape[1]
    step = step_ref[...]
    fade = fade_ref[...]
    b_all = bc_ref[:, 0:state_width].astype(jnp.float32)
    b_leaving = (b_all * meta_ref[:, 7:8]).astype(jnp.bfloat16)
    same = [jnp.broadcast_to(meta_ref[:, k : k + 1], (tok, LANES)) for k in range(3)]
    for q in range(inner // LANES):
        own = slice(q * LANES, (q + 1) * LANES)
        rounded = convolve(ext_ref, own, taps_ref[:, own], same).astype(jnp.bfloat16)
        x_ref[:, own] = rounded
        scaled = rounded.astype(jnp.float32) * widen(step, q, head_dim)
        stepx_ref[:, own] = scaled.astype(jnp.bfloat16)
        faded = (scaled * widen(fade, q, head_dim)).astype(jnp.bfloat16).T
        faded_ref[own, :] = faded
        leaving_ref[own, :] = dot32(faded, b_leaving).astype(jnp.bfloat16)


def before_device(ids_ref, position, tok):
    return jnp.where(position > 0, ids_ref[jnp.maximum(position * tok - 1, 0)], -1)


def table_kernel(ids_ref, bc_ref, faded_ref, meta_ref, prefix_ref, enter_ref, *table_refs):
    rows, state_width = table_refs[0].shape[1:]
    head_dim = LANES // 2
    tok = bc_ref.shape[0]
    b_all = bc_ref[:, 0:state_width].astype(jnp.float32)
    owner = jnp.where(meta_ref[:, 8:9] > 0.0, meta_ref[:, 6:7], -1.0)
    owner = jnp.broadcast_to(owner, (tok, state_width))
    for g in range(0, table_refs[0].shape[0], 2):
        pair = [jnp.where(owner == g + k, b_all, 0.0).astype(jnp.bfloat16) for k in range(2)]
        sums = dot32(faded_ref[...], jnp.concatenate(pair, axis=1)).astype(jnp.bfloat16)
        for n, table_ref in enumerate(table_refs):
            for k in range(2):
                table_ref[g + k] = sums[
                    n * rows : (n + 1) * rows, k * state_width : (k + 1) * state_width
                ]
    position = lax.axis_index("dp")
    before = before_device(ids_ref, position, tok)
    stop = (position + 1) * tok
    after = ids_ref[jnp.minimum(stop, ids_ref.shape[0] - 1)]
    goes_on = (after == before) & (stop < ids_ref.shape[0])
    ended = (ids_ref[position * tok] == before) & ((ids_ref[stop - 1] != before) | ~goes_on)

    @pl.when(ended)
    def add():
        inside = jnp.where(meta_ref[:, 3:4] > 0.0, prefix_ref[...], 0.0)
        gain = jnp.exp(jnp.min(inside, axis=0, keepdims=True))
        chunk = head_dim // 2
        for n in range(faded_ref.shape[0] // chunk):
            table_ref = table_refs[n * chunk // rows]
            own = slice(n * chunk % rows, n * chunk % rows + chunk)
            h = n * chunk // head_dim
            entering = enter_ref[n * chunk : (n + 1) * chunk, :].astype(jnp.float32)
            old = table_ref[before, own, :].astype(jnp.float32)
            table_ref[before, own, :] = (old + gain[:, h : h + 1] * entering).astype(jnp.bfloat16)


def local_kernel(
    x_ref,
    bc_ref,
    stepx_ref,
    prefix_ref,
    meta_ref,
    pen_ref,
    skip_ref,
    y_ref,
):
    inner = y_ref.shape[1]
    state_width = bc_ref.shape[1] // 2
    head_dim = LANES // 2
    tok = y_ref.shape[0]
    lane = lax.broadcasted_iota(jnp.int32, (BLOCK, LANES), 1)
    half = BLOCK // 2
    for b in range(tok // BLOCK):
        own_rows = slice(b * BLOCK, (b + 1) * BLOCK)
        b_blk = bc_ref[own_rows, 0:state_width]
        c_blk = bc_ref[own_rows, state_width:]
        scores = dot32(c_blk, b_blk, 1, 1)
        pen = pen_ref[b]
        prefix = prefix_ref[own_rows, :]
        across = prefix.T
        if b > 0:
            carried = jnp.exp(prefix - prefix_ref[b * BLOCK - 1 : b * BLOCK, :])
            carried = carried * meta_ref[own_rows, 4:5]
            before_rows = slice((b - 1) * BLOCK, b * BLOCK)
            before = prefix_ref[before_rows, :]
            fade = jnp.exp(before[BLOCK - 1 : BLOCK, :] - before)
            b_before = bc_ref[before_rows, 0:state_width].astype(jnp.float32)
            b_before = (b_before * meta_ref[before_rows, 5:6]).astype(jnp.bfloat16)
        for q in range(inner // LANES):
            own = slice(q * LANES, (q + 1) * LANES)
            x_pair = x_ref[own_rows, own].astype(jnp.float32)
            out = x_pair * jnp.where(lane < head_dim, skip_ref[2 * q], skip_ref[2 * q + 1])
            if b > 0:
                faded = stepx_ref[before_rows, own].astype(jnp.float32) * widen(fade, q, head_dim)
                middle = dot32(faded.astype(jnp.bfloat16).T, b_before).astype(jnp.bfloat16)
                out = out + widen(carried, q, head_dim) * dot32(c_blk, middle, 1, 1)
            sx = stepx_ref[own_rows, own].astype(jnp.float32)
            sides = [jnp.where(lane < head_dim, sx, 0.0), jnp.where(lane >= head_dim, sx, 0.0)]
            sides = [side.astype(jnp.bfloat16) for side in sides]
            for rows, seen in ((slice(0, half), half), (slice(half, BLOCK), BLOCK)):
                part = out[rows]
                for side in range(2):
                    h = 2 * q + side
                    gaps = prefix[rows, h : h + 1] - across[h : h + 1, 0:seen] + pen[rows, 0:seen]
                    mixing = (scores[rows, 0:seen] * jnp.exp(gaps)).astype(jnp.bfloat16)
                    part = part + dot32(mixing, sides[side][0:seen])
                y_ref[b * BLOCK + rows.start : b * BLOCK + rows.stop, own] = part


def z_most_kernel(normed_ref, own_ref, near_ref, far_ref, most_ref):
    most_ref[...] = sum(
        shard_product(normed_ref, j, w_ref) for j, w_ref in enumerate((own_ref, near_ref, far_ref))
    )


def z_last_kernel(normed_ref, last_ref, most_ref, gate_ref):
    gate_ref[...] = silu_tanh(most_ref[...] + shard_product(normed_ref, 3, last_ref))


def gate_kernel(enter_ref, bc_ref, prefix_ref, meta_ref, y_ref, z_ref, arrived_ref, *outs):
    scratch = outs[-1]
    inner = y_ref.shape[1]
    state_width = enter_ref.shape[1]
    head_dim = LANES // 2
    c_all = bc_ref[:, state_width:]
    inter = dot32(c_all, enter_ref[...], 1, 1)
    carried = jnp.exp(prefix_ref[...]) * meta_ref[:, 3:4]
    for q in range(inner // LANES):
        own = slice(q * LANES, (q + 1) * LANES)
        value = y_ref[:, own] + widen(carried, q, head_dim) * inter[:, own]
        scratch[:, own] = (value * z_ref[:, own]).astype(jnp.bfloat16)
    head = lax.axis_index("head")
    part = outs[0].shape[0] // 2
    for n, related in enumerate((PASSED, STAYING)):
        for out, owner in zip(outs[2 * n : 2 * n + 2], (head, jnp.bitwise_xor(head, Z_NEAR))):
            for k, bits in enumerate(related):
                at = pl.multiple_of(jnp.bitwise_xor(owner, bits) * part, part)
                out[k * part : (k + 1) * part, :] = scratch[pl.ds(at, part), :]


def pick_kernel(own_ref, far_ref, *refs):
    tables, others, (keep_ref, send_ref, send_last_ref, far_v, sem) = refs[:4], refs[4:8], refs[8:]
    count = keep_ref.shape[0]
    part = tables[0].shape[1]
    rows = far_ref.shape[0] - 6 * TILE_ROWS
    width = far_ref.shape[1]
    model_rows = rows // width
    at = rows + TILE_ROWS * model_rows
    lanes = rows - model_rows * width
    arrival = pltpu.make_async_copy(
        far_ref.at[at : at + TILE_ROWS, lanes : lanes + LANES], far_v, sem
    )
    arrival.start()

    def pick(k, g):
        total = tables[k][g].astype(jnp.float32) + others[k][g].astype(jnp.float32)
        return total.astype(jnp.bfloat16)

    for r in range(count):
        for k in range(len(tables)):
            keep_ref[r, k * part : (k + 1) * part] = pick(k, own_ref[r])
    arrival.wait()
    wanted = far_v[...].astype(jnp.float32)[0:1, :]
    lane = lax.broadcasted_iota(jnp.int32, (1, LANES), 1)
    for r in range(count):
        g = jnp.sum(jnp.where(lane == r, wanted, 0.0)).astype(jnp.int32)
        for k in range(len(tables) - 1):
            send_ref[r, k * part : (k + 1) * part] = pick(k, g)
        send_last_ref[r] = pick(len(tables) - 1, g)


def split_squares(squares):
    lane = lax.broadcasted_iota(jnp.int32, (squares.shape[0], LANES), 1)
    high = squares.astype(jnp.bfloat16).astype(jnp.float32)
    return jnp.where(lane == 0, high, squares - high).astype(jnp.bfloat16)


def joined_squares(ref, model):
    high = ref[:, model : model + 1].astype(jnp.float32)
    return high + ref[:, model + 1 : model + 2].astype(jnp.float32)


def out_kernel(kept_ref, got_ref, own_ref, part_ref, near_ref, wide_out, *refs):
    outs, sums_ref = refs[:-1], refs[-1]
    core = lax.axis_index("dp") % 2
    width = part_ref.shape[1]
    rows, model = sums_ref.shape
    part = wide_out.shape[0]
    kept, got = kept_ref[...], got_ref[...]
    squares = jnp.zeros((rows, 1), jnp.float32)
    for value in (kept, got):
        wide = value.astype(jnp.float32)
        squares = squares + jnp.sum(wide * wide, axis=1, keepdims=True)
    for j, other_ref in enumerate((part_ref, near_ref)):
        at = pl.multiple_of(jnp.bitwise_xor(core, j) * width, LANES)
        own = dot32(kept, own_ref[:, pl.ds(at, width)])
        sums_ref[:, pl.ds(at, width)] = own + dot32(got, other_ref[...])
    wide_out[:, 0:model] = sums_ref[0:part, :]
    wide_out[:, model:] = jnp.broadcast_to(squares[0:part], (part, LANES))
    size = part // len(outs)
    for k, out in enumerate(outs):
        own = slice(part + k * size, part + (k + 1) * size)
        out[:, 0:model] = sums_ref[own, :].astype(jnp.bfloat16)
        out[:, model:] = split_squares(squares[own])


def pass_kernel(pass_ref, cross_ref, arrived_ref, out_ref):
    model = out_ref.shape[1] - LANES
    total = pass_ref[:, 0:model] + cross_ref[:, 0:model].astype(jnp.float32)
    out_ref[:, 0:model] = total.astype(jnp.bfloat16)
    squares = pass_ref[:, model : model + 1] + joined_squares(cross_ref, model)
    out_ref[:, model:] = split_squares(squares)


def finish_kernel(inner_total, hidden_ref, joined_ref, keep_ref, passed_ref, *refs):
    nears, out_ref = refs[:-1], refs[-1]
    model = hidden_ref.shape[1]
    size = nears[0].shape[0]
    for k, near_ref in enumerate(nears):
        own = slice(k * size, (k + 1) * size)
        squares = keep_ref[own, model : model + 1] + joined_squares(near_ref, model)
        squares = squares + joined_squares(passed_ref.at[own], model)
        scale = lax.rsqrt(squares / inner_total + EPSILON)
        total = keep_ref[own, 0:model] + near_ref[:, 0:model].astype(jnp.float32)
        total = total + passed_ref[own, 0:model].astype(jnp.float32)
        hidden = hidden_ref[own, :].astype(jnp.float32)
        out_ref[own, :] = (hidden + scale * total).astype(jnp.bfloat16)


def join_kernel(keep_ref, *refs):
    fars, (out_ref, done_ref) = refs[:-2], refs[-2:]
    done_ref[...] = jnp.zeros_like(done_ref)
    at = 0
    for far_ref in fars:
        own = slice(at, at + far_ref.shape[1])
        out_ref[:, own] = keep_ref[:, own].astype(jnp.float32) + far_ref[...].astype(jnp.float32)
        at += far_ref.shape[1]


def fused_on_device(
    hidden,
    token_prompt,
    request_prompt,
    in_gain,
    w_zx,
    w_bc,
    w_dt,
    dt_bias,
    a_log,
    conv_x,
    conv_bc,
    skip_gain,
    out_gain,
    w_out,
):
    tok, model = hidden.shape
    rows = w_zx.shape[0]
    inner = w_zx.shape[2]
    heads = w_dt.shape[1]
    state_width = w_bc.shape[1] // 2
    tiles = inner // LANES
    peers = lax.axis_size("dp")
    head_count = lax.axis_size("head")
    bf16, f32 = jnp.bfloat16, jnp.float32
    shape = jax.ShapeDtypeStruct
    smem = pl.BlockSpec(memory_space=pltpu.SMEM)
    anywhere = pl.BlockSpec(memory_space=pl.ANY)
    in_hbm = pl.BlockSpec(memory_space=pltpu.HBM)

    extra = TILE_ROWS * (model // (2 * state_width))
    first_own = pl.pallas_call(
        pack_first_kernel,
        name="pack_first_weights",
        out_shape=shape((rows + extra, 2 * state_width), bf16),
        in_specs=[in_hbm] * 4,
        out_specs=in_vmem(1)[0],
        scratch_shapes=[
            pltpu.VMEM((1, request_prompt.shape[0]), jnp.int32),
            pltpu.VMEM(w_bc.shape, f32),
            pltpu.VMEM((heads, rows), f32),
            pltpu.VMEM((TILE_ROWS, model), bf16),
            pltpu.VMEM((TILE_ROWS, model), f32),
            pltpu.SemaphoreType.DMA((4,)),
        ],
        compiler_params=kernel_params(60),
        cost_estimate=LITTLE,
    )(request_prompt[None, :], w_bc, w_dt.T, hidden)
    first_far = exchange(first_own, "dp", 2)
    first_near = exchange(first_own, "dp", 1)
    x_own, gate_own = pl.pallas_call(
        pack_rest_kernel,
        name="pack_x_and_gate_weights",
        out_shape=(shape((rows, inner), bf16), shape((rows, inner), bf16)),
        in_specs=[in_hbm],
        out_specs=tuple(in_vmem(2)),
        scratch_shapes=[
            pltpu.VMEM((inner // LANES, rows, 2, LANES), f32),
            pltpu.SemaphoreType.DMA((inner // LANES,)),
        ],
        compiler_params=kernel_params(8),
        cost_estimate=LITTLE,
    )(w_zx)

    blocks = tok // BLOCK
    normed, meta, order, pen, own_hidden = pl.pallas_call(
        facts_kernel,
        name="norm_and_token_facts",
        out_shape=(
            shape((tok, model), bf16),
            shape((tok, LANES), f32),
            shape((2 * tok, tok), bf16),
            shape((blocks, BLOCK, BLOCK), f32),
            shape((tok // head_count, model), bf16),
        ),
        in_specs=in_vmem(1) + [in_hbm] + in_vmem(1),
        out_specs=tuple(in_vmem(5)),
        scratch_shapes=[pltpu.VMEM((tok, model), bf16), pltpu.SemaphoreType.DMA],
        compiler_params=kernel_params(16),
        cost_estimate=LITTLE,
    )(token_prompt[None, :], hidden, in_gain[None, :])
    scaled_out, half_out = pl.pallas_call(
        scale_kernel,
        name="scale_out_rows",
        out_shape=(shape(w_out.shape, bf16), shape((inner, model // 2), bf16)),
        in_specs=in_vmem(2),
        out_specs=tuple(in_vmem(2)),
        compiler_params=kernel_params(8),
        cost_estimate=LITTLE,
    )(w_out, out_gain[None, :])
    out_part = exchange(half_out, "head", Z_NEAR)
    out_near = exchange(out_part, "dp", 1)

    x_far = exchange(x_own, "dp", 2)
    first_most, first_raw = pl.pallas_call(
        functools.partial(first_most_kernel, heads),
        name="project_b_c_and_steps_of_chip",
        out_shape=(shape((tok, 2 * state_width), f32), shape((tok, LANES), f32)),
        in_specs=in_vmem(3),
        out_specs=tuple(in_vmem(2)),
        scratch_shapes=[pltpu.VMEM((LANES, rows), bf16)],
        compiler_params=kernel_params(8),
        cost_estimate=LITTLE,
    )(normed, first_own, first_near)
    x_near = exchange(x_own, "dp", 1)
    first_far, first_most, first_raw, meta, order, pen, gate_own = lax.optimization_barrier(
        (first_far, first_most, first_raw, meta, order, pen, gate_own)
    )
    gate_near = exchange(gate_own, "dp", 1)
    first_last = exchange(first_far, "dp", 1)
    bc, step, prefix, fade, halo = pl.pallas_call(
        first_kernel,
        name="project_b_c_and_steps",
        out_shape=(
            shape((tok, 2 * state_width), bf16),
            shape((tok, LANES), f32),
            shape((tok, LANES), f32),
            shape((tok, LANES), f32),
            shape((TILE_ROWS, model), bf16),
        ),
        in_specs=in_vmem(11) + [smem] * 2,
        out_specs=tuple(in_vmem(5)),
        scratch_shapes=[
            pltpu.VMEM((peers, TILE_ROWS, model), bf16),
            pltpu.VMEM((LANES, rows), bf16),
            pltpu.VMEM((TILE_ROWS + tok, 2 * state_width), f32),
        ],
        compiler_params=kernel_params(14),
        cost_estimate=LITTLE,
    )(
        normed,
        first_most,
        first_raw,
        first_own,
        first_near,
        first_far,
        first_last,
        in_gain[None, :],
        conv_bc,
        meta,
        order,
        dt_bias,
        a_log,
    )
    x_most = pl.pallas_call(
        inner_most_kernel,
        name="project_x_of_chip",
        out_shape=shape((tok, inner), f32),
        in_specs=in_vmem(3),
        out_specs=in_vmem(1)[0],
        compiler_params=kernel_params(8),
        cost_estimate=LITTLE,
    )(normed, x_own, x_near)
    x_far, x_most, gate_own, bc, step, prefix, fade, halo = lax.optimization_barrier(
        (x_far, x_most, gate_own, bc, step, prefix, fade, halo)
    )
    x_last = exchange(x_far, "dp", 1)
    gate_far = exchange(gate_own, "dp", 2)
    x, stepx, faded, leaving = pl.pallas_call(
        inner_kernel,
        name="project_and_convolve_x",
        out_shape=(
            shape((tok, inner), bf16),
            shape((tok, inner), bf16),
            shape((inner, tok), bf16),
            shape((inner, state_width), bf16),
        ),
        in_specs=in_vmem(12),
        out_specs=tuple(in_vmem(4)),
        scratch_shapes=[pltpu.VMEM((TILE_ROWS + tok, inner), f32)],
        compiler_params=kernel_params(14),
        cost_estimate=LITTLE,
    )(
        normed,
        x_most,
        x_own,
        x_near,
        x_far,
        x_last,
        halo,
        conv_x,
        meta,
        bc,
        step,
        fade,
    )

    entering = lax.ppermute(leaving, "dp", [(i, i + 1) for i in range(peers - 1)])

    y_local = pl.pallas_call(
        local_kernel,
        name="mix_within_blocks",
        out_shape=shape((tok, inner), f32),
        in_specs=in_vmem(6) + [smem],
        out_specs=in_vmem(1)[0],
        compiler_params=kernel_params(14),
        cost_estimate=LITTLE,
    )(x, bc, stepx, prefix, meta, pen, skip_gain)
    gate_far, gate_near, entering, y_local = lax.optimization_barrier(
        (gate_far, gate_near, entering, y_local)
    )
    gate_last = exchange(gate_far, "dp", 1)
    tables = pl.pallas_call(
        table_kernel,
        name="sum_ended_states",
        out_shape=(shape((PROMPTS, inner // 4, state_width), bf16),) * 4,
        in_specs=[smem] + in_vmem(5),
        out_specs=tuple(in_vmem(4)),
        compiler_params=kernel_params(8),
        cost_estimate=LITTLE,
    )(token_prompt, bc, faded, meta, prefix, entering)
    tables_near = [exchange(table, "dp", 1) for table in tables]

    gate_most = pl.pallas_call(
        z_most_kernel,
        name="project_gate_most",
        out_shape=shape((tok, inner), f32),
        in_specs=in_vmem(4),
        out_specs=in_vmem(1)[0],
        compiler_params=kernel_params(8),
        cost_estimate=LITTLE,
    )(normed, gate_own, gate_near, gate_far)
    gate = pl.pallas_call(
        z_last_kernel,
        name="project_gate_last",
        out_shape=shape((tok, inner), f32),
        in_specs=in_vmem(3),
        out_specs=in_vmem(1)[0],
        compiler_params=kernel_params(8),
        cost_estimate=LITTLE,
    )(normed, gate_last, gate_most)

    out_rows = tok // head_count
    kept_first, sent_first, kept_rest, sent_rest = pl.pallas_call(
        gate_kernel,
        name="add_entering_and_gate",
        out_shape=(shape((2 * out_rows, inner), bf16),) * 4,
        in_specs=in_vmem(6) + [anywhere],
        out_specs=tuple(in_vmem(4)),
        scratch_shapes=[pltpu.VMEM((tok, inner), bf16)],
        compiler_params=kernel_params(8),
        cost_estimate=LITTLE,
    )(entering, bc, prefix, meta, y_local, gate, out_near)
    got_first = exchange(sent_first, "head", Z_NEAR)
    got_rest = exchange(sent_rest, "head", Z_NEAR)

    requests = request_prompt.shape[0]
    part = inner // 4
    keep, *sends = pl.pallas_call(
        pick_kernel,
        name="pick_request_states",
        out_shape=tuple(
            shape((requests, size, state_width), bf16) for size in (inner, inner - part, part)
        ),
        in_specs=[smem, anywhere] + in_vmem(8),
        out_specs=tuple(in_vmem(3)),
        scratch_shapes=[pltpu.VMEM((TILE_ROWS, LANES), bf16), pltpu.SemaphoreType.DMA],
        compiler_params=kernel_params(8),
        cost_estimate=LITTLE,
    )(request_prompt, first_far, *tables, *tables_near)
    fars = [exchange(send, "dp", 2) for send in sends]

    sums_shape = (out_rows, model + LANES)

    def project(kept, got, pieces):
        piece = (out_rows // pieces, model + LANES)
        return pl.pallas_call(
            out_kernel,
            name="project_out",
            out_shape=(shape(sums_shape, f32),) + (shape(piece, bf16),) * pieces,
            in_specs=in_vmem(5),
            out_specs=tuple(in_vmem(1 + pieces)),
            scratch_shapes=[pltpu.VMEM((2 * out_rows, model), f32)],
            compiler_params=kernel_params(8),
            cost_estimate=LITTLE,
        )(kept, got, scaled_out, out_part, out_near)

    sums_pass, sums_cross = project(kept_first, got_first, 1)
    cross = exchange(sums_cross, "head", Y_NEAR)
    passed = pl.pallas_call(
        pass_kernel,
        name="add_sums_to_pass_on",
        out_shape=shape(sums_shape, bf16),
        in_specs=in_vmem(2) + [anywhere],
        out_specs=in_vmem(1)[0],
        compiler_params=kernel_params(4),
        cost_estimate=LITTLE,
    )(sums_pass, cross, got_rest)
    got_rest, passed = lax.optimization_barrier((got_rest, passed))
    passed = exchange(passed, "head", Z_FAR)
    sums_keep, *sums_near = project(kept_rest, got_rest, 2)
    sums_near = [exchange(part, "head", Y_NEAR) for part in sums_near]
    request_states, joined = pl.pallas_call(
        join_kernel,
        name="join_request_states",
        out_shape=(shape((requests, inner, state_width), f32), shape((8, LANES), f32)),
        in_specs=in_vmem(3),
        out_specs=tuple(in_vmem(2)),
        compiler_params=kernel_params(6),
        cost_estimate=LITTLE,
    )(keep, *fars)
    layer_out = pl.pallas_call(
        functools.partial(finish_kernel, inner * head_count),
        name="scale_and_add_hidden",
        out_shape=shape((out_rows, model), bf16),
        in_specs=in_vmem(1) + [anywhere] + in_vmem(4),
        out_specs=in_vmem(1)[0],
        compiler_params=kernel_params(4),
        cost_estimate=LITTLE,
    )(own_hidden, joined, sums_keep, passed, *sums_near)
    return (
        layer_out,
        request_states.reshape(requests, heads, inner // heads, state_width),
    )


def fits_fused(mesh):
    return dict(mesh.shape) == {"dp": 4, "head": 8}


def solution(mesh):
    in_specs = (
        P("dp", None),
        P(),
        P("dp"),
        P(),
        P("dp", None, "head"),
        P("dp", None),
        P("dp", "head"),
        P("head"),
        P("head"),
        P(None, "head"),
        P(),
        P("head"),
        P("head"),
        P("head", None),
    )
    out_specs = (P(("dp", "head"), None), P("dp", "head", None, None))
    program = fused_on_device if fits_fused(mesh) else on_device
    return jax.shard_map(
        program, mesh=mesh, in_specs=in_specs, out_specs=out_specs, check_vma=False
    )
```

```python
import functools

import jax
import jax.numpy as jnp
from jax import lax
from jax.experimental import pallas as pl
from jax.experimental.pallas import tpu as pltpu
from jax.sharding import PartitionSpec as P

BLOCK = 256
PROMPTS = 8


EPSILON = 1e-05


def from_behind(shard, axis, by):
    peers = lax.axis_size(axis)
    pairs = [(i, i + by) for i in range(peers) if 0 <= i + by < peers]
    return lax.ppermute(shard, axis, pairs)


def carried_in(shard, axis, combine, identity):
    peers, position = (lax.axis_size(axis), lax.axis_index(axis))
    everything = jax.tree.map(lambda part: lax.all_gather(part, axis), shard)
    start = jax.tree.map(
        lambda part, zero: jnp.broadcast_to(jnp.asarray(zero, part.dtype), part.shape),
        shard,
        identity,
    )

    def step(k, before):
        reached = k < position
        new = combine(before, jax.tree.map(lambda part: part[k], everything))
        return jax.tree.map(lambda a, b: jnp.where(reached, a, b), new, before)

    return lax.fori_loop(0, peers, step, start)


def rms_scale(values):
    return lax.rsqrt(jnp.mean(values * values, axis=-1, keepdims=True) + EPSILON)


def conv_core(extended, extended_ids, token_ids, weights):
    length = token_ids.shape[0]
    total = jnp.zeros((length, extended.shape[1]), jnp.float32)
    for offset in range(weights.shape[0]):
        same = (extended_ids[offset : offset + length] == token_ids)[:, None]
        total = total + jnp.where(
            same, weights[offset] * extended[offset : offset + length].astype(jnp.float32), 0.0
        )
    return jax.nn.silu(total).astype(jnp.bfloat16)


def block_local(x_blk, b_blk, c_blk, step_blk, rate_blk, ids_blk, before_id):
    length = ids_blk.shape[0]
    position = jnp.arange(length, dtype=jnp.int32)
    prefix = jnp.cumsum(rate_blk, axis=0)
    prefix_t = prefix.T
    same = (ids_blk[:, None] == ids_blk[None, :]) & (position[None, :] <= position[:, None])
    gaps = prefix_t[:, :, None] - prefix_t[:, None, :]
    decay = jnp.where(same[None], jnp.exp(jnp.where(same[None], gaps, 0.0)), 0.0)
    scores = jnp.dot(c_blk, b_blk.T, preferred_element_type=jnp.float32)
    mixing = (scores[None] * decay * step_blk.T[:, None, :]).astype(jnp.bfloat16)
    y_intra = jnp.einsum("hts,shp->thp", mixing, x_blk, preferred_element_type=jnp.float32)
    end_id = ids_blk[-1]
    alive = ids_blk == end_id
    weight_end = (
        jnp.where(
            alive[None, :],
            jnp.exp(jnp.where(alive[None, :], prefix_t[:, -1:] - prefix_t, 0.0)),
            0.0,
        )
        * step_blk.T
    )
    b_weighted = (weight_end[:, :, None] * b_blk[None]).astype(jnp.bfloat16)
    local_state = jnp.einsum("hsn,shp->hpn", b_weighted, x_blk, preferred_element_type=jnp.float32)
    carry_gain = jnp.where(end_id == before_id, jnp.exp(prefix_t[:, -1]), 0.0)
    return (y_intra, local_state, carry_gain, prefix)


def block_inter(c_blk, prefix, ids_blk, before_id, state_in):
    entering = ids_blk == before_id
    inter_scale = jnp.where(entering[:, None], jnp.exp(prefix), 0.0)
    return inter_scale[:, :, None] * jnp.einsum(
        "tn,hpn->thp", c_blk.astype(jnp.float32), state_in, precision=lax.Precision.HIGHEST
    )


def block_last(
    last_index, table, x_blk, b_blk, step_blk, prefix, ids_blk, before_id, state_in, start
):
    length = ids_blk.shape[0]
    position = jnp.arange(length, dtype=jnp.int32)
    prompt_ids = jnp.arange(last_index.shape[0], dtype=jnp.int32)
    local_last = last_index - start
    ends_here = (local_last >= 0) & (local_last < length)
    clipped = jnp.clip(local_last, 0, length - 1)

    def with_ends():
        prefix_t = prefix.T
        prefix_last = prefix[clipped]
        pick = (
            ends_here[:, None]
            & (ids_blk[None, :] == prompt_ids[:, None])
            & (position[None, :] <= clipped[:, None])
        )
        spans = prefix_last[:, :, None] - prefix_t[None]
        weight_last = (
            jnp.where(pick[:, None, :], jnp.exp(jnp.where(pick[:, None, :], spans, 0.0)), 0.0)
            * step_blk.T[None]
        )
        b_last = (weight_last[..., None] * b_blk[None, None]).astype(jnp.bfloat16)
        last_local = jnp.einsum("ghsn,shp->ghpn", b_last, x_blk, preferred_element_type=jnp.float32)
        last_gain = jnp.where(
            (ends_here & (prompt_ids == before_id))[:, None], jnp.exp(prefix_last), 0.0
        )
        return table + last_local + last_gain[:, :, None, None] * state_in[None]

    def without_ends():
        return table

    return lax.cond(jnp.any(ends_here), with_ends, without_ends)


def join_states(earlier, later):
    return (earlier[0] * later[0], later[0][:, None, None] * earlier[1] + later[1])


def on_device(
    hidden,
    token_prompt,
    request_prompt,
    in_gain,
    w_zx,
    w_bc,
    w_dt,
    dt_bias,
    a_log,
    conv_x,
    conv_bc,
    skip_gain,
    out_gain,
    w_out,
):
    tok_dev = hidden.shape[0]
    inner_dev = w_zx.shape[2]
    heads_dev = w_dt.shape[1]
    head_dim = inner_dev // heads_dev
    state_width = w_bc.shape[1] // 2
    taps = conv_x.shape[0]
    dp_index = lax.axis_index("dp")
    head_index = lax.axis_index("head")
    head_count = lax.axis_size("head")
    hidden_f = hidden.astype(jnp.float32)
    normed = (hidden_f * rms_scale(hidden_f) * in_gain).astype(jnp.bfloat16)
    pieces = (
        lax.all_gather(w_zx.astype(jnp.bfloat16), "dp", axis=0, tiled=True),
        lax.all_gather(w_dt.astype(jnp.bfloat16), "dp", axis=0, tiled=True),
        lax.all_gather(w_bc.astype(jnp.bfloat16), "dp", axis=0, tiled=True),
    )
    acc_zx, acc_step, acc_bc = tuple(
        (
            jnp.dot(normed, piece.reshape(piece.shape[0], -1), preferred_element_type=jnp.float32)
            for piece in pieces
        )
    )
    proj_bc = acc_bc.astype(jnp.bfloat16)
    proj_zx = acc_zx.astype(jnp.bfloat16)
    gate_z = proj_zx[:, :inner_dev]
    inner_x = proj_zx[:, inner_dev:]
    proj_dt = acc_step.astype(jnp.bfloat16)
    step_size = jax.nn.softplus(proj_dt.astype(jnp.float32) + dt_bias)
    rate = step_size * -jnp.exp(a_log)
    ids_own = lax.dynamic_slice_in_dim(token_prompt, dp_index * tok_dev, tok_dev)
    rim_start = jnp.maximum(dp_index * tok_dev - (taps - 1), 0)
    rim_ids = lax.dynamic_slice_in_dim(token_prompt, rim_start, taps - 1)
    tail_rows = jnp.concatenate(
        [inner_x[tok_dev - taps + 1 :], proj_bc[tok_dev - taps + 1 :]], axis=1
    )
    rim_rows = from_behind(tail_rows, "dp", 1)
    ext_ids = jnp.concatenate([rim_ids, ids_own])
    conv_inner = conv_core(
        jnp.concatenate([rim_rows[:, :inner_dev], inner_x], axis=0), ext_ids, ids_own, conv_x
    )
    conv_bc_out = conv_core(
        jnp.concatenate([rim_rows[:, inner_dev:], proj_bc], axis=0), ext_ids, ids_own, conv_bc
    )
    blocks = tok_dev // BLOCK
    x_heads = conv_inner.reshape(blocks, BLOCK, heads_dev, head_dim)
    b_conv = conv_bc_out[:, :state_width].reshape(blocks, BLOCK, state_width)
    c_conv = conv_bc_out[:, state_width:].reshape(blocks, BLOCK, state_width)
    step_blocks = step_size.reshape(blocks, BLOCK, heads_dev)
    rate_blocks = rate.reshape(blocks, BLOCK, heads_dev)
    id_blocks = ids_own.reshape(blocks, BLOCK)
    prev_last = jnp.where(dp_index > 0, token_prompt[jnp.maximum(dp_index * tok_dev - 1, 0)], -1)
    before_ids = jnp.concatenate([prev_last[None], id_blocks[:-1, -1]])
    y_intra, local_state, carry_gain, prefix = jax.vmap(block_local)(
        x_heads, b_conv, c_conv, step_blocks, rate_blocks, id_blocks, before_ids
    )

    def advance(carry, item):
        gain_acc, state_acc = carry
        gain, block_state = item
        return (
            (gain_acc * gain, gain[:, None, None] * state_acc + block_state),
            (gain_acc, state_acc),
        )

    unit_gain = jnp.ones((heads_dev,), jnp.float32)
    zero_state = jnp.zeros((heads_dev, head_dim, state_width), jnp.float32)
    (dev_gain, dev_state), (prior_gain, prior_state) = lax.scan(
        advance, (unit_gain, zero_state), (carry_gain, local_state)
    )
    scanned = carried_in((dev_gain, dev_state), "dp", join_states, (unit_gain, zero_state))
    incoming = scanned[1]
    block_in = prior_state + prior_gain[:, :, None, None] * incoming[None]
    prompt_ids = jnp.arange(PROMPTS, dtype=jnp.int32)
    last_index = (
        jnp.sum((token_prompt[None, :] <= prompt_ids[:, None]).astype(jnp.int32), axis=1) - 1
    )
    start_pos = (dp_index * blocks + jnp.arange(blocks, dtype=jnp.int32)) * BLOCK
    y_inter = jax.vmap(block_inter)(c_conv, prefix, id_blocks, before_ids, block_in)

    def collect(table, item):
        xb, bb, sb, pb, ib, fb, stb, ob = item
        return (block_last(last_index, table, xb, bb, sb, pb, ib, fb, stb, ob), None)

    empty_table = jnp.zeros((PROMPTS, heads_dev, head_dim, state_width), jnp.float32)
    local_table, unused = lax.scan(
        collect,
        empty_table,
        (x_heads, b_conv, step_blocks, prefix, id_blocks, before_ids, block_in, start_pos),
    )
    ssd_out = (y_intra + y_inter).reshape(tok_dev, heads_dev, head_dim) + skip_gain[
        None, :, None
    ] * conv_inner.astype(jnp.float32).reshape(tok_dev, heads_dev, head_dim)
    gated = ssd_out.reshape(tok_dev, inner_dev) * jax.nn.silu(gate_z.astype(jnp.float32))
    square_sum = lax.psum(jnp.sum(gated * gated, axis=1), "head")
    scale = lax.rsqrt(square_sum / (inner_dev * head_count) + EPSILON)
    normed_out = (gated * scale[:, None] * out_gain).astype(jnp.bfloat16)
    out_rows = tok_dev // head_count
    own_rows = lax.dynamic_slice_in_dim(hidden_f, head_index * out_rows, out_rows, 0)
    mixed = lax.psum_scatter(
        jnp.dot(normed_out, w_out, preferred_element_type=jnp.float32),
        "head",
        scatter_dimension=0,
        tiled=True,
    )
    layer_out = (own_rows + mixed).astype(jnp.bfloat16)
    table = lax.psum(local_table, "dp")
    one_hot = (request_prompt[:, None] == prompt_ids[None, :]).astype(jnp.float32)
    request_states = jnp.einsum("rg,ghpn->rhpn", one_hot, table, precision=lax.Precision.HIGHEST)
    return (layer_out, request_states)


LANES = 128
TILE_ROWS = 16
NEVER = -1e30
Y_NEAR, Z_NEAR, Z_FAR = 1, 2, 4
PASSED = (Z_FAR, Y_NEAR | Z_FAR)
STAYING = (0, Y_NEAR)
LITTLE = pl.CostEstimate(flops=1000, bytes_accessed=1000, transcendentals=0)


def kernel_params(mebibytes):
    return pltpu.CompilerParams(vmem_limit_bytes=mebibytes << 20)


def in_vmem(count):
    return [pl.BlockSpec(memory_space=pltpu.VMEM)] * count


def exchange(values, axis, bits):
    return lax.ppermute(values, axis, [(i, i ^ bits) for i in range(lax.axis_size(axis))])


def dot32(a, b, a_dim=1, b_dim=0):
    return lax.dot_general(
        a, b, (((a_dim,), (b_dim,)), ((), ())), preferred_element_type=jnp.float32
    )


def silu_tanh(values):
    half = 0.5 * values
    return half + half * jnp.tanh(half)


def widen(columns, pair, head_dim):
    rows = columns.shape[0]
    lane = lax.broadcasted_iota(jnp.int32, (rows, LANES), 1)
    first = jnp.broadcast_to(columns[:, 2 * pair : 2 * pair + 1], (rows, LANES))
    second = jnp.broadcast_to(columns[:, 2 * pair + 1 : 2 * pair + 2], (rows, LANES))
    return jnp.where(lane < head_dim, first, second)


def pack_first_kernel(
    req_ref, wbc_ref, wdt_ref, hidden_ref, first_ref, req_v, bc_v, dt_v, tail_v, dt_wide, sems
):
    rows, width = bc_v.shape
    tok, model = hidden_ref.shape
    arrivals = [
        pltpu.make_async_copy(source, target, sems.at[k])
        for k, (source, target) in enumerate(
            (
                (req_ref, req_v),
                (wdt_ref, dt_v),
                (hidden_ref.at[tok - TILE_ROWS : tok], tail_v),
                (wbc_ref, bc_v),
            )
        )
    ]
    for copy in arrivals:
        copy.start()
    dt_wide[...] = jnp.zeros_like(dt_wide)
    arrivals[0].wait()
    dt_wide[0:1, rows : rows + req_v.shape[1]] = req_v[...].astype(jnp.float32)
    arrivals[1].wait()
    dt_wide[0 : dt_v.shape[0], 0:rows] = dt_v[...]
    arrivals[2].wait()
    upper = lax.broadcasted_iota(jnp.int32, (TILE_ROWS, model), 0) < TILE_ROWS // 2
    below = jnp.where(upper, dt_wide[...], tail_v[...].astype(jnp.float32)).astype(jnp.bfloat16)
    for i in range(model // width):
        at = rows + TILE_ROWS * i
        first_ref[at : at + TILE_ROWS, :] = below[:, i * width : (i + 1) * width]
    arrivals[3].wait()
    first_ref[0:rows, :] = bc_v[...].astype(jnp.bfloat16)


def pack_rest_kernel(wzx_ref, x_ref, gate_ref, tiles_ref, sems):
    rows, inner = x_ref.shape
    arrivals = [
        pltpu.make_async_copy(
            wzx_ref.at[:, :, j * LANES : (j + 1) * LANES], tiles_ref.at[j], sems.at[j]
        )
        for j in range(inner // LANES)
    ]
    for copy in arrivals:
        copy.start()
    for j, copy in enumerate(arrivals):
        copy.wait()
        own = slice(j * LANES, (j + 1) * LANES)
        pair = tiles_ref.at[j].reshape(2 * rows, LANES)
        x_ref[:, own] = pair[pl.ds(1, rows, stride=2), :].astype(jnp.bfloat16)
        gate_ref[:, own] = pair[pl.ds(0, rows, stride=2), :].astype(jnp.bfloat16)


def facts_kernel(
    ids_ref,
    hidden_hbm,
    gain_ref,
    normed_ref,
    meta_ref,
    order_ref,
    pen_ref,
    rows_ref,
    hidden_ref,
    sem,
):
    tok = hidden_ref.shape[0]
    arrival = pltpu.make_async_copy(hidden_hbm, hidden_ref, sem)
    arrival.start()
    position = lax.axis_index("dp")
    start = pl.multiple_of(position * tok, tok)
    ids_i = ids_ref[:, pl.ds(start, tok)]
    behind = pl.multiple_of(jnp.maximum(start - LANES, 0), LANES)
    edge = ids_ref[:, pl.ds(behind, LANES)]
    edge = jnp.where(position > 0, edge, -1)
    ahead = pl.multiple_of(jnp.minimum(start + tok, ids_ref.shape[1] - LANES), LANES)
    after = jnp.where(start + tok < ids_ref.shape[1], ids_ref[:, pl.ds(ahead, LANES)], -1)
    after = after[:, 0:1].astype(jnp.float32)
    long = jnp.concatenate([edge, ids_i], axis=1).astype(jnp.float32)
    ids = ids_i.astype(jnp.float32)
    index = lax.broadcasted_iota(jnp.int32, (1, tok), 1)
    before, last = long[:, LANES - 1 : LANES], ids[:, tok - 1 : tok]
    middle = ids[:, BLOCK - 1 : BLOCK]
    one, zero = jnp.ones((1, tok), jnp.float32), jnp.zeros((1, tok), jnp.float32)
    flag = lambda what: jnp.where(what, one, zero)
    rows = [flag(ids == pltpu.roll(long, k, 1)[:, LANES:]) for k in (1, 2, 3)]
    rows.append(flag(ids == before))
    rows.append(flag((ids == middle) & (index >= BLOCK)))
    rows.append(flag((ids == middle) & (index < BLOCK)))
    rows.append(ids)
    rows.append(flag(ids == last))
    rows.append(flag((ids != last) | (after != last)))
    rows = jnp.concatenate(rows + [jnp.zeros((LANES - len(rows), tok), jnp.float32)], axis=0)
    facts = rows.T
    meta_ref[...] = facts
    column = facts[:, 6:7]
    here = lax.broadcasted_iota(jnp.int32, (tok, tok), 0)
    there = lax.broadcasted_iota(jnp.int32, (tok, tok), 1)
    same = column == ids
    order_ref[0:tok, :] = jnp.where(there <= here, 1.0, 0.0).astype(jnp.bfloat16)
    order_ref[tok:, :] = jnp.where((there > here) & same, 1.0, 0.0).astype(jnp.bfloat16)
    pen = jnp.where((there <= here) & same, 0.0, NEVER)
    for b in range(tok // BLOCK):
        own = slice(b * BLOCK, (b + 1) * BLOCK)
        pen_ref[b] = pen[own, own]
    arrival.wait()
    part = rows_ref.shape[0]
    at = pl.multiple_of(lax.axis_index("head") * part, part)
    rows_ref[...] = hidden_ref[pl.ds(at, part), :]
    hidden = hidden_ref[...].astype(jnp.float32)
    normed_ref[...] = (hidden * rms_scale(hidden) * gain_ref[...]).astype(jnp.bfloat16)


def scale_kernel(w_ref, gain_ref, whole_ref, part_ref):
    rows, model = w_ref.shape
    width = part_ref.shape[1]
    gain = jnp.broadcast_to(gain_ref[...], (LANES, rows)).T
    for j in range(model // LANES):
        own = slice(j * LANES, (j + 1) * LANES)
        whole_ref[:, own] = (w_ref[:, own].astype(jnp.float32) * gain).astype(jnp.bfloat16)
    at = pl.multiple_of((lax.axis_index("dp") % 2) * width, LANES)
    part_ref[...] = whole_ref[:, pl.ds(at, width)]


def gather_rows(position, buffers, rows, w_ref, sems):
    copies = []
    for j, buffer in enumerate(buffers):
        at = pl.multiple_of(jnp.bitwise_xor(position, j) * rows, rows)
        copies.append(
            pltpu.make_async_copy(buffer.at[0:rows], w_ref.at[pl.ds(at, rows)], sems.at[j])
        )
    return copies


def project_rows(normed, halo, w, ext_ref, at, stop):
    ext_ref[0:TILE_ROWS, at:stop] = dot32(halo, w)
    ext_ref[TILE_ROWS:, at:stop] = dot32(normed, w)


def convolve(ext_ref, own, taps, same):
    tok = same[0].shape[0]
    total = ext_ref[TILE_ROWS : TILE_ROWS + tok, own] * taps[3:4]
    for k in range(1, 4):
        total = total + same[k - 1] * (
            ext_ref[TILE_ROWS - k : TILE_ROWS - k + tok, own] * taps[3 - k : 4 - k]
        )
    return silu_tanh(total)


def below_rows(buffer, rows):
    count = (buffer.shape[0] - rows) // TILE_ROWS
    return jnp.concatenate(
        [buffer[rows + i * TILE_ROWS : rows + (i + 1) * TILE_ROWS, :] for i in range(count)], axis=1
    )


def project_shard(normed_ref, buffer, j, steps, dtw_ref):
    rows = dtw_ref.shape[1]
    at = pl.multiple_of(jnp.bitwise_xor(lax.axis_index("dp"), j) * rows, LANES)
    normed = normed_ref[:, pl.ds(at, rows)]
    row = lax.broadcasted_iota(jnp.int32, (TILE_ROWS, rows), 0)
    below = below_rows(buffer, rows)[:, 0:rows].astype(jnp.float32)
    dtw_ref[0:TILE_ROWS, :] = jnp.where(row < steps, below, 0.0).astype(jnp.bfloat16)
    return dot32(normed, buffer[0:rows, :]), dot32(normed, dtw_ref[...], 1, 1)


def first_most_kernel(steps, normed_ref, own_ref, near_ref, most_ref, raw_ref, dtw_ref):
    dtw_ref[...] = jnp.zeros_like(dtw_ref)
    most, raw = project_shard(normed_ref, own_ref, 0, steps, dtw_ref)
    more, more_raw = project_shard(normed_ref, near_ref, 1, steps, dtw_ref)
    most_ref[...] = most + more
    raw_ref[...] = raw + more_raw


def first_kernel(
    normed_ref,
    most_ref,
    most_raw_ref,
    own_ref,
    near_ref,
    far_ref,
    last_ref,
    gain_ref,
    taps_ref,
    meta_ref,
    order_ref,
    bias_ref,
    decay_ref,
    bc_ref,
    step_ref,
    prefix_ref,
    fade_ref,
    halo_ref,
    halo_rows_ref,
    dtw_ref,
    ext_ref,
):
    position = lax.axis_index("dp")
    tok, model = normed_ref.shape
    width = bc_ref.shape[1]
    rows = dtw_ref.shape[1]
    buffers = (own_ref, near_ref, far_ref, last_ref)
    for j, buffer in enumerate(buffers):
        halo_rows_ref[jnp.bitwise_xor(position, j)] = below_rows(buffer, rows)
    halo = halo_rows_ref[jnp.maximum(position - 1, 0)].astype(jnp.float32)
    halo_ref[...] = (halo * rms_scale(halo) * gain_ref[...]).astype(jnp.bfloat16)
    halo_sum = 0.0
    for j, buffer in enumerate(buffers):
        at = pl.multiple_of(jnp.bitwise_xor(position, j) * rows, LANES)
        halo_sum = halo_sum + dot32(halo_ref[:, pl.ds(at, rows)], buffer[0:rows, :])
    ext_ref[0:TILE_ROWS, :] = halo_sum
    dtw_ref[...] = jnp.zeros_like(dtw_ref)
    steps = bias_ref.shape[0]
    most, raw = project_shard(normed_ref, far_ref, 2, steps, dtw_ref)
    more, more_raw = project_shard(normed_ref, last_ref, 3, steps, dtw_ref)
    ext_ref[TILE_ROWS:, :] = most_ref[...] + most + more
    head_lane = lax.broadcasted_iota(jnp.int32, (1, LANES), 1)
    bias = jnp.zeros((1, LANES), jnp.float32)
    decay = jnp.zeros((1, LANES), jnp.float32)
    for h in range(steps):
        bias = jnp.where(head_lane == h, bias_ref[h], bias)
        decay = jnp.where(head_lane == h, decay_ref[h], decay)
    raw = most_raw_ref[...] + raw + more_raw + bias
    step = jnp.maximum(raw, 0.0) + jnp.log1p(jnp.exp(-jnp.abs(raw)))
    step_ref[...] = step
    lane = lax.broadcasted_iota(jnp.int32, (tok, LANES), 1)
    rate = jnp.where(lane < TILE_ROWS, -step * jnp.exp(decay), 0.0)
    high = rate.astype(jnp.bfloat16).astype(jnp.float32)
    rest = rate - high
    mid = rest.astype(jnp.bfloat16).astype(jnp.float32)
    low = rest - mid
    packed = high + pltpu.roll(mid, TILE_ROWS, 1) + pltpu.roll(low, 2 * TILE_ROWS, 1)
    sums = dot32(order_ref[...], packed.astype(jnp.bfloat16))
    sums = (
        sums
        + pltpu.roll(sums, LANES - TILE_ROWS, 1)
        + pltpu.roll(sums, LANES - 2 * TILE_ROWS, 1)
    )
    prefix_ref[...] = sums[0:tok]
    fade_ref[...] = jnp.exp(sums[tok : 2 * tok])
    same = [jnp.broadcast_to(meta_ref[:, k : k + 1], (tok, LANES)) for k in range(3)]
    for j in range(width // LANES):
        own = slice(j * LANES, (j + 1) * LANES)
        bc_ref[:, own] = convolve(ext_ref, own, taps_ref[:, own], same).astype(jnp.bfloat16)


def inner_kernel(
    normed_ref,
    own_ref,
    near_ref,
    far_ref,
    last_ref,
    halo_ref,
    taps_ref,
    meta_ref,
    bc_ref,
    step_ref,
    fade_ref,
    x_ref,
    stepx_ref,
    faded_ref,
    leaving_ref,
    w_ref,
    ext_ref,
    sems,
):
    position = lax.axis_index("dp")
    tok = normed_ref.shape[0]
    inner = x_ref.shape[1]
    rows = own_ref.shape[0]
    head_dim = LANES // 2
    copies = gather_rows(position, (own_ref, near_ref, far_ref, last_ref), rows, w_ref, sems)
    for copy in copies:
        copy.start()
    state_width = leaving_ref.shape[1]
    step = step_ref[...]
    fade = fade_ref[...]
    b_all = bc_ref[:, 0:state_width].astype(jnp.float32)
    b_leaving = (b_all * meta_ref[:, 7:8]).astype(jnp.bfloat16)
    same = [jnp.broadcast_to(meta_ref[:, k : k + 1], (tok, LANES)) for k in range(3)]
    for copy in copies:
        copy.wait()
    project_rows(normed_ref[...], halo_ref[...], w_ref[...], ext_ref, 0, inner)
    for q in range(inner // LANES):
        own = slice(q * LANES, (q + 1) * LANES)
        rounded = convolve(ext_ref, own, taps_ref[:, own], same).astype(jnp.bfloat16)
        x_ref[:, own] = rounded
        scaled = rounded.astype(jnp.float32) * widen(step, q, head_dim)
        stepx_ref[:, own] = scaled.astype(jnp.bfloat16)
        faded = (scaled * widen(fade, q, head_dim)).astype(jnp.bfloat16).T
        faded_ref[own, :] = faded
        leaving_ref[own, :] = dot32(faded, b_leaving).astype(jnp.bfloat16)


def before_device(ids_ref, position, tok):
    return jnp.where(position > 0, ids_ref[jnp.maximum(position * tok - 1, 0)], -1)


def table_kernel(ids_ref, bc_ref, faded_ref, meta_ref, prefix_ref, enter_ref, *table_refs):
    rows, state_width = table_refs[0].shape[1:]
    head_dim = LANES // 2
    tok = bc_ref.shape[0]
    b_all = bc_ref[:, 0:state_width].astype(jnp.float32)
    owner = jnp.where(meta_ref[:, 8:9] > 0.0, meta_ref[:, 6:7], -1.0)
    owner = jnp.broadcast_to(owner, (tok, state_width))
    for g in range(0, table_refs[0].shape[0], 2):
        pair = [jnp.where(owner == g + k, b_all, 0.0).astype(jnp.bfloat16) for k in range(2)]
        sums = dot32(faded_ref[...], jnp.concatenate(pair, axis=1)).astype(jnp.bfloat16)
        for n, table_ref in enumerate(table_refs):
            for k in range(2):
                table_ref[g + k] = sums[
                    n * rows : (n + 1) * rows, k * state_width : (k + 1) * state_width
                ]
    position = lax.axis_index("dp")
    before = before_device(ids_ref, position, tok)
    stop = (position + 1) * tok
    after = ids_ref[jnp.minimum(stop, ids_ref.shape[0] - 1)]
    goes_on = (after == before) & (stop < ids_ref.shape[0])
    ended = (ids_ref[position * tok] == before) & ((ids_ref[stop - 1] != before) | ~goes_on)

    @pl.when(ended)
    def add():
        inside = jnp.where(meta_ref[:, 3:4] > 0.0, prefix_ref[...], 0.0)
        gain = jnp.exp(jnp.min(inside, axis=0, keepdims=True))
        chunk = head_dim // 2
        for n in range(faded_ref.shape[0] // chunk):
            table_ref = table_refs[n * chunk // rows]
            own = slice(n * chunk % rows, n * chunk % rows + chunk)
            h = n * chunk // head_dim
            entering = enter_ref[n * chunk : (n + 1) * chunk, :].astype(jnp.float32)
            old = table_ref[before, own, :].astype(jnp.float32)
            table_ref[before, own, :] = (old + gain[:, h : h + 1] * entering).astype(jnp.bfloat16)


def local_kernel(
    x_ref,
    bc_ref,
    stepx_ref,
    prefix_ref,
    meta_ref,
    pen_ref,
    skip_ref,
    y_ref,
):
    inner = y_ref.shape[1]
    state_width = bc_ref.shape[1] // 2
    head_dim = LANES // 2
    tok = y_ref.shape[0]
    lane = lax.broadcasted_iota(jnp.int32, (BLOCK, LANES), 1)
    half = BLOCK // 2
    for b in range(tok // BLOCK):
        own_rows = slice(b * BLOCK, (b + 1) * BLOCK)
        b_blk = bc_ref[own_rows, 0:state_width]
        c_blk = bc_ref[own_rows, state_width:]
        scores = dot32(c_blk, b_blk, 1, 1)
        pen = pen_ref[b]
        prefix = prefix_ref[own_rows, :]
        across = prefix.T
        if b > 0:
            carried = jnp.exp(prefix - prefix_ref[b * BLOCK - 1 : b * BLOCK, :])
            carried = carried * meta_ref[own_rows, 4:5]
            before_rows = slice((b - 1) * BLOCK, b * BLOCK)
            before = prefix_ref[before_rows, :]
            fade = jnp.exp(before[BLOCK - 1 : BLOCK, :] - before)
            b_before = bc_ref[before_rows, 0:state_width].astype(jnp.float32)
            b_before = (b_before * meta_ref[before_rows, 5:6]).astype(jnp.bfloat16)
        for q in range(inner // LANES):
            own = slice(q * LANES, (q + 1) * LANES)
            x_pair = x_ref[own_rows, own].astype(jnp.float32)
            out = x_pair * jnp.where(lane < head_dim, skip_ref[2 * q], skip_ref[2 * q + 1])
            if b > 0:
                faded = stepx_ref[before_rows, own].astype(jnp.float32) * widen(fade, q, head_dim)
                middle = dot32(faded.astype(jnp.bfloat16).T, b_before).astype(jnp.bfloat16)
                out = out + widen(carried, q, head_dim) * dot32(c_blk, middle, 1, 1)
            sx = stepx_ref[own_rows, own].astype(jnp.float32)
            sides = [jnp.where(lane < head_dim, sx, 0.0), jnp.where(lane >= head_dim, sx, 0.0)]
            sides = [side.astype(jnp.bfloat16) for side in sides]
            for rows, seen in ((slice(0, half), half), (slice(half, BLOCK), BLOCK)):
                part = out[rows]
                for side in range(2):
                    h = 2 * q + side
                    gaps = prefix[rows, h : h + 1] - across[h : h + 1, 0:seen] + pen[rows, 0:seen]
                    mixing = (scores[rows, 0:seen] * jnp.exp(gaps)).astype(jnp.bfloat16)
                    part = part + dot32(mixing, sides[side][0:seen])
                y_ref[b * BLOCK + rows.start : b * BLOCK + rows.stop, own] = part


def z_most_kernel(normed_ref, own_ref, near_ref, far_ref, most_ref):
    position = lax.axis_index("dp")
    rows = own_ref.shape[0]
    total = 0.0
    for j, w_ref in enumerate((own_ref, near_ref, far_ref)):
        at = pl.multiple_of(jnp.bitwise_xor(position, j) * rows, LANES)
        total = total + dot32(normed_ref[:, pl.ds(at, rows)], w_ref[...])
    most_ref[...] = total


def z_last_kernel(normed_ref, last_ref, most_ref, gate_ref):
    rows = last_ref.shape[0]
    at = pl.multiple_of(jnp.bitwise_xor(lax.axis_index("dp"), 3) * rows, LANES)
    gate_ref[...] = silu_tanh(most_ref[...] + dot32(normed_ref[:, pl.ds(at, rows)], last_ref[...]))


def gate_kernel(enter_ref, bc_ref, prefix_ref, meta_ref, y_ref, z_ref, arrived_ref, *outs):
    scratch = outs[-1]
    inner = y_ref.shape[1]
    state_width = enter_ref.shape[1]
    head_dim = LANES // 2
    c_all = bc_ref[:, state_width:]
    inter = dot32(c_all, enter_ref[...], 1, 1)
    carried = jnp.exp(prefix_ref[...]) * meta_ref[:, 3:4]
    for q in range(inner // LANES):
        own = slice(q * LANES, (q + 1) * LANES)
        value = y_ref[:, own] + widen(carried, q, head_dim) * inter[:, own]
        scratch[:, own] = (value * z_ref[:, own]).astype(jnp.bfloat16)
    head = lax.axis_index("head")
    part = outs[0].shape[0] // 2
    for n, related in enumerate((PASSED, STAYING)):
        for out, owner in zip(outs[2 * n : 2 * n + 2], (head, jnp.bitwise_xor(head, Z_NEAR))):
            for k, bits in enumerate(related):
                at = pl.multiple_of(jnp.bitwise_xor(owner, bits) * part, part)
                out[k * part : (k + 1) * part, :] = scratch[pl.ds(at, part), :]


def pick_kernel(own_ref, far_ref, *refs):
    tables, others, (keep_ref, send_ref, send_last_ref, far_v, sem) = refs[:4], refs[4:8], refs[8:]
    count = keep_ref.shape[0]
    part = tables[0].shape[1]
    rows = far_ref.shape[0] - 6 * TILE_ROWS
    width = far_ref.shape[1]
    model_rows = rows // width
    at = rows + TILE_ROWS * model_rows
    lanes = rows - model_rows * width
    arrival = pltpu.make_async_copy(
        far_ref.at[at : at + TILE_ROWS, lanes : lanes + LANES], far_v, sem
    )
    arrival.start()

    def pick(k, g):
        total = tables[k][g].astype(jnp.float32) + others[k][g].astype(jnp.float32)
        return total.astype(jnp.bfloat16)

    for r in range(count):
        for k in range(len(tables)):
            keep_ref[r, k * part : (k + 1) * part] = pick(k, own_ref[r])
    arrival.wait()
    wanted = far_v[...].astype(jnp.float32)[0:1, :]
    lane = lax.broadcasted_iota(jnp.int32, (1, LANES), 1)
    for r in range(count):
        g = jnp.sum(jnp.where(lane == r, wanted, 0.0)).astype(jnp.int32)
        for k in range(len(tables) - 1):
            send_ref[r, k * part : (k + 1) * part] = pick(k, g)
        send_last_ref[r] = pick(len(tables) - 1, g)


def split_squares(squares):
    lane = lax.broadcasted_iota(jnp.int32, (squares.shape[0], LANES), 1)
    high = squares.astype(jnp.bfloat16).astype(jnp.float32)
    return jnp.where(lane == 0, high, squares - high).astype(jnp.bfloat16)


def joined_squares(ref, model):
    high = ref[:, model : model + 1].astype(jnp.float32)
    return high + ref[:, model + 1 : model + 2].astype(jnp.float32)


def out_kernel(kept_ref, got_ref, own_ref, part_ref, near_ref, wide_out, *refs):
    outs, sums_ref = refs[:-1], refs[-1]
    core = lax.axis_index("dp") % 2
    width = part_ref.shape[1]
    rows, model = sums_ref.shape
    part = wide_out.shape[0]
    kept, got = kept_ref[...], got_ref[...]
    squares = jnp.zeros((rows, 1), jnp.float32)
    for value in (kept, got):
        wide = value.astype(jnp.float32)
        squares = squares + jnp.sum(wide * wide, axis=1, keepdims=True)
    for j, other_ref in enumerate((part_ref, near_ref)):
        at = pl.multiple_of(jnp.bitwise_xor(core, j) * width, LANES)
        own = dot32(kept, own_ref[:, pl.ds(at, width)])
        sums_ref[:, pl.ds(at, width)] = own + dot32(got, other_ref[...])
    wide_out[:, 0:model] = sums_ref[0:part, :]
    wide_out[:, model:] = jnp.broadcast_to(squares[0:part], (part, LANES))
    size = part // len(outs)
    for k, out in enumerate(outs):
        own = slice(part + k * size, part + (k + 1) * size)
        out[:, 0:model] = sums_ref[own, :].astype(jnp.bfloat16)
        out[:, model:] = split_squares(squares[own])


def pass_kernel(pass_ref, cross_ref, arrived_ref, out_ref):
    model = out_ref.shape[1] - LANES
    total = pass_ref[:, 0:model] + cross_ref[:, 0:model].astype(jnp.float32)
    out_ref[:, 0:model] = total.astype(jnp.bfloat16)
    squares = pass_ref[:, model : model + 1] + joined_squares(cross_ref, model)
    out_ref[:, model:] = split_squares(squares)


def finish_kernel(inner_total, hidden_ref, joined_ref, keep_ref, passed_ref, *refs):
    nears, out_ref = refs[:-1], refs[-1]
    model = hidden_ref.shape[1]
    size = nears[0].shape[0]
    for k, near_ref in enumerate(nears):
        own = slice(k * size, (k + 1) * size)
        squares = keep_ref[own, model : model + 1] + joined_squares(near_ref, model)
        squares = squares + joined_squares(passed_ref.at[own], model)
        scale = lax.rsqrt(squares / inner_total + EPSILON)
        total = keep_ref[own, 0:model] + near_ref[:, 0:model].astype(jnp.float32)
        total = total + passed_ref[own, 0:model].astype(jnp.float32)
        hidden = hidden_ref[own, :].astype(jnp.float32)
        out_ref[own, :] = (hidden + scale * total).astype(jnp.bfloat16)


def join_kernel(keep_ref, *refs):
    fars, (out_ref, done_ref) = refs[:-2], refs[-2:]
    done_ref[...] = jnp.zeros_like(done_ref)
    at = 0
    for far_ref in fars:
        own = slice(at, at + far_ref.shape[1])
        out_ref[:, own] = keep_ref[:, own].astype(jnp.float32) + far_ref[...].astype(jnp.float32)
        at += far_ref.shape[1]


def fused_on_device(
    hidden,
    token_prompt,
    request_prompt,
    in_gain,
    w_zx,
    w_bc,
    w_dt,
    dt_bias,
    a_log,
    conv_x,
    conv_bc,
    skip_gain,
    out_gain,
    w_out,
):
    tok, model = hidden.shape
    rows = w_zx.shape[0]
    inner = w_zx.shape[2]
    heads = w_dt.shape[1]
    state_width = w_bc.shape[1] // 2
    tiles = inner // LANES
    peers = lax.axis_size("dp")
    head_count = lax.axis_size("head")
    bf16, f32 = jnp.bfloat16, jnp.float32
    shape = jax.ShapeDtypeStruct
    smem = pl.BlockSpec(memory_space=pltpu.SMEM)
    anywhere = pl.BlockSpec(memory_space=pl.ANY)
    in_hbm = pl.BlockSpec(memory_space=pltpu.HBM)

    extra = TILE_ROWS * (model // (2 * state_width))
    first_own = pl.pallas_call(
        pack_first_kernel,
        name="pack_first_weights",
        out_shape=shape((rows + extra, 2 * state_width), bf16),
        in_specs=[in_hbm] * 4,
        out_specs=in_vmem(1)[0],
        scratch_shapes=[
            pltpu.VMEM((1, request_prompt.shape[0]), jnp.int32),
            pltpu.VMEM(w_bc.shape, f32),
            pltpu.VMEM((heads, rows), f32),
            pltpu.VMEM((TILE_ROWS, model), bf16),
            pltpu.VMEM((TILE_ROWS, model), f32),
            pltpu.SemaphoreType.DMA((4,)),
        ],
        compiler_params=kernel_params(60),
        cost_estimate=LITTLE,
    )(request_prompt[None, :], w_bc, w_dt.T, hidden)
    first_far = exchange(first_own, "dp", 2)
    first_near = exchange(first_own, "dp", 1)
    x_own, gate_own = pl.pallas_call(
        pack_rest_kernel,
        name="pack_x_and_gate_weights",
        out_shape=(shape((rows, inner), bf16), shape((rows, inner), bf16)),
        in_specs=[in_hbm],
        out_specs=tuple(in_vmem(2)),
        scratch_shapes=[
            pltpu.VMEM((inner // LANES, rows, 2, LANES), f32),
            pltpu.SemaphoreType.DMA((inner // LANES,)),
        ],
        compiler_params=kernel_params(8),
        cost_estimate=LITTLE,
    )(w_zx)

    blocks = tok // BLOCK
    normed, meta, order, pen, own_hidden = pl.pallas_call(
        facts_kernel,
        name="norm_and_token_facts",
        out_shape=(
            shape((tok, model), bf16),
            shape((tok, LANES), f32),
            shape((2 * tok, tok), bf16),
            shape((blocks, BLOCK, BLOCK), f32),
            shape((tok // head_count, model), bf16),
        ),
        in_specs=in_vmem(1) + [in_hbm] + in_vmem(1),
        out_specs=tuple(in_vmem(5)),
        scratch_shapes=[pltpu.VMEM((tok, model), bf16), pltpu.SemaphoreType.DMA],
        compiler_params=kernel_params(16),
        cost_estimate=LITTLE,
    )(token_prompt[None, :], hidden, in_gain[None, :])
    scaled_out, half_out = pl.pallas_call(
        scale_kernel,
        name="scale_out_rows",
        out_shape=(shape(w_out.shape, bf16), shape((inner, model // 2), bf16)),
        in_specs=in_vmem(2),
        out_specs=tuple(in_vmem(2)),
        compiler_params=kernel_params(8),
        cost_estimate=LITTLE,
    )(w_out, out_gain[None, :])
    out_part = exchange(half_out, "head", Z_NEAR)
    out_near = exchange(out_part, "dp", 1)

    x_far = exchange(x_own, "dp", 2)
    first_most, first_raw = pl.pallas_call(
        functools.partial(first_most_kernel, heads),
        name="project_b_c_and_steps_of_chip",
        out_shape=(shape((tok, 2 * state_width), f32), shape((tok, LANES), f32)),
        in_specs=in_vmem(3),
        out_specs=tuple(in_vmem(2)),
        scratch_shapes=[pltpu.VMEM((LANES, rows), bf16)],
        compiler_params=kernel_params(8),
        cost_estimate=LITTLE,
    )(normed, first_own, first_near)
    first_far, first_most, first_raw, meta, order, pen, x_own, gate_own = lax.optimization_barrier(
        (first_far, first_most, first_raw, meta, order, pen, x_own, gate_own)
    )
    x_near = exchange(x_own, "dp", 1)
    gate_near = exchange(gate_own, "dp", 1)
    first_last = exchange(first_far, "dp", 1)
    bc, step, prefix, fade, halo = pl.pallas_call(
        first_kernel,
        name="project_b_c_and_steps",
        out_shape=(
            shape((tok, 2 * state_width), bf16),
            shape((tok, LANES), f32),
            shape((tok, LANES), f32),
            shape((tok, LANES), f32),
            shape((TILE_ROWS, model), bf16),
        ),
        in_specs=in_vmem(11) + [smem] * 2,
        out_specs=tuple(in_vmem(5)),
        scratch_shapes=[
            pltpu.VMEM((peers, TILE_ROWS, model), bf16),
            pltpu.VMEM((LANES, rows), bf16),
            pltpu.VMEM((TILE_ROWS + tok, 2 * state_width), f32),
        ],
        compiler_params=kernel_params(14),
        cost_estimate=LITTLE,
    )(
        normed,
        first_most,
        first_raw,
        first_own,
        first_near,
        first_far,
        first_last,
        in_gain[None, :],
        conv_bc,
        meta,
        order,
        dt_bias,
        a_log,
    )
    x_far, gate_own, bc, step, prefix, fade, halo = lax.optimization_barrier(
        (x_far, gate_own, bc, step, prefix, fade, halo)
    )
    x_last = exchange(x_far, "dp", 1)
    gate_far = exchange(gate_own, "dp", 2)
    x, stepx, faded, leaving = pl.pallas_call(
        inner_kernel,
        name="project_and_convolve_x",
        out_shape=(
            shape((tok, inner), bf16),
            shape((tok, inner), bf16),
            shape((inner, tok), bf16),
            shape((inner, state_width), bf16),
        ),
        in_specs=in_vmem(1) + [anywhere] * 4 + in_vmem(6),
        out_specs=tuple(in_vmem(4)),
        scratch_shapes=[
            pltpu.VMEM((model, inner), bf16),
            pltpu.VMEM((TILE_ROWS + tok, inner), f32),
            pltpu.SemaphoreType.DMA((peers,)),
        ],
        compiler_params=kernel_params(14),
        cost_estimate=LITTLE,
    )(
        normed,
        x_own,
        x_near,
        x_far,
        x_last,
        halo,
        conv_x,
        meta,
        bc,
        step,
        fade,
    )

    entering = lax.ppermute(leaving, "dp", [(i, i + 1) for i in range(peers - 1)])

    y_local = pl.pallas_call(
        local_kernel,
        name="mix_within_blocks",
        out_shape=shape((tok, inner), f32),
        in_specs=in_vmem(6) + [smem],
        out_specs=in_vmem(1)[0],
        compiler_params=kernel_params(14),
        cost_estimate=LITTLE,
    )(x, bc, stepx, prefix, meta, pen, skip_gain)
    gate_far, gate_near, entering, y_local = lax.optimization_barrier(
        (gate_far, gate_near, entering, y_local)
    )
    gate_last = exchange(gate_far, "dp", 1)
    tables = pl.pallas_call(
        table_kernel,
        name="sum_ended_states",
        out_shape=(shape((PROMPTS, inner // 4, state_width), bf16),) * 4,
        in_specs=[smem] + in_vmem(5),
        out_specs=tuple(in_vmem(4)),
        compiler_params=kernel_params(8),
        cost_estimate=LITTLE,
    )(token_prompt, bc, faded, meta, prefix, entering)
    tables_near = [exchange(table, "dp", 1) for table in tables]

    gate_most = pl.pallas_call(
        z_most_kernel,
        name="project_gate_most",
        out_shape=shape((tok, inner), f32),
        in_specs=in_vmem(4),
        out_specs=in_vmem(1)[0],
        compiler_params=kernel_params(8),
        cost_estimate=LITTLE,
    )(normed, gate_own, gate_near, gate_far)
    gate = pl.pallas_call(
        z_last_kernel,
        name="project_gate_last",
        out_shape=shape((tok, inner), f32),
        in_specs=in_vmem(3),
        out_specs=in_vmem(1)[0],
        compiler_params=kernel_params(8),
        cost_estimate=LITTLE,
    )(normed, gate_last, gate_most)

    out_rows = tok // head_count
    kept_first, sent_first, kept_rest, sent_rest = pl.pallas_call(
        gate_kernel,
        name="add_entering_and_gate",
        out_shape=(shape((2 * out_rows, inner), bf16),) * 4,
        in_specs=in_vmem(6) + [anywhere],
        out_specs=tuple(in_vmem(4)),
        scratch_shapes=[pltpu.VMEM((tok, inner), bf16)],
        compiler_params=kernel_params(8),
        cost_estimate=LITTLE,
    )(entering, bc, prefix, meta, y_local, gate, out_near)
    got_first = exchange(sent_first, "head", Z_NEAR)
    got_rest = exchange(sent_rest, "head", Z_NEAR)

    requests = request_prompt.shape[0]
    part = inner // 4
    keep, *sends = pl.pallas_call(
        pick_kernel,
        name="pick_request_states",
        out_shape=tuple(
            shape((requests, size, state_width), bf16) for size in (inner, inner - part, part)
        ),
        in_specs=[smem, anywhere] + in_vmem(8),
        out_specs=tuple(in_vmem(3)),
        scratch_shapes=[pltpu.VMEM((TILE_ROWS, LANES), bf16), pltpu.SemaphoreType.DMA],
        compiler_params=kernel_params(8),
        cost_estimate=LITTLE,
    )(request_prompt, first_far, *tables, *tables_near)
    fars = [exchange(send, "dp", 2) for send in sends]

    sums_shape = (out_rows, model + LANES)

    def project(kept, got, pieces):
        piece = (out_rows // pieces, model + LANES)
        return pl.pallas_call(
            out_kernel,
            name="project_out",
            out_shape=(shape(sums_shape, f32),) + (shape(piece, bf16),) * pieces,
            in_specs=in_vmem(5),
            out_specs=tuple(in_vmem(1 + pieces)),
            scratch_shapes=[pltpu.VMEM((2 * out_rows, model), f32)],
            compiler_params=kernel_params(8),
            cost_estimate=LITTLE,
        )(kept, got, scaled_out, out_part, out_near)

    sums_pass, sums_cross = project(kept_first, got_first, 1)
    cross = exchange(sums_cross, "head", Y_NEAR)
    passed = pl.pallas_call(
        pass_kernel,
        name="add_sums_to_pass_on",
        out_shape=shape(sums_shape, bf16),
        in_specs=in_vmem(2) + [anywhere],
        out_specs=in_vmem(1)[0],
        compiler_params=kernel_params(4),
        cost_estimate=LITTLE,
    )(sums_pass, cross, got_rest)
    got_rest, passed = lax.optimization_barrier((got_rest, passed))
    passed = exchange(passed, "head", Z_FAR)
    sums_keep, *sums_near = project(kept_rest, got_rest, 2)
    sums_near = [exchange(part, "head", Y_NEAR) for part in sums_near]
    request_states, joined = pl.pallas_call(
        join_kernel,
        name="join_request_states",
        out_shape=(shape((requests, inner, state_width), f32), shape((8, LANES), f32)),
        in_specs=in_vmem(3),
        out_specs=tuple(in_vmem(2)),
        compiler_params=kernel_params(6),
        cost_estimate=LITTLE,
    )(keep, *fars)
    layer_out = pl.pallas_call(
        functools.partial(finish_kernel, inner * head_count),
        name="scale_and_add_hidden",
        out_shape=shape((out_rows, model), bf16),
        in_specs=in_vmem(1) + [anywhere] + in_vmem(4),
        out_specs=in_vmem(1)[0],
        compiler_params=kernel_params(4),
        cost_estimate=LITTLE,
    )(own_hidden, joined, sums_keep, passed, *sums_near)
    return (
        layer_out,
        request_states.reshape(requests, heads, inner // heads, state_width),
    )


def fits_fused(mesh):
    return dict(mesh.shape) == {"dp": 4, "head": 8}


def solution(mesh):
    in_specs = (
        P("dp", None),
        P(),
        P("dp"),
        P(),
        P("dp", None, "head"),
        P("dp", None),
        P("dp", "head"),
        P("head"),
        P("head"),
        P(None, "head"),
        P(),
        P("head"),
        P("head"),
        P("head", None),
    )
    out_specs = (P(("dp", "head"), None), P("dp", "head", None, None))
    program = fused_on_device if fits_fused(mesh) else on_device
    return jax.shard_map(
        program, mesh=mesh, in_specs=in_specs, out_specs=out_specs, check_vma=False
    )
```

```python
import functools

import jax
import jax.numpy as jnp
from jax import lax
from jax.experimental import pallas as pl
from jax.experimental.pallas import tpu as pltpu
from jax.sharding import PartitionSpec as P

BLOCK = 256
PROMPTS = 8


EPSILON = 1e-05


def from_behind(shard, axis, by):
    peers = lax.axis_size(axis)
    pairs = [(i, i + by) for i in range(peers) if 0 <= i + by < peers]
    return lax.ppermute(shard, axis, pairs)


def carried_in(shard, axis, combine, identity):
    peers, position = (lax.axis_size(axis), lax.axis_index(axis))
    everything = jax.tree.map(lambda part: lax.all_gather(part, axis), shard)
    start = jax.tree.map(
        lambda part, zero: jnp.broadcast_to(jnp.asarray(zero, part.dtype), part.shape),
        shard,
        identity,
    )

    def step(k, before):
        reached = k < position
        new = combine(before, jax.tree.map(lambda part: part[k], everything))
        return jax.tree.map(lambda a, b: jnp.where(reached, a, b), new, before)

    return lax.fori_loop(0, peers, step, start)


def rms_scale(values):
    return lax.rsqrt(jnp.mean(values * values, axis=-1, keepdims=True) + EPSILON)


def conv_core(extended, extended_ids, token_ids, weights):
    length = token_ids.shape[0]
    total = jnp.zeros((length, extended.shape[1]), jnp.float32)
    for offset in range(weights.shape[0]):
        same = (extended_ids[offset : offset + length] == token_ids)[:, None]
        total = total + jnp.where(
            same, weights[offset] * extended[offset : offset + length].astype(jnp.float32), 0.0
        )
    return jax.nn.silu(total).astype(jnp.bfloat16)


def block_local(x_blk, b_blk, c_blk, step_blk, rate_blk, ids_blk, before_id):
    length = ids_blk.shape[0]
    position = jnp.arange(length, dtype=jnp.int32)
    prefix = jnp.cumsum(rate_blk, axis=0)
    prefix_t = prefix.T
    same = (ids_blk[:, None] == ids_blk[None, :]) & (position[None, :] <= position[:, None])
    gaps = prefix_t[:, :, None] - prefix_t[:, None, :]
    decay = jnp.where(same[None], jnp.exp(jnp.where(same[None], gaps, 0.0)), 0.0)
    scores = jnp.dot(c_blk, b_blk.T, preferred_element_type=jnp.float32)
    mixing = (scores[None] * decay * step_blk.T[:, None, :]).astype(jnp.bfloat16)
    y_intra = jnp.einsum("hts,shp->thp", mixing, x_blk, preferred_element_type=jnp.float32)
    end_id = ids_blk[-1]
    alive = ids_blk == end_id
    weight_end = (
        jnp.where(
            alive[None, :],
            jnp.exp(jnp.where(alive[None, :], prefix_t[:, -1:] - prefix_t, 0.0)),
            0.0,
        )
        * step_blk.T
    )
    b_weighted = (weight_end[:, :, None] * b_blk[None]).astype(jnp.bfloat16)
    local_state = jnp.einsum("hsn,shp->hpn", b_weighted, x_blk, preferred_element_type=jnp.float32)
    carry_gain = jnp.where(end_id == before_id, jnp.exp(prefix_t[:, -1]), 0.0)
    return (y_intra, local_state, carry_gain, prefix)


def block_inter(c_blk, prefix, ids_blk, before_id, state_in):
    entering = ids_blk == before_id
    inter_scale = jnp.where(entering[:, None], jnp.exp(prefix), 0.0)
    return inter_scale[:, :, None] * jnp.einsum(
        "tn,hpn->thp", c_blk.astype(jnp.float32), state_in, precision=lax.Precision.HIGHEST
    )


def block_last(
    last_index, table, x_blk, b_blk, step_blk, prefix, ids_blk, before_id, state_in, start
):
    length = ids_blk.shape[0]
    position = jnp.arange(length, dtype=jnp.int32)
    prompt_ids = jnp.arange(last_index.shape[0], dtype=jnp.int32)
    local_last = last_index - start
    ends_here = (local_last >= 0) & (local_last < length)
    clipped = jnp.clip(local_last, 0, length - 1)

    def with_ends():
        prefix_t = prefix.T
        prefix_last = prefix[clipped]
        pick = (
            ends_here[:, None]
            & (ids_blk[None, :] == prompt_ids[:, None])
            & (position[None, :] <= clipped[:, None])
        )
        spans = prefix_last[:, :, None] - prefix_t[None]
        weight_last = (
            jnp.where(pick[:, None, :], jnp.exp(jnp.where(pick[:, None, :], spans, 0.0)), 0.0)
            * step_blk.T[None]
        )
        b_last = (weight_last[..., None] * b_blk[None, None]).astype(jnp.bfloat16)
        last_local = jnp.einsum("ghsn,shp->ghpn", b_last, x_blk, preferred_element_type=jnp.float32)
        last_gain = jnp.where(
            (ends_here & (prompt_ids == before_id))[:, None], jnp.exp(prefix_last), 0.0
        )
        return table + last_local + last_gain[:, :, None, None] * state_in[None]

    def without_ends():
        return table

    return lax.cond(jnp.any(ends_here), with_ends, without_ends)


def join_states(earlier, later):
    return (earlier[0] * later[0], later[0][:, None, None] * earlier[1] + later[1])


def on_device(
    hidden,
    token_prompt,
    request_prompt,
    in_gain,
    w_zx,
    w_bc,
    w_dt,
    dt_bias,
    a_log,
    conv_x,
    conv_bc,
    skip_gain,
    out_gain,
    w_out,
):
    tok_dev = hidden.shape[0]
    inner_dev = w_zx.shape[2]
    heads_dev = w_dt.shape[1]
    head_dim = inner_dev // heads_dev
    state_width = w_bc.shape[1] // 2
    taps = conv_x.shape[0]
    dp_index = lax.axis_index("dp")
    head_index = lax.axis_index("head")
    head_count = lax.axis_size("head")
    hidden_f = hidden.astype(jnp.float32)
    normed = (hidden_f * rms_scale(hidden_f) * in_gain).astype(jnp.bfloat16)
    pieces = (
        lax.all_gather(w_zx.astype(jnp.bfloat16), "dp", axis=0, tiled=True),
        lax.all_gather(w_dt.astype(jnp.bfloat16), "dp", axis=0, tiled=True),
        lax.all_gather(w_bc.astype(jnp.bfloat16), "dp", axis=0, tiled=True),
    )
    acc_zx, acc_step, acc_bc = tuple(
        (
            jnp.dot(normed, piece.reshape(piece.shape[0], -1), preferred_element_type=jnp.float32)
            for piece in pieces
        )
    )
    proj_bc = acc_bc.astype(jnp.bfloat16)
    proj_zx = acc_zx.astype(jnp.bfloat16)
    gate_z = proj_zx[:, :inner_dev]
    inner_x = proj_zx[:, inner_dev:]
    proj_dt = acc_step.astype(jnp.bfloat16)
    step_size = jax.nn.softplus(proj_dt.astype(jnp.float32) + dt_bias)
    rate = step_size * -jnp.exp(a_log)
    ids_own = lax.dynamic_slice_in_dim(token_prompt, dp_index * tok_dev, tok_dev)
    rim_start = jnp.maximum(dp_index * tok_dev - (taps - 1), 0)
    rim_ids = lax.dynamic_slice_in_dim(token_prompt, rim_start, taps - 1)
    tail_rows = jnp.concatenate(
        [inner_x[tok_dev - taps + 1 :], proj_bc[tok_dev - taps + 1 :]], axis=1
    )
    rim_rows = from_behind(tail_rows, "dp", 1)
    ext_ids = jnp.concatenate([rim_ids, ids_own])
    conv_inner = conv_core(
        jnp.concatenate([rim_rows[:, :inner_dev], inner_x], axis=0), ext_ids, ids_own, conv_x
    )
    conv_bc_out = conv_core(
        jnp.concatenate([rim_rows[:, inner_dev:], proj_bc], axis=0), ext_ids, ids_own, conv_bc
    )
    blocks = tok_dev // BLOCK
    x_heads = conv_inner.reshape(blocks, BLOCK, heads_dev, head_dim)
    b_conv = conv_bc_out[:, :state_width].reshape(blocks, BLOCK, state_width)
    c_conv = conv_bc_out[:, state_width:].reshape(blocks, BLOCK, state_width)
    step_blocks = step_size.reshape(blocks, BLOCK, heads_dev)
    rate_blocks = rate.reshape(blocks, BLOCK, heads_dev)
    id_blocks = ids_own.reshape(blocks, BLOCK)
    prev_last = jnp.where(dp_index > 0, token_prompt[jnp.maximum(dp_index * tok_dev - 1, 0)], -1)
    before_ids = jnp.concatenate([prev_last[None], id_blocks[:-1, -1]])
    y_intra, local_state, carry_gain, prefix = jax.vmap(block_local)(
        x_heads, b_conv, c_conv, step_blocks, rate_blocks, id_blocks, before_ids
    )

    def advance(carry, item):
        gain_acc, state_acc = carry
        gain, block_state = item
        return (
            (gain_acc * gain, gain[:, None, None] * state_acc + block_state),
            (gain_acc, state_acc),
        )

    unit_gain = jnp.ones((heads_dev,), jnp.float32)
    zero_state = jnp.zeros((heads_dev, head_dim, state_width), jnp.float32)
    (dev_gain, dev_state), (prior_gain, prior_state) = lax.scan(
        advance, (unit_gain, zero_state), (carry_gain, local_state)
    )
    scanned = carried_in((dev_gain, dev_state), "dp", join_states, (unit_gain, zero_state))
    incoming = scanned[1]
    block_in = prior_state + prior_gain[:, :, None, None] * incoming[None]
    prompt_ids = jnp.arange(PROMPTS, dtype=jnp.int32)
    last_index = (
        jnp.sum((token_prompt[None, :] <= prompt_ids[:, None]).astype(jnp.int32), axis=1) - 1
    )
    start_pos = (dp_index * blocks + jnp.arange(blocks, dtype=jnp.int32)) * BLOCK
    y_inter = jax.vmap(block_inter)(c_conv, prefix, id_blocks, before_ids, block_in)

    def collect(table, item):
        xb, bb, sb, pb, ib, fb, stb, ob = item
        return (block_last(last_index, table, xb, bb, sb, pb, ib, fb, stb, ob), None)

    empty_table = jnp.zeros((PROMPTS, heads_dev, head_dim, state_width), jnp.float32)
    local_table, unused = lax.scan(
        collect,
        empty_table,
        (x_heads, b_conv, step_blocks, prefix, id_blocks, before_ids, block_in, start_pos),
    )
    ssd_out = (y_intra + y_inter).reshape(tok_dev, heads_dev, head_dim) + skip_gain[
        None, :, None
    ] * conv_inner.astype(jnp.float32).reshape(tok_dev, heads_dev, head_dim)
    gated = ssd_out.reshape(tok_dev, inner_dev) * jax.nn.silu(gate_z.astype(jnp.float32))
    square_sum = lax.psum(jnp.sum(gated * gated, axis=1), "head")
    scale = lax.rsqrt(square_sum / (inner_dev * head_count) + EPSILON)
    normed_out = (gated * scale[:, None] * out_gain).astype(jnp.bfloat16)
    out_rows = tok_dev // head_count
    own_rows = lax.dynamic_slice_in_dim(hidden_f, head_index * out_rows, out_rows, 0)
    mixed = lax.psum_scatter(
        jnp.dot(normed_out, w_out, preferred_element_type=jnp.float32),
        "head",
        scatter_dimension=0,
        tiled=True,
    )
    layer_out = (own_rows + mixed).astype(jnp.bfloat16)
    table = lax.psum(local_table, "dp")
    one_hot = (request_prompt[:, None] == prompt_ids[None, :]).astype(jnp.float32)
    request_states = jnp.einsum("rg,ghpn->rhpn", one_hot, table, precision=lax.Precision.HIGHEST)
    return (layer_out, request_states)


LANES = 128
TILE_ROWS = 16
NEVER = -1e30
Y_NEAR, Z_NEAR, Z_FAR = 1, 2, 4
PASSED = (Z_FAR, Y_NEAR | Z_FAR)
STAYING = (0, Y_NEAR)
LITTLE = pl.CostEstimate(flops=1000, bytes_accessed=1000, transcendentals=0)


def kernel_params(mebibytes):
    return pltpu.CompilerParams(vmem_limit_bytes=mebibytes << 20)


def in_vmem(count):
    return [pl.BlockSpec(memory_space=pltpu.VMEM)] * count


def exchange(values, axis, bits):
    return lax.ppermute(values, axis, [(i, i ^ bits) for i in range(lax.axis_size(axis))])


def dot32(a, b, a_dim=1, b_dim=0):
    return lax.dot_general(
        a, b, (((a_dim,), (b_dim,)), ((), ())), preferred_element_type=jnp.float32
    )


def silu_tanh(values):
    half = 0.5 * values
    return half + half * jnp.tanh(half)


def widen(columns, pair, head_dim):
    rows = columns.shape[0]
    lane = lax.broadcasted_iota(jnp.int32, (rows, LANES), 1)
    first = jnp.broadcast_to(columns[:, 2 * pair : 2 * pair + 1], (rows, LANES))
    second = jnp.broadcast_to(columns[:, 2 * pair + 1 : 2 * pair + 2], (rows, LANES))
    return jnp.where(lane < head_dim, first, second)


def pack_first_kernel(
    req_ref, wbc_ref, wdt_ref, hidden_ref, first_ref, req_v, bc_v, dt_v, tail_v, dt_wide, sems
):
    rows, width = bc_v.shape
    tok, model = hidden_ref.shape
    arrivals = [
        pltpu.make_async_copy(source, target, sems.at[k])
        for k, (source, target) in enumerate(
            (
                (req_ref, req_v),
                (wdt_ref, dt_v),
                (hidden_ref.at[tok - TILE_ROWS : tok], tail_v),
                (wbc_ref, bc_v),
            )
        )
    ]
    for copy in arrivals:
        copy.start()
    dt_wide[...] = jnp.zeros_like(dt_wide)
    arrivals[0].wait()
    dt_wide[0:1, rows : rows + req_v.shape[1]] = req_v[...].astype(jnp.float32)
    arrivals[1].wait()
    dt_wide[0 : dt_v.shape[0], 0:rows] = dt_v[...]
    arrivals[2].wait()
    upper = lax.broadcasted_iota(jnp.int32, (TILE_ROWS, model), 0) < TILE_ROWS // 2
    below = jnp.where(upper, dt_wide[...], tail_v[...].astype(jnp.float32)).astype(jnp.bfloat16)
    for i in range(model // width):
        at = rows + TILE_ROWS * i
        first_ref[at : at + TILE_ROWS, :] = below[:, i * width : (i + 1) * width]
    arrivals[3].wait()
    first_ref[0:rows, :] = bc_v[...].astype(jnp.bfloat16)


def pack_rest_kernel(wzx_ref, x_ref, gate_ref, tiles_ref, sems):
    rows, inner = x_ref.shape
    arrivals = [
        pltpu.make_async_copy(
            wzx_ref.at[:, :, j * LANES : (j + 1) * LANES], tiles_ref.at[j], sems.at[j]
        )
        for j in range(inner // LANES)
    ]
    for copy in arrivals:
        copy.start()
    for j, copy in enumerate(arrivals):
        copy.wait()
        own = slice(j * LANES, (j + 1) * LANES)
        pair = tiles_ref.at[j].reshape(2 * rows, LANES)
        x_ref[:, own] = pair[pl.ds(1, rows, stride=2), :].astype(jnp.bfloat16)
        gate_ref[:, own] = pair[pl.ds(0, rows, stride=2), :].astype(jnp.bfloat16)


def facts_kernel(
    ids_ref,
    hidden_hbm,
    gain_ref,
    normed_ref,
    meta_ref,
    order_ref,
    pen_ref,
    rows_ref,
    hidden_ref,
    sem,
):
    tok = hidden_ref.shape[0]
    arrival = pltpu.make_async_copy(hidden_hbm, hidden_ref, sem)
    arrival.start()
    position = lax.axis_index("dp")
    start = pl.multiple_of(position * tok, tok)
    ids_i = ids_ref[:, pl.ds(start, tok)]
    behind = pl.multiple_of(jnp.maximum(start - LANES, 0), LANES)
    edge = ids_ref[:, pl.ds(behind, LANES)]
    edge = jnp.where(position > 0, edge, -1)
    ahead = pl.multiple_of(jnp.minimum(start + tok, ids_ref.shape[1] - LANES), LANES)
    after = jnp.where(start + tok < ids_ref.shape[1], ids_ref[:, pl.ds(ahead, LANES)], -1)
    after = after[:, 0:1].astype(jnp.float32)
    long = jnp.concatenate([edge, ids_i], axis=1).astype(jnp.float32)
    ids = ids_i.astype(jnp.float32)
    index = lax.broadcasted_iota(jnp.int32, (1, tok), 1)
    before, last = long[:, LANES - 1 : LANES], ids[:, tok - 1 : tok]
    middle = ids[:, BLOCK - 1 : BLOCK]
    one, zero = jnp.ones((1, tok), jnp.float32), jnp.zeros((1, tok), jnp.float32)
    flag = lambda what: jnp.where(what, one, zero)
    rows = [flag(ids == pltpu.roll(long, k, 1)[:, LANES:]) for k in (1, 2, 3)]
    rows.append(flag(ids == before))
    rows.append(flag((ids == middle) & (index >= BLOCK)))
    rows.append(flag((ids == middle) & (index < BLOCK)))
    rows.append(ids)
    rows.append(flag(ids == last))
    rows.append(flag((ids != last) | (after != last)))
    rows = jnp.concatenate(rows + [jnp.zeros((LANES - len(rows), tok), jnp.float32)], axis=0)
    facts = rows.T
    meta_ref[...] = facts
    column = facts[:, 6:7]
    here = lax.broadcasted_iota(jnp.int32, (tok, tok), 0)
    there = lax.broadcasted_iota(jnp.int32, (tok, tok), 1)
    same = column == ids
    order_ref[0:tok, :] = jnp.where(there <= here, 1.0, 0.0).astype(jnp.bfloat16)
    order_ref[tok:, :] = jnp.where((there > here) & same, 1.0, 0.0).astype(jnp.bfloat16)
    pen = jnp.where((there <= here) & same, 0.0, NEVER)
    for b in range(tok // BLOCK):
        own = slice(b * BLOCK, (b + 1) * BLOCK)
        pen_ref[b] = pen[own, own]
    arrival.wait()
    part = rows_ref.shape[0]
    at = pl.multiple_of(lax.axis_index("head") * part, part)
    rows_ref[...] = hidden_ref[pl.ds(at, part), :]
    hidden = hidden_ref[...].astype(jnp.float32)
    normed_ref[...] = (hidden * rms_scale(hidden) * gain_ref[...]).astype(jnp.bfloat16)


def scale_kernel(w_ref, gain_ref, whole_ref, part_ref):
    rows, model = w_ref.shape
    width = part_ref.shape[1]
    gain = jnp.broadcast_to(gain_ref[...], (LANES, rows)).T
    for j in range(model // LANES):
        own = slice(j * LANES, (j + 1) * LANES)
        whole_ref[:, own] = (w_ref[:, own].astype(jnp.float32) * gain).astype(jnp.bfloat16)
    at = pl.multiple_of((lax.axis_index("dp") % 2) * width, LANES)
    part_ref[...] = whole_ref[:, pl.ds(at, width)]


def gather_rows(position, buffers, rows, w_ref, sems):
    copies = []
    for j, buffer in enumerate(buffers):
        at = pl.multiple_of(jnp.bitwise_xor(position, j) * rows, rows)
        copies.append(
            pltpu.make_async_copy(buffer.at[0:rows], w_ref.at[pl.ds(at, rows)], sems.at[j])
        )
    return copies


def project_rows(normed, halo, w, ext_ref, at, stop):
    ext_ref[0:TILE_ROWS, at:stop] = dot32(halo, w)
    ext_ref[TILE_ROWS:, at:stop] = dot32(normed, w)


def convolve(ext_ref, own, taps, same):
    tok = same[0].shape[0]
    total = ext_ref[TILE_ROWS : TILE_ROWS + tok, own] * taps[3:4]
    for k in range(1, 4):
        total = total + same[k - 1] * (
            ext_ref[TILE_ROWS - k : TILE_ROWS - k + tok, own] * taps[3 - k : 4 - k]
        )
    return silu_tanh(total)


def below_rows(buffer, rows):
    count = (buffer.shape[0] - rows) // TILE_ROWS
    return jnp.concatenate(
        [buffer[rows + i * TILE_ROWS : rows + (i + 1) * TILE_ROWS, :] for i in range(count)], axis=1
    )


def project_shard(normed_ref, buffer, j, steps, dtw_ref):
    rows = dtw_ref.shape[1]
    at = pl.multiple_of(jnp.bitwise_xor(lax.axis_index("dp"), j) * rows, LANES)
    normed = normed_ref[:, pl.ds(at, rows)]
    row = lax.broadcasted_iota(jnp.int32, (TILE_ROWS, rows), 0)
    below = below_rows(buffer, rows)[:, 0:rows].astype(jnp.float32)
    dtw_ref[0:TILE_ROWS, :] = jnp.where(row < steps, below, 0.0).astype(jnp.bfloat16)
    return dot32(normed, buffer[0:rows, :]), dot32(normed, dtw_ref[...], 1, 1)


def first_most_kernel(steps, normed_ref, own_ref, near_ref, most_ref, raw_ref, dtw_ref):
    dtw_ref[...] = jnp.zeros_like(dtw_ref)
    most, raw = project_shard(normed_ref, own_ref, 0, steps, dtw_ref)
    more, more_raw = project_shard(normed_ref, near_ref, 1, steps, dtw_ref)
    most_ref[...] = most + more
    raw_ref[...] = raw + more_raw


def first_kernel(
    normed_ref,
    most_ref,
    most_raw_ref,
    own_ref,
    near_ref,
    far_ref,
    last_ref,
    gain_ref,
    taps_ref,
    meta_ref,
    order_ref,
    bias_ref,
    decay_ref,
    bc_ref,
    step_ref,
    prefix_ref,
    fade_ref,
    halo_ref,
    halo_rows_ref,
    dtw_ref,
    ext_ref,
):
    position = lax.axis_index("dp")
    tok, model = normed_ref.shape
    width = bc_ref.shape[1]
    rows = dtw_ref.shape[1]
    buffers = (own_ref, near_ref, far_ref, last_ref)
    for j, buffer in enumerate(buffers):
        halo_rows_ref[jnp.bitwise_xor(position, j)] = below_rows(buffer, rows)
    halo = halo_rows_ref[jnp.maximum(position - 1, 0)].astype(jnp.float32)
    halo_ref[...] = (halo * rms_scale(halo) * gain_ref[...]).astype(jnp.bfloat16)
    halo_sum = 0.0
    for j, buffer in enumerate(buffers):
        at = pl.multiple_of(jnp.bitwise_xor(position, j) * rows, LANES)
        halo_sum = halo_sum + dot32(halo_ref[:, pl.ds(at, rows)], buffer[0:rows, :])
    ext_ref[0:TILE_ROWS, :] = halo_sum
    dtw_ref[...] = jnp.zeros_like(dtw_ref)
    steps = bias_ref.shape[0]
    most, raw = project_shard(normed_ref, far_ref, 2, steps, dtw_ref)
    more, more_raw = project_shard(normed_ref, last_ref, 3, steps, dtw_ref)
    ext_ref[TILE_ROWS:, :] = most_ref[...] + most + more
    head_lane = lax.broadcasted_iota(jnp.int32, (1, LANES), 1)
    bias = jnp.zeros((1, LANES), jnp.float32)
    decay = jnp.zeros((1, LANES), jnp.float32)
    for h in range(steps):
        bias = jnp.where(head_lane == h, bias_ref[h], bias)
        decay = jnp.where(head_lane == h, decay_ref[h], decay)
    raw = most_raw_ref[...] + raw + more_raw + bias
    step = jnp.maximum(raw, 0.0) + jnp.log1p(jnp.exp(-jnp.abs(raw)))
    step_ref[...] = step
    lane = lax.broadcasted_iota(jnp.int32, (tok, LANES), 1)
    rate = jnp.where(lane < TILE_ROWS, -step * jnp.exp(decay), 0.0)
    high = rate.astype(jnp.bfloat16).astype(jnp.float32)
    rest = rate - high
    mid = rest.astype(jnp.bfloat16).astype(jnp.float32)
    low = rest - mid
    packed = high + pltpu.roll(mid, TILE_ROWS, 1) + pltpu.roll(low, 2 * TILE_ROWS, 1)
    sums = dot32(order_ref[...], packed.astype(jnp.bfloat16))
    sums = (
        sums
        + pltpu.roll(sums, LANES - TILE_ROWS, 1)
        + pltpu.roll(sums, LANES - 2 * TILE_ROWS, 1)
    )
    prefix_ref[...] = sums[0:tok]
    fade_ref[...] = jnp.exp(sums[tok : 2 * tok])
    same = [jnp.broadcast_to(meta_ref[:, k : k + 1], (tok, LANES)) for k in range(3)]
    for j in range(width // LANES):
        own = slice(j * LANES, (j + 1) * LANES)
        bc_ref[:, own] = convolve(ext_ref, own, taps_ref[:, own], same).astype(jnp.bfloat16)


def inner_kernel(
    normed_ref,
    own_ref,
    near_ref,
    far_ref,
    last_ref,
    halo_ref,
    taps_ref,
    meta_ref,
    bc_ref,
    step_ref,
    fade_ref,
    x_ref,
    stepx_ref,
    faded_ref,
    leaving_ref,
    w_ref,
    ext_ref,
    sems,
):
    position = lax.axis_index("dp")
    tok = normed_ref.shape[0]
    inner = x_ref.shape[1]
    rows = own_ref.shape[0]
    head_dim = LANES // 2
    copies = gather_rows(position, (own_ref, near_ref, far_ref, last_ref), rows, w_ref, sems)
    for copy in copies:
        copy.start()
    state_width = leaving_ref.shape[1]
    step = step_ref[...]
    fade = fade_ref[...]
    b_all = bc_ref[:, 0:state_width].astype(jnp.float32)
    b_leaving = (b_all * meta_ref[:, 7:8]).astype(jnp.bfloat16)
    same = [jnp.broadcast_to(meta_ref[:, k : k + 1], (tok, LANES)) for k in range(3)]
    for copy in copies:
        copy.wait()
    project_rows(normed_ref[...], halo_ref[...], w_ref[...], ext_ref, 0, inner)
    for q in range(inner // LANES):
        own = slice(q * LANES, (q + 1) * LANES)
        rounded = convolve(ext_ref, own, taps_ref[:, own], same).astype(jnp.bfloat16)
        x_ref[:, own] = rounded
        scaled = rounded.astype(jnp.float32) * widen(step, q, head_dim)
        stepx_ref[:, own] = scaled.astype(jnp.bfloat16)
        faded = (scaled * widen(fade, q, head_dim)).astype(jnp.bfloat16).T
        faded_ref[own, :] = faded
        leaving_ref[own, :] = dot32(faded, b_leaving).astype(jnp.bfloat16)


def before_device(ids_ref, position, tok):
    return jnp.where(position > 0, ids_ref[jnp.maximum(position * tok - 1, 0)], -1)


def table_kernel(ids_ref, bc_ref, faded_ref, meta_ref, prefix_ref, enter_ref, *table_refs):
    rows, state_width = table_refs[0].shape[1:]
    head_dim = LANES // 2
    tok = bc_ref.shape[0]
    b_all = bc_ref[:, 0:state_width].astype(jnp.float32)
    owner = jnp.where(meta_ref[:, 8:9] > 0.0, meta_ref[:, 6:7], -1.0)
    owner = jnp.broadcast_to(owner, (tok, state_width))
    for g in range(0, table_refs[0].shape[0], 2):
        pair = [jnp.where(owner == g + k, b_all, 0.0).astype(jnp.bfloat16) for k in range(2)]
        sums = dot32(faded_ref[...], jnp.concatenate(pair, axis=1)).astype(jnp.bfloat16)
        for n, table_ref in enumerate(table_refs):
            for k in range(2):
                table_ref[g + k] = sums[
                    n * rows : (n + 1) * rows, k * state_width : (k + 1) * state_width
                ]
    position = lax.axis_index("dp")
    before = before_device(ids_ref, position, tok)
    stop = (position + 1) * tok
    after = ids_ref[jnp.minimum(stop, ids_ref.shape[0] - 1)]
    goes_on = (after == before) & (stop < ids_ref.shape[0])
    ended = (ids_ref[position * tok] == before) & ((ids_ref[stop - 1] != before) | ~goes_on)

    @pl.when(ended)
    def add():
        inside = jnp.where(meta_ref[:, 3:4] > 0.0, prefix_ref[...], 0.0)
        gain = jnp.exp(jnp.min(inside, axis=0, keepdims=True))
        chunk = head_dim // 2
        for n in range(faded_ref.shape[0] // chunk):
            table_ref = table_refs[n * chunk // rows]
            own = slice(n * chunk % rows, n * chunk % rows + chunk)
            h = n * chunk // head_dim
            entering = enter_ref[n * chunk : (n + 1) * chunk, :].astype(jnp.float32)
            old = table_ref[before, own, :].astype(jnp.float32)
            table_ref[before, own, :] = (old + gain[:, h : h + 1] * entering).astype(jnp.bfloat16)


def mixing_kernel(bc_ref, prefix_ref, pen_ref, mixing_ref):
    blocks, heads = mixing_ref.shape[0:2]
    state_width = bc_ref.shape[1] // 2
    half = BLOCK // 2
    for b in range(blocks):
        own_rows = slice(b * BLOCK, (b + 1) * BLOCK)
        scores = dot32(bc_ref[own_rows, state_width:], bc_ref[own_rows, 0:state_width], 1, 1)
        prefix = prefix_ref[own_rows, :]
        across = prefix.T
        for h in range(heads):
            for rows, seen in ((slice(0, half), half), (slice(half, BLOCK), BLOCK)):
                gaps = prefix[rows, h : h + 1] - across[h : h + 1, 0:seen] + pen_ref[b, rows, 0:seen]
                mixing_ref[b, h, rows, 0:seen] = (scores[rows, 0:seen] * jnp.exp(gaps)).astype(
                    jnp.bfloat16
                )


def local_kernel(x_ref, bc_ref, stepx_ref, prefix_ref, meta_ref, mixing_ref, skip_ref, y_ref):
    inner = y_ref.shape[1]
    state_width = bc_ref.shape[1] // 2
    head_dim = LANES // 2
    tok = y_ref.shape[0]
    half = BLOCK // 2
    lane = lax.broadcasted_iota(jnp.int32, (BLOCK, LANES), 1)
    for b in range(tok // BLOCK):
        own_rows = slice(b * BLOCK, (b + 1) * BLOCK)
        c_blk = bc_ref[own_rows, state_width:]
        if b > 0:
            before_rows = slice((b - 1) * BLOCK, b * BLOCK)
            before = prefix_ref[before_rows, :]
            carried = jnp.exp(prefix_ref[own_rows, :] - before[BLOCK - 1 : BLOCK, :])
            carried = carried * meta_ref[own_rows, 4:5]
            fade = jnp.exp(before[BLOCK - 1 : BLOCK, :] - before)
            b_before = bc_ref[before_rows, 0:state_width].astype(jnp.float32)
            b_before = (b_before * meta_ref[before_rows, 5:6]).astype(jnp.bfloat16)
        for q in range(inner // LANES):
            own = slice(q * LANES, (q + 1) * LANES)
            x_pair = x_ref[own_rows, own].astype(jnp.float32)
            out = x_pair * jnp.where(lane < head_dim, skip_ref[2 * q], skip_ref[2 * q + 1])
            if b > 0:
                faded = stepx_ref[before_rows, own].astype(jnp.float32) * widen(fade, q, head_dim)
                middle = dot32(faded.astype(jnp.bfloat16).T, b_before).astype(jnp.bfloat16)
                out = out + widen(carried, q, head_dim) * dot32(c_blk, middle, 1, 1)
            sx = stepx_ref[own_rows, own].astype(jnp.float32)
            sides = [jnp.where(lane < head_dim, sx, 0.0), jnp.where(lane >= head_dim, sx, 0.0)]
            sides = [side.astype(jnp.bfloat16) for side in sides]
            for rows, seen in ((slice(0, half), half), (slice(half, BLOCK), BLOCK)):
                part = out[rows]
                for side in range(2):
                    mixing = mixing_ref[b, 2 * q + side, rows, 0:seen]
                    part = part + dot32(mixing, sides[side][0:seen])
                y_ref[b * BLOCK + rows.start : b * BLOCK + rows.stop, own] = part


def z_most_kernel(normed_ref, own_ref, near_ref, far_ref, most_ref):
    position = lax.axis_index("dp")
    rows = own_ref.shape[0]
    total = 0.0
    for j, w_ref in enumerate((own_ref, near_ref, far_ref)):
        at = pl.multiple_of(jnp.bitwise_xor(position, j) * rows, LANES)
        total = total + dot32(normed_ref[:, pl.ds(at, rows)], w_ref[...])
    most_ref[...] = total


def z_last_kernel(normed_ref, last_ref, most_ref, gate_ref):
    rows = last_ref.shape[0]
    at = pl.multiple_of(jnp.bitwise_xor(lax.axis_index("dp"), 3) * rows, LANES)
    gate_ref[...] = silu_tanh(most_ref[...] + dot32(normed_ref[:, pl.ds(at, rows)], last_ref[...]))


def gate_kernel(enter_ref, bc_ref, prefix_ref, meta_ref, y_ref, z_ref, arrived_ref, *outs):
    scratch = outs[-1]
    inner = y_ref.shape[1]
    state_width = enter_ref.shape[1]
    head_dim = LANES // 2
    c_all = bc_ref[:, state_width:]
    inter = dot32(c_all, enter_ref[...], 1, 1)
    carried = jnp.exp(prefix_ref[...]) * meta_ref[:, 3:4]
    for q in range(inner // LANES):
        own = slice(q * LANES, (q + 1) * LANES)
        value = y_ref[:, own] + widen(carried, q, head_dim) * inter[:, own]
        scratch[:, own] = (value * z_ref[:, own]).astype(jnp.bfloat16)
    head = lax.axis_index("head")
    part = outs[0].shape[0] // 2
    for n, related in enumerate((PASSED, STAYING)):
        for out, owner in zip(outs[2 * n : 2 * n + 2], (head, jnp.bitwise_xor(head, Z_NEAR))):
            for k, bits in enumerate(related):
                at = pl.multiple_of(jnp.bitwise_xor(owner, bits) * part, part)
                out[k * part : (k + 1) * part, :] = scratch[pl.ds(at, part), :]


def pick_kernel(own_ref, far_ref, *refs):
    tables, others, (keep_ref, send_ref, send_last_ref, far_v, sem) = refs[:4], refs[4:8], refs[8:]
    count = keep_ref.shape[0]
    part = tables[0].shape[1]
    rows = far_ref.shape[0] - 6 * TILE_ROWS
    width = far_ref.shape[1]
    model_rows = rows // width
    at = rows + TILE_ROWS * model_rows
    lanes = rows - model_rows * width
    arrival = pltpu.make_async_copy(
        far_ref.at[at : at + TILE_ROWS, lanes : lanes + LANES], far_v, sem
    )
    arrival.start()

    def pick(k, g):
        total = tables[k][g].astype(jnp.float32) + others[k][g].astype(jnp.float32)
        return total.astype(jnp.bfloat16)

    for r in range(count):
        for k in range(len(tables)):
            keep_ref[r, k * part : (k + 1) * part] = pick(k, own_ref[r])
    arrival.wait()
    wanted = far_v[...].astype(jnp.float32)[0:1, :]
    lane = lax.broadcasted_iota(jnp.int32, (1, LANES), 1)
    for r in range(count):
        g = jnp.sum(jnp.where(lane == r, wanted, 0.0)).astype(jnp.int32)
        for k in range(len(tables) - 1):
            send_ref[r, k * part : (k + 1) * part] = pick(k, g)
        send_last_ref[r] = pick(len(tables) - 1, g)


def split_squares(squares):
    lane = lax.broadcasted_iota(jnp.int32, (squares.shape[0], LANES), 1)
    high = squares.astype(jnp.bfloat16).astype(jnp.float32)
    return jnp.where(lane == 0, high, squares - high).astype(jnp.bfloat16)


def joined_squares(ref, model):
    high = ref[:, model : model + 1].astype(jnp.float32)
    return high + ref[:, model + 1 : model + 2].astype(jnp.float32)


def out_kernel(kept_ref, got_ref, own_ref, part_ref, near_ref, wide_out, *refs):
    outs, sums_ref = refs[:-1], refs[-1]
    core = lax.axis_index("dp") % 2
    width = part_ref.shape[1]
    rows, model = sums_ref.shape
    part = wide_out.shape[0]
    kept, got = kept_ref[...], got_ref[...]
    squares = jnp.zeros((rows, 1), jnp.float32)
    for value in (kept, got):
        wide = value.astype(jnp.float32)
        squares = squares + jnp.sum(wide * wide, axis=1, keepdims=True)
    for j, other_ref in enumerate((part_ref, near_ref)):
        at = pl.multiple_of(jnp.bitwise_xor(core, j) * width, LANES)
        own = dot32(kept, own_ref[:, pl.ds(at, width)])
        sums_ref[:, pl.ds(at, width)] = own + dot32(got, other_ref[...])
    wide_out[:, 0:model] = sums_ref[0:part, :]
    wide_out[:, model:] = jnp.broadcast_to(squares[0:part], (part, LANES))
    size = part // len(outs)
    for k, out in enumerate(outs):
        own = slice(part + k * size, part + (k + 1) * size)
        out[:, 0:model] = sums_ref[own, :].astype(jnp.bfloat16)
        out[:, model:] = split_squares(squares[own])


def pass_kernel(pass_ref, cross_ref, arrived_ref, out_ref):
    model = out_ref.shape[1] - LANES
    total = pass_ref[:, 0:model] + cross_ref[:, 0:model].astype(jnp.float32)
    out_ref[:, 0:model] = total.astype(jnp.bfloat16)
    squares = pass_ref[:, model : model + 1] + joined_squares(cross_ref, model)
    out_ref[:, model:] = split_squares(squares)


def finish_kernel(inner_total, hidden_ref, joined_ref, keep_ref, passed_ref, *refs):
    nears, out_ref = refs[:-1], refs[-1]
    model = hidden_ref.shape[1]
    size = nears[0].shape[0]
    for k, near_ref in enumerate(nears):
        own = slice(k * size, (k + 1) * size)
        squares = keep_ref[own, model : model + 1] + joined_squares(near_ref, model)
        squares = squares + joined_squares(passed_ref.at[own], model)
        scale = lax.rsqrt(squares / inner_total + EPSILON)
        total = keep_ref[own, 0:model] + near_ref[:, 0:model].astype(jnp.float32)
        total = total + passed_ref[own, 0:model].astype(jnp.float32)
        hidden = hidden_ref[own, :].astype(jnp.float32)
        out_ref[own, :] = (hidden + scale * total).astype(jnp.bfloat16)


def join_kernel(keep_ref, *refs):
    fars, (out_ref, done_ref) = refs[:-2], refs[-2:]
    done_ref[...] = jnp.zeros_like(done_ref)
    at = 0
    for far_ref in fars:
        own = slice(at, at + far_ref.shape[1])
        out_ref[:, own] = keep_ref[:, own].astype(jnp.float32) + far_ref[...].astype(jnp.float32)
        at += far_ref.shape[1]


def fused_on_device(
    hidden,
    token_prompt,
    request_prompt,
    in_gain,
    w_zx,
    w_bc,
    w_dt,
    dt_bias,
    a_log,
    conv_x,
    conv_bc,
    skip_gain,
    out_gain,
    w_out,
):
    tok, model = hidden.shape
    rows = w_zx.shape[0]
    inner = w_zx.shape[2]
    heads = w_dt.shape[1]
    state_width = w_bc.shape[1] // 2
    tiles = inner // LANES
    peers = lax.axis_size("dp")
    head_count = lax.axis_size("head")
    bf16, f32 = jnp.bfloat16, jnp.float32
    shape = jax.ShapeDtypeStruct
    smem = pl.BlockSpec(memory_space=pltpu.SMEM)
    anywhere = pl.BlockSpec(memory_space=pl.ANY)
    in_hbm = pl.BlockSpec(memory_space=pltpu.HBM)

    extra = TILE_ROWS * (model // (2 * state_width))
    first_own = pl.pallas_call(
        pack_first_kernel,
        name="pack_first_weights",
        out_shape=shape((rows + extra, 2 * state_width), bf16),
        in_specs=[in_hbm] * 4,
        out_specs=in_vmem(1)[0],
        scratch_shapes=[
            pltpu.VMEM((1, request_prompt.shape[0]), jnp.int32),
            pltpu.VMEM(w_bc.shape, f32),
            pltpu.VMEM((heads, rows), f32),
            pltpu.VMEM((TILE_ROWS, model), bf16),
            pltpu.VMEM((TILE_ROWS, model), f32),
            pltpu.SemaphoreType.DMA((4,)),
        ],
        compiler_params=kernel_params(60),
        cost_estimate=LITTLE,
    )(request_prompt[None, :], w_bc, w_dt.T, hidden)
    first_far = exchange(first_own, "dp", 2)
    first_near = exchange(first_own, "dp", 1)
    x_own, gate_own = pl.pallas_call(
        pack_rest_kernel,
        name="pack_x_and_gate_weights",
        out_shape=(shape((rows, inner), bf16), shape((rows, inner), bf16)),
        in_specs=[in_hbm],
        out_specs=tuple(in_vmem(2)),
        scratch_shapes=[
            pltpu.VMEM((inner // LANES, rows, 2, LANES), f32),
            pltpu.SemaphoreType.DMA((inner // LANES,)),
        ],
        compiler_params=kernel_params(8),
        cost_estimate=LITTLE,
    )(w_zx)

    blocks = tok // BLOCK
    normed, meta, order, pen, own_hidden = pl.pallas_call(
        facts_kernel,
        name="norm_and_token_facts",
        out_shape=(
            shape((tok, model), bf16),
            shape((tok, LANES), f32),
            shape((2 * tok, tok), bf16),
            shape((blocks, BLOCK, BLOCK), f32),
            shape((tok // head_count, model), bf16),
        ),
        in_specs=in_vmem(1) + [in_hbm] + in_vmem(1),
        out_specs=tuple(in_vmem(5)),
        scratch_shapes=[pltpu.VMEM((tok, model), bf16), pltpu.SemaphoreType.DMA],
        compiler_params=kernel_params(16),
        cost_estimate=LITTLE,
    )(token_prompt[None, :], hidden, in_gain[None, :])
    scaled_out, half_out = pl.pallas_call(
        scale_kernel,
        name="scale_out_rows",
        out_shape=(shape(w_out.shape, bf16), shape((inner, model // 2), bf16)),
        in_specs=in_vmem(2),
        out_specs=tuple(in_vmem(2)),
        compiler_params=kernel_params(8),
        cost_estimate=LITTLE,
    )(w_out, out_gain[None, :])
    out_part = exchange(half_out, "head", Z_NEAR)
    out_near = exchange(out_part, "dp", 1)

    x_far = exchange(x_own, "dp", 2)
    first_most, first_raw = pl.pallas_call(
        functools.partial(first_most_kernel, heads),
        name="project_b_c_and_steps_of_chip",
        out_shape=(shape((tok, 2 * state_width), f32), shape((tok, LANES), f32)),
        in_specs=in_vmem(3),
        out_specs=tuple(in_vmem(2)),
        scratch_shapes=[pltpu.VMEM((LANES, rows), bf16)],
        compiler_params=kernel_params(8),
        cost_estimate=LITTLE,
    )(normed, first_own, first_near)
    first_far, first_most, first_raw, meta, order, pen, x_own, gate_own = lax.optimization_barrier(
        (first_far, first_most, first_raw, meta, order, pen, x_own, gate_own)
    )
    x_near = exchange(x_own, "dp", 1)
    gate_near = exchange(gate_own, "dp", 1)
    first_last = exchange(first_far, "dp", 1)
    bc, step, prefix, fade, halo = pl.pallas_call(
        first_kernel,
        name="project_b_c_and_steps",
        out_shape=(
            shape((tok, 2 * state_width), bf16),
            shape((tok, LANES), f32),
            shape((tok, LANES), f32),
            shape((tok, LANES), f32),
            shape((TILE_ROWS, model), bf16),
        ),
        in_specs=in_vmem(11) + [smem] * 2,
        out_specs=tuple(in_vmem(5)),
        scratch_shapes=[
            pltpu.VMEM((peers, TILE_ROWS, model), bf16),
            pltpu.VMEM((LANES, rows), bf16),
            pltpu.VMEM((TILE_ROWS + tok, 2 * state_width), f32),
        ],
        compiler_params=kernel_params(14),
        cost_estimate=LITTLE,
    )(
        normed,
        first_most,
        first_raw,
        first_own,
        first_near,
        first_far,
        first_last,
        in_gain[None, :],
        conv_bc,
        meta,
        order,
        dt_bias,
        a_log,
    )
    mixing = pl.pallas_call(
        mixing_kernel,
        name="mixing_weights",
        out_shape=shape((blocks, heads, BLOCK, BLOCK), bf16),
        in_specs=in_vmem(3),
        out_specs=in_vmem(1)[0],
        compiler_params=kernel_params(8),
        cost_estimate=LITTLE,
    )(bc, prefix, pen)
    x_far, gate_own, bc, step, prefix, fade, halo, mixing = lax.optimization_barrier(
        (x_far, gate_own, bc, step, prefix, fade, halo, mixing)
    )
    x_last = exchange(x_far, "dp", 1)
    gate_far = exchange(gate_own, "dp", 2)
    x, stepx, faded, leaving = pl.pallas_call(
        inner_kernel,
        name="project_and_convolve_x",
        out_shape=(
            shape((tok, inner), bf16),
            shape((tok, inner), bf16),
            shape((inner, tok), bf16),
            shape((inner, state_width), bf16),
        ),
        in_specs=in_vmem(1) + [anywhere] * 4 + in_vmem(6),
        out_specs=tuple(in_vmem(4)),
        scratch_shapes=[
            pltpu.VMEM((model, inner), bf16),
            pltpu.VMEM((TILE_ROWS + tok, inner), f32),
            pltpu.SemaphoreType.DMA((peers,)),
        ],
        compiler_params=kernel_params(14),
        cost_estimate=LITTLE,
    )(
        normed,
        x_own,
        x_near,
        x_far,
        x_last,
        halo,
        conv_x,
        meta,
        bc,
        step,
        fade,
    )

    entering = lax.ppermute(leaving, "dp", [(i, i + 1) for i in range(peers - 1)])

    y_local = pl.pallas_call(
        local_kernel,
        name="mix_within_blocks",
        out_shape=shape((tok, inner), f32),
        in_specs=in_vmem(6) + [smem],
        out_specs=in_vmem(1)[0],
        compiler_params=kernel_params(14),
        cost_estimate=LITTLE,
    )(x, bc, stepx, prefix, meta, mixing, skip_gain)
    gate_far, gate_near, entering, y_local = lax.optimization_barrier(
        (gate_far, gate_near, entering, y_local)
    )
    gate_last = exchange(gate_far, "dp", 1)
    tables = pl.pallas_call(
        table_kernel,
        name="sum_ended_states",
        out_shape=(shape((PROMPTS, inner // 4, state_width), bf16),) * 4,
        in_specs=[smem] + in_vmem(5),
        out_specs=tuple(in_vmem(4)),
        compiler_params=kernel_params(8),
        cost_estimate=LITTLE,
    )(token_prompt, bc, faded, meta, prefix, entering)
    tables_near = [exchange(table, "dp", 1) for table in tables]

    gate_most = pl.pallas_call(
        z_most_kernel,
        name="project_gate_most",
        out_shape=shape((tok, inner), f32),
        in_specs=in_vmem(4),
        out_specs=in_vmem(1)[0],
        compiler_params=kernel_params(8),
        cost_estimate=LITTLE,
    )(normed, gate_own, gate_near, gate_far)
    gate = pl.pallas_call(
        z_last_kernel,
        name="project_gate_last",
        out_shape=shape((tok, inner), f32),
        in_specs=in_vmem(3),
        out_specs=in_vmem(1)[0],
        compiler_params=kernel_params(8),
        cost_estimate=LITTLE,
    )(normed, gate_last, gate_most)

    out_rows = tok // head_count
    kept_first, sent_first, kept_rest, sent_rest = pl.pallas_call(
        gate_kernel,
        name="add_entering_and_gate",
        out_shape=(shape((2 * out_rows, inner), bf16),) * 4,
        in_specs=in_vmem(6) + [anywhere],
        out_specs=tuple(in_vmem(4)),
        scratch_shapes=[pltpu.VMEM((tok, inner), bf16)],
        compiler_params=kernel_params(8),
        cost_estimate=LITTLE,
    )(entering, bc, prefix, meta, y_local, gate, out_near)
    got_first = exchange(sent_first, "head", Z_NEAR)
    got_rest = exchange(sent_rest, "head", Z_NEAR)

    requests = request_prompt.shape[0]
    part = inner // 4
    keep, *sends = pl.pallas_call(
        pick_kernel,
        name="pick_request_states",
        out_shape=tuple(
            shape((requests, size, state_width), bf16) for size in (inner, inner - part, part)
        ),
        in_specs=[smem, anywhere] + in_vmem(8),
        out_specs=tuple(in_vmem(3)),
        scratch_shapes=[pltpu.VMEM((TILE_ROWS, LANES), bf16), pltpu.SemaphoreType.DMA],
        compiler_params=kernel_params(8),
        cost_estimate=LITTLE,
    )(request_prompt, first_far, *tables, *tables_near)
    fars = [exchange(send, "dp", 2) for send in sends]

    sums_shape = (out_rows, model + LANES)

    def project(kept, got, pieces):
        piece = (out_rows // pieces, model + LANES)
        return pl.pallas_call(
            out_kernel,
            name="project_out",
            out_shape=(shape(sums_shape, f32),) + (shape(piece, bf16),) * pieces,
            in_specs=in_vmem(5),
            out_specs=tuple(in_vmem(1 + pieces)),
            scratch_shapes=[pltpu.VMEM((2 * out_rows, model), f32)],
            compiler_params=kernel_params(8),
            cost_estimate=LITTLE,
        )(kept, got, scaled_out, out_part, out_near)

    sums_pass, sums_cross = project(kept_first, got_first, 1)
    cross = exchange(sums_cross, "head", Y_NEAR)
    passed = pl.pallas_call(
        pass_kernel,
        name="add_sums_to_pass_on",
        out_shape=shape(sums_shape, bf16),
        in_specs=in_vmem(2) + [anywhere],
        out_specs=in_vmem(1)[0],
        compiler_params=kernel_params(4),
        cost_estimate=LITTLE,
    )(sums_pass, cross, got_rest)
    got_rest, passed = lax.optimization_barrier((got_rest, passed))
    passed = exchange(passed, "head", Z_FAR)
    sums_keep, *sums_near = project(kept_rest, got_rest, 2)
    sums_near = [exchange(part, "head", Y_NEAR) for part in sums_near]
    request_states, joined = pl.pallas_call(
        join_kernel,
        name="join_request_states",
        out_shape=(shape((requests, inner, state_width), f32), shape((8, LANES), f32)),
        in_specs=in_vmem(3),
        out_specs=tuple(in_vmem(2)),
        compiler_params=kernel_params(6),
        cost_estimate=LITTLE,
    )(keep, *fars)
    layer_out = pl.pallas_call(
        functools.partial(finish_kernel, inner * head_count),
        name="scale_and_add_hidden",
        out_shape=shape((out_rows, model), bf16),
        in_specs=in_vmem(1) + [anywhere] + in_vmem(4),
        out_specs=in_vmem(1)[0],
        compiler_params=kernel_params(4),
        cost_estimate=LITTLE,
    )(own_hidden, joined, sums_keep, passed, *sums_near)
    return (
        layer_out,
        request_states.reshape(requests, heads, inner // heads, state_width),
    )


def fits_fused(mesh):
    return dict(mesh.shape) == {"dp": 4, "head": 8}


def solution(mesh):
    in_specs = (
        P("dp", None),
        P(),
        P("dp"),
        P(),
        P("dp", None, "head"),
        P("dp", None),
        P("dp", "head"),
        P("head"),
        P("head"),
        P(None, "head"),
        P(),
        P("head"),
        P("head"),
        P("head", None),
    )
    out_specs = (P(("dp", "head"), None), P("dp", "head", None, None))
    program = fused_on_device if fits_fused(mesh) else on_device
    return jax.shard_map(
        program, mesh=mesh, in_specs=in_specs, out_specs=out_specs, check_vma=False
    )
```
